32 devices in a mesh: dp: 8 (over z, x), mp: 4 (over y, core).
Axes of the slice: x: 2, y: 2, z: 4, core: 2. Of those that a mesh axis runs over, the one named last changes fastest.
Arguments:
- dense_values: float32 [4096, 13], P('dp'), may hold values from 0 to 14, as said below
- field_ids: int32 [26, 4, 4096], P(None, None, 'dp'), may hold values from 0 to 65535
- lengths: int32 [26, 4096], P(None, 'dp'), may hold values from 1 to 4, as said below
- labels: int32 [4096], P('dp'), may hold values 0 or 1
- num_embed: float32 [13, 16], replicated, may hold values from -6 to 6
- embed_table: float32 [16, 65536], P(None, 'dp'), may hold values from -6 to 6
- gate_weight: bfloat16 [2, 624, 624], P(None, 'mp'), may hold values from -0.25 to 0.25
- gate_bias: float32 [2, 624], P(None, 'mp'), may hold values from -3 to 3
- narrow_first: bfloat16 [400, 624], P('mp'), may hold values from -0.25 to 0.25
- narrow_rest: bfloat16 [2, 400, 400], P(None, 'mp'), may hold values from -0.3125 to 0.3125
- narrow_gain: float32 [3, 400], P(None, 'mp'), may hold values from 0.1 to 1.9
- narrow_shift: float32 [3, 400], P(None, 'mp'), may hold values from -3 to 3
- broad_first: bfloat16 [800, 624], P('mp'), may hold values from -0.25 to 0.25
- broad_rest: bfloat16 [800, 800], P('mp'), may hold values from -0.21875 to 0.21875
- broad_gain: float32 [2, 800], P(None, 'mp'), may hold values from 0.1 to 1.9
- broad_shift: float32 [2, 800], P(None, 'mp'), may hold values from -3 to 3
- joining_left: float32 [400], replicated, may hold values from -0.3125 to 0.3125
- joining_right: float32 [800], replicated, may hold values from -0.21875 to 0.21875
- joining_pair: float32 [50, 8, 16], replicated, may hold values from -0.15625 to 0.15625
- joining_bias: float32 [1], replicated, may hold values from -3 to 3
Outputs:
- logits: float32 [4096], P('dp')
- num_embed_grad: float32 [13, 16], replicated
- embed_table_grad: float32 [16, 65536], P(None, 'dp')
- gate_weight_grad: float32 [2, 624, 624], P(None, 'mp')
- gate_bias_grad: float32 [2, 624], P(None, 'mp')
- narrow_first_grad: float32 [400, 624], P('mp')
- narrow_rest_grad: float32 [2, 400, 400], P(None, 'mp')
- narrow_gain_grad: float32 [3, 400], P(None, 'mp')
- narrow_shift_grad: float32 [3, 400], P(None, 'mp')
- broad_first_grad: float32 [800, 624], P('mp')
- broad_rest_grad: float32 [800, 800], P('mp')
- broad_gain_grad: float32 [2, 800], P(None, 'mp')
- broad_shift_grad: float32 [2, 800], P(None, 'mp')
- joining_left_grad: float32 [400], replicated
- joining_right_grad: float32 [800], replicated
- joining_pair_grad: float32 [50, 8, 16], replicated
- joining_bias_grad: float32 [1], replicated
The draws below stay inside these ranges and needn't reach their ends.
Inputs may be any that keep to these rules, and one draw needn't show every extreme that they name: `lengths`: slots at or past a bag's length hold padding ids that count for nothing. `dense_values`: numeric features are positive.
All inputs are finite; a program needn't handle non-finite values. No bound on the sum of `labels` on one device may be relied on, other than what follows from the above.
Results may differ from the reference program's by a relative error of at most 0.015.
The reference program's roundings to bfloat16 on the way count: a program that leaves them out, or rounds other values in their place, can miss the bound.
Values may be sent and summed in bfloat16 or wider, within the bound.
A program may use at most 320 MiB of HBM per device.

```python
import math
import jax
import jax.numpy as jnp
import numpy as np
from jax import lax

NUM = 13
CAT = 26
FDIM = 16
H1 = 400
H2 = 800
HEADS = 50
BAG = 4
D = 624
HX = 8
HY = 16
TOKENS = 4096
VOCAB = 65536


def draw_dense_values(key, part):
    key = jax.random.fold_in(key, 7)
    ramp = jnp.arange(TOKENS, dtype=jnp.float32)[:, None] / max(TOKENS - 1, 1)
    return jnp.exp(0.5 * jnp.clip(jax.random.normal(key, (TOKENS, NUM), jnp.float32), -3.0, 3.0)) * (1.0 + 2.0 * ramp)


def draw_lengths(key, part):
    key = jax.random.fold_in(key, 11)
    first_key, second_key = jax.random.split(key)
    levels = jax.random.randint(first_key, (CAT, TOKENS), 0, BAG.bit_length())
    spans = jnp.right_shift(jnp.full((CAT, TOKENS), BAG, jnp.int32), levels)
    picked = 1 + jax.random.randint(second_key, (CAT, TOKENS), 0, BAG) % spans
    return picked.at[0, 0].set(BAG).astype(jnp.int32)


def set_ends(values, rng, smallest, top_value):
    longest = values.shape.index(max(values.shape))
    spots = []
    for shift in (0, 1):
        where = [jax.random.randint(jax.random.fold_in(rng, axis), (), 0, length) for axis, length in enumerate(values.shape)]
        where[longest] = (where[longest] + shift) % values.shape[longest]
        spots.append(tuple(where))
    return values.at[spots[0]].set(smallest).at[spots[1]].set(top_value)


def block_levels(rng, extent, shards, low, largest):
    def one(dim, parts):
        heights = jax.random.uniform(jax.random.fold_in(jax.random.fold_in(rng, 6), dim), (parts,), jnp.float32, low / len(shards), largest / len(shards))
        return jnp.repeat(jnp.exp(heights), extent[dim] // parts).reshape((-1,) + (1,) * (len(extent) - dim - 1))

    gain = one(*shards[0])
    for cut in shards[1:]:
        gain = gain * one(*cut)
    return gain


def cumulative_ranks(count, slope):
    portions = [(1 << 20) // math.isqrt(rank ** slope) + 1 for rank in range(1, count + 1)]
    width = 1 + sum(portions) // (1 << 30)
    return np.cumsum(np.array([max(1, weight // width) for weight in portions]))


def skewed_ids(key, shape, amount, lean):
    grid = cumulative_ranks(amount, lean)
    lot = jax.random.randint(jax.random.fold_in(key, 1), shape, 0, int(grid[amount - 1]))
    rank = jnp.searchsorted(jnp.asarray(grid, jnp.int32), lot, side="right")
    return jax.random.permutation(jax.random.fold_in(key, 2), amount)[rank].astype(jnp.int32)


def scatter_about(rng, shape, spread, reach, cuts=(), held_as=jnp.bfloat16):
    level = block_levels(rng, shape, cuts, -0.22, 0.18) if cuts else 1.0
    array = jax.random.normal(rng, shape, jnp.float32) * spread * level
    return jnp.minimum(jnp.maximum(array, -reach), reach).astype(held_as)


def setup_inputs(seed: int = 0) -> dict:
    seeds = jax.random.split(jax.random.key(seed), 21)
    return {
        "dense_values": draw_dense_values(jax.random.fold_in(seeds[20], 71), 0),
        "field_ids": set_ends(skewed_ids(seeds[1], (CAT, BAG, TOKENS), VOCAB, 2), jax.random.fold_in(seeds[1], 3), 0, VOCAB - 1).astype(jnp.int32),
        "lengths": draw_lengths(jax.random.fold_in(seeds[20], 71), 0),
        "labels": set_ends((jax.random.randint(seeds[3], (TOKENS,), 0, 4) < 1).astype(jnp.int32), jax.random.fold_in(seeds[3], 1), 0, 1),
        "num_embed": scatter_about(seeds[4], (NUM, FDIM), 1.0, 6.0, (), jnp.float32),
        "embed_table": scatter_about(seeds[5], (FDIM, VOCAB), 1.0, 6.0, ((1, 8),), jnp.float32),
        "gate_weight": scatter_about(seeds[6], (2, D, D), D ** -0.5, 0.25, ((1, 4),)),
        "gate_bias": scatter_about(seeds[7], (2, D), 0.5, 3.0, ((1, 4),), jnp.float32),
        "narrow_first": scatter_about(seeds[8], (H1, D), D ** -0.5, 0.25, ((0, 4),)),
        "narrow_rest": scatter_about(seeds[9], (2, H1, H1), H1 ** -0.5, 0.3125, ((1, 4),)),
        "narrow_gain": jnp.clip(1.0 + 0.18 * jax.random.normal(seeds[10], (3, H1), jnp.float32), 0.1, 1.9),
        "narrow_shift": scatter_about(seeds[11], (3, H1), 0.5, 3.0, ((1, 4),), jnp.float32),
        "broad_first": scatter_about(seeds[12], (H2, D), D ** -0.5, 0.25, ((0, 4),)),
        "broad_rest": scatter_about(seeds[13], (H2, H2), H2 ** -0.5, 0.21875, ((0, 4),)),
        "broad_gain": jnp.clip(1.0 + 0.18 * jax.random.normal(seeds[14], (2, H2), jnp.float32), 0.1, 1.9),
        "broad_shift": scatter_about(seeds[15], (2, H2), 0.5, 3.0, ((1, 4),), jnp.float32),
        "joining_left": scatter_about(seeds[16], (H1,), H1 ** -0.5, 0.3125, (), jnp.float32),
        "joining_right": scatter_about(seeds[17], (H2,), H2 ** -0.5, 0.21875, (), jnp.float32),
        "joining_pair": scatter_about(seeds[18], (HEADS, HX, HY), (HX * HY * HEADS // 4) ** -0.5, 0.15625, (), jnp.float32),
        "joining_bias": scatter_about(seeds[19], (1,), 1.0, 3.0, (), jnp.float32),
    }


@jax.custom_vjp
def low(v):
    return lax.optimization_barrier(v.astype(jnp.bfloat16)).astype(jnp.float32)

@jax.custom_vjp
def low_back(v):
    return v

def low_keep(v):
    return (low(v), None)

def low_pass(kept, grad):
    return (grad,)

def back_keep(v):
    return (v, None)

def back_low(kept, grad):
    return (low(grad),)
low.defvjp(low_keep, low_pass)
low_back.defvjp(back_keep, back_low)

def stream(inputs, weights, gain_rows, shifts):
    highest = lax.Precision.HIGHEST
    for position in range(len(weights)):
        hidden = low_back(jnp.dot(inputs, weights[position].T, precision=highest))
        batch_mean = lax.optimization_barrier(jnp.mean(hidden, axis=0))
        batch_var = lax.optimization_barrier(jnp.mean(hidden * hidden, axis=0)) - batch_mean * batch_mean
        normed = (hidden - batch_mean) * lax.rsqrt(batch_var + 1e-05)
        inputs = low(jax.nn.silu(gain_rows[position] * normed + shifts[position]))
    return inputs

def reference(dense_values, field_ids, lengths, labels, num_embed, embed_table, gate_weight, gate_bias, narrow_first, narrow_rest, narrow_gain, narrow_shift, broad_first, broad_rest, broad_gain, broad_shift, joining_left, joining_right, joining_pair, joining_bias):
    highest = lax.Precision.HIGHEST
    positions = lax.broadcasted_iota(jnp.int32, field_ids.shape, 1)
    live_mask = (positions < lengths[:, None, :]).astype(jnp.float32)
    batch_rows = dense_values.shape[0]

    def forward(num_embed, embed_table, gate_weight, gate_bias, narrow_first, narrow_rest, narrow_gain, narrow_shift, broad_first, broad_rest, broad_gain, broad_shift, joining_left, joining_right, joining_pair, joining_bias):
        numeric = (dense_values[:, :, None] * num_embed[None, :, :]).reshape(batch_rows, -1)
        pooled_t = jnp.zeros((embed_table.shape[0], field_ids.shape[0], batch_rows), jnp.float32)
        for position in range(field_ids.shape[1]):
            pooled_t = pooled_t + live_mask[None, :, position, :] * embed_table[:, field_ids[:, position, :]]
        pooled = jnp.transpose(pooled_t, (2, 1, 0)).reshape(batch_rows, -1)
        features = low(low_back(jnp.concatenate([numeric, pooled], axis=1)))
        gated_list = []
        for position in range(2):
            gate_input = low_back(jnp.dot(features, gate_weight[position].T, precision=highest) + gate_bias[position])
            gated_list.append(low(features * (2.0 * jax.nn.sigmoid(gate_input))))
        first_out = stream(gated_list[0], [narrow_first, narrow_rest[0], narrow_rest[1]], narrow_gain, narrow_shift)
        second_out = stream(gated_list[1], [broad_first, broad_rest], broad_gain, broad_shift)
        head_count = joining_pair.shape[0]
        first_heads = first_out.reshape(batch_rows, head_count, -1)
        second_heads = second_out.reshape(batch_rows, head_count, -1)
        paired = jnp.einsum('bhi,hij,bhj->b', first_heads, joining_pair, second_heads, precision=highest)
        linear_part = jnp.dot(first_out, joining_left, precision=highest) + jnp.dot(second_out, joining_right, precision=highest)
        return linear_part + paired + joining_bias[0]
    logits, pullback = jax.vjp(forward, num_embed, embed_table, gate_weight.astype(jnp.float32), gate_bias, narrow_first.astype(jnp.float32), narrow_rest.astype(jnp.float32), narrow_gain, narrow_shift, broad_first.astype(jnp.float32), broad_rest.astype(jnp.float32), broad_gain, broad_shift, joining_left, joining_right, joining_pair, joining_bias)
    grad_logit = jax.nn.sigmoid(logits) - labels.astype(jnp.float32)
    num_embed_grad, embed_table_grad, gate_weight_grad, gate_bias_grad, narrow_first_grad, narrow_rest_grad, narrow_gain_grad, narrow_shift_grad, broad_first_grad, broad_rest_grad, broad_gain_grad, broad_shift_grad, joining_left_grad, joining_right_grad, joining_pair_grad, joining_bias_grad = pullback(grad_logit)
    return (logits, num_embed_grad, embed_table_grad, gate_weight_grad, gate_bias_grad, narrow_first_grad, narrow_rest_grad, narrow_gain_grad, narrow_shift_grad, broad_first_grad, broad_rest_grad, broad_gain_grad, broad_shift_grad, joining_left_grad, joining_right_grad, joining_pair_grad, joining_bias_grad)
```

```python
import functools
import jax
import jax.numpy as jnp
from jax import lax
from jax.experimental import pallas as pl
from jax.experimental.pallas import tpu as pltpu
from jax.sharding import PartitionSpec as P

MESH = pl.DeviceIdType.MESH
VM = pl.BlockSpec(memory_space=pltpu.VMEM)
HI = 256
CHUNK = 512


def params(cid, mib=48):
    if cid is None:
        return pltpu.CompilerParams(vmem_limit_bytes=mib << 20)
    return pltpu.CompilerParams(
        collective_id=cid, has_side_effects=True, vmem_limit_bytes=mib << 20
    )


def greet(dp, mp):
    me, mine = lax.axis_index("dp"), lax.axis_index("mp")
    barrier = pltpu.get_barrier_semaphore()
    for step in range(1, dp):
        pl.semaphore_signal(
            barrier, inc=1, device_id={"dp": lax.rem(me + step, dp)}, device_id_type=MESH
        )
    for step in range(1, mp):
        pl.semaphore_signal(
            barrier, inc=1, device_id={"mp": lax.rem(mine + step, mp)}, device_id_type=MESH
        )
    pl.semaphore_wait(barrier, dp - 1 + mp - 1)


def remote(src, dst, send, recv, where):
    return pltpu.make_async_remote_copy(
        src_ref=src, dst_ref=dst, send_sem=send, recv_sem=recv,
        device_id=where, device_id_type=MESH,
    )


def spread_dp(dp, pick, send, recv):
    me = lax.axis_index("dp")
    out = []
    for step in range(1, dp):
        to = lax.rem(me + step, dp)
        copy = remote(pick(me), pick(me), send.at[step - 1], recv.at[step - 1], {"dp": to})
        copy.start()
        out.append(copy)
    return out


def compact_keys(key):
    count = key.shape[0]
    dead = (key < 0).astype(jnp.int32)
    sub = lax.broadcasted_iota(jnp.int32, (8, 128), 0)
    lane = lax.broadcasted_iota(jnp.int32, (8, 128), 1)
    running = jnp.zeros((8, 128), jnp.int32)
    before = []
    for v in range(count):
        before.append(running)
        running = running + dead[v]
    scan = running
    for k in (1, 2, 4):
        scan = scan + jnp.where(sub >= k, pltpu.roll(scan, k, 0), 0)
    over_sub = scan - running
    column = jnp.broadcast_to(jnp.sum(running, axis=0, keepdims=True), (8, 128))
    scan = column
    for k in (1, 2, 4, 8, 16, 32, 64):
        scan = scan + jnp.where(lane >= k, pltpu.roll(scan, k, 1), 0)
    base = over_sub + scan - column
    shift = jnp.stack([jnp.where(dead[v] > 0, 0, before[v] + base) for v in range(count)])

    def next_place(x):
        n = x.shape[0]
        flat = x.reshape(n * 8, 128)
        y = jnp.stack([pltpu.roll(x[v], 7, 0) for v in range(n)])
        z = jnp.stack([pltpu.roll(y[v], 127, 1) for v in range(n)])
        return jnp.where(sub[None] < 7, y, z)

    bit = 0
    step = 1
    while step < count:
        moved_key = jnp.concatenate([key[step:], next_place(key[:step])], axis=0)
        moved_shift = jnp.concatenate([shift[step:], next_place(shift[:step])], axis=0)
        key, shift = settle(key, shift, moved_key, moved_shift, bit)
        bit, step = bit + 1, step * 2
    for j in (1, 2, 4):
        def roll_sub(x):
            y = jnp.stack([pltpu.roll(x[v], 8 - j, 0) for v in range(count)])
            z = jnp.stack([pltpu.roll(y[v], 127, 1) for v in range(count)])
            return jnp.where(sub[None] < 8 - j, y, z)
        key, shift = settle(key, shift, roll_sub(key), roll_sub(shift), bit)
        bit += 1
    for j in (1, 2, 4, 8, 16, 32, 64):
        def roll_lane(x):
            return jnp.stack([pltpu.roll(x[v], 128 - j, 1) for v in range(count)])
        key, shift = settle(key, shift, roll_lane(key), roll_lane(shift), bit)
        bit += 1
    return key


def settle(key, shift, moved_key, moved_shift, bit):
    take = (moved_shift & (1 << bit)) != 0
    stay = (shift & (1 << bit)) == 0
    key = jnp.where(take, moved_key, jnp.where(stay, key, -1))
    shift = jnp.where(take, moved_shift, jnp.where(stay, shift, 0))
    return key, shift


def make_keys(ids, lens, scratch, own_rows, mp, bits):
    cats, slots, rows = ids.shape
    part = own_rows // mp
    mine = lax.axis_index("mp")
    scratch[...] = jnp.full_like(scratch, -1)
    slot = lax.broadcasted_iota(jnp.int32, (slots, rows), 0)
    event = lax.broadcasted_iota(jnp.int32, (slots, rows), 1)

    def body(c, carry):
        values = ids[c]
        holder = values // own_rows
        inner = values - holder * own_rows
        owner = inner // part
        place = holder * part + inner - owner * part
        live = (slot < lens[pl.ds(c, 1), :]) & (owner == mine)
        key = jnp.where(live, place * (1 << bits) + c * rows + event, -1)
        for q in range(rows // 128):
            scratch[pl.ds((c * (rows // 128) + q) * slots, slots), :] = key[:, q * 128 : (q + 1) * 128]
        return carry

    lax.fori_loop(0, cats, body, 0)


def table_kernel(dp, mp, own_rows, bits, ids, lens, table, t2, keys, scratch, send, recv):
    part = own_rows // mp
    blocks = part // HI
    tall = blocks * 16
    me, mine = lax.axis_index("dp"), lax.axis_index("mp")
    greet(dp, mp)
    own = table[:, pl.ds(pl.multiple_of(mine * part, HI), part)].astype(jnp.bfloat16)
    for b in range(blocks):
        t2[pl.ds(pl.multiple_of(me * tall + b * 16, 16), 16), :] = own[:, b * HI : (b + 1) * HI]

    def slot(i):
        return t2.at[pl.ds(pl.multiple_of(i * tall, 16), tall), :]

    copies = spread_dp(dp, slot, send, recv)
    make_keys(ids, lens, scratch, own_rows, mp, bits)
    count = scratch.shape[0] // 8
    packed = compact_keys(scratch[...].reshape(count, 8, 128))
    keys[...] = jnp.transpose(packed.reshape(count * 8, 128))
    for copy in copies:
        copy.wait()


def lookup_kernel(cats, rows, bits, keys, t2, pooled, total):
    lows = t2.shape[0] // 16
    filled = jnp.max(keys[...], axis=1, keepdims=True) >= 0
    chunks = jnp.sum(filled.astype(jnp.int32))
    total[...] = jnp.zeros_like(total)
    hi_iota = lax.broadcasted_iota(jnp.int32, (HI, CHUNK), 0)
    event_iota = lax.broadcasted_iota(jnp.int32, (rows, CHUNK), 0)

    def body(k, carry):
        key = keys[pl.ds(k, 1), :]
        place = lax.shift_right_arithmetic(key, bits)
        bag = key & ((1 << bits) - 1)
        cat = bag // rows
        event = bag - cat * rows
        low = lax.shift_right_arithmetic(place, 8)
        high = place & (HI - 1)
        pick = jnp.where(hi_iota == high, 1.0, 0.0).astype(jnp.bfloat16)
        z = jnp.zeros((16, CHUNK), jnp.float32)
        for b in range(0, lows, 16):
            n = min(16, lows - b)
            y = jnp.dot(t2[b * 16 : (b + n) * 16, :], pick, preferred_element_type=jnp.float32)
            for j in range(n):
                z = z + jnp.where(low == b + j, y[j * 16 : (j + 1) * 16], 0.0)
        z = z.astype(jnp.bfloat16)
        zero = jnp.zeros_like(z)
        wide = jnp.concatenate([jnp.where(cat == c, z, zero) for c in range(cats)], axis=0)
        place_of = jnp.where(event_iota == event, 1.0, 0.0).astype(jnp.bfloat16)
        total[...] += lax.dot_general(
            wide, place_of, (((1,), (1,)), ((), ())), preferred_element_type=jnp.float32
        )
        return carry

    lax.fori_loop(0, chunks, body, 0)
    pooled[...] = total[...].astype(pooled.dtype)


def scatter_kernel(cats, rows, bits, keys, grad, out, total):
    lows = total.shape[0] // 16
    filled = jnp.max(keys[...], axis=1, keepdims=True) >= 0
    chunks = jnp.sum(filled.astype(jnp.int32))
    total[...] = jnp.zeros_like(total)
    hi_iota = lax.broadcasted_iota(jnp.int32, (HI, CHUNK), 0)
    event_iota = lax.broadcasted_iota(jnp.int32, (rows, CHUNK), 0)

    def body(k, carry):
        key = keys[pl.ds(k, 1), :]
        place = lax.shift_right_arithmetic(key, bits)
        bag = key & ((1 << bits) - 1)
        cat = bag // rows
        event = bag - cat * rows
        low = lax.shift_right_arithmetic(place, 8)
        high = place & (HI - 1)
        place_of = jnp.where(event_iota == event, 1.0, 0.0).astype(jnp.bfloat16)
        wide = jnp.dot(grad[...], place_of, preferred_element_type=jnp.float32)
        g = jnp.zeros((16, CHUNK), jnp.float32)
        for c in range(cats):
            g = g + jnp.where(cat == c, wide[c * 16 : (c + 1) * 16], 0.0)
        g = g.astype(jnp.bfloat16)
        zero = jnp.zeros_like(g)
        pick = jnp.where(hi_iota == high, 1.0, 0.0).astype(jnp.bfloat16)
        for b in range(0, lows, 16):
            n = min(16, lows - b)
            tall = jnp.concatenate([jnp.where(low == b + j, g, zero) for j in range(n)], axis=0)
            total[b * 16 : (b + n) * 16, :] += lax.dot_general(
                tall, pick, (((1,), (1,)), ((), ())), preferred_element_type=jnp.float32
            )
        return carry

    lax.fori_loop(0, chunks, body, 0)
    out[...] = total[...].astype(out.dtype)


def relay_own(mp, slot, send, recv):
    mine = lax.axis_index("mp")
    core = lax.rem(mine, 2)
    other = mine + 1 - 2 * core
    chips = mp // 2
    out = []
    for k in range(1, chips):
        to = lax.rem(mine + 2 * k, mp)
        copy = remote(slot(mine), slot(mine), send.at[2 * k], recv.at[2 * k], {"mp": to})
        copy.start()
        out.append(copy)
    copy = remote(slot(mine), slot(mine), send.at[1], recv.at[1], {"mp": other})
    copy.start()
    out.append(copy)
    return out


def relay_rest(mp, slot, send, recv, started):
    mine = lax.axis_index("mp")
    core = lax.rem(mine, 2)
    other = mine + 1 - 2 * core
    chips = mp // 2
    passed = []
    for k in range(1, chips):
        source = lax.rem(mine + mp - 2 * k, mp)
        remote(slot(source), slot(source), send.at[2 * k], recv.at[2 * k], {"mp": other}).wait_recv()
        copy = remote(slot(source), slot(source), send.at[2 * k + 1], recv.at[2 * k + 1], {"mp": other})
        copy.start()
        passed.append(copy)
    remote(slot(other), slot(other), send.at[1], recv.at[1], {"mp": other}).wait_recv()
    for k in range(1, chips):
        far = lax.rem(other + mp - 2 * k, mp)
        remote(slot(far), slot(far), send.at[2 * k + 1], recv.at[2 * k + 1], {"mp": other}).wait_recv()
    for copy in started + passed:
        copy.wait_send()


def rows_kernel(dp, mp, grads, out, landed, shares, send, recv, send2, recv2):
    tall = grads.shape[0] // dp
    me, mine = lax.axis_index("dp"), lax.axis_index("mp")
    greet(dp, mp)
    copies = []
    for step in range(1, dp):
        to = lax.rem(me + step, dp)
        copy = remote(
            grads.at[pl.ds(pl.multiple_of(to * tall, 16), tall), :],
            landed.at[step - 1], send.at[step - 1], recv.at[step - 1], {"dp": to},
        )
        copy.start()
        copies.append(copy)
    total = grads[pl.ds(pl.multiple_of(me * tall, 16), tall), :].astype(jnp.float32)
    for step in range(1, dp):
        copies[step - 1].wait_recv()
        total = total + landed[step - 1].astype(jnp.float32)
    shares[mine] = total.astype(jnp.bfloat16)

    def slot(i):
        return shares.at[i]

    started = relay_own(mp, slot, send2, recv2)
    relay_rest(mp, slot, send2, recv2, started)
    blocks = tall // 16
    for m in range(mp):
        for b in range(blocks):
            out[:, (m * blocks + b) * HI : (m * blocks + b + 1) * HI] = shares[
                m, b * 16 : (b + 1) * 16, :
            ].astype(jnp.float32)
    for copy in copies:
        copy.wait_send()


def layer_forward(inputs, weight, gain_row, shift_row, batch_size):
    hidden = lax.dot_general(
        inputs, weight, (((1,), (1,)), ((), ())), preferred_element_type=jnp.float32
    )
    total_sum, square_sum = lax.psum(
        (jnp.sum(hidden, axis=0), jnp.sum(hidden * hidden, axis=0)), "dp"
    )
    batch_mean = total_sum / batch_size
    batch_var = square_sum / batch_size - batch_mean * batch_mean
    inverse = lax.rsqrt(batch_var + 1e-05)
    normed = (hidden - batch_mean) * inverse
    shaped = gain_row * normed + shift_row
    active = jax.nn.silu(shaped).astype(jnp.bfloat16)
    return (lax.all_gather(active, "mp", axis=1, tiled=True), (normed, shaped, inverse))


def layer_backward(grad_out, inputs, weight, gain_row, saved, batch_size):
    normed, shaped, inverse = saved
    sigma = jax.nn.sigmoid(shaped)
    grad_shaped = grad_out * sigma * (1.0 + shaped * (1.0 - sigma))
    shift_grad, gain_grad = lax.psum(
        (jnp.sum(grad_shaped, axis=0), jnp.sum(grad_shaped * normed, axis=0)), "dp"
    )
    grad_hidden = (
        gain_row
        * inverse
        * (grad_shaped - shift_grad / batch_size - normed * gain_grad / batch_size)
    ).astype(jnp.bfloat16)
    weight_grad = lax.dot_general(
        grad_hidden, inputs, (((0,), (0,)), ((), ())), preferred_element_type=jnp.float32
    )
    weight_grad = lax.psum(weight_grad, "dp")
    partial_input = jnp.dot(grad_hidden, weight, preferred_element_type=jnp.float32)
    grad_input = lax.psum_scatter(partial_input, "mp", scatter_dimension=1, tiled=True)
    return (grad_input, weight_grad, gain_grad, shift_grad)


def run_stream(start_input, weights, gain_rows, shifts, batch_size):
    inputs_list = [start_input]
    saved_list = []
    for position in range(len(weights)):
        output, saved = layer_forward(
            inputs_list[-1], weights[position], gain_rows[position], shifts[position], batch_size
        )
        inputs_list.append(output)
        saved_list.append(saved)
    return (inputs_list, saved_list)


def back_stream(grad_out, inputs_list, saved_list, weights, gain_rows, batch_size):
    weight_grads = []
    gain_grads = []
    shift_grads = []
    for position in reversed(range(len(weights))):
        grad_out, weight_grad, gain_grad, shift_grad = layer_backward(
            grad_out,
            inputs_list[position],
            weights[position],
            gain_rows[position],
            saved_list[position],
            batch_size,
        )
        weight_grads.insert(0, weight_grad)
        gain_grads.insert(0, gain_grad)
        shift_grads.insert(0, shift_grad)
    return (grad_out, weight_grads, jnp.stack(gain_grads), jnp.stack(shift_grads))


def shards(
    dense_values,
    field_ids,
    lengths,
    labels,
    num_embed,
    embed_table,
    gate_weight,
    gate_bias,
    narrow_first,
    narrow_rest,
    narrow_gain,
    narrow_shift,
    broad_first,
    broad_rest,
    broad_gain,
    broad_shift,
    joining_left,
    joining_right,
    joining_pair,
    joining_bias,
):
    highest = lax.Precision.HIGHEST
    tok_rows = dense_values.shape[0]
    batch_size = float(tok_rows * lax.axis_size("dp"))
    cat_fields = field_ids.shape[0]
    bag_size = field_ids.shape[1]
    own_rows = embed_table.shape[1]
    width = embed_table.shape[0]
    numeric_cols = dense_values.shape[1] * width
    dp, mp = lax.axis_size("dp"), lax.axis_size("mp")
    bits = (cat_fields * tok_rows - 1).bit_length()
    part = own_rows // mp
    tall = part // HI * 16
    lookups = cat_fields * bag_size * tok_rows
    vregs = 1 << (-(-lookups // 1024) - 1).bit_length()
    t2, keys = pl.pallas_call(
        functools.partial(table_kernel, dp, mp, own_rows, bits),
        out_shape=(
            jax.ShapeDtypeStruct((dp * tall, HI), jnp.bfloat16),
            jax.ShapeDtypeStruct((128, vregs * 8), jnp.int32),
        ),
        in_specs=[VM] * 3,
        out_specs=(VM, VM),
        scratch_shapes=[
            pltpu.VMEM((vregs * 8, 128), jnp.int32),
            pltpu.SemaphoreType.DMA((dp - 1,)),
            pltpu.SemaphoreType.DMA((dp - 1,)),
        ],
        compiler_params=params(0),
        name="table",
    )(field_ids, lengths, embed_table)
    pooled_t = pl.pallas_call(
        functools.partial(lookup_kernel, cat_fields, tok_rows, bits),
        out_shape=jax.ShapeDtypeStruct((cat_fields * 16, tok_rows), jnp.float32),
        in_specs=[VM] * 2,
        out_specs=VM,
        scratch_shapes=[pltpu.VMEM((cat_fields * 16, tok_rows), jnp.float32)],
        compiler_params=params(None),
        name="lookup",
    )(keys, t2)
    pooled = lax.psum(pooled_t, "mp").T
    numeric = (dense_values[:, :, None] * num_embed[None, :, :]).reshape(tok_rows, numeric_cols)
    features = jnp.concatenate([numeric, pooled], axis=1).astype(jnp.bfloat16)
    local_cols = gate_weight.shape[1]
    start_col = lax.axis_index("mp") * local_cols
    feature_cols = lax.dynamic_slice_in_dim(features, start_col, local_cols, 1).astype(jnp.float32)
    gate_input = (
        jnp.einsum("bd,khd->kbh", features, gate_weight, preferred_element_type=jnp.float32)
        + gate_bias[:, None, :]
    )
    gate_value = 2.0 * jax.nn.sigmoid(gate_input)
    fields_part = (feature_cols[None, :, :] * gate_value).astype(jnp.bfloat16)
    fields = lax.all_gather(fields_part, "mp", axis=2, tiled=True)
    narrow_weights = [narrow_first, narrow_rest[0], narrow_rest[1]]
    broad_weights = [broad_first, broad_rest]
    narrow_inputs, narrow_saved = run_stream(
        fields[0], narrow_weights, narrow_gain, narrow_shift, batch_size
    )
    broad_inputs, broad_saved = run_stream(
        fields[1], broad_weights, broad_gain, broad_shift, batch_size
    )
    head_count = joining_pair.shape[0]
    first_flat = narrow_inputs[-1].astype(jnp.float32)
    second_flat = broad_inputs[-1].astype(jnp.float32)
    first_heads = first_flat.reshape(tok_rows, head_count, -1)
    second_heads = second_flat.reshape(tok_rows, head_count, -1)
    turned = jnp.einsum("bhi,hij->bhj", first_heads, joining_pair, precision=highest)
    linear_part = jnp.dot(first_flat, joining_left, precision=highest) + jnp.dot(
        second_flat, joining_right, precision=highest
    )
    logits = linear_part + jnp.sum(turned * second_heads, axis=(1, 2)) + joining_bias[0]
    grad_logit = jax.nn.sigmoid(logits) - labels.astype(jnp.float32)
    joining_left_grad = jnp.sum(first_flat * grad_logit[:, None], axis=0)
    joining_right_grad = jnp.sum(second_flat * grad_logit[:, None], axis=0)
    joining_pair_grad = jnp.einsum(
        "bhi,bhj->hij", first_heads * grad_logit[:, None, None], second_heads, precision=highest
    )
    joining_bias_grad = jnp.sum(grad_logit).reshape(1)
    back_turned = jnp.einsum("hij,bhj->bhi", joining_pair, second_heads, precision=highest).reshape(
        tok_rows, -1
    )
    grad_first = grad_logit[:, None] * (joining_left[None, :] + back_turned)
    grad_second = grad_logit[:, None] * (joining_right[None, :] + turned.reshape(tok_rows, -1))
    narrow_cols = narrow_first.shape[0]
    broad_cols = broad_first.shape[0]
    grad_first = lax.dynamic_slice_in_dim(
        grad_first, lax.axis_index("mp") * narrow_cols, narrow_cols, 1
    )
    grad_second = lax.dynamic_slice_in_dim(
        grad_second, lax.axis_index("mp") * broad_cols, broad_cols, 1
    )
    grad_fields_first, narrow_wgrads, narrow_gain_grad, narrow_shift_grad = back_stream(
        grad_first, narrow_inputs, narrow_saved, narrow_weights, narrow_gain, batch_size
    )
    grad_fields_second, broad_wgrads, broad_gain_grad, broad_shift_grad = back_stream(
        grad_second, broad_inputs, broad_saved, broad_weights, broad_gain, batch_size
    )
    grad_fields = jnp.stack([grad_fields_first, grad_fields_second])
    grad_gate = (
        grad_fields * feature_cols[None, :, :] * gate_value * (1.0 - 0.5 * gate_value)
    ).astype(jnp.bfloat16)
    gate_weight_grad = jnp.einsum(
        "bd,kbh->khd", features, grad_gate, preferred_element_type=jnp.float32
    )
    gate_bias_grad = jnp.sum(grad_gate.astype(jnp.float32), axis=1)
    partial_features = jnp.einsum(
        "kbh,khd->bd", grad_gate, gate_weight, preferred_element_type=jnp.float32
    )
    own_term = jnp.sum(grad_fields * gate_value, axis=0)
    own_slice = lax.dynamic_slice_in_dim(partial_features, start_col, local_cols, 1) + own_term
    partial_features = lax.dynamic_update_slice_in_dim(partial_features, own_slice, start_col, 1)
    grad_features = lax.psum(partial_features, "mp").astype(jnp.bfloat16)
    numeric_grad = grad_features[:, :numeric_cols].astype(jnp.float32).reshape(tok_rows, -1, width)
    num_embed_grad = jnp.sum(dense_values[:, :, None] * numeric_grad, axis=0)
    pooled_grad = grad_features[:, numeric_cols:]
    row_sums = pl.pallas_call(
        functools.partial(scatter_kernel, cat_fields, tok_rows, bits),
        out_shape=jax.ShapeDtypeStruct((dp * tall, HI), jnp.bfloat16),
        in_specs=[VM] * 2,
        out_specs=VM,
        scratch_shapes=[pltpu.VMEM((dp * tall, HI), jnp.float32)],
        compiler_params=params(None),
        name="scatter",
    )(keys, pooled_grad.T)
    embed_table_grad = pl.pallas_call(
        functools.partial(rows_kernel, dp, mp),
        out_shape=jax.ShapeDtypeStruct((width, own_rows), jnp.float32),
        in_specs=[VM],
        out_specs=VM,
        scratch_shapes=[
            pltpu.VMEM((dp - 1, tall, HI), jnp.bfloat16),
            pltpu.VMEM((mp, tall, HI), jnp.bfloat16),
            pltpu.SemaphoreType.DMA((dp - 1,)),
            pltpu.SemaphoreType.DMA((dp - 1,)),
            pltpu.SemaphoreType.DMA((mp,)),
            pltpu.SemaphoreType.DMA((mp,)),
        ],
        compiler_params=params(1),
        name="rows",
    )(row_sums)
    (
        joining_left_grad,
        joining_right_grad,
        joining_pair_grad,
        joining_bias_grad,
        gate_weight_grad,
        gate_bias_grad,
        num_embed_grad,
    ) = lax.psum(
        (
            joining_left_grad,
            joining_right_grad,
            joining_pair_grad,
            joining_bias_grad,
            gate_weight_grad,
            gate_bias_grad,
            num_embed_grad,
        ),
        "dp",
    )
    narrow_first_grad = narrow_wgrads[0]
    narrow_rest_grad = jnp.stack([narrow_wgrads[1], narrow_wgrads[2]])
    broad_first_grad = broad_wgrads[0]
    broad_rest_grad = broad_wgrads[1]
    return (
        logits,
        num_embed_grad,
        embed_table_grad,
        gate_weight_grad,
        gate_bias_grad,
        narrow_first_grad,
        narrow_rest_grad,
        narrow_gain_grad,
        narrow_shift_grad,
        broad_first_grad,
        broad_rest_grad,
        broad_gain_grad,
        broad_shift_grad,
        joining_left_grad,
        joining_right_grad,
        joining_pair_grad,
        joining_bias_grad,
    )


def solution(mesh):
    placed = (
        P("dp", None),
        P(None, None, "dp"),
        P(None, "dp"),
        P("dp"),
        P(),
        P(None, "dp"),
        P(None, "mp", None),
        P(None, "mp"),
        P("mp", None),
        P(None, "mp", None),
        P(None, "mp"),
        P(None, "mp"),
        P("mp", None),
        P("mp", None),
        P(None, "mp"),
        P(None, "mp"),
        P(),
        P(),
        P(),
        P(),
    )
    return jax.shard_map(
        shards,
        mesh=mesh,
        in_specs=placed,
        out_specs=(
            P("dp"),
            P(),
            P(None, "dp"),
            P(None, "mp", None),
            P(None, "mp"),
            P("mp", None),
            P(None, "mp", None),
            P(None, "mp"),
            P(None, "mp"),
            P("mp", None),
            P("mp", None),
            P(None, "mp"),
            P(None, "mp"),
            P(),
            P(),
            P(),
            P(),
        ),
        check_vma=False,
    )
```

```python
import functools
import jax
import jax.numpy as jnp
from jax import lax
from jax.experimental import pallas as pl
from jax.experimental.pallas import tpu as pltpu
from jax.sharding import PartitionSpec as P

MESH = pl.DeviceIdType.MESH
VM = pl.BlockSpec(memory_space=pltpu.VMEM)
HI = 256
CHUNK = 512


def params(cid, mib=48):
    if cid is None:
        return pltpu.CompilerParams(vmem_limit_bytes=mib << 20)
    return pltpu.CompilerParams(
        collective_id=cid, has_side_effects=True, vmem_limit_bytes=mib << 20
    )


def greet(dp, mp):
    me, mine = lax.axis_index("dp"), lax.axis_index("mp")
    barrier = pltpu.get_barrier_semaphore()
    for step in range(1, dp):
        pl.semaphore_signal(
            barrier, inc=1, device_id={"dp": lax.rem(me + step, dp)}, device_id_type=MESH
        )
    for step in range(1, mp):
        pl.semaphore_signal(
            barrier, inc=1, device_id={"mp": lax.rem(mine + step, mp)}, device_id_type=MESH
        )
    pl.semaphore_wait(barrier, dp - 1 + mp - 1)


def remote(src, dst, send, recv, where):
    return pltpu.make_async_remote_copy(
        src_ref=src, dst_ref=dst, send_sem=send, recv_sem=recv,
        device_id=where, device_id_type=MESH,
    )


def spread_dp(dp, pick, send, recv):
    me = lax.axis_index("dp")
    out = []
    for step in range(1, dp):
        to = lax.rem(me + step, dp)
        copy = remote(pick(me), pick(me), send.at[step - 1], recv.at[step - 1], {"dp": to})
        copy.start()
        out.append(copy)
    return out


def compact_keys(key):
    count = key.shape[0]
    dead = (key < 0).astype(jnp.int32)
    sub = lax.broadcasted_iota(jnp.int32, (8, 128), 0)
    lane = lax.broadcasted_iota(jnp.int32, (8, 128), 1)
    running = jnp.zeros((8, 128), jnp.int32)
    before = []
    for v in range(count):
        before.append(running)
        running = running + dead[v]
    scan = running
    for k in (1, 2, 4):
        scan = scan + jnp.where(sub >= k, pltpu.roll(scan, k, 0), 0)
    over_sub = scan - running
    column = jnp.broadcast_to(jnp.sum(running, axis=0, keepdims=True), (8, 128))
    scan = column
    for k in (1, 2, 4, 8, 16, 32, 64):
        scan = scan + jnp.where(lane >= k, pltpu.roll(scan, k, 1), 0)
    base = over_sub + scan - column
    shift = jnp.stack([jnp.where(dead[v] > 0, 0, before[v] + base) for v in range(count)])

    def next_place(x):
        n = x.shape[0]
        flat = x.reshape(n * 8, 128)
        y = jnp.stack([pltpu.roll(x[v], 7, 0) for v in range(n)])
        z = jnp.stack([pltpu.roll(y[v], 127, 1) for v in range(n)])
        return jnp.where(sub[None] < 7, y, z)

    bit = 0
    step = 1
    while step < count:
        moved_key = jnp.concatenate([key[step:], next_place(key[:step])], axis=0)
        moved_shift = jnp.concatenate([shift[step:], next_place(shift[:step])], axis=0)
        key, shift = settle(key, shift, moved_key, moved_shift, bit)
        bit, step = bit + 1, step * 2
    for j in (1, 2, 4):
        def roll_sub(x):
            y = jnp.stack([pltpu.roll(x[v], 8 - j, 0) for v in range(count)])
            z = jnp.stack([pltpu.roll(y[v], 127, 1) for v in range(count)])
            return jnp.where(sub[None] < 8 - j, y, z)
        key, shift = settle(key, shift, roll_sub(key), roll_sub(shift), bit)
        bit += 1
    for j in (1, 2, 4, 8, 16, 32, 64):
        def roll_lane(x):
            return jnp.stack([pltpu.roll(x[v], 128 - j, 1) for v in range(count)])
        key, shift = settle(key, shift, roll_lane(key), roll_lane(shift), bit)
        bit += 1
    return key


def settle(key, shift, moved_key, moved_shift, bit):
    take = (moved_shift & (1 << bit)) != 0
    stay = (shift & (1 << bit)) == 0
    key = jnp.where(take, moved_key, jnp.where(stay, key, -1))
    shift = jnp.where(take, moved_shift, jnp.where(stay, shift, 0))
    return key, shift


def make_keys(ids, lens, scratch, own_rows, mp, bits):
    cats, slots, rows = ids.shape
    part = own_rows // mp
    mine = lax.axis_index("mp")
    scratch[...] = jnp.full_like(scratch, -1)
    slot = lax.broadcasted_iota(jnp.int32, (slots, rows), 0)
    event = lax.broadcasted_iota(jnp.int32, (slots, rows), 1)

    def body(c, carry):
        values = ids[c]
        holder = values // own_rows
        inner = values - holder * own_rows
        owner = inner // part
        place = holder * part + inner - owner * part
        live = (slot < lens[pl.ds(c, 1), :]) & (owner == mine)
        key = jnp.where(live, place * (1 << bits) + c * rows + event, -1)
        for q in range(rows // 128):
            scratch[pl.ds((c * (rows // 128) + q) * slots, slots), :] = key[:, q * 128 : (q + 1) * 128]
        return carry

    lax.fori_loop(0, cats, body, 0)


def lookup_kernel(cats, rows, bits, keys, t2, pooled, total):
    lows = t2.shape[0] // 16
    filled = jnp.max(keys[...], axis=1, keepdims=True) >= 0
    chunks = jnp.sum(filled.astype(jnp.int32))
    total[...] = jnp.zeros_like(total)
    hi_iota = lax.broadcasted_iota(jnp.int32, (HI, CHUNK), 0)
    event_iota = lax.broadcasted_iota(jnp.int32, (rows, CHUNK), 0)

    def body(k, carry):
        key = keys[pl.ds(k, 1), :]
        place = lax.shift_right_arithmetic(key, bits)
        bag = key & ((1 << bits) - 1)
        cat = bag // rows
        event = bag - cat * rows
        low = lax.shift_right_arithmetic(place, 8)
        high = place & (HI - 1)
        pick = jnp.where(hi_iota == high, 1.0, 0.0).astype(jnp.bfloat16)
        z = jnp.zeros((16, CHUNK), jnp.float32)
        for b in range(0, lows, 16):
            n = min(16, lows - b)
            y = jnp.dot(t2[b * 16 : (b + n) * 16, :], pick, preferred_element_type=jnp.float32)
            for j in range(n):
                z = z + jnp.where(low == b + j, y[j * 16 : (j + 1) * 16], 0.0)
        z = z.astype(jnp.bfloat16)
        zero = jnp.zeros_like(z)
        wide = jnp.concatenate([jnp.where(cat == c, z, zero) for c in range(cats)], axis=0)
        place_of = jnp.where(event_iota == event, 1.0, 0.0).astype(jnp.bfloat16)
        total[...] += lax.dot_general(
            wide, place_of, (((1,), (1,)), ((), ())), preferred_element_type=jnp.float32
        )
        return carry

    lax.fori_loop(0, chunks, body, 0)
    pooled[...] = total[...].astype(pooled.dtype)


def scatter_kernel(cats, rows, bits, keys, grad, out, total):
    lows = total.shape[0] // 16
    filled = jnp.max(keys[...], axis=1, keepdims=True) >= 0
    chunks = jnp.sum(filled.astype(jnp.int32))
    total[...] = jnp.zeros_like(total)
    hi_iota = lax.broadcasted_iota(jnp.int32, (HI, CHUNK), 0)
    event_iota = lax.broadcasted_iota(jnp.int32, (rows, CHUNK), 0)

    def body(k, carry):
        key = keys[pl.ds(k, 1), :]
        place = lax.shift_right_arithmetic(key, bits)
        bag = key & ((1 << bits) - 1)
        cat = bag // rows
        event = bag - cat * rows
        low = lax.shift_right_arithmetic(place, 8)
        high = place & (HI - 1)
        place_of = jnp.where(event_iota == event, 1.0, 0.0).astype(jnp.bfloat16)
        wide = jnp.dot(grad[...], place_of, preferred_element_type=jnp.float32)
        g = jnp.zeros((16, CHUNK), jnp.float32)
        for c in range(cats):
            g = g + jnp.where(cat == c, wide[c * 16 : (c + 1) * 16], 0.0)
        g = g.astype(jnp.bfloat16)
        zero = jnp.zeros_like(g)
        pick = jnp.where(hi_iota == high, 1.0, 0.0).astype(jnp.bfloat16)
        for b in range(0, lows, 16):
            n = min(16, lows - b)
            tall = jnp.concatenate([jnp.where(low == b + j, g, zero) for j in range(n)], axis=0)
            total[b * 16 : (b + n) * 16, :] += lax.dot_general(
                tall, pick, (((1,), (1,)), ((), ())), preferred_element_type=jnp.float32
            )
        return carry

    lax.fori_loop(0, chunks, body, 0)
    out[...] = total[...].astype(out.dtype)


def relay_own(mp, slot, send, recv):
    mine = lax.axis_index("mp")
    core = lax.rem(mine, 2)
    other = mine + 1 - 2 * core
    chips = mp // 2
    out = []
    for k in range(1, chips):
        to = lax.rem(mine + 2 * k, mp)
        copy = remote(slot(mine), slot(mine), send.at[2 * k], recv.at[2 * k], {"mp": to})
        copy.start()
        out.append(copy)
    copy = remote(slot(mine), slot(mine), send.at[1], recv.at[1], {"mp": other})
    copy.start()
    out.append(copy)
    return out


def relay_rest(mp, slot, send, recv, started):
    mine = lax.axis_index("mp")
    core = lax.rem(mine, 2)
    other = mine + 1 - 2 * core
    chips = mp // 2
    passed = []
    for k in range(1, chips):
        source = lax.rem(mine + mp - 2 * k, mp)
        remote(slot(source), slot(source), send.at[2 * k], recv.at[2 * k], {"mp": other}).wait_recv()
        copy = remote(slot(source), slot(source), send.at[2 * k + 1], recv.at[2 * k + 1], {"mp": other})
        copy.start()
        passed.append(copy)
    remote(slot(other), slot(other), send.at[1], recv.at[1], {"mp": other}).wait_recv()
    for k in range(1, chips):
        far = lax.rem(other + mp - 2 * k, mp)
        remote(slot(far), slot(far), send.at[2 * k + 1], recv.at[2 * k + 1], {"mp": other}).wait_recv()
    for copy in started + passed:
        copy.wait_send()


def nn(a, b):
    return jnp.dot(a, b, preferred_element_type=jnp.float32)


def nt(a, b):
    return lax.dot_general(a, b, (((1,), (1,)), ((), ())), preferred_element_type=jnp.float32)


def tn(a, b):
    return lax.dot_general(a, b, (((0,), (0,)), ((), ())), preferred_element_type=jnp.float32)


def sigmoid(x):
    return 0.5 * jnp.tanh(0.5 * x) + 0.5


def low(x):
    return x.astype(jnp.bfloat16)


def column_sum(x):
    return jnp.sum(x, axis=0, keepdims=True)


def widen_dense(dense, width):
    fields = dense.shape[1]
    row = lax.broadcasted_iota(jnp.int32, (fields, fields * width), 0)
    col = lax.broadcasted_iota(jnp.int32, (fields, fields * width), 1)
    ones = jnp.where(col // width == row, 1.0, 0.0)
    return jnp.dot(dense, ones, precision=lax.Precision.HIGHEST, preferred_element_type=jnp.float32)


def first_kernel(
    dp, mp, own_rows, bits,
    ids, lens, table, dense, num_row, gate_w, gate_b, n_first, n_gain, n_shift, b_first, b_gain, b_shift,
    t2, keys, numeric, gates, n1, b1, vec,
    scratch, gate_slots, n_slots, b_slots, v_slots, send, recv, send2, recv2,
):
    part = own_rows // mp
    blocks = part // HI
    tall = blocks * 16
    me, mine = lax.axis_index("dp"), lax.axis_index("mp")
    greet(dp, mp)
    own = table[:, pl.ds(pl.multiple_of(mine * part, HI), part)].astype(jnp.bfloat16)
    for b in range(blocks):
        t2[pl.ds(pl.multiple_of(me * tall + b * 16, 16), 16), :] = own[:, b * HI : (b + 1) * HI]

    def slot(i):
        return t2.at[pl.ds(pl.multiple_of(i * tall, 16), tall), :]

    copies = spread_dp(dp, slot, send, recv)
    gate_slots[mine] = gate_w[...]
    n_slots[mine] = n_first[...]
    b_slots[mine] = b_first[...]
    row = 0
    for ref in (gate_b, n_gain, n_shift, b_gain, b_shift):
        v_slots[mine, row : row + ref.shape[0], : ref.shape[1]] = ref[...]
        row += ref.shape[0]
    groups = []
    for i, ref in enumerate((gate_slots, n_slots, b_slots, v_slots)):
        started = relay_own(mp, lambda k, ref=ref: ref.at[k], send2.at[i], recv2.at[i])
        groups.append((ref, i, started))
    numeric[...] = low(widen_dense(dense[...], 16) * num_row[...])
    make_keys(ids, lens, scratch, own_rows, mp, bits)
    count = scratch.shape[0] // 8
    packed = compact_keys(scratch[...].reshape(count, 8, 128))
    keys[...] = jnp.transpose(packed.reshape(count * 8, 128))
    for ref, i, started in groups:
        relay_rest(mp, lambda k, ref=ref: ref.at[k], send2.at[i], recv2.at[i], started)
    cols, small, large = gate_w.shape[1], n_first.shape[0], b_first.shape[0]
    for m in range(mp):
        for k in range(2):
            gates[k, m * cols : (m + 1) * cols, :] = gate_slots[m, k]
        n1[m * small : (m + 1) * small, :] = n_slots[m]
        b1[m * large : (m + 1) * large, :] = b_slots[m]
    row = 0
    for ref in (gate_b, n_gain, n_shift, b_gain, b_shift):
        r, w = ref.shape
        vec[row : row + r, : mp * w] = jnp.concatenate(
            [v_slots[m, row : row + r, :w] for m in range(mp)], axis=1
        )
        row += r
    for copy in copies:
        copy.wait()


def own_columns(x, mine, width, mp):
    out = jnp.zeros((x.shape[0], width), x.dtype)
    for m in range(mp):
        out = jnp.where(mine == m, x[:, m * width : (m + 1) * width], out)
    return out


def dense_kernel(
    dp, mp, hx, batch,
    partial, numeric, gates, n1, b1, n_rest, b_rest, vec, left, right, pair, bias, labels, dense,
    logits, grads_t, p_out, q_out, small, n_gain_g, n_shift_g, b_gain_g, b_shift_g, left_g, right_g, bias_g,
    half_a, half_c, pooled, feat, gate, fields, own_term, grad_gate, n_slots, b_slots, n23, b2,
    yn, dn, yb, db, un, ub, gyn, gyb, pair_hi, pair_lo, pair_g, sums,
    fsend, frecv, wsend, wrecv, ssend, srecv,
):
    me, mine = lax.axis_index("dp"), lax.axis_index("mp")
    core = lax.rem(mine, 2)
    chip = mine // 2
    chips = mp // 2
    other = mine + 1 - 2 * core
    rows = feat.shape[0]
    block = 128
    steps = rows // block
    h1, h2 = n1.shape[0], b1.shape[0]
    s1, s2 = h1 // mp, h2 // mp
    wide = feat.shape[1]
    num = numeric.shape[1]
    gcols = wide // mp
    half = partial.shape[0] // 2
    greet(dp, mp)

    def rowset(i):
        return pl.ds(pl.multiple_of(i * block, block), block)

    def part(c):
        return pl.ds(pl.multiple_of(c * half, 16), half)

    copy_a = remote(partial.at[part(1 - core), :], half_a, fsend.at[0], frecv.at[0], {"mp": other})
    copy_a.start()
    n_slots[mine] = n_rest[...]
    b_slots[mine] = b_rest[...]
    copy_a.wait_recv()
    half_c[chip] = low(partial[part(core), :] + half_a[...])
    copies = []
    for k in range(1, chips):
        copy = remote(
            half_c.at[chip], half_c.at[chip], fsend.at[k], frecv.at[k],
            {"mp": lax.rem(mine + 2 * k, mp)},
        )
        copy.start()
        copies.append(copy)
    for i in range(0, h1, 80):
        row = lax.broadcasted_iota(jnp.int32, (80, h2), 0) + i
        col = lax.broadcasted_iota(jnp.int32, (80, h2), 1)
        pieces = jnp.concatenate([pair[i : i + 80, :]] * (h2 // 16), axis=1)
        spread = jnp.where(row // hx == col // 16, pieces, 0.0)
        high = low(spread)
        pair_hi[i : i + 80, :] = high
        pair_lo[i : i + 80, :] = low(spread - high.astype(jnp.float32))
    for copy in copies:
        copy.wait_recv()
    total = half_c[0].astype(jnp.float32)
    for k in range(1, chips):
        total = total + half_c[k].astype(jnp.float32)
    pooled[part(core), :] = low(total)
    copy_b = remote(
        pooled.at[part(core), :], pooled.at[part(core), :], fsend.at[chips], frecv.at[chips], {"mp": other}
    )
    copy_b.start()
    n_started = relay_own(mp, lambda k: n_slots.at[k], wsend.at[0], wrecv.at[0])
    b_started = relay_own(mp, lambda k: b_slots.at[k], wsend.at[1], wrecv.at[1])
    feat[:, :num] = numeric[...]
    copy_b.wait_recv()
    feat[:, num:] = low(jnp.transpose(pooled[...].astype(jnp.float32)))

    def push(slot):
        out = []
        for step in range(1, dp):
            copy = remote(
                sums.at[slot, me], sums.at[slot, me], ssend.at[slot, step - 1], srecv.at[slot, step - 1],
                {"dp": lax.rem(me + step, dp)},
            )
            copy.start()
            out.append(copy)
        return out

    def pull(slot, copies):
        for copy in copies:
            copy.wait_recv()
        total = sums[slot, 0]
        for d in range(1, dp):
            total = total + sums[slot, d]
        return total

    def put(slot, row, value):
        sums[slot, me, row : row + 1, : value.shape[1]] = value

    def norm(total, row, width):
        mean = total[row : row + 1, :width] / batch
        var = total[row + 1 : row + 2, :width] / batch - mean * mean
        return mean, lax.rsqrt(var + 1e-05)

    def activate(y_ref, d_ref, u_ref, layer, at, mean, rstd, gain, shift):
        normed = (y_ref[layer, at, :] - mean) * rstd
        z = gain * normed + shift
        s = sigmoid(z)
        u = z * s
        y_ref[layer, at, :] = normed
        d_ref[layer, at, :] = s + u * (1.0 - s)
        u = low(u)
        u_ref[layer, at, :] = u
        return u

    def gain_n(layer):
        return vec[2 + layer : 3 + layer, :h1], vec[5 + layer : 6 + layer, :h1]

    def gain_b(layer):
        return vec[8 + layer : 9 + layer, :h2], vec[10 + layer : 11 + layer, :h2]

    zero1 = jnp.zeros((1, h1), jnp.float32)
    zero2 = jnp.zeros((1, h2), jnp.float32)

    def forward_one(i, carry):
        a, b, c, d = carry
        at = rowset(i)
        x = feat[at, :]
        wide_x = x.astype(jnp.float32)
        for k in range(2):
            value = 2.0 * sigmoid(nt(x, gates[k]) + vec[k : k + 1, :wide])
            gate[k, at, :] = value
            fields[k, at, :] = low(wide_x * value)
        y = nt(fields[0, at, :], n1[...])
        yn[0, at, :] = y
        v = nt(fields[1, at, :], b1[...])
        yb[0, at, :] = v
        return a + column_sum(y), b + column_sum(y * y), c + column_sum(v), d + column_sum(v * v)

    stats = lax.fori_loop(0, steps, forward_one, (zero1, zero1, zero2, zero2))
    for r in range(4):
        put(0, r, stats[r])
    sent = [push(0)]
    relay_rest(mp, lambda k: n_slots.at[k], wsend.at[0], wrecv.at[0], n_started)
    relay_rest(mp, lambda k: b_slots.at[k], wsend.at[1], wrecv.at[1], b_started)
    for m in range(mp):
        for k in range(2):
            n23[k, m * s1 : (m + 1) * s1, :] = n_slots[m, k]
        b2[m * s2 : (m + 1) * s2, :] = b_slots[m]
    total = pull(0, sent[0])
    mean_n, rstd_n = norm(total, 0, h1)
    mean_b, rstd_b = norm(total, 2, h2)
    rstd_n1, rstd_b1 = rstd_n, rstd_b

    def forward_two(i, carry):
        a, b, c, d = carry
        at = rowset(i)
        u = activate(yn, dn, un, 0, at, mean_n, rstd_n, *gain_n(0))
        y = nt(u, n23[0])
        yn[1, at, :] = y
        u = activate(yb, db, ub, 0, at, mean_b, rstd_b, *gain_b(0))
        v = nt(u, b2[...])
        yb[1, at, :] = v
        return a + column_sum(y), b + column_sum(y * y), c + column_sum(v), d + column_sum(v * v)

    stats = lax.fori_loop(0, steps, forward_two, (zero1, zero1, zero2, zero2))
    for r in range(4):
        put(1, r, stats[r])
    sent.append(push(1))
    total = pull(1, sent[1])
    mean_n2, rstd_n2 = norm(total, 0, h1)
    mean_b2, rstd_b2 = norm(total, 2, h2)

    def forward_three(i, carry):
        a, b = carry
        at = rowset(i)
        u = activate(yn, dn, un, 1, at, mean_n2, rstd_n2, *gain_n(1))
        y = nt(u, n23[1])
        yn[2, at, :] = y
        return a + column_sum(y), b + column_sum(y * y)

    stats = lax.fori_loop(0, steps, forward_three, (zero1, zero1))
    for r in range(2):
        put(2, r, stats[r])
    sent.append(push(2))

    def broad_out(i, carry):
        activate(yb, db, ub, 1, rowset(i), mean_b2, rstd_b2, *gain_b(1))
        return carry

    lax.fori_loop(0, steps, broad_out, 0)
    pair_g[...] = jnp.zeros_like(pair_g)
    label = jnp.transpose(jnp.broadcast_to(labels[...].astype(jnp.float32), (8, rows)))[:, 0:1]
    own_term[:, 0:1] = label
    total = pull(2, sent[2])
    mean_n3, rstd_n3 = norm(total, 0, h1)

    def join(i, carry):
        l_sum, r_sum, g_sum, a, b, c, d = carry
        at = rowset(i)
        first = activate(yn, dn, un, 2, at, mean_n3, rstd_n3, *gain_n(2))
        second = ub[1, at, :]
        turned = nn(first, pair_hi[...]) + nn(first, pair_lo[...])
        first32, second32 = first.astype(jnp.float32), second.astype(jnp.float32)
        to_second = right[...] + turned
        logit = (
            jnp.sum(first32 * left[...], axis=1, keepdims=True)
            + jnp.sum(second32 * to_second, axis=1, keepdims=True)
            + bias[...]
        )
        g = sigmoid(logit) - own_term[at, 0:1]
        own_term[at, 1:2] = logit
        back = nt(second, pair_hi[...]) + nt(second, pair_lo[...])
        weighted = g * first32
        l_sum = l_sum + column_sum(weighted)
        r_sum = r_sum + column_sum(g * second32)
        g_sum = g_sum + column_sum(g)
        pair_g[...] += tn(second, low(weighted))
        gz = g * (left[...] + back) * dn[2, at, :]
        dn[2, at, :] = gz
        a = a + column_sum(gz)
        b = b + column_sum(gz * yn[2, at, :])
        gz = g * to_second * db[1, at, :]
        db[1, at, :] = gz
        c = c + column_sum(gz)
        d = d + column_sum(gz * yb[1, at, :])
        return l_sum, r_sum, g_sum, a, b, c, d

    l_sum, r_sum, g_sum, a, b, c, d = lax.fori_loop(
        0, steps, join, (zero1, zero2, jnp.zeros((1, 1), jnp.float32), zero1, zero1, zero2, zero2)
    )
    for r, value in enumerate((a, b, c, d)):
        put(3, r, value)
    sent.append(push(3))
    for r, value in enumerate((l_sum, r_sum, g_sum)):
        put(6, r, value)
    join_sent = push(6)
    logits[...] = jnp.transpose(own_term[:, 0:128])[1:2, :]

    def own_part(x, width):
        full = x.shape[1]
        pad = -(-width // 128) * 128
        row = lax.broadcasted_iota(jnp.int32, (full, pad), 0)
        col = lax.broadcasted_iota(jnp.int32, (full, pad), 1)
        choose = jnp.where((row == col + mine * width) & (col < width), 1.0, 0.0).astype(jnp.bfloat16)
        return low(nn(x, choose))

    def weight_grad(grad_y, inputs, width):
        return low(tn(own_part(grad_y, width), inputs)[:width, :])

    def up16(x):
        return -(-x // 16) * 16

    g_rows, n_rows, b_rows = up16(gcols), up16(s1), up16(s2)
    p_out[...] = jnp.zeros_like(p_out)
    q_out[...] = jnp.zeros_like(q_out)
    folded = jnp.zeros((16, h1), jnp.float32)
    col = lax.broadcasted_iota(jnp.int32, (16, h1), 1)
    for h in range(h2 // 16):
        folded = folded + jnp.where(col // hx == h, pair_g[h * 16 : (h + 1) * 16, :], 0.0)
    q_out[n_rows + b_rows : n_rows + b_rows + 16, :h1] = low(folded)

    total = pull(3, sent[3])

    def grad_y(gz, normed, rstd, gain, total_rows):
        return low(gain * rstd * (gz - total_rows[0:1] / batch - normed * (total_rows[1:2] / batch)))

    t_n3, t_b2 = total[0:2, :h1], total[2:4, :h2]

    def back_one(i, carry):
        a, b, c, d = carry
        at = rowset(i)
        g = grad_y(dn[2, at, :], yn[2, at, :], rstd_n3, gain_n(2)[0], t_n3)
        gyn[2, at, :] = g
        gz = nn(g, n23[1]) * dn[1, at, :]
        dn[1, at, :] = gz
        a, b = a + column_sum(gz), b + column_sum(gz * yn[1, at, :])
        g = grad_y(db[1, at, :], yb[1, at, :], rstd_b2, gain_b(1)[0], t_b2)
        gyb[1, at, :] = g
        gz = nn(g, b2[...]) * db[0, at, :]
        db[0, at, :] = gz
        c, d = c + column_sum(gz), d + column_sum(gz * yb[0, at, :])
        return a, b, c, d

    stats = lax.fori_loop(0, steps, back_one, (zero1, zero1, zero2, zero2))
    for r in range(4):
        put(4, r, stats[r])
    sent.append(push(4))
    q_out[:s1, h1 : 2 * h1] = weight_grad(gyn[2], un[1], s1)
    q_out[n_rows : n_rows + s2, :] = weight_grad(gyb[1], ub[0], s2)
    total = pull(4, sent[4])
    t_n2, t_b1 = total[0:2, :h1], total[2:4, :h2]

    def back_two(i, carry):
        a, b = carry
        at = rowset(i)
        g = grad_y(dn[1, at, :], yn[1, at, :], rstd_n2, gain_n(1)[0], t_n2)
        gyn[1, at, :] = g
        gz = nn(g, n23[0]) * dn[0, at, :]
        dn[0, at, :] = gz
        return a + column_sum(gz), b + column_sum(gz * yn[0, at, :])

    stats = lax.fori_loop(0, steps, back_two, (zero1, zero1))
    for r in range(2):
        put(5, r, stats[r])
    sent.append(push(5))

    def gate_back(k, at, grad):
        x = feat[at, :].astype(jnp.float32)
        value = gate[k, at, :]
        g = low(grad * x * value * (1.0 - 0.5 * value))
        grad_gate[k, at, :] = g
        return grad * value, g

    def back_broad(i, carry):
        at = rowset(i)
        g = grad_y(db[0, at, :], yb[0, at, :], rstd_b1, gain_b(0)[0], t_b1)
        gyb[0, at, :] = g
        term, _ = gate_back(1, at, nn(g, b1[...]))
        own_term[at, :] = term
        return carry

    lax.fori_loop(0, steps, back_broad, 0)
    q_out[:s1, :h1] = weight_grad(gyn[1], un[0], s1)
    p_out[2 * g_rows + n_rows : 2 * g_rows + n_rows + s2, :] = weight_grad(gyb[0], fields[1], s2)
    p_out[g_rows : g_rows + gcols, :] = weight_grad(grad_gate[1], feat[...], gcols)
    total = pull(5, sent[5])
    t_n1 = total[0:2, :h1]

    def back_narrow(i, carry):
        ga, gb, ne = carry
        at = rowset(i)
        g = grad_y(dn[0, at, :], yn[0, at, :], rstd_n1, gain_n(0)[0], t_n1)
        gyn[0, at, :] = g
        term, g0 = gate_back(0, at, nn(g, n1[...]))
        g1 = grad_gate[1, at, :]
        whole = nn(g0, gates[0]) + nn(g1, gates[1]) + term + own_term[at, :]
        whole = low(whole).astype(jnp.float32)
        own_term[at, :] = whole
        ne = ne + column_sum(whole[:, :num] * widen_dense(dense[at, :], 16))
        return ga + column_sum(g0.astype(jnp.float32)), gb + column_sum(g1.astype(jnp.float32)), ne

    zero_g = jnp.zeros((1, wide), jnp.float32)
    ga, gb, ne = lax.fori_loop(
        0, steps, back_narrow, (zero_g, zero_g, jnp.zeros((1, num), jnp.float32))
    )
    grads_t[...] = low(jnp.transpose(own_term[:, num:]))
    p_out[:gcols, :] = weight_grad(grad_gate[0], feat[...], gcols)
    p_out[2 * g_rows : 2 * g_rows + s1, :] = weight_grad(gyn[0], fields[0], s1)
    small[...] = jnp.zeros_like(small)
    small[0:1, :gcols] = own_columns(ga, mine, gcols, mp)
    small[1:2, :gcols] = own_columns(gb, mine, gcols, mp)
    small[2:3, :num] = ne
    for layer, t in enumerate((t_n1, t_n2, t_n3)):
        n_shift_g[layer : layer + 1, :] = own_columns(t[0:1], mine, s1, mp)
        n_gain_g[layer : layer + 1, :] = own_columns(t[1:2], mine, s1, mp)
    for layer, t in enumerate((t_b1, t_b2)):
        b_shift_g[layer : layer + 1, :] = own_columns(t[0:1], mine, s2, mp)
        b_gain_g[layer : layer + 1, :] = own_columns(t[1:2], mine, s2, mp)
    total = pull(6, join_sent)
    left_g[...] = total[0:1, :h1]
    right_g[...] = total[1:2, :h2]
    bias_g[...] = total[2:3, 0:1]
    copy_a.wait_send()
    copy_b.wait_send()
    for copy in copies:
        copy.wait_send()
    for group in sent + [join_sent]:
        for copy in group:
            copy.wait_send()


def reduce_kernel(
    dp, mp,
    grads, p_in, q_in, small,
    table_g, gate_g, n_first_g, n_rest_g, b_first_g, b_rest_g, pair_g, small_out,
    landed, shares, s_slots, p_work, q_work, p_land, q_land, p_full, q_full,
    send, recv, send2, recv2, send3, recv3, psend, precv,
):
    tall = grads.shape[0] // dp
    me, mine = lax.axis_index("dp"), lax.axis_index("mp")
    greet(dp, mp)
    levels = dp.bit_length() - 1
    orders = (list(range(levels)), list(range(1, levels)) + [0])
    p_work[...] = p_in[...]
    q_work[...] = q_in[...]
    s_slots[me] = small[...]
    works = (p_work, q_work)
    lands = (p_land, q_land)
    fulls = (p_full, q_full)
    starts = [0, 0]
    sizes = [p_work.shape[0], q_work.shape[0]]
    waits = []

    def flip(bit):
        return me + (1 << bit) - 2 * (1 << bit) * lax.rem(me // (1 << bit), 2)

    def halve(w, level):
        bit = orders[w][level]
        size = sizes[w] // 2
        up = lax.rem(me // (1 << bit), 2)
        keep = starts[w] + up * size
        give = starts[w] + (1 - up) * size
        offset = works[w].shape[0] - 2 * size
        where = pl.ds(offset, size)
        copy = remote(
            works[w].at[pl.ds(pl.multiple_of(give, 16), size), :], lands[w].at[where, :],
            psend.at[w, level], precv.at[w, level], {"dp": flip(bit)},
        )
        copy.start()
        starts[w], sizes[w] = keep, size
        return copy, where

    def add(w, copy, where):
        copy.wait_recv()
        at = pl.ds(pl.multiple_of(starts[w], 16), sizes[w])
        works[w][at, :] = low(
            works[w][at, :].astype(jnp.float32) + lands[w][where, :].astype(jnp.float32)
        )
        waits.append(copy)

    def double(w, level):
        bit = orders[w][level]
        at = fulls[w].at[pl.ds(pl.multiple_of(starts[w], 16), sizes[w]), :]
        copy = remote(at, at, psend.at[w, levels + level], precv.at[w, levels + level], {"dp": flip(bit)})
        copy.start()
        up = lax.rem(me // (1 << bit), 2)
        starts[w] = starts[w] - up * sizes[w]
        sizes[w] = sizes[w] * 2
        return copy

    pend = [halve(w, 0) for w in (0, 1)]
    copies = []
    for step in range(1, dp):
        to = lax.rem(me + step, dp)
        copy = remote(
            grads.at[pl.ds(pl.multiple_of(to * tall, 16), tall), :],
            landed.at[step - 1], send.at[step - 1], recv.at[step - 1], {"dp": to},
        )
        copy.start()
        copies.append(copy)
    small_copies = spread_dp(dp, lambda k: s_slots.at[k], send3, recv3)
    for level in range(1, levels):
        for w in (0, 1):
            add(w, *pend[w])
            pend[w] = halve(w, level)
    total = grads[pl.ds(pl.multiple_of(me * tall, 16), tall), :].astype(jnp.float32)
    for step in range(1, dp):
        copies[step - 1].wait_recv()
        total = total + landed[step - 1].astype(jnp.float32)
    shares[mine] = total.astype(jnp.bfloat16)

    def slot(i):
        return shares.at[i]

    started = relay_own(mp, slot, send2, recv2)
    back = []
    for w in (0, 1):
        add(w, *pend[w])
        at = pl.ds(pl.multiple_of(starts[w], 16), sizes[w])
        fulls[w][at, :] = works[w][at, :]
        back.append(double(w, levels - 1))
    relay_rest(mp, slot, send2, recv2, started)
    blocks = tall // 16
    for m in range(mp):
        for b in range(blocks):
            table_g[:, (m * blocks + b) * HI : (m * blocks + b + 1) * HI] = shares[
                m, b * 16 : (b + 1) * 16, :
            ].astype(jnp.float32)
    for level in range(levels - 2, -1, -1):
        for w in (0, 1):
            back[w].wait_recv()
            waits.append(back[w])
            back[w] = double(w, level)
    for copy in small_copies:
        copy.wait_recv()
    value = s_slots[0]
    for d in range(1, dp):
        value = value + s_slots[d]
    small_out[...] = value
    for w in (0, 1):
        back[w].wait_recv()
        waits.append(back[w])
    def up16(x):
        return -(-x // 16) * 16

    gcols, s1, s2, h1 = gate_g.shape[1], n_first_g.shape[0], b_first_g.shape[0], n_rest_g.shape[2]
    g_rows, n_rows, b_rows = up16(gcols), up16(s1), up16(s2)

    def full(work, row, count, col, width):
        return work[row : row + count, col : col + width].astype(jnp.float32)

    wide = n_first_g.shape[1]
    gate_g[0] = full(p_full, 0, gcols, 0, wide)
    gate_g[1] = full(p_full, g_rows, gcols, 0, wide)
    n_first_g[...] = full(p_full, 2 * g_rows, s1, 0, wide)
    b_first_g[...] = full(p_full, 2 * g_rows + n_rows, s2, 0, wide)
    n_rest_g[0] = full(q_full, 0, s1, 0, h1)
    n_rest_g[1] = full(q_full, 0, s1, h1, h1)
    b_rest_g[...] = full(q_full, n_rows, s2, 0, 2 * h1)
    pair_g[...] = jnp.transpose(full(q_full, n_rows + b_rows, 16, 0, 512))[:h1, :]
    for copy in copies + small_copies + waits:
        copy.wait_send()


def f32(*shape):
    return jax.ShapeDtypeStruct(shape, jnp.float32)


def b16(*shape):
    return jax.ShapeDtypeStruct(shape, jnp.bfloat16)


def held(*shape):
    return pltpu.VMEM(shape, jnp.float32)


def held16(*shape):
    return pltpu.VMEM(shape, jnp.bfloat16)


def dma(*shape):
    return pltpu.SemaphoreType.DMA(shape)


def shards(
    dense_values,
    field_ids,
    lengths,
    labels,
    num_embed,
    embed_table,
    gate_weight,
    gate_bias,
    narrow_first,
    narrow_rest,
    narrow_gain,
    narrow_shift,
    broad_first,
    broad_rest,
    broad_gain,
    broad_shift,
    joining_left,
    joining_right,
    joining_pair,
    joining_bias,
):
    dp, mp = lax.axis_size("dp"), lax.axis_size("mp")
    chips = mp // 2
    rows = dense_values.shape[0]
    cats, slots = field_ids.shape[:2]
    width, own_rows = embed_table.shape
    num = dense_values.shape[1] * width
    wide = gate_weight.shape[2]
    gcols = gate_weight.shape[1]
    s1, s2 = narrow_first.shape[0], broad_first.shape[0]
    h1, h2 = s1 * mp, s2 * mp
    hx = joining_pair.shape[1]
    bits = (cats * rows - 1).bit_length()
    tall = own_rows // mp // HI * 16
    vregs = 1 << (-(-(cats * slots * rows) // 1024) - 1).bit_length()
    t2, keys, numeric, gates, n1, b1, vec = pl.pallas_call(
        functools.partial(first_kernel, dp, mp, own_rows, bits),
        out_shape=(
            b16(dp * tall, HI),
            jax.ShapeDtypeStruct((128, vregs * 8), jnp.int32),
            b16(rows, num),
            b16(2, wide, wide),
            b16(h1, wide),
            b16(h2, wide),
            f32(16, 896),
        ),
        in_specs=[VM] * 13,
        out_specs=(VM,) * 7,
        scratch_shapes=[
            pltpu.VMEM((vregs * 8, 128), jnp.int32),
            held16(mp, 2, gcols, wide),
            held16(mp, s1, wide),
            held16(mp, s2, wide),
            held(mp, 16, 256),
            dma(dp - 1),
            dma(dp - 1),
            dma(4, mp),
            dma(4, mp),
        ],
        compiler_params=params(0),
        name="first",
    )(
        field_ids, lengths, embed_table, dense_values, num_embed.reshape(1, num), gate_weight, gate_bias,
        narrow_first, narrow_gain, narrow_shift, broad_first, broad_gain, broad_shift,
    )
    partial = pl.pallas_call(
        functools.partial(lookup_kernel, cats, rows, bits),
        out_shape=f32(cats * 16, rows),
        in_specs=[VM] * 2,
        out_specs=VM,
        scratch_shapes=[held(cats * 16, rows)],
        compiler_params=params(None),
        name="lookup",
    )(keys, t2)

    def up(x, n):
        return -(-x // n) * n

    p_rows = up(2 * up(gcols, 16) + up(s1, 16) + up(s2, 16), 16 * dp)
    q_rows = up(up(s1, 16) + up(s2, 16) + 16, 16 * dp)
    (
        logits, grads_t, p_part, q_part, small,
        n_gain_g, n_shift_g, b_gain_g, b_shift_g, left_g, right_g, bias_g,
    ) = pl.pallas_call(
        functools.partial(dense_kernel, dp, mp, hx, float(rows * dp)),
        out_shape=(
            f32(1, rows),
            b16(cats * 16, rows),
            b16(p_rows, wide),
            b16(q_rows, h2),
            f32(8, 256),
            f32(3, s1),
            f32(3, s1),
            f32(2, s2),
            f32(2, s2),
            f32(1, h1),
            f32(1, h2),
            f32(1, 1),
        ),
        in_specs=[VM] * 14,
        out_specs=(VM,) * 12,
        scratch_shapes=[
            held(cats * 8, rows),
            held16(chips, cats * 8, rows),
            held16(cats * 16, rows),
            held16(rows, wide),
            held(2, rows, wide),
            held16(2, rows, wide),
            held(rows, wide),
            held16(2, rows, wide),
            held16(mp, 2, s1, h1),
            held16(mp, s2, h2),
            held16(2, h1, h1),
            held16(h2, h2),
            held(3, rows, h1),
            held(3, rows, h1),
            held(2, rows, h2),
            held(2, rows, h2),
            held16(3, rows, h1),
            held16(2, rows, h2),
            held16(3, rows, h1),
            held16(2, rows, h2),
            held16(h1, h2),
            held16(h1, h2),
            held(h2, h1),
            held(7, dp, 4, 896),
            dma(chips + 1),
            dma(chips + 1),
            dma(2, mp),
            dma(2, mp),
            dma(7, dp - 1),
            dma(7, dp - 1),
        ],
        compiler_params=params(1, 60),
        name="dense",
    )(
        partial, numeric, gates, n1, b1, narrow_rest, broad_rest, vec,
        joining_left.reshape(1, h1), joining_right.reshape(1, h2), joining_pair.reshape(h1, width),
        joining_bias.reshape(1, 1), labels.reshape(1, rows), dense_values,
    )
    row_sums = pl.pallas_call(
        functools.partial(scatter_kernel, cats, rows, bits),
        out_shape=b16(dp * tall, HI),
        in_specs=[VM] * 2,
        out_specs=VM,
        scratch_shapes=[held(dp * tall, HI)],
        compiler_params=params(None),
        name="scatter",
    )(keys, grads_t)
    (
        embed_table_grad, gate_weight_grad, narrow_first_grad, narrow_rest_grad,
        broad_first_grad, broad_rest_grad, pair_g, small,
    ) = pl.pallas_call(
        functools.partial(reduce_kernel, dp, mp),
        out_shape=(
            f32(width, own_rows),
            f32(2, gcols, wide),
            f32(s1, wide),
            f32(2, s1, h1),
            f32(s2, wide),
            f32(s2, h2),
            f32(h1, width),
            f32(8, 256),
        ),
        in_specs=[VM] * 4,
        out_specs=(VM,) * 8,
        scratch_shapes=[
            held16(dp - 1, tall, HI),
            held16(mp, tall, HI),
            held(dp, 8, 256),
            held16(p_rows, wide),
            held16(q_rows, h2),
            held16(p_rows, wide),
            held16(q_rows, h2),
            held16(p_rows, wide),
            held16(q_rows, h2),
            dma(dp - 1),
            dma(dp - 1),
            dma(mp),
            dma(mp),
            dma(dp - 1),
            dma(dp - 1),
            dma(2, 2 * (dp.bit_length() - 1)),
            dma(2, 2 * (dp.bit_length() - 1)),
        ],
        compiler_params=params(2),
        name="reduce",
    )(row_sums, p_part, q_part, small)
    return (
        logits.reshape(rows),
        small[2, :num].reshape(-1, width),
        embed_table_grad,
        gate_weight_grad,
        small[:2, :gcols],
        narrow_first_grad,
        narrow_rest_grad,
        n_gain_g,
        n_shift_g,
        broad_first_grad,
        broad_rest_grad,
        b_gain_g,
        b_shift_g,
        left_g.reshape(h1),
        right_g.reshape(h2),
        pair_g.reshape(joining_pair.shape),
        bias_g.reshape(1),
    )


def solution(mesh):
    placed = (
        P("dp", None),
        P(None, None, "dp"),
        P(None, "dp"),
        P("dp"),
        P(),
        P(None, "dp"),
        P(None, "mp", None),
        P(None, "mp"),
        P("mp", None),
        P(None, "mp", None),
        P(None, "mp"),
        P(None, "mp"),
        P("mp", None),
        P("mp", None),
        P(None, "mp"),
        P(None, "mp"),
        P(),
        P(),
        P(),
        P(),
    )
    return jax.shard_map(
        shards,
        mesh=mesh,
        in_specs=placed,
        out_specs=(
            P("dp"),
            P(),
            P(None, "dp"),
            P(None, "mp", None),
            P(None, "mp"),
            P("mp", None),
            P(None, "mp", None),
            P(None, "mp"),
            P(None, "mp"),
            P("mp", None),
            P("mp", None),
            P(None, "mp"),
            P(None, "mp"),
            P(),
            P(),
            P(),
            P(),
        ),
        check_vma=False,
    )
```

```python
import functools
import jax
import jax.numpy as jnp
from jax import lax
from jax.experimental import pallas as pl
from jax.experimental.pallas import tpu as pltpu
from jax.sharding import PartitionSpec as P

MESH = pl.DeviceIdType.MESH
VM = pl.BlockSpec(memory_space=pltpu.VMEM)
ANY = pl.BlockSpec(memory_space=pltpu.HBM)
HI = 256
CHUNK = 512


def params(cid, mib=48):
    if cid is None:
        return pltpu.CompilerParams(vmem_limit_bytes=mib << 20)
    return pltpu.CompilerParams(
        collective_id=cid, has_side_effects=True, vmem_limit_bytes=mib << 20
    )


def hail(dp, mp):
    me, mine = lax.axis_index("dp"), lax.axis_index("mp")
    barrier = pltpu.get_barrier_semaphore()
    for step in range(1, dp):
        pl.semaphore_signal(
            barrier, inc=1, device_id={"dp": lax.rem(me + step, dp)}, device_id_type=MESH
        )
    for step in range(1, mp):
        pl.semaphore_signal(
            barrier, inc=1, device_id={"mp": lax.rem(mine + step, mp)}, device_id_type=MESH
        )


def all_in(dp, mp):
    pl.semaphore_wait(pltpu.get_barrier_semaphore(), dp - 1 + mp - 1)


def remote(src, dst, send, recv, where):
    return pltpu.make_async_remote_copy(
        src_ref=src, dst_ref=dst, send_sem=send, recv_sem=recv,
        device_id=where, device_id_type=MESH,
    )


def spread_dp(dp, pick, send, recv):
    me = lax.axis_index("dp")
    out = []
    for step in range(1, dp):
        to = lax.rem(me + step, dp)
        copy = remote(pick(me), pick(me), send.at[step - 1], recv.at[step - 1], {"dp": to})
        copy.start()
        out.append(copy)
    return out


def compact_keys(key):
    count = key.shape[0]
    dead = (key < 0).astype(jnp.int32)
    sub = lax.broadcasted_iota(jnp.int32, (8, 128), 0)
    lane = lax.broadcasted_iota(jnp.int32, (8, 128), 1)
    running = jnp.zeros((8, 128), jnp.int32)
    before = []
    for v in range(count):
        before.append(running)
        running = running + dead[v]
    scan = running
    for k in (1, 2, 4):
        scan = scan + jnp.where(sub >= k, pltpu.roll(scan, k, 0), 0)
    over_sub = scan - running
    column = jnp.broadcast_to(jnp.sum(running, axis=0, keepdims=True), (8, 128))
    scan = column
    for k in (1, 2, 4, 8, 16, 32, 64):
        scan = scan + jnp.where(lane >= k, pltpu.roll(scan, k, 1), 0)
    base = over_sub + scan - column
    shift = jnp.stack([jnp.where(dead[v] > 0, 0, before[v] + base) for v in range(count)])

    def next_place(x):
        n = x.shape[0]
        flat = x.reshape(n * 8, 128)
        y = jnp.stack([pltpu.roll(x[v], 7, 0) for v in range(n)])
        z = jnp.stack([pltpu.roll(y[v], 127, 1) for v in range(n)])
        return jnp.where(sub[None] < 7, y, z)

    bit = 0
    step = 1
    while step < count:
        moved_key = jnp.concatenate([key[step:], next_place(key[:step])], axis=0)
        moved_shift = jnp.concatenate([shift[step:], next_place(shift[:step])], axis=0)
        key, shift = settle(key, shift, moved_key, moved_shift, bit)
        bit, step = bit + 1, step * 2
    for j in (1, 2, 4):
        def roll_sub(x):
            y = jnp.stack([pltpu.roll(x[v], 8 - j, 0) for v in range(count)])
            z = jnp.stack([pltpu.roll(y[v], 127, 1) for v in range(count)])
            return jnp.where(sub[None] < 8 - j, y, z)
        key, shift = settle(key, shift, roll_sub(key), roll_sub(shift), bit)
        bit += 1
    for j in (1, 2, 4, 8, 16, 32, 64):
        def roll_lane(x):
            return jnp.stack([pltpu.roll(x[v], 128 - j, 1) for v in range(count)])
        key, shift = settle(key, shift, roll_lane(key), roll_lane(shift), bit)
        bit += 1
    return key


def settle(key, shift, moved_key, moved_shift, bit):
    take = (moved_shift & (1 << bit)) != 0
    stay = (shift & (1 << bit)) == 0
    key = jnp.where(take, moved_key, jnp.where(stay, key, -1))
    shift = jnp.where(take, moved_shift, jnp.where(stay, shift, 0))
    return key, shift


def make_keys(ids, lens, scratch, own_rows, mp, bits):
    cats, slots, rows = ids.shape
    part = own_rows // mp
    mine = lax.axis_index("mp")
    scratch[...] = jnp.full_like(scratch, -1)
    slot = lax.broadcasted_iota(jnp.int32, (slots, rows), 0)
    event = lax.broadcasted_iota(jnp.int32, (slots, rows), 1)

    def body(c, carry):
        values = ids[c]
        holder = values // own_rows
        inner = values - holder * own_rows
        owner = inner // part
        place = holder * part + inner - owner * part
        live = (slot < lens[pl.ds(c, 1), :]) & (owner == mine)
        key = jnp.where(live, place * (1 << bits) + c * rows + event, -1)
        for q in range(rows // 128):
            scratch[pl.ds((c * (rows // 128) + q) * slots, slots), :] = key[:, q * 128 : (q + 1) * 128]
        return carry

    lax.fori_loop(0, cats, body, 0)


def lookup_kernel(cats, rows, bits, keys, t2, pooled, total):
    lows = t2.shape[0] // 16
    filled = jnp.max(keys[...], axis=1, keepdims=True) >= 0
    chunks = jnp.sum(filled.astype(jnp.int32))
    total[...] = jnp.zeros_like(total)
    hi_iota = lax.broadcasted_iota(jnp.int32, (HI, CHUNK), 0)
    event_iota = lax.broadcasted_iota(jnp.int32, (rows, CHUNK), 0)

    def body(k, carry):
        key = keys[pl.ds(k, 1), :]
        place = lax.shift_right_arithmetic(key, bits)
        bag = key & ((1 << bits) - 1)
        cat = bag // rows
        event = bag - cat * rows
        low = lax.shift_right_arithmetic(place, 8)
        high = place & (HI - 1)
        pick = jnp.where(hi_iota == high, 1.0, 0.0).astype(jnp.bfloat16)
        z = jnp.zeros((16, CHUNK), jnp.float32)
        for b in range(0, lows, 16):
            n = min(16, lows - b)
            y = jnp.dot(t2[b * 16 : (b + n) * 16, :], pick, preferred_element_type=jnp.float32)
            for j in range(n):
                z = z + jnp.where(low == b + j, y[j * 16 : (j + 1) * 16], 0.0)
        z = z.astype(jnp.bfloat16)
        zero = jnp.zeros_like(z)
        wide = jnp.concatenate([jnp.where(cat == c, z, zero) for c in range(cats)], axis=0)
        place_of = jnp.where(event_iota == event, 1.0, 0.0).astype(jnp.bfloat16)
        total[...] += lax.dot_general(
            wide, place_of, (((1,), (1,)), ((), ())), preferred_element_type=jnp.float32
        )
        return carry

    lax.fori_loop(0, chunks, body, 0)
    pooled[...] = total[...].astype(pooled.dtype)


def scatter_kernel(cats, rows, bits, keys, grad, out, total):
    lows = total.shape[0] // 16
    filled = jnp.max(keys[...], axis=1, keepdims=True) >= 0
    chunks = jnp.sum(filled.astype(jnp.int32))
    total[...] = jnp.zeros_like(total)
    hi_iota = lax.broadcasted_iota(jnp.int32, (HI, CHUNK), 0)
    event_iota = lax.broadcasted_iota(jnp.int32, (rows, CHUNK), 0)

    def body(k, carry):
        key = keys[pl.ds(k, 1), :]
        place = lax.shift_right_arithmetic(key, bits)
        bag = key & ((1 << bits) - 1)
        cat = bag // rows
        event = bag - cat * rows
        low = lax.shift_right_arithmetic(place, 8)
        high = place & (HI - 1)
        place_of = jnp.where(event_iota == event, 1.0, 0.0).astype(jnp.bfloat16)
        wide = jnp.dot(grad[...], place_of, preferred_element_type=jnp.float32)
        g = jnp.zeros((16, CHUNK), jnp.float32)
        for c in range(cats):
            g = g + jnp.where(cat == c, wide[c * 16 : (c + 1) * 16], 0.0)
        g = g.astype(jnp.bfloat16)
        zero = jnp.zeros_like(g)
        pick = jnp.where(hi_iota == high, 1.0, 0.0).astype(jnp.bfloat16)
        for b in range(0, lows, 16):
            n = min(16, lows - b)
            tall = jnp.concatenate([jnp.where(low == b + j, g, zero) for j in range(n)], axis=0)
            total[b * 16 : (b + n) * 16, :] += lax.dot_general(
                tall, pick, (((1,), (1,)), ((), ())), preferred_element_type=jnp.float32
            )
        return carry

    lax.fori_loop(0, chunks, body, 0)
    out[...] = total[...].astype(out.dtype)


def relay_own(mp, slot, send, recv):
    mine = lax.axis_index("mp")
    core = lax.rem(mine, 2)
    other = mine + 1 - 2 * core
    chips = mp // 2
    out = []
    for k in range(1, chips):
        to = lax.rem(mine + 2 * k, mp)
        copy = remote(slot(mine), slot(mine), send.at[2 * k], recv.at[2 * k], {"mp": to})
        copy.start()
        out.append(copy)
    copy = remote(slot(mine), slot(mine), send.at[1], recv.at[1], {"mp": other})
    copy.start()
    out.append(copy)
    return out


def relay_rest(mp, slot, send, recv, started):
    mine = lax.axis_index("mp")
    core = lax.rem(mine, 2)
    other = mine + 1 - 2 * core
    chips = mp // 2
    passed = []
    for k in range(1, chips):
        source = lax.rem(mine + mp - 2 * k, mp)
        remote(slot(source), slot(source), send.at[2 * k], recv.at[2 * k], {"mp": other}).wait_recv()
        copy = remote(slot(source), slot(source), send.at[2 * k + 1], recv.at[2 * k + 1], {"mp": other})
        copy.start()
        passed.append(copy)
    remote(slot(other), slot(other), send.at[1], recv.at[1], {"mp": other}).wait_recv()
    for k in range(1, chips):
        far = lax.rem(other + mp - 2 * k, mp)
        remote(slot(far), slot(far), send.at[2 * k + 1], recv.at[2 * k + 1], {"mp": other}).wait_recv()
    for copy in started + passed:
        copy.wait_send()


def nn(a, b):
    return jnp.dot(a, b, preferred_element_type=jnp.float32)


def nt(a, b):
    return lax.dot_general(a, b, (((1,), (1,)), ((), ())), preferred_element_type=jnp.float32)


def tn(a, b):
    return lax.dot_general(a, b, (((0,), (0,)), ((), ())), preferred_element_type=jnp.float32)


def sigmoid(x):
    return 0.5 * jnp.tanh(0.5 * x) + 0.5


def low(x):
    return x.astype(jnp.bfloat16)


def column_sum(x):
    return jnp.sum(x, axis=0, keepdims=True)


def widen_dense(dense_t, width):
    fields = dense_t.shape[0]
    row = lax.broadcasted_iota(jnp.int32, (fields, fields * width), 0)
    col = lax.broadcasted_iota(jnp.int32, (fields, fields * width), 1)
    ones = jnp.where(col // width == row, 1.0, 0.0)
    return lax.dot_general(
        dense_t, ones, (((0,), (0,)), ((), ())),
        precision=lax.Precision.HIGHEST, preferred_element_type=jnp.float32,
    )


def bring(sources, places, sem):
    copies = []
    for i, (source, place) in enumerate(zip(sources, places)):
        copy = pltpu.make_async_copy(source, place, sem.at[i])
        copy.start()
        copies.append(copy)
    return copies


def first_kernel(dp, mp, own_rows, bits, *refs):
    count = 13
    sources, refs = refs[:count], refs[count:]
    t2, keys, numeric, gates, n1, vec, n_own = refs[:7]
    places, refs = refs[7 : 7 + count], refs[7 + count :]
    scratch, gate_slots, n_slots, v_slots, send, recv, send2, recv2, sem = refs
    brought = bring(sources, places, sem)
    (
        table, gate_w, n_first, gate_b, n_gain, n_shift, b_gain, b_shift,
        ids, lens, dense_t, num_embed, n_rest,
    ) = places
    part = own_rows // mp
    blocks = part // HI
    tall = blocks * 16
    me, mine = lax.axis_index("dp"), lax.axis_index("mp")
    hail(dp, mp)
    for copy in brought[:8]:
        copy.wait()
    own = table[:, pl.ds(pl.multiple_of(mine * part, HI), part)].astype(jnp.bfloat16)
    for b in range(blocks):
        t2[pl.ds(pl.multiple_of(me * tall + b * 16, 16), 16), :] = own[:, b * HI : (b + 1) * HI]
    for k in range(2):
        gate_slots[mine, k] = gate_w[:, k, :]
    n_slots[mine] = n_first[...]
    row = 0
    for ref in (gate_b, n_gain, n_shift, b_gain, b_shift):
        v_slots[mine, row : row + ref.shape[0], : ref.shape[1]] = ref[...]
        row += ref.shape[0]
    all_in(dp, mp)

    def slot(i):
        return t2.at[pl.ds(pl.multiple_of(i * tall, 16), tall), :]

    groups = []
    for i, ref in enumerate((gate_slots, n_slots, v_slots)):
        started = relay_own(mp, lambda k, ref=ref: ref.at[k], send2.at[i], recv2.at[i])
        groups.append((ref, i, started))
    copies = spread_dp(dp, slot, send, recv)
    for copy in brought[8:]:
        copy.wait()
    for k in range(2):
        n_own[k] = n_rest[:, k, :]
    fields, width = num_embed.shape
    tiled = jnp.concatenate([num_embed[...]] * fields, axis=1)
    row = lax.broadcasted_iota(jnp.int32, tiled.shape, 0)
    col = lax.broadcasted_iota(jnp.int32, tiled.shape, 1)
    num_row = column_sum(jnp.where(col // width == row, tiled, 0.0))
    numeric[...] = low(widen_dense(dense_t[...], width) * num_row)
    make_keys(ids, lens, scratch, own_rows, mp, bits)
    count = scratch.shape[0] // 8
    packed = compact_keys(scratch[...].reshape(count, 8, 128))
    keys[...] = jnp.transpose(packed.reshape(count * 8, 128))
    for ref, i, started in groups:
        relay_rest(mp, lambda k, ref=ref: ref.at[k], send2.at[i], recv2.at[i], started)
    cols, small = gate_slots.shape[2], n_first.shape[0]
    for m in range(mp):
        for k in range(2):
            gates[k, m * cols : (m + 1) * cols, :] = gate_slots[m, k]
        n1[m * small : (m + 1) * small, :] = n_slots[m]
    row = 0
    for ref in (gate_b, n_gain, n_shift, b_gain, b_shift):
        r, w = ref.shape
        vec[row : row + r, : mp * w] = jnp.concatenate(
            [v_slots[m, row : row + r, :w] for m in range(mp)], axis=1
        )
        row += r
    for copy in copies:
        copy.wait()


def own_columns(x, mine, width, mp):
    out = jnp.zeros((x.shape[0], width), x.dtype)
    for m in range(mp):
        out = jnp.where(mine == m, x[:, m * width : (m + 1) * width], out)
    return out


def up16(x):
    return -(-x // 16) * 16


def own_part(x, mine, width):
    full = x.shape[1]
    pad = -(-width // 128) * 128
    row = lax.broadcasted_iota(jnp.int32, (full, pad), 0)
    col = lax.broadcasted_iota(jnp.int32, (full, pad), 1)
    choose = jnp.where((row == col + mine * width) & (col < width), 1.0, 0.0).astype(jnp.bfloat16)
    return low(nn(x, choose))


def weight_grad(grad_y, inputs, mine, width):
    return low(tn(own_part(grad_y, mine, width), inputs)[:width, :])


def dense_kernel(
    dp, mp, hx, batch,
    partial, numeric, gates, n1, n_rest, vec,
    b_first_hbm, b_rest_hbm, left_hbm, right_hbm, pair_hbm, bias_hbm, labels_hbm, dense_hbm,
    logits, grads_t, feat, fields, grad_gate, gyn1, gyb1, q_out, small,
    n_gain_g, n_shift_g, b_gain_g, b_shift_g, left_g, right_g, bias_g,
    half_a, half_c, pooled, gate, own_term, b1_slots, n_slots, b_slots, b1, n23, b2,
    yn, dn, yb, db, un, ub, gyn, gyb, pair_hi, pair_lo, pair_g, to_first, sums,
    fsend, frecv, wsend, wrecv, ssend, srecv,
    b_first, b_rest, left, right, pair_t, bias, labels, dense_t, sem,
):
    brought = bring(
        (b_first_hbm, b_rest_hbm, left_hbm, right_hbm, pair_hbm, bias_hbm, labels_hbm, dense_hbm),
        (b_first, b_rest, left, right, pair_t, bias, labels, dense_t),
        sem,
    )
    me, mine = lax.axis_index("dp"), lax.axis_index("mp")
    core = lax.rem(mine, 2)
    chip = mine // 2
    chips = mp // 2
    other = mine + 1 - 2 * core
    rows = feat.shape[0]
    block = 128
    steps = rows // block
    h1, h2 = n1.shape[0], b1.shape[0]
    s1, s2 = h1 // mp, h2 // mp
    wide = feat.shape[1]
    num = numeric.shape[1]
    gcols = wide // mp
    half = partial.shape[0] // 2
    hail(dp, mp)
    n_slots[mine] = n_rest[...]
    all_in(dp, mp)

    def rowset(i):
        return pl.ds(pl.multiple_of(i * block, block), block)

    def part(c):
        return pl.ds(pl.multiple_of(c * half, 16), half)

    copy_a = remote(partial.at[part(1 - core), :], half_a, fsend.at[0], frecv.at[0], {"mp": other})
    copy_a.start()
    for copy in brought:
        copy.wait()
    b1_slots[mine] = b_first[...]
    b_slots[mine] = b_rest[...]
    copy_a.wait_recv()
    half_c[chip] = low(partial[part(core), :] + half_a[...])
    copies = []
    for k in range(1, chips):
        copy = remote(
            half_c.at[chip], half_c.at[chip], fsend.at[k], frecv.at[k],
            {"mp": lax.rem(mine + 2 * k, mp)},
        )
        copy.start()
        copies.append(copy)
    heads = pair_t.shape[2]
    by_head = jnp.transpose(pair_t[...].reshape(hx * 16, heads))
    row = lax.broadcasted_iota(jnp.int32, (h1, heads), 0)
    col = lax.broadcasted_iota(jnp.int32, (h1, heads), 1)
    repeat = jnp.where(row // hx == col, 1.0, 0.0)
    tall = jnp.dot(repeat, by_head, precision=lax.Precision.HIGHEST, preferred_element_type=jnp.float32)
    row = lax.broadcasted_iota(jnp.int32, (h1, 16), 0)
    pick = jnp.zeros((h1, 16), jnp.float32)
    for i in range(hx):
        pick = jnp.where(row % hx == i, tall[:, i * 16 : (i + 1) * 16], pick)
    for i in range(0, h1, 80):
        row = lax.broadcasted_iota(jnp.int32, (80, h2), 0) + i
        col = lax.broadcasted_iota(jnp.int32, (80, h2), 1)
        pieces = jnp.concatenate([pick[i : i + 80, :]] * heads, axis=1)
        spread = jnp.where(row // hx == col // 16, pieces, 0.0)
        high = low(spread)
        pair_hi[i : i + 80, :] = high
        pair_lo[i : i + 80, :] = low(spread - high.astype(jnp.float32))
    for copy in copies:
        copy.wait_recv()
    total = half_c[0].astype(jnp.float32)
    for k in range(1, chips):
        total = total + half_c[k].astype(jnp.float32)
    pooled[part(core), :] = low(total)
    copy_b = remote(
        pooled.at[part(core), :], pooled.at[part(core), :], fsend.at[chips], frecv.at[chips], {"mp": other}
    )
    copy_b.start()
    weights = (b1_slots, n_slots, b_slots)
    moving = [
        relay_own(mp, lambda k, ref=ref: ref.at[k], wsend.at[i], wrecv.at[i])
        for i, ref in enumerate(weights)
    ]

    def arrive(i):
        relay_rest(mp, lambda k: weights[i].at[k], wsend.at[i], wrecv.at[i], moving[i])

    feat[:, :num] = numeric[...]
    copy_b.wait_recv()
    feat[:, num:] = low(jnp.transpose(pooled[...].astype(jnp.float32)))
    started = []

    def push(slot, *values):
        width = -(-values[0].shape[1] // 128) * 128
        for r, value in enumerate(values):
            sums[slot, me, r : r + 1, : value.shape[1]] = value
        out = []
        for step in range(1, dp):
            at = sums.at[slot, me, :, pl.ds(0, width)]
            copy = remote(
                at, at, ssend.at[slot, step - 1], srecv.at[slot, step - 1], {"dp": lax.rem(me + step, dp)}
            )
            copy.start()
            out.append(copy)
        started.append(out)
        return slot, width, out

    def pull(sent):
        slot, width, out = sent
        for copy in out:
            copy.wait_recv()
        total = sums[slot, 0, :, :width]
        for d in range(1, dp):
            total = total + sums[slot, d, :, :width]
        return total

    def norm(sent, width):
        total = pull(sent)
        mean = total[0:1, :width] / batch
        var = total[1:2, :width] / batch - mean * mean
        return mean, lax.rsqrt(var + 1e-05)

    def activate(y_ref, d_ref, u_ref, layer, at, mean, rstd, gain, shift):
        normed = (y_ref[layer, at, :] - mean) * rstd
        z = gain * normed + shift
        s = sigmoid(z)
        u = z * s
        y_ref[layer, at, :] = normed
        d_ref[layer, at, :] = s + u * (1.0 - s)
        u = low(u)
        u_ref[layer, at, :] = u
        return u

    def gain_n(layer):
        return vec[2 + layer : 3 + layer, :h1], vec[5 + layer : 6 + layer, :h1]

    def gain_b(layer):
        return vec[8 + layer : 9 + layer, :h2], vec[10 + layer : 11 + layer, :h2]

    zero1 = jnp.zeros((1, h1), jnp.float32)
    zero2 = jnp.zeros((1, h2), jnp.float32)

    def loop(body, *start):
        return lax.fori_loop(0, steps, lambda i, carry: body(rowset(i), *carry), tuple(start))

    def gates_and_first(at, a, b):
        x = feat[at, :]
        wide_x = x.astype(jnp.float32)
        for k in range(2):
            value = 2.0 * sigmoid(nt(x, gates[k]) + vec[k : k + 1, :wide])
            gate[k, at, :] = value
            fields[k, at, :] = low(wide_x * value)
        y = nt(fields[0, at, :], n1[...])
        yn[0, at, :] = y
        return a + column_sum(y), b + column_sum(y * y)

    sent_n = push(0, *loop(gates_and_first, zero1, zero1))
    arrive(0)
    for m in range(mp):
        b1[m * s2 : (m + 1) * s2, :] = b1_slots[m]

    def broad_first(at, a, b):
        y = nt(fields[1, at, :], b1[...])
        yb[0, at, :] = y
        return a + column_sum(y), b + column_sum(y * y)

    sent_b = push(1, *loop(broad_first, zero2, zero2))
    arrive(1)
    for m in range(mp):
        for k in range(2):
            n23[k, m * s1 : (m + 1) * s1, :] = n_slots[m, k]
    mean_n1, rstd_n1 = norm(sent_n, h1)

    def narrow_second(at, a, b):
        y = nt(activate(yn, dn, un, 0, at, mean_n1, rstd_n1, *gain_n(0)), n23[0])
        yn[1, at, :] = y
        return a + column_sum(y), b + column_sum(y * y)

    sent_n = push(2, *loop(narrow_second, zero1, zero1))
    arrive(2)
    for m in range(mp):
        b2[m * s2 : (m + 1) * s2, :] = b_slots[m]
    mean_b1, rstd_b1 = norm(sent_b, h2)

    def broad_second(at, a, b):
        y = nt(activate(yb, db, ub, 0, at, mean_b1, rstd_b1, *gain_b(0)), b2[...])
        yb[1, at, :] = y
        return a + column_sum(y), b + column_sum(y * y)

    sent_b = push(3, *loop(broad_second, zero2, zero2))
    mean_n2, rstd_n2 = norm(sent_n, h1)

    def narrow_third(at, a, b):
        y = nt(activate(yn, dn, un, 1, at, mean_n2, rstd_n2, *gain_n(1)), n23[1])
        yn[2, at, :] = y
        return a + column_sum(y), b + column_sum(y * y)

    sent_n = push(4, *loop(narrow_third, zero1, zero1))
    label = jnp.transpose(jnp.broadcast_to(labels[...].astype(jnp.float32), (8, rows)))[:, 0:1]
    own_term[:, 0:1] = label
    pair_g[...] = jnp.zeros_like(pair_g)
    mean_b2, rstd_b2 = norm(sent_b, h2)

    def broad_out(at):
        second = activate(yb, db, ub, 1, at, mean_b2, rstd_b2, *gain_b(1))
        to_first[at, :] = left[...] + (nt(second, pair_hi[...]) + nt(second, pair_lo[...]))
        return ()

    loop(broad_out)
    mean_n3, rstd_n3 = norm(sent_n, h1)
    to_right = right[...].reshape(1, h2)

    def join_narrow(at, l_sum, g_sum, a, b):
        first = activate(yn, dn, un, 2, at, mean_n3, rstd_n3, *gain_n(2)).astype(jnp.float32)
        second = ub[1, at, :].astype(jnp.float32)
        logit = (
            jnp.sum(first * to_first[at, :], axis=1, keepdims=True)
            + jnp.sum(second * to_right, axis=1, keepdims=True)
            + bias[...]
        )
        g = sigmoid(logit) - own_term[at, 0:1]
        own_term[at, 1:2] = logit
        own_term[at, 2:3] = g
        gz = g * to_first[at, :] * dn[2, at, :]
        dn[2, at, :] = gz
        return (
            l_sum + column_sum(g * first), g_sum + column_sum(g),
            a + column_sum(gz), b + column_sum(gz * yn[2, at, :]),
        )

    l_sum, g_sum, a, b = loop(join_narrow, zero1, jnp.zeros((1, 1), jnp.float32), zero1, zero1)
    sent_n = push(5, a, b)

    def join_broad(at, r_sum, a, b):
        first = un[2, at, :]
        second = ub[1, at, :]
        g = own_term[at, 2:3]
        turned = nn(first, pair_hi[...]) + nn(first, pair_lo[...])
        pair_g[...] += tn(second, low(g * first.astype(jnp.float32)))
        gz = g * (to_right + turned) * db[1, at, :]
        db[1, at, :] = gz
        return (
            r_sum + column_sum(g * second.astype(jnp.float32)),
            a + column_sum(gz), b + column_sum(gz * yb[1, at, :]),
        )

    r_sum, a, b = loop(join_broad, zero2, zero2, zero2)
    sent_b = push(6, a, b)
    sums[10, me, 1:2, 512:513] = g_sum
    sent_join = push(10, r_sum, l_sum)
    logits[...] = jnp.transpose(own_term[:, 0:128])[1:2, :]
    n_rows, b_rows = up16(s1), up16(s2)

    def grad_y(gz, normed, rstd, gain, total):
        return low(gain * rstd * (gz - total[0:1] / batch - normed * (total[1:2] / batch)))

    t_n3 = pull(sent_n)[:, :h1]

    def back_n3(at, a, b):
        g = grad_y(dn[2, at, :], yn[2, at, :], rstd_n3, gain_n(2)[0], t_n3)
        gyn[1, at, :] = g
        gz = nn(g, n23[1]) * dn[1, at, :]
        dn[1, at, :] = gz
        return a + column_sum(gz), b + column_sum(gz * yn[1, at, :])

    sent_n = push(7, *loop(back_n3, zero1, zero1))
    q_out[...] = jnp.zeros_like(q_out)
    q_out[:s1, h1 : 2 * h1] = weight_grad(gyn[1], un[1], mine, s1)
    t_b2 = pull(sent_b)[:, :h2]

    def back_b2(at, a, b):
        g = grad_y(db[1, at, :], yb[1, at, :], rstd_b2, gain_b(1)[0], t_b2)
        gyb[at, :] = g
        gz = nn(g, b2[...]) * db[0, at, :]
        db[0, at, :] = gz
        return a + column_sum(gz), b + column_sum(gz * yb[0, at, :])

    sent_b = push(8, *loop(back_b2, zero2, zero2))
    t_n2 = pull(sent_n)[:, :h1]

    def back_n2(at, a, b):
        g = grad_y(dn[1, at, :], yn[1, at, :], rstd_n2, gain_n(1)[0], t_n2)
        gyn[0, at, :] = g
        gz = nn(g, n23[0]) * dn[0, at, :]
        dn[0, at, :] = gz
        return a + column_sum(gz), b + column_sum(gz * yn[0, at, :])

    sent_n = push(9, *loop(back_n2, zero1, zero1))
    q_out[n_rows : n_rows + s2, :] = weight_grad(gyb[...], ub[0], mine, s2)
    t_b1 = pull(sent_b)[:, :h2]

    def gate_back(k, at, grad):
        x = feat[at, :].astype(jnp.float32)
        value = gate[k, at, :]
        g = low(grad * x * value * (1.0 - 0.5 * value))
        grad_gate[k, at, :] = g
        return grad * value, g

    def back_b1(at):
        g = grad_y(db[0, at, :], yb[0, at, :], rstd_b1, gain_b(0)[0], t_b1)
        gyb1[at, :] = g
        own_term[at, :] = gate_back(1, at, nn(g, b1[...]))[0]
        return ()

    loop(back_b1)
    q_out[:s1, :h1] = weight_grad(gyn[0], un[0], mine, s1)
    folded = jnp.zeros((16, h1), jnp.float32)
    col = lax.broadcasted_iota(jnp.int32, (16, h1), 1)
    for h in range(heads):
        folded = folded + jnp.where(col // hx == h, pair_g[h * 16 : (h + 1) * 16, :], 0.0)
    q_out[n_rows + b_rows : n_rows + b_rows + 16, :h1] = low(folded)
    t_n1 = pull(sent_n)[:, :h1]

    def back_n1(at, ga, gb, ne):
        g = grad_y(dn[0, at, :], yn[0, at, :], rstd_n1, gain_n(0)[0], t_n1)
        gyn1[at, :] = g
        term, g0 = gate_back(0, at, nn(g, n1[...]))
        g1 = grad_gate[1, at, :]
        whole = nn(g0, gates[0]) + nn(g1, gates[1]) + term + own_term[at, :]
        whole = low(whole).astype(jnp.float32)
        own_term[at, :] = whole
        ne = ne + column_sum(whole[:, :num] * widen_dense(dense_t[:, at], 16))
        return ga + column_sum(g0.astype(jnp.float32)), gb + column_sum(g1.astype(jnp.float32)), ne

    zero_g = jnp.zeros((1, wide), jnp.float32)
    ga, gb, ne = loop(back_n1, zero_g, zero_g, jnp.zeros((1, num), jnp.float32))
    grads_t[...] = low(jnp.transpose(own_term[:, num:]))
    small[...] = jnp.zeros_like(small)
    small[0:1, :gcols] = own_columns(ga, mine, gcols, mp)
    small[1:2, :gcols] = own_columns(gb, mine, gcols, mp)
    small[2:3, :num] = ne
    for layer, t in enumerate((t_n1, t_n2, t_n3)):
        n_shift_g[layer : layer + 1, :] = own_columns(t[0:1], mine, s1, mp)
        n_gain_g[layer : layer + 1, :] = own_columns(t[1:2], mine, s1, mp)
    for layer, t in enumerate((t_b1, t_b2)):
        b_shift_g[layer : layer + 1, :] = own_columns(t[0:1], mine, s2, mp)
        b_gain_g[layer : layer + 1, :] = own_columns(t[1:2], mine, s2, mp)
    total = pull(sent_join)
    right_g[...] = total[0:1, :h2]
    left_g[...] = total[1:2, :h1]
    bias_g[...] = total[1:2, 512:513]
    copy_a.wait_send()
    copy_b.wait_send()
    for copy in copies:
        copy.wait_send()
    for group in started:
        for copy in group:
            copy.wait_send()


def reduce_kernel(
    dp, mp,
    grads, feat, fields, grad_gate, gyn1, gyb1, q_in, small,
    shares, p_full, q_full, small_out,
    landed, s_slots, p_work, q_work, p_land, q_land,
    send, recv, send2, recv2, send3, recv3, psend, precv,
):
    tall = grads.shape[0] // dp
    me, mine = lax.axis_index("dp"), lax.axis_index("mp")
    hail(dp, mp)
    levels = dp.bit_length() - 1
    orders = (list(range(levels)), list(range(1, levels)) + [0])
    q_work[...] = q_in[...]
    s_slots[me] = small[...]
    all_in(dp, mp)
    works = (p_work, q_work)
    lands = (p_land, q_land)
    fulls = (p_full, q_full)
    starts = [0, 0]
    sizes = [p_work.shape[0], q_work.shape[0]]
    waits = []

    def flip(bit):
        return me + (1 << bit) - 2 * (1 << bit) * lax.rem(me // (1 << bit), 2)

    def halve(w, level):
        bit = orders[w][level]
        size = sizes[w] // 2
        up = lax.rem(me // (1 << bit), 2)
        keep = starts[w] + up * size
        give = starts[w] + (1 - up) * size
        offset = works[w].shape[0] - 2 * size
        where = pl.ds(offset, size)
        copy = remote(
            works[w].at[pl.ds(pl.multiple_of(give, 16), size), :], lands[w].at[where, :],
            psend.at[w, level], precv.at[w, level], {"dp": flip(bit)},
        )
        copy.start()
        starts[w], sizes[w] = keep, size
        return copy, where

    def add(w, copy, where):
        copy.wait_recv()
        at = pl.ds(pl.multiple_of(starts[w], 16), sizes[w])
        works[w][at, :] = low(
            works[w][at, :].astype(jnp.float32) + lands[w][where, :].astype(jnp.float32)
        )
        waits.append(copy)

    def double(w, level):
        bit = orders[w][level]
        at = fulls[w].at[pl.ds(pl.multiple_of(starts[w], 16), sizes[w]), :]
        copy = remote(at, at, psend.at[w, levels + level], precv.at[w, levels + level], {"dp": flip(bit)})
        copy.start()
        up = lax.rem(me // (1 << bit), 2)
        starts[w] = starts[w] - up * sizes[w]
        sizes[w] = sizes[w] * 2
        return copy

    copies = []
    for step in range(1, dp):
        to = lax.rem(me + step, dp)
        copy = remote(
            grads.at[pl.ds(pl.multiple_of(to * tall, 16), tall), :],
            landed.at[step - 1], send.at[step - 1], recv.at[step - 1], {"dp": to},
        )
        copy.start()
        copies.append(copy)
    small_copies = spread_dp(dp, lambda k: s_slots.at[k], send3, recv3)
    pend = [None, halve(1, 0)]
    gcols, s1, s2 = feat.shape[1] // mp, gyn1.shape[1] // mp, gyb1.shape[1] // mp
    g_rows, n_rows, b_rows = up16(gcols), up16(s1), up16(s2)
    p_work[...] = jnp.zeros_like(p_work)
    for k in range(2):
        p_work[k * g_rows : k * g_rows + gcols, :] = weight_grad(grad_gate[k], feat[...], mine, gcols)
    row = 2 * g_rows
    p_work[row : row + s1, :] = weight_grad(gyn1[...], fields[0], mine, s1)
    row += n_rows
    p_work[row : row + s2, :] = weight_grad(gyb1[...], fields[1], mine, s2)
    pend[0] = halve(0, 0)
    for level in range(1, levels):
        for w in (0, 1):
            add(w, *pend[w])
            pend[w] = halve(w, level)
    total = grads[pl.ds(pl.multiple_of(me * tall, 16), tall), :].astype(jnp.float32)
    for step in range(1, dp):
        copies[step - 1].wait_recv()
        total = total + landed[step - 1].astype(jnp.float32)
    shares[mine] = total.astype(jnp.bfloat16)

    def slot(i):
        return shares.at[i]

    started = relay_own(mp, slot, send2, recv2)
    back = []
    for w in (0, 1):
        add(w, *pend[w])
        at = pl.ds(pl.multiple_of(starts[w], 16), sizes[w])
        fulls[w][at, :] = works[w][at, :]
        back.append(double(w, levels - 1))
    relay_rest(mp, slot, send2, recv2, started)
    for level in range(levels - 2, -1, -1):
        for w in (0, 1):
            back[w].wait_recv()
            waits.append(back[w])
            back[w] = double(w, level)
    for copy in small_copies:
        copy.wait_recv()
    value = s_slots[0]
    for d in range(1, dp):
        value = value + s_slots[d]
    small_out[...] = value
    for w in (0, 1):
        back[w].wait_recv()
        waits.append(back[w])
    for copy in copies + small_copies + waits:
        copy.wait_send()


def final_kernel(
    mp, hx, shares, p_full, q_full, small, logits_in, n_gain_in, n_shift_in, b_gain_in, b_shift_in,
    left_in, right_in, bias_in,
    logits, num_g, table_g, gate_g, gate_bias_g, n_first_g, n_rest_g, n_gain_g, n_shift_g,
    b_first_g, b_rest_g, b_gain_g, b_shift_g, left_g, right_g, pair_g, bias_g,
):
    gcols, s1, s2, h1 = gate_g.shape[0], n_first_g.shape[0], b_first_g.shape[0], n_rest_g.shape[2]
    g_rows, n_rows, b_rows = up16(gcols), up16(s1), up16(s2)
    wide = n_first_g.shape[1]

    def full(work, row, count, col, width):
        return work[row : row + count, col : col + width].astype(jnp.float32)

    blocks = shares.shape[1] // 16
    for m in range(mp):
        for b in range(blocks):
            table_g[:, (m * blocks + b) * HI : (m * blocks + b + 1) * HI] = shares[
                m, b * 16 : (b + 1) * 16, :
            ].astype(jnp.float32)
    gate_g[:, 0, :] = full(p_full, 0, gcols, 0, wide)
    gate_g[:, 1, :] = full(p_full, g_rows, gcols, 0, wide)
    n_first_g[...] = full(p_full, 2 * g_rows, s1, 0, wide)
    b_first_g[...] = full(p_full, 2 * g_rows + n_rows, s2, 0, wide)
    n_rest_g[:, 0, :] = full(q_full, 0, s1, 0, h1)
    n_rest_g[:, 1, :] = full(q_full, 0, s1, h1, h1)
    b_rest_g[...] = full(q_full, n_rows, s2, 0, 2 * h1)
    heads = pair_g.shape[2]
    pairs = q_full[n_rows + b_rows : n_rows + b_rows + 16, :h1]
    row = lax.broadcasted_iota(jnp.int32, (h1, heads), 0)
    col = lax.broadcasted_iota(jnp.int32, (h1, heads), 1)
    for i in range(hx):
        choose = jnp.where(row == col * hx + i, 1.0, 0.0).astype(jnp.bfloat16)
        pair_g[i] = nn(pairs, choose)
    fields, width = num_g.shape
    gate_bias_g[...] = small[0:2, :gcols]
    spread = jnp.broadcast_to(small[2:3, : fields * width], (fields, fields * width))
    row = lax.broadcasted_iota(jnp.int32, spread.shape, 0)
    col = lax.broadcasted_iota(jnp.int32, spread.shape, 1)
    spread = jnp.where(col // width == row, spread, 0.0)
    total = spread[:, :width]
    for i in range(1, fields):
        total = total + spread[:, i * width : (i + 1) * width]
    num_g[...] = total
    logits[...] = logits_in[...]
    n_gain_g[...] = n_gain_in[...]
    n_shift_g[...] = n_shift_in[...]
    b_gain_g[...] = b_gain_in[...]
    b_shift_g[...] = b_shift_in[...]
    left_g[...] = left_in[...]
    right_g[...] = right_in[...].reshape(right_g.shape)
    bias_g[...] = bias_in[...]


def f32(*shape):
    return jax.ShapeDtypeStruct(shape, jnp.float32)


def b16(*shape):
    return jax.ShapeDtypeStruct(shape, jnp.bfloat16)


def held(*shape):
    return pltpu.VMEM(shape, jnp.float32)


def held16(*shape):
    return pltpu.VMEM(shape, jnp.bfloat16)


def dma(*shape):
    return pltpu.SemaphoreType.DMA(shape)


def shards(
    dense_values,
    field_ids,
    lengths,
    labels,
    num_embed,
    embed_table,
    gate_weight,
    gate_bias,
    narrow_first,
    narrow_rest,
    narrow_gain,
    narrow_shift,
    broad_first,
    broad_rest,
    broad_gain,
    broad_shift,
    joining_left,
    joining_right,
    joining_pair,
    joining_bias,
):
    dp, mp = lax.axis_size("dp"), lax.axis_size("mp")
    chips = mp // 2
    rows = dense_values.shape[0]
    cats, slots = field_ids.shape[:2]
    width, own_rows = embed_table.shape
    num = dense_values.shape[1] * width
    wide = gate_weight.shape[2]
    gcols = gate_weight.shape[1]
    s1, s2 = narrow_first.shape[0], broad_first.shape[0]
    h1, h2 = s1 * mp, s2 * mp
    hx = joining_pair.shape[1]
    bits = (cats * rows - 1).bit_length()
    dense_t = dense_values.T
    tall = own_rows // mp // HI * 16
    vregs = 1 << (-(-(cats * slots * rows) // 1024) - 1).bit_length()
    first_args = (
        embed_table, jnp.transpose(gate_weight, (1, 0, 2)), narrow_first, gate_bias,
        narrow_gain, narrow_shift, broad_gain, broad_shift,
        field_ids, lengths, dense_t, num_embed, jnp.transpose(narrow_rest, (1, 0, 2)),
    )
    t2, keys, numeric, gates, n1, vec, n_own = pl.pallas_call(
        functools.partial(first_kernel, dp, mp, own_rows, bits),
        out_shape=(
            b16(dp * tall, HI),
            jax.ShapeDtypeStruct((128, vregs * 8), jnp.int32),
            b16(rows, num),
            b16(2, wide, wide),
            b16(h1, wide),
            f32(16, 896),
            b16(2, s1, h1),
        ),
        in_specs=[ANY] * 13,
        out_specs=(VM,) * 7,
        scratch_shapes=[pltpu.VMEM(x.shape, x.dtype) for x in first_args]
        + [
            pltpu.VMEM((vregs * 8, 128), jnp.int32),
            held16(mp, 2, gcols, wide),
            held16(mp, s1, wide),
            held(mp, 16, 256),
            dma(dp - 1),
            dma(dp - 1),
            dma(3, mp),
            dma(3, mp),
            dma(13),
        ],
        compiler_params=params(0, 54),
        name="first",
    )(*first_args)
    partial = pl.pallas_call(
        functools.partial(lookup_kernel, cats, rows, bits),
        out_shape=f32(cats * 16, rows),
        in_specs=[VM] * 2,
        out_specs=VM,
        scratch_shapes=[held(cats * 16, rows)],
        compiler_params=params(None, 12),
        name="lookup",
    )(keys, t2)

    def up(x, n):
        return -(-x // n) * n

    p_rows = up(2 * up(gcols, 16) + up(s1, 16) + up(s2, 16), 16 * dp)
    q_rows = up(up(s1, 16) + up(s2, 16) + 16, 16 * dp)
    dense_args = (
        broad_first, broad_rest, joining_left.reshape(1, h1), joining_right,
        jnp.transpose(joining_pair, (1, 2, 0)), joining_bias.reshape(1, 1), labels.reshape(1, rows), dense_t,
    )
    (
        logits, grads_t, feat, fields, grad_gate, gyn1, gyb1, q_part, small,
        n_gain_g, n_shift_g, b_gain_g, b_shift_g, left_g, right_g, bias_g,
    ) = pl.pallas_call(
        functools.partial(dense_kernel, dp, mp, hx, float(rows * dp)),
        out_shape=(
            f32(1, rows),
            b16(cats * 16, rows),
            b16(rows, wide),
            b16(2, rows, wide),
            b16(2, rows, wide),
            b16(rows, h1),
            b16(rows, h2),
            b16(q_rows, h2),
            f32(8, 256),
            f32(3, s1),
            f32(3, s1),
            f32(2, s2),
            f32(2, s2),
            f32(1, h1),
            f32(1, h2),
            f32(1, 1),
        ),
        in_specs=[VM] * 6 + [ANY] * 8,
        out_specs=(VM,) * 16,
        scratch_shapes=[
            held(cats * 8, rows),
            held16(chips, cats * 8, rows),
            held16(cats * 16, rows),
            held(2, rows, wide),
            held(rows, wide),
            held16(mp, s2, wide),
            held16(mp, 2, s1, h1),
            held16(mp, s2, h2),
            held16(h2, wide),
            held16(2, h1, h1),
            held16(h2, h2),
            held(3, rows, h1),
            held(3, rows, h1),
            held(2, rows, h2),
            held(2, rows, h2),
            held16(3, rows, h1),
            held16(2, rows, h2),
            held16(2, rows, h1),
            held16(rows, h2),
            held16(h1, h2),
            held16(h1, h2),
            held(h2, h1),
            held(rows, h1),
            held(11, dp, 2, 896),
            dma(chips + 1),
            dma(chips + 1),
            dma(3, mp),
            dma(3, mp),
            dma(11, dp - 1),
            dma(11, dp - 1),
        ]
        + [pltpu.VMEM(x.shape, x.dtype) for x in dense_args]
        + [dma(8)],
        compiler_params=params(1, 39),
        name="dense",
    )(partial, numeric, gates, n1, n_own, vec, *dense_args)
    row_sums = pl.pallas_call(
        functools.partial(scatter_kernel, cats, rows, bits),
        out_shape=b16(dp * tall, HI),
        in_specs=[VM] * 2,
        out_specs=VM,
        scratch_shapes=[held(dp * tall, HI)],
        compiler_params=params(None, 12),
        name="scatter",
    )(keys, grads_t)
    shares, p_full, q_full, small = pl.pallas_call(
        functools.partial(reduce_kernel, dp, mp),
        out_shape=(
            b16(mp, tall, HI),
            b16(p_rows, wide),
            b16(q_rows, h2),
            f32(8, 256),
        ),
        in_specs=[VM] * 8,
        out_specs=(VM,) * 4,
        scratch_shapes=[
            held16(dp - 1, tall, HI),
            held(dp, 8, 256),
            held16(p_rows, wide),
            held16(q_rows, h2),
            held16(p_rows, wide),
            held16(q_rows, h2),
            dma(dp - 1),
            dma(dp - 1),
            dma(mp),
            dma(mp),
            dma(dp - 1),
            dma(dp - 1),
            dma(2, 2 * (dp.bit_length() - 1)),
            dma(2, 2 * (dp.bit_length() - 1)),
        ],
        compiler_params=params(2, 24),
        name="reduce",
    )(row_sums, feat, fields, grad_gate, gyn1, gyb1, q_part, small)
    outs = pl.pallas_call(
        functools.partial(final_kernel, mp, hx),
        out_shape=(
            f32(1, rows),
            f32(*num_embed.shape),
            f32(width, own_rows),
            f32(gcols, 2, wide),
            f32(2, gcols),
            f32(s1, wide),
            f32(s1, 2, h1),
            f32(3, s1),
            f32(3, s1),
            f32(s2, wide),
            f32(s2, h2),
            f32(2, s2),
            f32(2, s2),
            f32(1, h1),
            f32(h2),
            f32(hx, width, joining_pair.shape[0]),
            f32(1, 1),
        ),
        in_specs=[VM] * 12,
        out_specs=(VM,) * 17,
        compiler_params=params(None, 16),
        name="final",
    )(
        shares, p_full, q_full, small, logits, n_gain_g, n_shift_g, b_gain_g, b_shift_g,
        left_g, right_g, bias_g,
    )
    outs = list(outs)
    outs[0] = outs[0].reshape(rows)
    outs[3] = jnp.transpose(outs[3], (1, 0, 2))
    outs[6] = jnp.transpose(outs[6], (1, 0, 2))
    outs[13] = outs[13].reshape(h1)
    outs[15] = jnp.transpose(outs[15], (2, 0, 1))
    outs[16] = outs[16].reshape(1)
    return tuple(outs)


def solution(mesh):
    placed = (
        P("dp", None),
        P(None, None, "dp"),
        P(None, "dp"),
        P("dp"),
        P(),
        P(None, "dp"),
        P(None, "mp", None),
        P(None, "mp"),
        P("mp", None),
        P(None, "mp", None),
        P(None, "mp"),
        P(None, "mp"),
        P("mp", None),
        P("mp", None),
        P(None, "mp"),
        P(None, "mp"),
        P(),
        P(),
        P(),
        P(),
    )
    return jax.shard_map(
        shards,
        mesh=mesh,
        in_specs=placed,
        out_specs=(
            P("dp"),
            P(),
            P(None, "dp"),
            P(None, "mp", None),
            P(None, "mp"),
            P("mp", None),
            P(None, "mp", None),
            P(None, "mp"),
            P(None, "mp"),
            P("mp", None),
            P("mp", None),
            P(None, "mp"),
            P(None, "mp"),
            P(),
            P(),
            P(),
            P(),
        ),
        check_vma=False,
    )
```

```python
import functools
import jax
import jax.numpy as jnp
from jax import lax
from jax.experimental import pallas as pl
from jax.experimental.pallas import tpu as pltpu
from jax.sharding import PartitionSpec as P

MESH = pl.DeviceIdType.MESH
VM = pl.BlockSpec(memory_space=pltpu.VMEM)
ANY = pl.BlockSpec(memory_space=pltpu.HBM)
HI = 256
CHUNK = 512


def params(cid, mib=48):
    if cid is None:
        return pltpu.CompilerParams(vmem_limit_bytes=mib << 20)
    return pltpu.CompilerParams(
        collective_id=cid, has_side_effects=True, vmem_limit_bytes=mib << 20
    )


def hail(dp, mp):
    me, mine = lax.axis_index("dp"), lax.axis_index("mp")
    barrier = pltpu.get_barrier_semaphore()
    for step in range(1, dp):
        pl.semaphore_signal(
            barrier, inc=1, device_id={"dp": lax.rem(me + step, dp)}, device_id_type=MESH
        )
    for step in range(1, mp):
        pl.semaphore_signal(
            barrier, inc=1, device_id={"mp": lax.rem(mine + step, mp)}, device_id_type=MESH
        )


def all_in(dp, mp):
    pl.semaphore_wait(pltpu.get_barrier_semaphore(), dp - 1 + mp - 1)


def remote(src, dst, send, recv, where):
    return pltpu.make_async_remote_copy(
        src_ref=src, dst_ref=dst, send_sem=send, recv_sem=recv,
        device_id=where, device_id_type=MESH,
    )


def spread_dp(dp, pick, send, recv):
    me = lax.axis_index("dp")
    out = []
    for step in range(1, dp):
        to = lax.rem(me + step, dp)
        copy = remote(pick(me), pick(me), send.at[step - 1], recv.at[step - 1], {"dp": to})
        copy.start()
        out.append(copy)
    return out


def compact_keys(key):
    count = key.shape[0]
    dead = (key < 0).astype(jnp.int32)
    sub = lax.broadcasted_iota(jnp.int32, (8, 128), 0)
    lane = lax.broadcasted_iota(jnp.int32, (8, 128), 1)
    running = jnp.zeros((8, 128), jnp.int32)
    before = []
    for v in range(count):
        before.append(running)
        running = running + dead[v]
    scan = running
    for k in (1, 2, 4):
        scan = scan + jnp.where(sub >= k, pltpu.roll(scan, k, 0), 0)
    over_sub = scan - running
    column = jnp.broadcast_to(jnp.sum(running, axis=0, keepdims=True), (8, 128))
    scan = column
    for k in (1, 2, 4, 8, 16, 32, 64):
        scan = scan + jnp.where(lane >= k, pltpu.roll(scan, k, 1), 0)
    base = over_sub + scan - column
    shift = jnp.stack([jnp.where(dead[v] > 0, 0, before[v] + base) for v in range(count)])

    def next_place(x):
        n = x.shape[0]
        flat = x.reshape(n * 8, 128)
        y = jnp.stack([pltpu.roll(x[v], 7, 0) for v in range(n)])
        z = jnp.stack([pltpu.roll(y[v], 127, 1) for v in range(n)])
        return jnp.where(sub[None] < 7, y, z)

    bit = 0
    step = 1
    while step < count:
        moved_key = jnp.concatenate([key[step:], next_place(key[:step])], axis=0)
        moved_shift = jnp.concatenate([shift[step:], next_place(shift[:step])], axis=0)
        key, shift = settle(key, shift, moved_key, moved_shift, bit)
        bit, step = bit + 1, step * 2
    for j in (1, 2, 4):
        def roll_sub(x):
            y = jnp.stack([pltpu.roll(x[v], 8 - j, 0) for v in range(count)])
            z = jnp.stack([pltpu.roll(y[v], 127, 1) for v in range(count)])
            return jnp.where(sub[None] < 8 - j, y, z)
        key, shift = settle(key, shift, roll_sub(key), roll_sub(shift), bit)
        bit += 1
    for j in (1, 2, 4, 8, 16, 32, 64):
        def roll_lane(x):
            return jnp.stack([pltpu.roll(x[v], 128 - j, 1) for v in range(count)])
        key, shift = settle(key, shift, roll_lane(key), roll_lane(shift), bit)
        bit += 1
    return key


def settle(key, shift, moved_key, moved_shift, bit):
    take = (moved_shift & (1 << bit)) != 0
    stay = (shift & (1 << bit)) == 0
    key = jnp.where(take, moved_key, jnp.where(stay, key, -1))
    shift = jnp.where(take, moved_shift, jnp.where(stay, shift, 0))
    return key, shift


def seat(i, dp):
    return i % 2 * (dp // 2) + i // 2


def make_keys(ids, lens, scratch, own_rows, dp, mp, bits):
    cats, slots, rows = ids.shape
    part = own_rows // mp
    mine = lax.axis_index("mp")
    scratch[...] = jnp.full_like(scratch, -1)
    slot = lax.broadcasted_iota(jnp.int32, (slots, rows), 0)
    event = lax.broadcasted_iota(jnp.int32, (slots, rows), 1)

    def body(c, carry):
        values = ids[c]
        holder = values // own_rows
        inner = values - holder * own_rows
        owner = inner // part
        place = seat(holder, dp) * part + inner - owner * part
        live = (slot < lens[pl.ds(c, 1), :]) & (owner == mine)
        key = jnp.where(live, place * (1 << bits) + c * rows + event, -1)
        for q in range(rows // 128):
            scratch[pl.ds((c * (rows // 128) + q) * slots, slots), :] = key[:, q * 128 : (q + 1) * 128]
        return carry

    lax.fori_loop(0, cats, body, 0)


def lookup_kernel(cats, rows, bits, keys, t2, pooled, total):
    lows = t2.shape[0] // 16
    filled = jnp.max(keys[...], axis=1, keepdims=True) >= 0
    chunks = jnp.sum(filled.astype(jnp.int32))
    total[...] = jnp.zeros_like(total)
    hi_iota = lax.broadcasted_iota(jnp.int32, (HI, CHUNK), 0)
    event_iota = lax.broadcasted_iota(jnp.int32, (rows, CHUNK), 0)

    def body(k, carry):
        key = keys[pl.ds(k, 1), :]
        place = lax.shift_right_arithmetic(key, bits)
        bag = key & ((1 << bits) - 1)
        cat = bag // rows
        event = bag - cat * rows
        low = lax.shift_right_arithmetic(place, 8)
        high = place & (HI - 1)
        pick = jnp.where(hi_iota == high, 1.0, 0.0).astype(jnp.bfloat16)
        z = jnp.zeros((16, CHUNK), jnp.float32)
        for b in range(0, lows, 16):
            n = min(16, lows - b)
            y = jnp.dot(t2[b * 16 : (b + n) * 16, :], pick, preferred_element_type=jnp.float32)
            for j in range(n):
                z = z + jnp.where(low == b + j, y[j * 16 : (j + 1) * 16], 0.0)
        z = z.astype(jnp.bfloat16)
        zero = jnp.zeros_like(z)
        wide = jnp.concatenate([jnp.where(cat == c, z, zero) for c in range(cats)], axis=0)
        place_of = jnp.where(event_iota == event, 1.0, 0.0).astype(jnp.bfloat16)
        total[...] += lax.dot_general(
            wide, place_of, (((1,), (1,)), ((), ())), preferred_element_type=jnp.float32
        )
        return carry

    lax.fori_loop(0, chunks, body, 0)
    pooled[...] = total[...].astype(pooled.dtype)


def scatter_kernel(cats, rows, bits, keys, grad, out, total):
    lows = total.shape[0] // 16
    filled = jnp.max(keys[...], axis=1, keepdims=True) >= 0
    chunks = jnp.sum(filled.astype(jnp.int32))
    total[...] = jnp.zeros_like(total)
    hi_iota = lax.broadcasted_iota(jnp.int32, (HI, CHUNK), 0)
    event_iota = lax.broadcasted_iota(jnp.int32, (rows, CHUNK), 0)

    def body(k, carry):
        key = keys[pl.ds(k, 1), :]
        place = lax.shift_right_arithmetic(key, bits)
        bag = key & ((1 << bits) - 1)
        cat = bag // rows
        event = bag - cat * rows
        low = lax.shift_right_arithmetic(place, 8)
        high = place & (HI - 1)
        place_of = jnp.where(event_iota == event, 1.0, 0.0).astype(jnp.bfloat16)
        wide = jnp.dot(grad[...], place_of, preferred_element_type=jnp.float32)
        g = jnp.zeros((16, CHUNK), jnp.float32)
        for c in range(cats):
            g = g + jnp.where(cat == c, wide[c * 16 : (c + 1) * 16], 0.0)
        g = g.astype(jnp.bfloat16)
        zero = jnp.zeros_like(g)
        pick = jnp.where(hi_iota == high, 1.0, 0.0).astype(jnp.bfloat16)
        for b in range(0, lows, 16):
            n = min(16, lows - b)
            tall = jnp.concatenate([jnp.where(low == b + j, g, zero) for j in range(n)], axis=0)
            total[b * 16 : (b + n) * 16, :] += lax.dot_general(
                tall, pick, (((1,), (1,)), ((), ())), preferred_element_type=jnp.float32
            )
        return carry

    lax.fori_loop(0, chunks, body, 0)
    out[...] = total[...].astype(out.dtype)


def relay_own(mp, slot, send, recv):
    mine = lax.axis_index("mp")
    core = lax.rem(mine, 2)
    other = mine + 1 - 2 * core
    chips = mp // 2
    out = []
    for k in range(1, chips):
        to = lax.rem(mine + 2 * k, mp)
        copy = remote(slot(mine), slot(mine), send.at[2 * k], recv.at[2 * k], {"mp": to})
        copy.start()
        out.append(copy)
    copy = remote(slot(mine), slot(mine), send.at[1], recv.at[1], {"mp": other})
    copy.start()
    out.append(copy)
    return out


def relay_rest(mp, slot, send, recv, started):
    mine = lax.axis_index("mp")
    core = lax.rem(mine, 2)
    other = mine + 1 - 2 * core
    chips = mp // 2
    passed = []
    for k in range(1, chips):
        source = lax.rem(mine + mp - 2 * k, mp)
        remote(slot(source), slot(source), send.at[2 * k], recv.at[2 * k], {"mp": other}).wait_recv()
        copy = remote(slot(source), slot(source), send.at[2 * k + 1], recv.at[2 * k + 1], {"mp": other})
        copy.start()
        passed.append(copy)
    remote(slot(other), slot(other), send.at[1], recv.at[1], {"mp": other}).wait_recv()
    for k in range(1, chips):
        far = lax.rem(other + mp - 2 * k, mp)
        remote(slot(far), slot(far), send.at[2 * k + 1], recv.at[2 * k + 1], {"mp": other}).wait_recv()
    for copy in started + passed:
        copy.wait_send()


def nn(a, b):
    return jnp.dot(a, b, preferred_element_type=jnp.float32)


def nt(a, b):
    return lax.dot_general(a, b, (((1,), (1,)), ((), ())), preferred_element_type=jnp.float32)


def tn(a, b):
    return lax.dot_general(a, b, (((0,), (0,)), ((), ())), preferred_element_type=jnp.float32)


def sigmoid(x):
    return 0.5 * jnp.tanh(0.5 * x) + 0.5


def low(x):
    return x.astype(jnp.bfloat16)


def column_sum(x):
    return jnp.sum(x, axis=0, keepdims=True)


def widen_dense(dense_t, width):
    fields = dense_t.shape[0]
    row = lax.broadcasted_iota(jnp.int32, (fields, fields * width), 0)
    col = lax.broadcasted_iota(jnp.int32, (fields, fields * width), 1)
    ones = jnp.where(col // width == row, 1.0, 0.0)
    return lax.dot_general(
        dense_t, ones, (((0,), (0,)), ((), ())),
        precision=lax.Precision.HIGHEST, preferred_element_type=jnp.float32,
    )


def bring(sources, places, sem):
    copies = []
    for i, (source, place) in enumerate(zip(sources, places)):
        copy = pltpu.make_async_copy(source, place, sem.at[i])
        copy.start()
        copies.append(copy)
    return copies


def first_kernel(dp, mp, own_rows, bits, *refs):
    count = 13
    sources, refs = refs[:count], refs[count:]
    t2, keys, numeric, gates, n1, vec, n_own = refs[:7]
    places, refs = refs[7 : 7 + count], refs[7 + count :]
    scratch, gate_slots, n_slots, v_slots, send, recv, send2, recv2, sem = refs
    brought = bring(sources, places, sem)
    (
        table, gate_w, n_first, gate_b, n_gain, n_shift, b_gain, b_shift,
        ids, lens, dense_t, num_embed, n_rest,
    ) = places
    part = own_rows // mp
    blocks = part // HI
    tall = blocks * 16
    me, mine = lax.axis_index("dp"), lax.axis_index("mp")
    hail(dp, mp)
    for copy in brought[:8]:
        copy.wait()
    own = table[:, pl.ds(pl.multiple_of(mine * part, HI), part)].astype(jnp.bfloat16)
    for b in range(blocks):
        t2[pl.ds(pl.multiple_of(seat(me, dp) * tall + b * 16, 16), 16), :] = own[:, b * HI : (b + 1) * HI]
    for k in range(2):
        gate_slots[mine, k] = gate_w[:, k, :]
    n_slots[mine] = n_first[...]
    row = 0
    for ref in (gate_b, n_gain, n_shift, b_gain, b_shift):
        v_slots[mine, row : row + ref.shape[0], : ref.shape[1]] = ref[...]
        row += ref.shape[0]
    all_in(dp, mp)

    def slot(i):
        return t2.at[pl.ds(pl.multiple_of(seat(i, dp) * tall, 16), tall), :]

    groups = []
    for i, ref in enumerate((gate_slots, n_slots, v_slots)):
        started = relay_own(mp, lambda k, ref=ref: ref.at[k], send2.at[i], recv2.at[i])
        groups.append((ref, i, started))
    copies = spread_dp(dp, slot, send, recv)
    for copy in brought[8:]:
        copy.wait()
    for k in range(2):
        n_own[k] = n_rest[:, k, :]
    fields, width = num_embed.shape
    tiled = jnp.concatenate([num_embed[...]] * fields, axis=1)
    row = lax.broadcasted_iota(jnp.int32, tiled.shape, 0)
    col = lax.broadcasted_iota(jnp.int32, tiled.shape, 1)
    num_row = column_sum(jnp.where(col // width == row, tiled, 0.0))
    numeric[...] = low(widen_dense(dense_t[...], width) * num_row)
    make_keys(ids, lens, scratch, own_rows, dp, mp, bits)
    count = scratch.shape[0] // 8
    packed = compact_keys(scratch[...].reshape(count, 8, 128))
    keys[...] = jnp.transpose(packed.reshape(count * 8, 128))
    for ref, i, started in groups:
        relay_rest(mp, lambda k, ref=ref: ref.at[k], send2.at[i], recv2.at[i], started)
    cols, small = gate_slots.shape[2], n_first.shape[0]
    for m in range(mp):
        for k in range(2):
            gates[k, m * cols : (m + 1) * cols, :] = gate_slots[m, k]
        n1[m * small : (m + 1) * small, :] = n_slots[m]
    row = 0
    for ref in (gate_b, n_gain, n_shift, b_gain, b_shift):
        r, w = ref.shape
        vec[row : row + r, : mp * w] = jnp.concatenate(
            [v_slots[m, row : row + r, :w] for m in range(mp)], axis=1
        )
        row += r
    for copy in copies:
        copy.wait()


def own_columns(x, mine, width, mp):
    out = jnp.zeros((x.shape[0], width), x.dtype)
    for m in range(mp):
        out = jnp.where(mine == m, x[:, m * width : (m + 1) * width], out)
    return out


def up16(x):
    return -(-x // 16) * 16


def own_part(x, mine, width):
    full = x.shape[1]
    pad = -(-width // 128) * 128
    row = lax.broadcasted_iota(jnp.int32, (full, pad), 0)
    col = lax.broadcasted_iota(jnp.int32, (full, pad), 1)
    choose = jnp.where((row == col + mine * width) & (col < width), 1.0, 0.0).astype(jnp.bfloat16)
    return low(nn(x, choose))


def weight_grad(grad_y, inputs, mine, width):
    return low(tn(own_part(grad_y, mine, width), inputs)[:width, :])


def flip(me, level):
    bit = 1 << level
    return me + bit - 2 * bit * lax.rem(me // bit, 2)


def upper(me, level):
    return lax.rem(me // (1 << level), 2)


def give_half(me, level, start, size, work, land, send, recv):
    half = size // 2
    mine = upper(me, level)
    at = pl.ds(pl.multiple_of(start + (1 - mine) * half, 16), half)
    copy = remote(work.at[at, :], land, send, recv, {"dp": flip(me, level)})
    copy.start()
    return copy, start + mine * half


def add_half(copy, start, half, work, land):
    copy.wait_recv()
    at = pl.ds(pl.multiple_of(start, 16), half)
    return low(work[at, :].astype(jnp.float32) + land[...].astype(jnp.float32))


def dense_kernel(
    dp, mp, hx, batch,
    partial, numeric, gates, n1, n_rest, vec,
    b_first_hbm, b_rest_hbm, left_hbm, right_hbm, pair_hbm, bias_hbm, labels_hbm, dense_hbm,
    logits, grads_t, feat, fields, grad_gate, gyn1, a_out, b_out, small,
    n_gain_g, n_shift_g, b_gain_g, b_shift_g, left_g, right_g, bias_g,
    half_a, half_c, pooled, gate, own_term, b1_slots, n_slots, b_slots, b1, n23, b2,
    yn, dn, yb, db, un, ub, gyn, gyb, pair_hi, pair_lo, pair_g, to_first, sums, spill,
    fsend, frecv, wsend, wrecv, ssend, srecv,
    gyb1, a_work, b_work, a_land, b_land, hsend, hrecv,
    b_first, b_rest, left, right, pair_t, bias, labels, dense_t, sem,
):
    brought = bring(
        (b_first_hbm, b_rest_hbm, left_hbm, right_hbm, pair_hbm, bias_hbm, labels_hbm, dense_hbm),
        (b_first, b_rest, left, right, pair_t, bias, labels, dense_t),
        sem,
    )
    me, mine = lax.axis_index("dp"), lax.axis_index("mp")
    core = lax.rem(mine, 2)
    chip = mine // 2
    chips = mp // 2
    other = mine + 1 - 2 * core
    rows = feat.shape[0]
    block = 128
    steps = rows // block
    h1, h2 = n1.shape[0], b1.shape[0]
    s1, s2 = h1 // mp, h2 // mp
    wide = feat.shape[1]
    num = numeric.shape[1]
    gcols = wide // mp
    half = partial.shape[0] // 2
    hail(dp, mp)
    n_slots[mine] = n_rest[...]
    all_in(dp, mp)

    def rowset(i):
        return pl.ds(pl.multiple_of(i * block, block), block)

    def part(c):
        return pl.ds(pl.multiple_of(c * half, 16), half)

    copy_a = remote(partial.at[part(1 - core), :], half_a, fsend.at[0], frecv.at[0], {"mp": other})
    copy_a.start()
    for copy in brought:
        copy.wait()
    b1_slots[mine] = b_first[...]
    b_slots[mine] = b_rest[...]
    copy_a.wait_recv()
    half_c[chip] = low(partial[part(core), :] + half_a[...])
    copies = []
    for k in range(1, chips):
        copy = remote(
            half_c.at[chip], half_c.at[chip], fsend.at[k], frecv.at[k],
            {"mp": lax.rem(mine + 2 * k, mp)},
        )
        copy.start()
        copies.append(copy)
    heads = pair_t.shape[2]
    by_head = jnp.transpose(pair_t[...].reshape(hx * 16, heads))
    row = lax.broadcasted_iota(jnp.int32, (h1, heads), 0)
    col = lax.broadcasted_iota(jnp.int32, (h1, heads), 1)
    repeat = jnp.where(row // hx == col, 1.0, 0.0)
    tall = jnp.dot(repeat, by_head, precision=lax.Precision.HIGHEST, preferred_element_type=jnp.float32)
    row = lax.broadcasted_iota(jnp.int32, (h1, 16), 0)
    pick = jnp.zeros((h1, 16), jnp.float32)
    for i in range(hx):
        pick = jnp.where(row % hx == i, tall[:, i * 16 : (i + 1) * 16], pick)
    for i in range(0, h1, 80):
        row = lax.broadcasted_iota(jnp.int32, (80, h2), 0) + i
        col = lax.broadcasted_iota(jnp.int32, (80, h2), 1)
        pieces = jnp.concatenate([pick[i : i + 80, :]] * heads, axis=1)
        spread = jnp.where(row // hx == col // 16, pieces, 0.0)
        high = low(spread)
        pair_hi[i : i + 80, :] = high
        pair_lo[i : i + 80, :] = low(spread - high.astype(jnp.float32))
    for copy in copies:
        copy.wait_recv()
    total = half_c[0].astype(jnp.float32)
    for k in range(1, chips):
        total = total + half_c[k].astype(jnp.float32)
    pooled[part(core), :] = low(total)
    copy_b = remote(
        pooled.at[part(core), :], pooled.at[part(core), :], fsend.at[chips], frecv.at[chips], {"mp": other}
    )
    copy_b.start()
    weights = (b1_slots, n_slots, b_slots)
    moving = [
        relay_own(mp, lambda k, ref=ref: ref.at[k], wsend.at[i], wrecv.at[i])
        for i, ref in enumerate(weights)
    ]

    def arrive(i):
        relay_rest(mp, lambda k: weights[i].at[k], wsend.at[i], wrecv.at[i], moving[i])

    feat[:, :num] = numeric[...]
    copy_b.wait_recv()
    feat[:, num:] = low(jnp.transpose(pooled[...].astype(jnp.float32)))
    started = []

    def push(slot, *values):
        width = -(-values[0].shape[1] // 128) * 128
        for r, value in enumerate(values):
            sums[slot, me, r : r + 1, : value.shape[1]] = value
        out = []
        for step in range(1, dp):
            at = sums.at[slot, me, :, pl.ds(0, width)]
            copy = remote(
                at, at, ssend.at[slot, step - 1], srecv.at[slot, step - 1], {"dp": lax.rem(me + step, dp)}
            )
            copy.start()
            out.append(copy)
        started.append(out)
        return slot, width, out

    def pull(sent):
        slot, width, out = sent
        for copy in out:
            copy.wait_recv()
        total = sums[slot, 0, :, :width]
        for d in range(1, dp):
            total = total + sums[slot, d, :, :width]
        return total

    def norm(sent, width):
        total = pull(sent)
        mean = total[0:1, :width] / batch
        var = total[1:2, :width] / batch - mean * mean
        return mean, lax.rsqrt(var + 1e-05)

    def activate(y_ref, d_ref, u_ref, layer, at, mean, rstd, gain, shift):
        normed = (y_ref[layer, at, :] - mean) * rstd
        z = gain * normed + shift
        s = sigmoid(z)
        u = z * s
        y_ref[layer, at, :] = normed
        d_ref[layer, at, :] = s + u * (1.0 - s)
        u = low(u)
        u_ref[layer, at, :] = u
        return u

    def gain_n(layer):
        return vec[2 + layer : 3 + layer, :h1], vec[5 + layer : 6 + layer, :h1]

    def gain_b(layer):
        return vec[8 + layer : 9 + layer, :h2], vec[10 + layer : 11 + layer, :h2]

    zero1 = jnp.zeros((1, h1), jnp.float32)
    zero2 = jnp.zeros((1, h2), jnp.float32)

    def loop(body, *start):
        return lax.fori_loop(0, steps, lambda i, carry: body(rowset(i), *carry), tuple(start))

    def gates_and_first(at, a, b):
        x = feat[at, :]
        wide_x = x.astype(jnp.float32)
        for k in range(2):
            value = 2.0 * sigmoid(nt(x, gates[k]) + vec[k : k + 1, :wide])
            gate[k, at, :] = value
            fields[k, at, :] = low(wide_x * value)
        y = nt(fields[0, at, :], n1[...])
        yn[0, at, :] = y
        return a + column_sum(y), b + column_sum(y * y)

    sent_n = push(0, *loop(gates_and_first, zero1, zero1))
    arrive(0)
    for m in range(mp):
        b1[m * s2 : (m + 1) * s2, :] = b1_slots[m]

    def broad_first(at, a, b):
        y = nt(fields[1, at, :], b1[...])
        yb[0, at, :] = y
        return a + column_sum(y), b + column_sum(y * y)

    sent_b = push(1, *loop(broad_first, zero2, zero2))
    arrive(1)
    for m in range(mp):
        for k in range(2):
            n23[k, m * s1 : (m + 1) * s1, :] = n_slots[m, k]
    mean_n1, rstd_n1 = norm(sent_n, h1)

    def narrow_second(at, a, b):
        y = nt(activate(yn, dn, un, 0, at, mean_n1, rstd_n1, *gain_n(0)), n23[0])
        yn[1, at, :] = y
        return a + column_sum(y), b + column_sum(y * y)

    sent_n = push(2, *loop(narrow_second, zero1, zero1))
    arrive(2)
    for m in range(mp):
        b2[m * s2 : (m + 1) * s2, :] = b_slots[m]
    mean_b1, rstd_b1 = norm(sent_b, h2)

    def broad_second(at, a, b):
        y = nt(activate(yb, db, ub, 0, at, mean_b1, rstd_b1, *gain_b(0)), b2[...])
        yb[1, at, :] = y
        return a + column_sum(y), b + column_sum(y * y)

    sent_b = push(3, *loop(broad_second, zero2, zero2))
    mean_n2, rstd_n2 = norm(sent_n, h1)

    def narrow_third(at, a, b):
        y = nt(activate(yn, dn, un, 1, at, mean_n2, rstd_n2, *gain_n(1)), n23[1])
        yn[2, at, :] = y
        return a + column_sum(y), b + column_sum(y * y)

    sent_n = push(4, *loop(narrow_third, zero1, zero1))
    label = jnp.transpose(jnp.broadcast_to(labels[...].astype(jnp.float32), (8, rows)))[:, 0:1]
    own_term[:, 0:1] = label
    pair_g[...] = jnp.zeros_like(pair_g)
    mean_b2, rstd_b2 = norm(sent_b, h2)

    def broad_out(at):
        second = activate(yb, db, ub, 1, at, mean_b2, rstd_b2, *gain_b(1))
        to_first[at, :] = left[...] + (nt(second, pair_hi[...]) + nt(second, pair_lo[...]))
        return ()

    loop(broad_out)
    mean_n3, rstd_n3 = norm(sent_n, h1)
    to_right = right[...].reshape(1, h2)

    def join_narrow(at, l_sum, g_sum, a, b):
        first = activate(yn, dn, un, 2, at, mean_n3, rstd_n3, *gain_n(2)).astype(jnp.float32)
        second = ub[1, at, :].astype(jnp.float32)
        logit = (
            jnp.sum(first * to_first[at, :], axis=1, keepdims=True)
            + jnp.sum(second * to_right, axis=1, keepdims=True)
            + bias[...]
        )
        g = sigmoid(logit) - own_term[at, 0:1]
        own_term[at, 1:2] = logit
        own_term[at, 2:3] = g
        gz = g * to_first[at, :] * dn[2, at, :]
        dn[2, at, :] = gz
        return (
            l_sum + column_sum(g * first), g_sum + column_sum(g),
            a + column_sum(gz), b + column_sum(gz * yn[2, at, :]),
        )

    l_sum, g_sum, a, b = loop(join_narrow, zero1, jnp.zeros((1, 1), jnp.float32), zero1, zero1)
    sent_n = push(5, a, b)

    def join_broad(at, r_sum, a, b):
        first = un[2, at, :]
        second = ub[1, at, :]
        g = own_term[at, 2:3]
        turned = nn(first, pair_hi[...]) + nn(first, pair_lo[...])
        pair_g[...] += tn(second, low(g * first.astype(jnp.float32)))
        gz = g * (to_right + turned) * db[1, at, :]
        db[1, at, :] = gz
        return (
            r_sum + column_sum(g * second.astype(jnp.float32)),
            a + column_sum(gz), b + column_sum(gz * yb[1, at, :]),
        )

    r_sum, a, b = loop(join_broad, zero2, zero2, zero2)
    sent_b = push(6, a, b)
    sums[10, me, 1:2, 512:513] = g_sum
    sent_join = push(10, r_sum, l_sum)
    logits[...] = jnp.transpose(own_term[:, 0:128])[1:2, :]

    def grad_y(gz, normed, rstd, gain, total):
        return low(gain * rstd * (gz - total[0:1] / batch - normed * (total[1:2] / batch)))

    t_n3 = pull(sent_n)[:, :h1]

    def back_n3(at, a, b):
        g = grad_y(dn[2, at, :], yn[2, at, :], rstd_n3, gain_n(2)[0], t_n3)
        gyn[1, at, :] = g
        gz = nn(g, n23[1]) * dn[1, at, :]
        dn[1, at, :] = gz
        return a + column_sum(gz), b + column_sum(gz * yn[1, at, :])

    sent_n = push(7, *loop(back_n3, zero1, zero1))
    main = a_work.shape[1]
    rest = h2 - main
    parts = main // rest
    tall_a = s2 + s1
    short = -(-tall_a // parts)
    a_work[...] = jnp.zeros_like(a_work)
    b_work[...] = jnp.zeros_like(b_work)
    grad_n3 = weight_grad(gyn[1], un[1], mine, s1)
    t_b2 = pull(sent_b)[:, :h2]

    def back_b2(at, a, b):
        g = grad_y(db[1, at, :], yb[1, at, :], rstd_b2, gain_b(1)[0], t_b2)
        gyb[at, :] = g
        gz = nn(g, b2[...]) * db[0, at, :]
        db[0, at, :] = gz
        return a + column_sum(gz), b + column_sum(gz * yb[0, at, :])

    sent_b = push(8, *loop(back_b2, zero2, zero2))
    t_n2 = pull(sent_n)[:, :h1]

    def back_n2(at, a, b):
        g = grad_y(dn[1, at, :], yn[1, at, :], rstd_n2, gain_n(1)[0], t_n2)
        gyn[0, at, :] = g
        gz = nn(g, n23[0]) * dn[0, at, :]
        dn[0, at, :] = gz
        return a + column_sum(gz), b + column_sum(gz * yn[0, at, :])

    sent_n = push(9, *loop(back_n2, zero1, zero1))
    grad_n2 = weight_grad(gyn[0], un[0], mine, s1)
    grad_b2 = weight_grad(gyb[...], ub[0], mine, s2)
    a_work[:s2, :] = grad_b2[:, :main]
    a_work[s2:tall_a, :] = jnp.concatenate([grad_n2, grad_n3], axis=1)[:, :main]
    spill[:s2, :] = grad_b2[:, main:]
    spill[s2:tall_a, :] = jnp.concatenate([grad_n2, grad_n3], axis=1)[:, main:]
    for p in range(parts):
        n = min(short, tall_a - p * short)
        a_work[tall_a : tall_a + n, p * rest : (p + 1) * rest] = spill[p * short : p * short + n, :]
    size_a, size_b = a_work.shape[0], b_work.shape[0]
    copy_ax, start_a = give_half(me, 0, 0, size_a, a_work, a_land.at[pl.ds(0, size_a // 2), :], hsend.at[0], hrecv.at[0])
    folded = jnp.zeros((16, h1), jnp.float32)
    col = lax.broadcasted_iota(jnp.int32, (16, h1), 1)
    for h in range(heads):
        folded = folded + jnp.where(col // hx == h, pair_g[h * 16 : (h + 1) * 16, :], 0.0)
    b_work[size_b - 16 :, :h1] = low(folded)
    t_b1 = pull(sent_b)[:, :h2]

    def gate_back(k, at, grad):
        x = feat[at, :].astype(jnp.float32)
        value = gate[k, at, :]
        g = low(grad * x * value * (1.0 - 0.5 * value))
        grad_gate[k, at, :] = g
        return grad * value, g

    def back_b1(at):
        g = grad_y(db[0, at, :], yb[0, at, :], rstd_b1, gain_b(0)[0], t_b1)
        gyb1[at, :] = g
        own_term[at, :] = gate_back(1, at, nn(g, b1[...]))[0]
        return ()

    loop(back_b1)
    b_work[:s2, :wide] = weight_grad(gyb1[...], fields[1], mine, s2)
    b_work[s2 : s2 + gcols, :wide] = weight_grad(grad_gate[1], feat[...], mine, gcols)
    copy_bx, start_b = give_half(me, 0, 0, size_b, b_work, b_land, hsend.at[2], hrecv.at[2])
    a_work[pl.ds(pl.multiple_of(start_a, 16), size_a // 2), :] = add_half(
        copy_ax, start_a, size_a // 2, a_work, a_land.at[pl.ds(0, size_a // 2), :]
    )
    copy_az, start_a = give_half(
        me, 1, start_a, size_a // 2, a_work, a_land.at[pl.ds(size_a // 2, size_a // 4), :], hsend.at[1], hrecv.at[1]
    )
    t_n1 = pull(sent_n)[:, :h1]

    def back_n1(at, ga, gb, ne):
        g = grad_y(dn[0, at, :], yn[0, at, :], rstd_n1, gain_n(0)[0], t_n1)
        gyn1[at, :] = g
        term, g0 = gate_back(0, at, nn(g, n1[...]))
        g1 = grad_gate[1, at, :]
        whole = nn(g0, gates[0]) + nn(g1, gates[1]) + term + own_term[at, :]
        whole = low(whole).astype(jnp.float32)
        own_term[at, :] = whole
        ne = ne + column_sum(whole[:, :num] * widen_dense(dense_t[:, at], 16))
        return ga + column_sum(g0.astype(jnp.float32)), gb + column_sum(g1.astype(jnp.float32)), ne

    zero_g = jnp.zeros((1, wide), jnp.float32)
    ga, gb, ne = loop(back_n1, zero_g, zero_g, jnp.zeros((1, num), jnp.float32))
    grads_t[...] = low(jnp.transpose(own_term[:, num:]))
    small[...] = jnp.zeros_like(small)
    small[0:1, :gcols] = own_columns(ga, mine, gcols, mp)
    small[1:2, :gcols] = own_columns(gb, mine, gcols, mp)
    small[2:3, :num] = ne
    for layer, t in enumerate((t_n1, t_n2, t_n3)):
        n_shift_g[layer : layer + 1, :] = own_columns(t[0:1], mine, s1, mp)
        n_gain_g[layer : layer + 1, :] = own_columns(t[1:2], mine, s1, mp)
    for layer, t in enumerate((t_b1, t_b2)):
        b_shift_g[layer : layer + 1, :] = own_columns(t[0:1], mine, s2, mp)
        b_gain_g[layer : layer + 1, :] = own_columns(t[1:2], mine, s2, mp)
    total = pull(sent_join)
    right_g[...] = total[0:1, :h2]
    left_g[...] = total[1:2, :h1]
    bias_g[...] = total[1:2, 512:513]
    a_out[...] = add_half(
        copy_az, start_a, size_a // 4, a_work, a_land.at[pl.ds(size_a // 2, size_a // 4), :]
    )
    b_out[...] = add_half(copy_bx, start_b, size_b // 2, b_work, b_land)
    for copy in [copy_a, copy_b, copy_ax, copy_az, copy_bx] + copies:
        copy.wait_send()
    for group in started:
        for copy in group:
            copy.wait_send()


def reduce_kernel(
    dp, mp,
    grads, feat, fields, grad_gate, gyn1, a_in, b_in, small,
    shares, a_full, b_full, c_full, small_out,
    t_work, t_land, t_slots, s_slots, a_work, a_land, b_work, b_land, c_work, c_land, c_slots,
    tsend, trecv, ysend, yrecv, ssend, srecv, asend, arecv, bsend, brecv, csend, crecv,
):
    tall = grads.shape[0] // dp
    me, mine = lax.axis_index("dp"), lax.axis_index("mp")
    hail(dp, mp)
    levels = dp.bit_length() - 1
    far = dp // 2
    side, place = upper(me, 0), me // 2
    size_a, size_b, size_c = a_full.shape[0], b_full.shape[0], c_full.shape[0]
    s_slots[me] = small[...]
    pending = []
    all_in(dp, mp)

    def send_to(copy):
        copy.start()
        pending.append(copy)
        return copy

    def across(k):
        return {"dp": lax.rem(me + 2 * k, dp)}

    def rows_at(start, size):
        return pl.ds(pl.multiple_of(start, 16), size)

    half_t = grads.shape[0] // 2
    copy_t = send_to(
        remote(grads.at[rows_at((1 - side) * half_t, half_t), :], t_land, tsend.at[0], trecv.at[0], {"dp": flip(me, 0)})
    )
    start_a, start_b = 0, side * (size_b // 2)
    for level in range(2):
        start_a = start_a + upper(me, level) * (size_a >> (level + 1))
    a_work[...] = a_in[...]
    b_work[...] = b_in[...]

    def halves(name, level, work, land, size, sems, off):
        half = size // 2
        mine_up = upper(me, level)
        copy = send_to(
            remote(
                work.at[rows_at(off + (1 - mine_up) * half, half), :], land.at[pl.ds(0, half), :],
                sems[0].at[level], sems[1].at[level], {"dp": flip(me, level)},
            )
        )
        return copy, off + mine_up * half, half

    def fold(step, work, land):
        copy, off, half = step
        copy.wait_recv()
        at = rows_at(off, half)
        work[at, :] = low(work[at, :].astype(jnp.float32) + land[pl.ds(0, half), :].astype(jnp.float32))
        return off, half

    def double(level, full, start, size, sems):
        at = full.at[rows_at(start, size), :]
        copy = send_to(
            remote(at, at, sems[0].at[levels + level], sems[1].at[levels + level], {"dp": flip(me, level)})
        )
        return copy, start - upper(me, level) * size, size * 2

    sems_a, sems_b = (asend, arecv), (bsend, brecv)
    step_b = halves("b", 1, b_work, b_land.at[0], size_b // 2, sems_b, 0)
    step_a = halves("a", 2, a_work, a_land.at[0], size_a // 4, sems_a, 0) if levels > 2 else None
    gcols, s1 = feat.shape[1] // mp, gyn1.shape[1] // mp
    wide = feat.shape[1]
    c_work[...] = jnp.zeros_like(c_work)
    c_work[:gcols, :wide] = weight_grad(grad_gate[0], feat[...], mine, gcols)
    c_work[gcols : gcols + s1, :wide] = weight_grad(gyn1[...], fields[0], mine, s1)
    half_c = size_c // 2
    copy_c = send_to(
        remote(c_work.at[rows_at((1 - side) * half_c, half_c), :], c_land, csend.at[0], crecv.at[0], {"dp": flip(me, 0)})
    )
    small_copies = spread_dp(dp, lambda k: s_slots.at[k], ssend, srecv)
    off_b, held_b = fold(step_b, b_work, b_land.at[0])
    step_b = halves("b", 2, b_work, b_land.at[1], held_b, sems_b, off_b)
    off_a, held_a = fold(step_a, a_work, a_land.at[0])
    for level in range(3, levels):
        step_a = halves("a", level, a_work, a_land.at[level - 2], held_a, sems_a, off_a)
        off_a, held_a = fold(step_a, a_work, a_land.at[level - 2])
    start_a = start_a + off_a
    a_full[rows_at(start_a, held_a), :] = a_work[rows_at(off_a, held_a), :]
    back_a = double(levels - 1, a_full, start_a, held_a, sems_a)
    copy_t.wait_recv()
    at = rows_at(side * half_t, half_t)
    t_work[...] = low(grads[at, :].astype(jnp.float32) + t_land[...].astype(jnp.float32))
    t_copies = []
    for k in range(1, far):
        to = lax.rem(place + k, far)
        t_copies.append(
            send_to(
                remote(t_work.at[rows_at(to * tall, tall), :], t_slots.at[k - 1], tsend.at[k], trecv.at[k], across(k))
            )
        )
    copy_c.wait_recv()
    at = rows_at(side * half_c, half_c)
    c_work[at, :] = low(c_work[at, :].astype(jnp.float32) + c_land[...].astype(jnp.float32))
    piece = half_c // far
    c_copies = []
    for k in range(1, far):
        to = lax.rem(place + k, far)
        c_copies.append(
            send_to(
                remote(
                    c_work.at[rows_at(side * half_c + to * piece, piece), :], c_slots.at[k - 1],
                    csend.at[k], crecv.at[k], across(k),
                )
            )
        )
    off_b, held_b = fold(step_b, b_work, b_land.at[1])
    for level in range(3, levels):
        step_b = halves("b", level, b_work, b_land.at[level - 1], held_b, sems_b, off_b)
        off_b, held_b = fold(step_b, b_work, b_land.at[level - 1])
    start_b = start_b + off_b
    b_full[rows_at(start_b, held_b), :] = b_work[rows_at(off_b, held_b), :]
    back_b = double(levels - 1, b_full, start_b, held_b, sems_b)

    def onward(back, level, full, sems):
        copy, start, size = back
        copy.wait_recv()
        return double(level, full, start, size, sems)

    for level in range(levels - 2, 0, -1):
        back_a = onward(back_a, level, a_full, sems_a)
    total = t_work[rows_at(place * tall, tall), :].astype(jnp.float32)
    for k in range(1, far):
        t_copies[k - 1].wait_recv()
        total = total + t_slots[k - 1].astype(jnp.float32)
    shares[mine] = low(total)
    started = relay_own(mp, lambda k: shares.at[k], ysend, yrecv)
    own = rows_at(side * half_c + place * piece, piece)
    total = c_work[own, :].astype(jnp.float32)
    for k in range(1, far):
        c_copies[k - 1].wait_recv()
        total = total + c_slots[k - 1].astype(jnp.float32)
    c_full[own, :] = low(total)
    c_back = []
    for k in range(1, far):
        c_back.append(
            send_to(
                remote(c_full.at[own, :], c_full.at[own, :], csend.at[far + k], crecv.at[far + k], across(k))
            )
        )
    back_a = onward(back_a, 0, a_full, sems_a)
    for level in range(levels - 2, 0, -1):
        back_b = onward(back_b, level, b_full, sems_b)
    relay_rest(mp, lambda k: shares.at[k], ysend, yrecv, started)
    for copy in c_back:
        copy.wait_recv()
    at = c_full.at[rows_at(side * half_c, half_c), :]
    last_c = send_to(remote(at, at, csend.at[far], crecv.at[far], {"dp": flip(me, 0)}))
    back_b = onward(back_b, 0, b_full, sems_b)
    for copy in small_copies:
        copy.wait_recv()
    value = s_slots[0]
    for d in range(1, dp):
        value = value + s_slots[d]
    small_out[...] = value
    back_a[0].wait_recv()
    last_c.wait_recv()
    back_b[0].wait_recv()
    for copy in pending + small_copies:
        copy.wait_send()


def final_kernel(
    mp, hx, shares, a_full, b_full, c_full, small, logits_in, n_gain_in, n_shift_in, b_gain_in, b_shift_in,
    left_in, right_in, bias_in,
    logits, num_g, table_g, gate_g, gate_bias_g, n_first_g, n_rest_g, n_gain_g, n_shift_g,
    b_first_g, b_rest_g, b_gain_g, b_shift_g, left_g, right_g, pair_g, bias_g,
):
    gcols, s1, s2, h1 = gate_g.shape[0], n_first_g.shape[0], b_first_g.shape[0], n_rest_g.shape[2]
    wide = n_first_g.shape[1]

    def full(work, row, count, col, width):
        return work[row : row + count, col : col + width].astype(jnp.float32)

    blocks = shares.shape[1] // 16
    for m in range(mp):
        for b in range(blocks):
            table_g[:, (m * blocks + b) * HI : (m * blocks + b + 1) * HI] = shares[
                m, b * 16 : (b + 1) * 16, :
            ].astype(jnp.float32)
    gate_g[:, 0, :] = full(c_full, 0, gcols, 0, wide)
    gate_g[:, 1, :] = full(b_full, s2, gcols, 0, wide)
    n_first_g[...] = full(c_full, gcols, s1, 0, wide)
    b_first_g[...] = full(b_full, 0, s2, 0, wide)
    main = a_full.shape[1]
    rest = 2 * h1 - main
    parts = main // rest
    tall_a = s2 + s1
    short = -(-tall_a // parts)
    tail = jnp.concatenate(
        [
            full(a_full, tall_a, min(short, tall_a - p * short), p * rest, rest)
            for p in range(parts)
        ],
        axis=0,
    )
    b_rest_g[:, :main] = full(a_full, 0, s2, 0, main)
    b_rest_g[:, main:] = tail[:s2]
    both = jnp.concatenate([full(a_full, s2, s1, 0, main), tail[s2:]], axis=1)
    n_rest_g[:, 0, :] = both[:, :h1]
    n_rest_g[:, 1, :] = both[:, h1:]
    heads = pair_g.shape[2]
    pairs = b_full[b_full.shape[0] - 16 :, :h1]
    row = lax.broadcasted_iota(jnp.int32, (h1, heads), 0)
    col = lax.broadcasted_iota(jnp.int32, (h1, heads), 1)
    for i in range(hx):
        choose = jnp.where(row == col * hx + i, 1.0, 0.0).astype(jnp.bfloat16)
        pair_g[i] = nn(pairs, choose)
    fields, width = num_g.shape
    gate_bias_g[...] = small[0:2, :gcols]
    spread = jnp.broadcast_to(small[2:3, : fields * width], (fields, fields * width))
    row = lax.broadcasted_iota(jnp.int32, spread.shape, 0)
    col = lax.broadcasted_iota(jnp.int32, spread.shape, 1)
    spread = jnp.where(col // width == row, spread, 0.0)
    total = spread[:, :width]
    for i in range(1, fields):
        total = total + spread[:, i * width : (i + 1) * width]
    num_g[...] = total
    logits[...] = logits_in[...]
    n_gain_g[...] = n_gain_in[...]
    n_shift_g[...] = n_shift_in[...]
    b_gain_g[...] = b_gain_in[...]
    b_shift_g[...] = b_shift_in[...]
    left_g[...] = left_in[...]
    right_g[...] = right_in[...].reshape(right_g.shape)
    bias_g[...] = bias_in[...]


def f32(*shape):
    return jax.ShapeDtypeStruct(shape, jnp.float32)


def b16(*shape):
    return jax.ShapeDtypeStruct(shape, jnp.bfloat16)


def held(*shape):
    return pltpu.VMEM(shape, jnp.float32)


def held16(*shape):
    return pltpu.VMEM(shape, jnp.bfloat16)


def dma(*shape):
    return pltpu.SemaphoreType.DMA(shape)


def shards(
    dense_values,
    field_ids,
    lengths,
    labels,
    num_embed,
    embed_table,
    gate_weight,
    gate_bias,
    narrow_first,
    narrow_rest,
    narrow_gain,
    narrow_shift,
    broad_first,
    broad_rest,
    broad_gain,
    broad_shift,
    joining_left,
    joining_right,
    joining_pair,
    joining_bias,
):
    dp, mp = lax.axis_size("dp"), lax.axis_size("mp")
    chips = mp // 2
    rows = dense_values.shape[0]
    cats, slots = field_ids.shape[:2]
    width, own_rows = embed_table.shape
    num = dense_values.shape[1] * width
    wide = gate_weight.shape[2]
    gcols = gate_weight.shape[1]
    s1, s2 = narrow_first.shape[0], broad_first.shape[0]
    h1, h2 = s1 * mp, s2 * mp
    hx = joining_pair.shape[1]
    bits = (cats * rows - 1).bit_length()
    dense_t = dense_values.T
    tall = own_rows // mp // HI * 16
    vregs = 1 << (-(-(cats * slots * rows) // 1024) - 1).bit_length()
    first_args = (
        embed_table, jnp.transpose(gate_weight, (1, 0, 2)), narrow_first, gate_bias,
        narrow_gain, narrow_shift, broad_gain, broad_shift,
        field_ids, lengths, dense_t, num_embed, jnp.transpose(narrow_rest, (1, 0, 2)),
    )
    t2, keys, numeric, gates, n1, vec, n_own = pl.pallas_call(
        functools.partial(first_kernel, dp, mp, own_rows, bits),
        out_shape=(
            b16(dp * tall, HI),
            jax.ShapeDtypeStruct((128, vregs * 8), jnp.int32),
            b16(rows, num),
            b16(2, wide, wide),
            b16(h1, wide),
            f32(16, 896),
            b16(2, s1, h1),
        ),
        in_specs=[ANY] * 13,
        out_specs=(VM,) * 7,
        scratch_shapes=[pltpu.VMEM(x.shape, x.dtype) for x in first_args]
        + [
            pltpu.VMEM((vregs * 8, 128), jnp.int32),
            held16(mp, 2, gcols, wide),
            held16(mp, s1, wide),
            held(mp, 16, 256),
            dma(dp - 1),
            dma(dp - 1),
            dma(3, mp),
            dma(3, mp),
            dma(13),
        ],
        compiler_params=params(0, 54),
        name="first",
    )(*first_args)
    partial = pl.pallas_call(
        functools.partial(lookup_kernel, cats, rows, bits),
        out_shape=f32(cats * 16, rows),
        in_specs=[VM] * 2,
        out_specs=VM,
        scratch_shapes=[held(cats * 16, rows)],
        compiler_params=params(None, 12),
        name="lookup",
    )(keys, t2)

    def up(x, n):
        return -(-x // n) * n

    main = wide // 128 * 128 + 128
    short = -(-(s1 + s2) // (main // (h2 - main)))
    a_rows = up(s1 + s2 + short, 16 * dp)
    b_rows = up(s2 + gcols, 16) + 16
    b_rows = up(b_rows, 16 * dp)
    c_rows = up(gcols + s1, 16 * dp)
    levels = dp.bit_length() - 1
    dense_args = (
        broad_first, broad_rest, joining_left.reshape(1, h1), joining_right,
        jnp.transpose(joining_pair, (1, 2, 0)), joining_bias.reshape(1, 1), labels.reshape(1, rows), dense_t,
    )
    (
        logits, grads_t, feat, fields, grad_gate, gyn1, a_part, b_part, small,
        n_gain_g, n_shift_g, b_gain_g, b_shift_g, left_g, right_g, bias_g,
    ) = pl.pallas_call(
        functools.partial(dense_kernel, dp, mp, hx, float(rows * dp)),
        out_shape=(
            f32(1, rows),
            b16(cats * 16, rows),
            b16(rows, wide),
            b16(2, rows, wide),
            b16(2, rows, wide),
            b16(rows, h1),
            b16(a_rows // 4, main),
            b16(b_rows // 2, main),
            f32(8, 256),
            f32(3, s1),
            f32(3, s1),
            f32(2, s2),
            f32(2, s2),
            f32(1, h1),
            f32(1, h2),
            f32(1, 1),
        ),
        in_specs=[VM] * 6 + [ANY] * 8,
        out_specs=(VM,) * 16,
        scratch_shapes=[
            held(cats * 8, rows),
            held16(chips, cats * 8, rows),
            held16(cats * 16, rows),
            held(2, rows, wide),
            held(rows, wide),
            held16(mp, s2, wide),
            held16(mp, 2, s1, h1),
            held16(mp, s2, h2),
            held16(h2, wide),
            held16(2, h1, h1),
            held16(h2, h2),
            held(3, rows, h1),
            held(3, rows, h1),
            held(2, rows, h2),
            held(2, rows, h2),
            held16(3, rows, h1),
            held16(2, rows, h2),
            held16(2, rows, h1),
            held16(rows, h2),
            held16(h1, h2),
            held16(h1, h2),
            held(h2, h1),
            held(rows, h1),
            held(11, dp, 2, 896),
            held16(s1 + s2, h2 - main),
            dma(chips + 1),
            dma(chips + 1),
            dma(3, mp),
            dma(3, mp),
            dma(11, dp - 1),
            dma(11, dp - 1),
            held16(rows, h2),
            held16(a_rows, main),
            held16(b_rows, main),
            held16(a_rows * 3 // 4, main),
            held16(b_rows // 2, main),
            dma(3),
            dma(3),
        ]
        + [pltpu.VMEM(x.shape, x.dtype) for x in dense_args]
        + [dma(8)],
        compiler_params=params(1, 39 + dp // 16),
        name="dense",
    )(partial, numeric, gates, n1, n_own, vec, *dense_args)
    row_sums = pl.pallas_call(
        functools.partial(scatter_kernel, cats, rows, bits),
        out_shape=b16(dp * tall, HI),
        in_specs=[VM] * 2,
        out_specs=VM,
        scratch_shapes=[held(dp * tall, HI)],
        compiler_params=params(None, 12),
        name="scatter",
    )(keys, grads_t)
    shares, a_full, b_full, c_full, small = pl.pallas_call(
        functools.partial(reduce_kernel, dp, mp),
        out_shape=(
            b16(mp, tall, HI),
            b16(a_rows, main),
            b16(b_rows, main),
            b16(c_rows, main),
            f32(8, 256),
        ),
        in_specs=[VM] * 8,
        out_specs=(VM,) * 5,
        scratch_shapes=[
            held16(dp // 2 * tall, HI),
            held16(dp // 2 * tall, HI),
            held16(dp // 2 - 1, tall, HI),
            held(dp, 8, 256),
            held16(a_rows // 4, main),
            held16(max(levels - 2, 1), a_rows // 8, main),
            held16(b_rows // 2, main),
            held16(max(levels - 1, 1), b_rows // 4, main),
            held16(c_rows, main),
            held16(c_rows // 2, main),
            held16(dp // 2 - 1, c_rows // dp, main),
            dma(dp // 2),
            dma(dp // 2),
            dma(mp),
            dma(mp),
            dma(dp - 1),
            dma(dp - 1),
            dma(2 * levels),
            dma(2 * levels),
            dma(2 * levels),
            dma(2 * levels),
            dma(dp),
            dma(dp),
        ],
        compiler_params=params(2, 24),
        name="reduce",
    )(row_sums, feat, fields, grad_gate, gyn1, a_part, b_part, small)
    outs = pl.pallas_call(
        functools.partial(final_kernel, mp, hx),
        out_shape=(
            f32(1, rows),
            f32(*num_embed.shape),
            f32(width, own_rows),
            f32(gcols, 2, wide),
            f32(2, gcols),
            f32(s1, wide),
            f32(s1, 2, h1),
            f32(3, s1),
            f32(3, s1),
            f32(s2, wide),
            f32(s2, h2),
            f32(2, s2),
            f32(2, s2),
            f32(1, h1),
            f32(h2),
            f32(hx, width, joining_pair.shape[0]),
            f32(1, 1),
        ),
        in_specs=[VM] * 13,
        out_specs=(VM,) * 17,
        compiler_params=params(None, 16),
        name="final",
    )(
        shares, a_full, b_full, c_full, small, logits, n_gain_g, n_shift_g, b_gain_g, b_shift_g,
        left_g, right_g, bias_g,
    )
    outs = list(outs)
    outs[0] = outs[0].reshape(rows)
    outs[3] = jnp.transpose(outs[3], (1, 0, 2))
    outs[6] = jnp.transpose(outs[6], (1, 0, 2))
    outs[13] = outs[13].reshape(h1)
    outs[15] = jnp.transpose(outs[15], (2, 0, 1))
    outs[16] = outs[16].reshape(1)
    return tuple(outs)


def solution(mesh):
    placed = (
        P("dp", None),
        P(None, None, "dp"),
        P(None, "dp"),
        P("dp"),
        P(),
        P(None, "dp"),
        P(None, "mp", None),
        P(None, "mp"),
        P("mp", None),
        P(None, "mp", None),
        P(None, "mp"),
        P(None, "mp"),
        P("mp", None),
        P("mp", None),
        P(None, "mp"),
        P(None, "mp"),
        P(),
        P(),
        P(),
        P(),
    )
    return jax.shard_map(
        shards,
        mesh=mesh,
        in_specs=placed,
        out_specs=(
            P("dp"),
            P(),
            P(None, "dp"),
            P(None, "mp", None),
            P(None, "mp"),
            P("mp", None),
            P(None, "mp", None),
            P(None, "mp"),
            P(None, "mp"),
            P("mp", None),
            P("mp", None),
            P(None, "mp"),
            P(None, "mp"),
            P(),
            P(),
            P(),
            P(),
        ),
        check_vma=False,
    )
```

```python
import functools
import jax
import jax.numpy as jnp
from jax import lax
from jax.experimental import pallas as pl
from jax.experimental.pallas import tpu as pltpu
from jax.sharding import PartitionSpec as P

MESH = pl.DeviceIdType.MESH
VM = pl.BlockSpec(memory_space=pltpu.VMEM)
ANY = pl.BlockSpec(memory_space=pltpu.HBM)
HI = 256
CHUNK = 1024


def params(cid, mib=48):
    if cid is None:
        return pltpu.CompilerParams(vmem_limit_bytes=mib << 20)
    return pltpu.CompilerParams(
        collective_id=cid, has_side_effects=True, vmem_limit_bytes=mib << 20
    )


def hail(dp, mp):
    me, mine = lax.axis_index("dp"), lax.axis_index("mp")
    barrier = pltpu.get_barrier_semaphore()
    for step in range(1, dp):
        pl.semaphore_signal(
            barrier, inc=1, device_id={"dp": lax.rem(me + step, dp)}, device_id_type=MESH
        )
    for step in range(1, mp):
        pl.semaphore_signal(
            barrier, inc=1, device_id={"mp": lax.rem(mine + step, mp)}, device_id_type=MESH
        )


def all_in(dp, mp):
    pl.semaphore_wait(pltpu.get_barrier_semaphore(), dp - 1 + mp - 1)


def remote(src, dst, send, recv, where):
    return pltpu.make_async_remote_copy(
        src_ref=src, dst_ref=dst, send_sem=send, recv_sem=recv,
        device_id=where, device_id_type=MESH,
    )


def spread_dp(dp, pick, send, recv):
    me = lax.axis_index("dp")
    out = []
    for step in range(1, dp):
        to = lax.rem(me + step, dp)
        copy = remote(pick(me), pick(me), send.at[step - 1], recv.at[step - 1], {"dp": to})
        copy.start()
        out.append(copy)
    return out


def over(x, n):
    if n & (n - 1) == 0:
        return lax.shift_right_logical(x, n.bit_length() - 1)
    return x // n


def compact_keys(key):
    count = key.shape[0]
    rows = count * 8
    dead = jnp.where(key.reshape(rows, 128) < 0, 1.0, 0.0).astype(jnp.bfloat16)
    row = lax.broadcasted_iota(jnp.int32, (128, 128), 0)
    col = lax.broadcasted_iota(jnp.int32, (128, 128), 1)
    in_row = jnp.dot(dead, jnp.where(row < col, 1.0, 0.0).astype(jnp.bfloat16), preferred_element_type=jnp.float32)
    row_sum = jnp.dot(dead, jnp.ones((128, 128), jnp.bfloat16), preferred_element_type=jnp.float32)
    row = lax.broadcasted_iota(jnp.int32, (rows, rows), 0)
    col = lax.broadcasted_iota(jnp.int32, (rows, rows), 1)
    above = jnp.where(col < row, 1.0, 0.0).astype(jnp.bfloat16)
    before = jnp.dot(above, row_sum.astype(jnp.bfloat16), preferred_element_type=jnp.float32)
    shift = (in_row + before).astype(jnp.int32).reshape(count, 8, 128)
    shift = jnp.where(key < 0, 0, shift)
    sub = lax.broadcasted_iota(jnp.int32, (8, 128), 0)
    lane = lax.broadcasted_iota(jnp.int32, (8, 128), 1)

    def rows_up(x, j):
        t = [pltpu.roll(x[v], 8 - j, 0) for v in range(count)]
        return jnp.stack([jnp.where(sub < 8 - j, t[v], t[(v + 1) % count]) for v in range(count)])

    bit = 0
    for j in (1, 2, 4, 8, 16, 32, 64):
        def lanes_up(x):
            y = jnp.stack([pltpu.roll(x[v], 128 - j, 1) for v in range(count)])
            return jnp.where(lane[None] < 128 - j, y, rows_up(y, 1))
        key, shift = settle(key, shift, lanes_up(key), lanes_up(shift), bit)
        bit += 1
    for j in (1, 2, 4):
        key, shift = settle(key, shift, rows_up(key, j), rows_up(shift, j), bit)
        bit += 1
    step = 1
    while step < count:
        moved_key = jnp.concatenate([key[step:], key[:step]], axis=0)
        moved_shift = jnp.concatenate([shift[step:], shift[:step]], axis=0)
        key, shift = settle(key, shift, moved_key, moved_shift, bit)
        bit, step = bit + 1, step * 2
    return key


def settle(key, shift, moved_key, moved_shift, bit):
    take = (moved_shift & (1 << bit)) != 0
    stay = (shift & (1 << bit)) == 0
    key = jnp.where(take, moved_key, jnp.where(stay, key, -1))
    shift = jnp.where(take, moved_shift, jnp.where(stay, shift, 0))
    return key, shift


def seat(i, dp):
    return i % 2 * (dp // 2) + i // 2


def make_keys(ids, lens, scratch, own_rows, dp, mp, bits):
    cats, slots, rows = ids.shape
    part = own_rows // mp
    mine = lax.axis_index("mp")
    scratch[...] = jnp.full_like(scratch, -1)
    slot = lax.broadcasted_iota(jnp.int32, (slots, rows), 0)
    event = lax.broadcasted_iota(jnp.int32, (slots, rows), 1)

    def body(c, carry):
        values = ids[c]
        holder = values // own_rows
        inner = values - holder * own_rows
        owner = inner // part
        place = seat(holder, dp) * part + inner - owner * part
        live = (slot < lens[pl.ds(c, 1), :]) & (owner == mine)
        key = jnp.where(live, place * (1 << bits) + c * rows + event, -1)
        for q in range(rows // 128):
            scratch[pl.ds((c * (rows // 128) + q) * slots, slots), :] = key[:, q * 128 : (q + 1) * 128]
        return carry

    lax.fori_loop(0, cats, body, 0)


WINDOW = 16


def chunk_parts(key, rows, bits):
    place = lax.shift_right_arithmetic(key, bits)
    bag = key & ((1 << bits) - 1)
    cat = over(bag, rows)
    return place, cat, bag - cat * rows


def short(row):
    return jnp.broadcast_to(row, (16, row.shape[1])).astype(jnp.int16)


def one_hot(row, size):
    apart = short(row) - lax.broadcasted_iota(jnp.int32, (16, row.shape[1]), 0).astype(jnp.int16)
    one = jnp.ones(apart.shape, jnp.bfloat16)
    zero = jnp.zeros(apart.shape, jnp.bfloat16)
    return jnp.concatenate([jnp.where(apart == i, one, zero) for i in range(0, size, 16)], axis=0)


def spread_rows(row, values, first, size):
    zero = jnp.zeros_like(values)
    apart = short(row - first)
    return jnp.concatenate([jnp.where(apart == i, values, zero) for i in range(size)], axis=0)


def chunk_key(keys, half, k):
    tall = CHUNK // 128
    key = keys[half, pl.ds(pl.multiple_of(k * tall, tall), tall), :]
    return jnp.concatenate([key[i : i + 1, :] for i in range(tall)], axis=1)


def chunk_span(keys, half, k, cats, rows, bits):
    tall = CHUNK // 128
    most = keys.shape[1] // tall - 1
    key = keys[half, pl.ds(pl.multiple_of(jnp.minimum(k, most) * tall, tall), tall), :]
    cat = over(key & ((1 << bits) - 1), rows)
    first = jnp.min(jnp.where(key >= 0, cat, cats - 1))
    last = jnp.max(jnp.where(key >= 0, cat, 0))
    return first, (last - first) // WINDOW + 1


def each_chunk(keys, half, cats, rows, bits, body):
    live = jnp.sum((keys[half] >= 0).astype(jnp.int32))
    chunks = (live + CHUNK - 1) // CHUNK

    def step(k, carry):
        later = chunk_span(keys, half, k + 1, cats, rows, bits)
        body(chunk_key(keys, half, k), *carry)
        return later

    lax.fori_loop(0, chunks, step, chunk_span(keys, half, 0, cats, rows, bits))


def lookup_kernel(cats, rows, bits, keys, t2, pooled, total):
    lows = t2.shape[0] // 32
    total[...] = jnp.zeros_like(total)

    def half_table(half, carry):
        def body(key, first, windows):
            place, cat, event = chunk_parts(key, rows, bits)
            low = jnp.broadcast_to(lax.shift_right_arithmetic(place, 8) - half * lows, (16, CHUNK))
            pick = one_hot(place & (HI - 1), HI)
            z = jnp.zeros((16, CHUNK), jnp.float32)
            for b in range(0, lows, 32):
                n = min(32, lows - b)
                at = pl.ds(pl.multiple_of((half * lows + b) * 16, 16), n * 16)
                y = jnp.dot(t2[at, :], pick, preferred_element_type=jnp.float32)
                for j in range(n):
                    z = z + jnp.where(low == b + j, y[j * 16 : (j + 1) * 16], 0.0)
            z = z.astype(jnp.bfloat16)
            cat = jnp.where(key >= 0, cat, -1)
            place_of = one_hot(event, rows)

            def window(w):
                start = first + w * WINDOW
                at = pl.ds(pl.multiple_of(start * 16, 16), WINDOW * 16)
                total[at, :] += lax.dot_general(
                    spread_rows(cat, z, start, WINDOW), place_of, (((1,), (1,)), ((), ())),
                    preferred_element_type=jnp.float32,
                )

            window(0)

            def more(w, carry):
                window(w)
                return carry

            lax.fori_loop(1, windows, more, 0)

        each_chunk(keys, half, cats, rows, bits, body)
        return carry

    lax.fori_loop(0, 2, half_table, 0)
    pooled[...] = total[: cats * 16, :].astype(pooled.dtype)


def scatter_kernel(cats, rows, bits, keys, grad, out, total, grad_pad):
    lows = total.shape[0] // 32
    total[...] = jnp.zeros_like(total)
    grad_pad[: cats * 16, :] = grad[...]
    grad_pad[cats * 16 :, :] = jnp.zeros((WINDOW * 16, rows), jnp.bfloat16)

    def half_table(half, carry):
        def body(key, first, windows):
            place, cat, event = chunk_parts(key, rows, bits)
            low = lax.shift_right_arithmetic(place, 8) - half * lows
            pick = one_hot(place & (HI - 1), HI)
            place_of = one_hot(event, rows)
            cat = jnp.broadcast_to(jnp.where(key >= 0, cat, -1), (16, CHUNK))

            def window(w, g):
                start = first + w * WINDOW
                at = pl.ds(pl.multiple_of(start * 16, 16), WINDOW * 16)
                wide = jnp.dot(grad_pad[at, :], place_of, preferred_element_type=jnp.float32)
                for c in range(WINDOW):
                    g = g + jnp.where(cat == start + c, wide[c * 16 : (c + 1) * 16], 0.0)
                return g

            g = window(0, jnp.zeros((16, CHUNK), jnp.float32))
            g = lax.fori_loop(1, windows, window, g).astype(jnp.bfloat16)
            for b in range(0, lows, 32):
                n = min(32, lows - b)
                at = pl.ds(pl.multiple_of((half * lows + b) * 16, 16), n * 16)
                total[at, :] += lax.dot_general(
                    spread_rows(low, g, b, n), pick, (((1,), (1,)), ((), ())),
                    preferred_element_type=jnp.float32,
                )

        each_chunk(keys, half, cats, rows, bits, body)
        return carry

    lax.fori_loop(0, 2, half_table, 0)
    out[...] = total[...].astype(out.dtype)


def relay_own(mp, slot, send, recv):
    mine = lax.axis_index("mp")
    core = lax.rem(mine, 2)
    other = mine + 1 - 2 * core
    chips = mp // 2
    out = []
    for k in range(1, chips):
        to = lax.rem(mine + 2 * k, mp)
        copy = remote(slot(mine), slot(mine), send.at[2 * k], recv.at[2 * k], {"mp": to})
        copy.start()
        out.append(copy)
    copy = remote(slot(mine), slot(mine), send.at[1], recv.at[1], {"mp": other})
    copy.start()
    out.append(copy)
    return out


def relay_rest(mp, slot, send, recv, started):
    mine = lax.axis_index("mp")
    core = lax.rem(mine, 2)
    other = mine + 1 - 2 * core
    chips = mp // 2
    passed = []
    for k in range(1, chips):
        source = lax.rem(mine + mp - 2 * k, mp)
        remote(slot(source), slot(source), send.at[2 * k], recv.at[2 * k], {"mp": other}).wait_recv()
        copy = remote(slot(source), slot(source), send.at[2 * k + 1], recv.at[2 * k + 1], {"mp": other})
        copy.start()
        passed.append(copy)
    remote(slot(other), slot(other), send.at[1], recv.at[1], {"mp": other}).wait_recv()
    for k in range(1, chips):
        far = lax.rem(other + mp - 2 * k, mp)
        remote(slot(far), slot(far), send.at[2 * k + 1], recv.at[2 * k + 1], {"mp": other}).wait_recv()
    for copy in started + passed:
        copy.wait_send()


def nn(a, b):
    return jnp.dot(a, b, preferred_element_type=jnp.float32)


def nt(a, b):
    return lax.dot_general(a, b, (((1,), (1,)), ((), ())), preferred_element_type=jnp.float32)


def tn(a, b):
    return lax.dot_general(a, b, (((0,), (0,)), ((), ())), preferred_element_type=jnp.float32)


def sigmoid(x):
    return 0.5 * jnp.tanh(0.5 * x) + 0.5


def low(x):
    return x.astype(jnp.bfloat16)


def column_sum(x):
    return jnp.sum(x, axis=0, keepdims=True)


def widen_dense(dense_t, width):
    fields = dense_t.shape[0]
    row = lax.broadcasted_iota(jnp.int32, (fields, fields * width), 0)
    col = lax.broadcasted_iota(jnp.int32, (fields, fields * width), 1)
    ones = jnp.where(col // width == row, 1.0, 0.0)
    return lax.dot_general(
        dense_t, ones, (((0,), (0,)), ((), ())),
        precision=lax.Precision.HIGHEST, preferred_element_type=jnp.float32,
    )


def split_relay(dp, mp, ref, send, recv):
    me, mine = lax.axis_index("dp"), lax.axis_index("mp")
    other = mine + 1 - 2 * lax.rem(mine, 2)
    chips = mp // 2
    near = lax.rem(me, 2)
    beside = {"dp": me + 1 - 2 * near}
    started = []

    def move(place, i, where):
        return remote(place, place, send.at[i], recv.at[i], where)

    def go(place, i, where):
        copy = move(place, i, where)
        copy.start()
        started.append(copy)

    def source(k):
        return lax.rem(mine + mp - 2 * k, mp)

    def begin():
        for k in range(1, chips):
            go(ref.at[mine, near], k, {"mp": lax.rem(mine + 2 * k, mp)})
        go(ref.at[mine], 0, {"mp": other})

    def middle():
        for k in range(1, chips):
            place = ref.at[source(k), near]
            move(place, k, beside).wait_recv()
            go(place, 2 * chips + k, beside)
            go(place, chips + k, {"mp": other})

    def later():
        for k in range(1, chips):
            place = ref.at[source(k), 1 - near]
            move(place, 2 * chips + k, beside).wait_recv()
            go(place, 3 * chips + k, {"mp": other})

    def end():
        move(ref.at[other], 0, beside).wait_recv()
        for k in range(1, chips):
            far = lax.rem(other + mp - 2 * k, mp)
            move(ref.at[far, near], chips + k, beside).wait_recv()
            move(ref.at[far, 1 - near], 3 * chips + k, beside).wait_recv()
        for copy in started:
            copy.wait_send()

    return begin, middle, later, end


def bring(sources, places, sem):
    copies = []
    for i, (source, place) in enumerate(zip(sources, places)):
        copy = pltpu.make_async_copy(source, place, sem.at[i])
        copy.start()
        copies.append(copy)
    return copies


def first_kernel(dp, mp, own_rows, bits, *refs):
    count = 14
    sources, refs = refs[:count], refs[count:]
    t2, keys, numeric, weights, vec, n_own = refs[:6]
    places, refs = refs[6 : 6 + count], refs[6 + count :]
    (
        scratch, gate_slots, n_slots, b_slots, v_slots,
        send, recv, send2, recv2, send3, recv3, sem,
    ) = refs
    brought = bring(sources, places, sem)
    (
        table, gate_w, n_first, gate_b, n_gain, n_shift, b_gain, b_shift, b_first,
        ids, lens, dense_t, num_embed, n_rest,
    ) = places
    part = own_rows // mp
    blocks = part // HI
    tall = blocks * 16
    me, mine = lax.axis_index("dp"), lax.axis_index("mp")
    hail(dp, mp)
    for copy in brought[:9]:
        copy.wait()
    own = table[:, pl.ds(pl.multiple_of(mine * part, HI), part)].astype(jnp.bfloat16)
    for b in range(blocks):
        t2[pl.ds(pl.multiple_of(seat(me, dp) * tall + b * 16, 16), 16), :] = own[:, b * HI : (b + 1) * HI]
    for k in range(2):
        gate_slots[mine, k] = gate_w[:, k, :]
    small, large = n_slots.shape[2], b_slots.shape[2]
    for k in range(2):
        n_slots[mine, k] = n_first[k * small : (k + 1) * small, :]
        b_slots[mine, k] = b_first[k * large : (k + 1) * large, :]
    row = 0
    for ref in (gate_b, n_gain, n_shift, b_gain, b_shift):
        v_slots[mine, row : row + ref.shape[0], : ref.shape[1]] = ref[...]
        row += ref.shape[0]
    all_in(dp, mp)

    def slot(i):
        return t2.at[pl.ds(pl.multiple_of(seat(i, dp) * tall, 16), tall), :]

    pairs = [
        split_relay(dp, mp, ref, send3.at[i], recv3.at[i]) for i, ref in enumerate((n_slots, b_slots))
    ]
    for steps in pairs:
        steps[0]()
    groups = []
    for i, ref in enumerate((gate_slots, v_slots)):
        started = relay_own(mp, lambda k, ref=ref: ref.at[k], send2.at[i], recv2.at[i])
        groups.append((ref, i, started))
    copies = spread_dp(dp, slot, send, recv)
    for copy in brought[9:]:
        copy.wait()
    for k in range(2):
        n_own[k] = n_rest[:, k, :]
    fields, width = num_embed.shape
    tiled = jnp.concatenate([num_embed[...]] * fields, axis=1)
    row = lax.broadcasted_iota(jnp.int32, tiled.shape, 0)
    col = lax.broadcasted_iota(jnp.int32, tiled.shape, 1)
    num_row = column_sum(jnp.where(col // width == row, tiled, 0.0))
    numeric[...] = low(widen_dense(dense_t[...], width) * num_row)
    make_keys(ids, lens, scratch, own_rows, dp, mp, bits)
    count = scratch.shape[0] // 8
    middle = (dp * part // 2) << bits

    def pack(half, carry):
        key = scratch[...]
        key = jnp.where((key < middle) == (half == 0), key, -1)
        keys[half] = compact_keys(key.reshape(count, 8, 128)).reshape(count * 8, 128)
        return carry

    lax.fori_loop(0, 2, pack, 0)
    for steps in pairs:
        steps[1]()
    for ref, i, started in groups:
        relay_rest(mp, lambda k, ref=ref: ref.at[k], send2.at[i], recv2.at[i], started)
    cols, wide = gate_slots.shape[2], gate_slots.shape[3]
    for m in range(mp):
        for k in range(2):
            row = k * wide + m * cols
            weights[row : row + cols, :] = gate_slots[m, k]
    for steps in pairs:
        steps[2]()
    row = 2 * wide
    for ref, steps in zip((n_slots, b_slots), pairs):
        steps[3]()
        tall = ref.shape[2]
        for m in range(mp):
            for k in range(2):
                weights[row : row + tall, :] = ref[m, k]
                row += tall
    row = 0
    for ref in (gate_b, n_gain, n_shift, b_gain, b_shift):
        r, w = ref.shape
        vec[row : row + r, : mp * w] = jnp.concatenate(
            [v_slots[m, row : row + r, :w] for m in range(mp)], axis=1
        )
        row += r
    for copy in copies:
        copy.wait()


def own_columns(x, mine, width, mp):
    out = jnp.zeros((x.shape[0], width), x.dtype)
    for m in range(mp):
        out = jnp.where(mine == m, x[:, m * width : (m + 1) * width], out)
    return out


def up16(x):
    return -(-x // 16) * 16


def weight_grad(grad_y, inputs, own, mine, width, mp):
    for m in range(mp):

        @pl.when(mine == m)
        def _():
            own[:, :width] = grad_y[:, m * width : (m + 1) * width]

    return low(tn(own[:, :width], inputs))


def flip(me, level):
    bit = 1 << level
    return me + bit - 2 * bit * lax.rem(me // bit, 2)


def upper(me, level):
    return lax.rem(me // (1 << level), 2)


def give_half(me, level, start, size, work, land, send, recv):
    half = size // 2
    mine = upper(me, level)
    at = pl.ds(pl.multiple_of(start + (1 - mine) * half, 16), half)
    copy = remote(work.at[at, :], land, send, recv, {"dp": flip(me, level)})
    copy.start()
    return copy, start + mine * half


def add_half(copy, start, half, work, land):
    copy.wait_recv()
    at = pl.ds(pl.multiple_of(start, 16), half)
    return low(work[at, :].astype(jnp.float32) + land[...].astype(jnp.float32))


def dense_kernel(
    dp, mp, hx, batch,
    partial, numeric, weights, n_rest, vec,
    b_rest_hbm, left_hbm, right_hbm, pair_hbm, bias_hbm, labels_hbm, dense_hbm,
    logits, grads_t, feat, fields, grad_gate, gyn1, a_out, b_out, small,
    n_gain_g, n_shift_g, b_gain_g, b_shift_g, left_g, right_g, bias_g,
    half_a, half_c, pooled, gate, own_term, n_slots, b_slots, n23, b2,
    yn, dn, yb, db, un, ub, gyn, gyb, pair_hi, pair_lo, pair_g, to_first, sums, spill,
    fsend, frecv, wsend, wrecv, ssend, srecv,
    gyb1, a_work, b_work, a_land, b_land, hsend, hrecv, own_cols,
    b_rest, left, right, pair_t, bias, labels, dense_t, sem,
):
    brought = bring(
        (b_rest_hbm, left_hbm, right_hbm, pair_hbm, bias_hbm, labels_hbm, dense_hbm),
        (b_rest, left, right, pair_t, bias, labels, dense_t),
        sem,
    )
    me, mine = lax.axis_index("dp"), lax.axis_index("mp")
    core = lax.rem(mine, 2)
    chip = mine // 2
    chips = mp // 2
    other = mine + 1 - 2 * core
    rows = feat.shape[0]
    block = 256
    steps = rows // block
    h1, h2 = n23.shape[1], b2.shape[0]
    s1, s2 = h1 // mp, h2 // mp
    wide = feat.shape[1]
    gates = (weights.at[pl.ds(0, wide), :], weights.at[pl.ds(wide, wide), :])
    n1 = weights.at[pl.ds(2 * wide, h1), :]
    b1 = weights.at[pl.ds(2 * wide + h1, h2), :]
    num = numeric.shape[1]
    gcols = wide // mp
    half = partial.shape[0] // 2
    hail(dp, mp)
    n_slots[mine] = n_rest[...]
    all_in(dp, mp)

    def rowset(i):
        return pl.ds(pl.multiple_of(i * block, block), block)

    def part(c):
        return pl.ds(pl.multiple_of(c * half, 16), half)

    def events(h):
        return pl.ds(h * (rows // 2), rows // 2)

    copies_a, copies_y, copies_b = [], [], []
    for h in range(2):
        copy = remote(
            partial.at[part(1 - core), events(h)], half_a.at[:, events(h)], fsend.at[h, 0], frecv.at[h, 0],
            {"mp": other},
        )
        copy.start()
        copies_a.append(copy)
    for copy in brought:
        copy.wait()
    for k in range(2):
        b_slots[mine, k] = b_rest[k * (s2 // 2) : (k + 1) * (s2 // 2), :]
    for h in range(2):
        copies_a[h].wait_recv()
        half_c[chip, :, events(h)] = low(partial[part(core), events(h)] + half_a[:, events(h)])
        for k in range(1, chips):
            place = half_c.at[chip, :, events(h)]
            copy = remote(
                place, place, fsend.at[h, k], frecv.at[h, k], {"mp": lax.rem(mine + 2 * k, mp)}
            )
            copy.start()
            copies_y.append(copy)
    heads = pair_t.shape[2]
    by_head = jnp.transpose(pair_t[...].reshape(hx * 16, heads))
    row = lax.broadcasted_iota(jnp.int32, (h1, heads), 0)
    col = lax.broadcasted_iota(jnp.int32, (h1, heads), 1)
    repeat = jnp.where(row // hx == col, 1.0, 0.0)
    tall = jnp.dot(repeat, by_head, precision=lax.Precision.HIGHEST, preferred_element_type=jnp.float32)
    row = lax.broadcasted_iota(jnp.int32, (h1, 16), 0)
    pick = jnp.zeros((h1, 16), jnp.float32)
    for i in range(hx):
        pick = jnp.where(row % hx == i, tall[:, i * 16 : (i + 1) * 16], pick)
    for i in range(0, h1, 80):
        row = lax.broadcasted_iota(jnp.int32, (80, h2), 0) + i
        col = lax.broadcasted_iota(jnp.int32, (80, h2), 1)
        pieces = jnp.concatenate([pick[i : i + 80, :]] * heads, axis=1)
        spread = jnp.where(row // hx == col // 16, pieces, 0.0)
        high = low(spread)
        pair_hi[i : i + 80, :] = high
        pair_lo[i : i + 80, :] = low(spread - high.astype(jnp.float32))
    for h in range(2):
        for copy in copies_y[h * (chips - 1) : (h + 1) * (chips - 1)]:
            copy.wait_recv()
        total = half_c[0, :, events(h)].astype(jnp.float32)
        for k in range(1, chips):
            total = total + half_c[k, :, events(h)].astype(jnp.float32)
        pooled[part(core), events(h)] = low(total)
        place = pooled.at[part(core), events(h)]
        copy = remote(place, place, fsend.at[h, chips], frecv.at[h, chips], {"mp": other})
        copy.start()
        copies_b.append(copy)
    n_steps = split_relay(dp, mp, n_slots, wsend.at[0], wrecv.at[0])
    b_steps = split_relay(dp, mp, b_slots, wsend.at[1], wrecv.at[1])
    n_steps[0]()
    b_steps[0]()
    feat[:, :num] = numeric[...]
    started = []

    def push(slot, *values):
        width = -(-values[0].shape[1] // 128) * 128
        for r, value in enumerate(values):
            sums[slot, me, r : r + 1, : value.shape[1]] = value
        out = []
        for step in range(1, dp):
            at = sums.at[slot, me, :, pl.ds(0, width)]
            copy = remote(
                at, at, ssend.at[slot, step - 1], srecv.at[slot, step - 1], {"dp": lax.rem(me + step, dp)}
            )
            copy.start()
            out.append(copy)
        started.append(out)
        return slot, width, out

    def pull(sent):
        slot, width, out = sent
        for copy in out:
            copy.wait_recv()
        total = sums[slot, 0, :, :width]
        for d in range(1, dp):
            total = total + sums[slot, d, :, :width]
        return total

    def norm(sent, width):
        total = pull(sent)
        mean = total[0:1, :width] / batch
        var = total[1:2, :width] / batch - mean * mean
        return mean, lax.rsqrt(var + 1e-05)

    def activate(y_ref, d_ref, u_ref, layer, at, mean, rstd, gain, shift):
        normed = (y_ref[layer, at, :] - mean) * rstd
        z = gain * normed + shift
        s = sigmoid(z)
        u = z * s
        y_ref[layer, at, :] = normed
        d_ref[layer, at, :] = s + u * (1.0 - s)
        u = low(u)
        u_ref[layer, at, :] = u
        return u

    def gain_n(layer):
        return vec[2 + layer : 3 + layer, :h1], vec[5 + layer : 6 + layer, :h1]

    def gain_b(layer):
        return vec[8 + layer : 9 + layer, :h2], vec[10 + layer : 11 + layer, :h2]

    zero1 = jnp.zeros((1, h1), jnp.float32)
    zero2 = jnp.zeros((1, h2), jnp.float32)

    def loop(body, *start):
        return lax.fori_loop(0, steps, lambda i, carry: body(rowset(i), *carry), tuple(start))

    def gates_and_first(at, a, b):
        x = feat[at, :]
        wide_x = x.astype(jnp.float32)
        for k in range(2):
            value = 2.0 * sigmoid(nt(x, gates[k][...]) + vec[k : k + 1, :wide])
            gate[k, at, :] = value
            fields[k, at, :] = low(wide_x * value)
        y = nt(fields[0, at, :], n1[...])
        yn[0, at, :] = y
        return a + column_sum(y), b + column_sum(y * y)

    a, b = zero1, zero1
    for h in range(2):
        copies_b[h].wait_recv()
        at = events(h)
        feat[at, num:] = low(jnp.transpose(pooled[:, at].astype(jnp.float32)))
        a, b = gates_and_first(at, a, b)
    sent_n = push(0, a, b)
    n_steps[1]()

    def broad_first(at, a, b):
        y = nt(fields[1, at, :], b1[...])
        yb[0, at, :] = y
        return a + column_sum(y), b + column_sum(y * y)

    sent_b = push(1, *loop(broad_first, zero2, zero2))
    b_steps[1]()
    n_steps[2]()
    n_steps[3]()
    for m in range(mp):
        for k in range(2):
            n23[k, m * s1 : (m + 1) * s1, :] = n_slots[m, k]
    mean_n1, rstd_n1 = norm(sent_n, h1)

    def narrow_second(at, a, b):
        y = nt(activate(yn, dn, un, 0, at, mean_n1, rstd_n1, *gain_n(0)), n23[0])
        yn[1, at, :] = y
        return a + column_sum(y), b + column_sum(y * y)

    sent_n = push(2, *loop(narrow_second, zero1, zero1))
    b_steps[2]()
    b_steps[3]()
    for m in range(mp):
        for k in range(2):
            row = (2 * m + k) * (s2 // 2)
            b2[row : row + s2 // 2, :] = b_slots[m, k]
    mean_b1, rstd_b1 = norm(sent_b, h2)

    def broad_second(at, a, b):
        y = nt(activate(yb, db, ub, 0, at, mean_b1, rstd_b1, *gain_b(0)), b2[...])
        yb[1, at, :] = y
        return a + column_sum(y), b + column_sum(y * y)

    sent_b = push(3, *loop(broad_second, zero2, zero2))
    mean_n2, rstd_n2 = norm(sent_n, h1)

    def narrow_third(at, a, b):
        y = nt(activate(yn, dn, un, 1, at, mean_n2, rstd_n2, *gain_n(1)), n23[1])
        yn[2, at, :] = y
        return a + column_sum(y), b + column_sum(y * y)

    sent_n = push(4, *loop(narrow_third, zero1, zero1))
    label = jnp.transpose(jnp.broadcast_to(labels[...].astype(jnp.float32), (8, rows)))[:, 0:1]
    own_term[:, 0:1] = label
    pair_g[...] = jnp.zeros_like(pair_g)
    mean_b2, rstd_b2 = norm(sent_b, h2)

    def broad_out(at):
        second = activate(yb, db, ub, 1, at, mean_b2, rstd_b2, *gain_b(1))
        to_first[at, :] = left[...] + (nt(second, pair_hi[...]) + nt(second, pair_lo[...]))
        return ()

    loop(broad_out)
    mean_n3, rstd_n3 = norm(sent_n, h1)
    to_right = right[...].reshape(1, h2)

    def join_narrow(at, l_sum, g_sum, a, b):
        first = activate(yn, dn, un, 2, at, mean_n3, rstd_n3, *gain_n(2)).astype(jnp.float32)
        second = ub[1, at, :].astype(jnp.float32)
        logit = (
            jnp.sum(first * to_first[at, :], axis=1, keepdims=True)
            + jnp.sum(second * to_right, axis=1, keepdims=True)
            + bias[...]
        )
        g = sigmoid(logit) - own_term[at, 0:1]
        own_term[at, 1:2] = logit
        own_term[at, 2:3] = g
        gz = g * to_first[at, :] * dn[2, at, :]
        dn[2, at, :] = gz
        return (
            l_sum + column_sum(g * first), g_sum + column_sum(g),
            a + column_sum(gz), b + column_sum(gz * yn[2, at, :]),
        )

    l_sum, g_sum, a, b = loop(join_narrow, zero1, jnp.zeros((1, 1), jnp.float32), zero1, zero1)
    sent_n = push(5, a, b)

    def join_broad(at, r_sum, a, b):
        first = un[2, at, :]
        second = ub[1, at, :]
        g = own_term[at, 2:3]
        turned = nn(first, pair_hi[...]) + nn(first, pair_lo[...])
        pair_g[...] += tn(second, low(g * first.astype(jnp.float32)))
        gz = g * (to_right + turned) * db[1, at, :]
        db[1, at, :] = gz
        return (
            r_sum + column_sum(g * second.astype(jnp.float32)),
            a + column_sum(gz), b + column_sum(gz * yb[1, at, :]),
        )

    r_sum, a, b = loop(join_broad, zero2, zero2, zero2)
    sent_b = push(6, a, b)
    sums[10, me, 1:2, 512:513] = g_sum
    sent_join = push(10, r_sum, l_sum)
    logits[...] = jnp.transpose(own_term[:, 0:128])[1:2, :]

    def grad_y(gz, normed, rstd, gain, total):
        return low(gain * rstd * (gz - total[0:1] / batch - normed * (total[1:2] / batch)))

    t_n3 = pull(sent_n)[:, :h1]

    def back_n3(at, a, b):
        g = grad_y(dn[2, at, :], yn[2, at, :], rstd_n3, gain_n(2)[0], t_n3)
        gyn[1, at, :] = g
        gz = nn(g, n23[1]) * dn[1, at, :]
        dn[1, at, :] = gz
        return a + column_sum(gz), b + column_sum(gz * yn[1, at, :])

    sent_n = push(7, *loop(back_n3, zero1, zero1))
    main = a_work.shape[1]
    rest = h2 - main
    parts = main // rest
    tall_a = s2 + s1
    short = -(-tall_a // parts)
    a_work[...] = jnp.zeros_like(a_work)
    b_work[...] = jnp.zeros_like(b_work)
    grad_n3 = weight_grad(gyn.at[1], un[1], own_cols, mine, s1, mp)
    t_b2 = pull(sent_b)[:, :h2]

    def back_b2(at, a, b):
        g = grad_y(db[1, at, :], yb[1, at, :], rstd_b2, gain_b(1)[0], t_b2)
        gyb[at, :] = g
        gz = nn(g, b2[...]) * db[0, at, :]
        db[0, at, :] = gz
        return a + column_sum(gz), b + column_sum(gz * yb[0, at, :])

    sent_b = push(8, *loop(back_b2, zero2, zero2))
    t_n2 = pull(sent_n)[:, :h1]

    def back_n2(at, a, b):
        g = grad_y(dn[1, at, :], yn[1, at, :], rstd_n2, gain_n(1)[0], t_n2)
        gyn[0, at, :] = g
        gz = nn(g, n23[0]) * dn[0, at, :]
        dn[0, at, :] = gz
        return a + column_sum(gz), b + column_sum(gz * yn[0, at, :])

    sent_n = push(9, *loop(back_n2, zero1, zero1))
    grad_n2 = weight_grad(gyn.at[0], un[0], own_cols, mine, s1, mp)
    grad_b2 = weight_grad(gyb, ub[0], own_cols, mine, s2, mp)
    a_work[:s2, :] = grad_b2[:, :main]
    a_work[s2:tall_a, :] = jnp.concatenate([grad_n2, grad_n3], axis=1)[:, :main]
    spill[:s2, :] = grad_b2[:, main:]
    spill[s2:tall_a, :] = jnp.concatenate([grad_n2, grad_n3], axis=1)[:, main:]
    for p in range(parts):
        n = min(short, tall_a - p * short)
        a_work[tall_a : tall_a + n, p * rest : (p + 1) * rest] = spill[p * short : p * short + n, :]
    size_a, size_b = a_work.shape[0], b_work.shape[0]
    copy_ax, start_a = give_half(me, 0, 0, size_a, a_work, a_land.at[pl.ds(0, size_a // 2), :], hsend.at[0], hrecv.at[0])
    folded = jnp.zeros((16, h1), jnp.float32)
    col = lax.broadcasted_iota(jnp.int32, (16, h1), 1)
    for h in range(heads):
        folded = folded + jnp.where(col // hx == h, pair_g[h * 16 : (h + 1) * 16, :], 0.0)
    b_work[size_b - 16 :, :h1] = low(folded)
    t_b1 = pull(sent_b)[:, :h2]

    def gate_back(k, at, grad):
        x = feat[at, :].astype(jnp.float32)
        value = gate[k, at, :]
        g = low(grad * x * value * (1.0 - 0.5 * value))
        grad_gate[k, at, :] = g
        return grad * value, g

    def back_b1(at):
        g = grad_y(db[0, at, :], yb[0, at, :], rstd_b1, gain_b(0)[0], t_b1)
        gyb1[at, :] = g
        own_term[at, :] = gate_back(1, at, nn(g, b1[...]))[0]
        return ()

    loop(back_b1)
    b_work[:s2, :wide] = weight_grad(gyb1, fields[1], own_cols, mine, s2, mp)
    b_work[s2 : s2 + gcols, :wide] = weight_grad(grad_gate.at[1], feat[...], own_cols, mine, gcols, mp)
    copy_bx, start_b = give_half(me, 0, 0, size_b, b_work, b_land, hsend.at[2], hrecv.at[2])
    a_work[pl.ds(pl.multiple_of(start_a, 16), size_a // 2), :] = add_half(
        copy_ax, start_a, size_a // 2, a_work, a_land.at[pl.ds(0, size_a // 2), :]
    )
    copy_az, start_a = give_half(
        me, 1, start_a, size_a // 2, a_work, a_land.at[pl.ds(size_a // 2, size_a // 4), :], hsend.at[1], hrecv.at[1]
    )
    t_n1 = pull(sent_n)[:, :h1]

    def back_n1(at, ga, gb, ne):
        g = grad_y(dn[0, at, :], yn[0, at, :], rstd_n1, gain_n(0)[0], t_n1)
        gyn1[at, :] = g
        term, g0 = gate_back(0, at, nn(g, n1[...]))
        g1 = grad_gate[1, at, :]
        whole = nn(g0, gates[0][...]) + nn(g1, gates[1][...]) + term + own_term[at, :]
        whole = low(whole).astype(jnp.float32)
        own_term[at, :] = whole
        ne = ne + column_sum(whole[:, :num] * widen_dense(dense_t[:, at], 16))
        return ga + column_sum(g0.astype(jnp.float32)), gb + column_sum(g1.astype(jnp.float32)), ne

    zero_g = jnp.zeros((1, wide), jnp.float32)
    ga, gb, ne = loop(back_n1, zero_g, zero_g, jnp.zeros((1, num), jnp.float32))
    grads_t[...] = low(jnp.transpose(own_term[:, num:]))
    small[...] = jnp.zeros_like(small)
    small[0:1, :gcols] = own_columns(ga, mine, gcols, mp)
    small[1:2, :gcols] = own_columns(gb, mine, gcols, mp)
    small[2:3, :num] = ne
    for layer, t in enumerate((t_n1, t_n2, t_n3)):
        n_shift_g[layer : layer + 1, :] = own_columns(t[0:1], mine, s1, mp)
        n_gain_g[layer : layer + 1, :] = own_columns(t[1:2], mine, s1, mp)
    for layer, t in enumerate((t_b1, t_b2)):
        b_shift_g[layer : layer + 1, :] = own_columns(t[0:1], mine, s2, mp)
        b_gain_g[layer : layer + 1, :] = own_columns(t[1:2], mine, s2, mp)
    total = pull(sent_join)
    right_g[...] = total[0:1, :h2]
    left_g[...] = total[1:2, :h1]
    bias_g[...] = total[1:2, 512:513]
    a_out[...] = add_half(
        copy_az, start_a, size_a // 4, a_work, a_land.at[pl.ds(size_a // 2, size_a // 4), :]
    )
    b_out[...] = add_half(copy_bx, start_b, size_b // 2, b_work, b_land)
    for copy in [copy_ax, copy_az, copy_bx] + copies_a + copies_y + copies_b:
        copy.wait_send()
    for group in started:
        for copy in group:
            copy.wait_send()


def reduce_kernel(
    dp, mp,
    grads, feat, fields, grad_gate, gyn1, a_in, b_in, small,
    shares, a_full, b_full, c_full, small_out,
    t_work, t_land, t_slots, s_slots, a_work, a_land, b_work, b_land, c_work, c_land, c_slots, own_cols,
    tsend, trecv, ysend, yrecv, ssend, srecv, asend, arecv, bsend, brecv, csend, crecv,
):
    tall = grads.shape[0] // dp
    me, mine = lax.axis_index("dp"), lax.axis_index("mp")
    hail(dp, mp)
    levels = dp.bit_length() - 1
    far = dp // 2
    side, place = upper(me, 0), me // 2
    size_a, size_b, size_c = a_full.shape[0], b_full.shape[0], c_full.shape[0]
    s_slots[me] = small[...]
    pending = []
    all_in(dp, mp)

    def send_to(copy):
        copy.start()
        pending.append(copy)
        return copy

    def across(k):
        return {"dp": lax.rem(me + 2 * k, dp)}

    def rows_at(start, size):
        return pl.ds(pl.multiple_of(start, 16), size)

    half_t = grads.shape[0] // 2
    copy_t = send_to(
        remote(grads.at[rows_at((1 - side) * half_t, half_t), :], t_land, tsend.at[0], trecv.at[0], {"dp": flip(me, 0)})
    )
    start_a, start_b = 0, side * (size_b // 2)
    for level in range(2):
        start_a = start_a + upper(me, level) * (size_a >> (level + 1))
    a_work[...] = a_in[...]
    b_work[...] = b_in[...]

    def halves(name, level, work, land, size, sems, off):
        half = size // 2
        mine_up = upper(me, level)
        copy = send_to(
            remote(
                work.at[rows_at(off + (1 - mine_up) * half, half), :], land.at[pl.ds(0, half), :],
                sems[0].at[level], sems[1].at[level], {"dp": flip(me, level)},
            )
        )
        return copy, off + mine_up * half, half

    def fold(step, work, land):
        copy, off, half = step
        copy.wait_recv()
        at = rows_at(off, half)
        work[at, :] = low(work[at, :].astype(jnp.float32) + land[pl.ds(0, half), :].astype(jnp.float32))
        return off, half

    def double(level, full, start, size, sems):
        at = full.at[rows_at(start, size), :]
        copy = send_to(
            remote(at, at, sems[0].at[levels + level], sems[1].at[levels + level], {"dp": flip(me, level)})
        )
        return copy, start - upper(me, level) * size, size * 2

    sems_a, sems_b = (asend, arecv), (bsend, brecv)
    step_b = halves("b", 1, b_work, b_land.at[0], size_b // 2, sems_b, 0)
    step_a = halves("a", 2, a_work, a_land.at[0], size_a // 4, sems_a, 0) if levels > 2 else None
    gcols, s1 = feat.shape[1] // mp, gyn1.shape[1] // mp
    wide = feat.shape[1]
    c_work[...] = jnp.zeros_like(c_work)
    c_work[:gcols, :wide] = weight_grad(grad_gate.at[0], feat[...], own_cols, mine, gcols, mp)
    c_work[gcols : gcols + s1, :wide] = weight_grad(gyn1, fields[0], own_cols, mine, s1, mp)
    half_c = size_c // 2
    copy_c = send_to(
        remote(c_work.at[rows_at((1 - side) * half_c, half_c), :], c_land, csend.at[0], crecv.at[0], {"dp": flip(me, 0)})
    )
    small_copies = spread_dp(dp, lambda k: s_slots.at[k], ssend, srecv)
    off_b, held_b = fold(step_b, b_work, b_land.at[0])
    step_b = halves("b", 2, b_work, b_land.at[1], held_b, sems_b, off_b)
    off_a, held_a = fold(step_a, a_work, a_land.at[0])
    for level in range(3, levels):
        step_a = halves("a", level, a_work, a_land.at[level - 2], held_a, sems_a, off_a)
        off_a, held_a = fold(step_a, a_work, a_land.at[level - 2])
    start_a = start_a + off_a
    a_full[rows_at(start_a, held_a), :] = a_work[rows_at(off_a, held_a), :]
    back_a = double(levels - 1, a_full, start_a, held_a, sems_a)
    copy_t.wait_recv()
    at = rows_at(side * half_t, half_t)
    t_work[...] = low(grads[at, :].astype(jnp.float32) + t_land[...].astype(jnp.float32))
    t_copies = []
    for k in range(1, far):
        to = lax.rem(place + k, far)
        t_copies.append(
            send_to(
                remote(t_work.at[rows_at(to * tall, tall), :], t_slots.at[k - 1], tsend.at[k], trecv.at[k], across(k))
            )
        )
    copy_c.wait_recv()
    at = rows_at(side * half_c, half_c)
    c_work[at, :] = low(c_work[at, :].astype(jnp.float32) + c_land[...].astype(jnp.float32))
    piece = half_c // far
    c_copies = []
    for k in range(1, far):
        to = lax.rem(place + k, far)
        c_copies.append(
            send_to(
                remote(
                    c_work.at[rows_at(side * half_c + to * piece, piece), :], c_slots.at[k - 1],
                    csend.at[k], crecv.at[k], across(k),
                )
            )
        )
    off_b, held_b = fold(step_b, b_work, b_land.at[1])
    for level in range(3, levels):
        step_b = halves("b", level, b_work, b_land.at[level - 1], held_b, sems_b, off_b)
        off_b, held_b = fold(step_b, b_work, b_land.at[level - 1])
    start_b = start_b + off_b
    b_full[rows_at(start_b, held_b), :] = b_work[rows_at(off_b, held_b), :]
    back_b = double(levels - 1, b_full, start_b, held_b, sems_b)

    def onward(back, level, full, sems):
        copy, start, size = back
        copy.wait_recv()
        return double(level, full, start, size, sems)

    for level in range(levels - 2, 0, -1):
        back_a = onward(back_a, level, a_full, sems_a)
    total = t_work[rows_at(place * tall, tall), :].astype(jnp.float32)
    for k in range(1, far):
        t_copies[k - 1].wait_recv()
        total = total + t_slots[k - 1].astype(jnp.float32)
    shares[mine] = low(total)
    started = relay_own(mp, lambda k: shares.at[k], ysend, yrecv)
    own = rows_at(side * half_c + place * piece, piece)
    total = c_work[own, :].astype(jnp.float32)
    for k in range(1, far):
        c_copies[k - 1].wait_recv()
        total = total + c_slots[k - 1].astype(jnp.float32)
    c_full[own, :] = low(total)
    c_back = []
    for k in range(1, far):
        c_back.append(
            send_to(
                remote(c_full.at[own, :], c_full.at[own, :], csend.at[far + k], crecv.at[far + k], across(k))
            )
        )
    back_a = onward(back_a, 0, a_full, sems_a)
    for level in range(levels - 2, 0, -1):
        back_b = onward(back_b, level, b_full, sems_b)
    relay_rest(mp, lambda k: shares.at[k], ysend, yrecv, started)
    for copy in c_back:
        copy.wait_recv()
    at = c_full.at[rows_at(side * half_c, half_c), :]
    last_c = send_to(remote(at, at, csend.at[far], crecv.at[far], {"dp": flip(me, 0)}))
    back_b = onward(back_b, 0, b_full, sems_b)
    for copy in small_copies:
        copy.wait_recv()
    value = s_slots[0]
    for d in range(1, dp):
        value = value + s_slots[d]
    small_out[...] = value
    back_a[0].wait_recv()
    last_c.wait_recv()
    back_b[0].wait_recv()
    for copy in pending + small_copies:
        copy.wait_send()


def final_kernel(
    mp, hx, shares, a_full, b_full, c_full, small, logits_in, n_gain_in, n_shift_in, b_gain_in, b_shift_in,
    left_in, right_in, bias_in,
    logits, num_g, table_g, gate_g, gate_bias_g, n_first_g, n_rest_g, n_gain_g, n_shift_g,
    b_first_g, b_rest_g, b_gain_g, b_shift_g, left_g, right_g, pair_g, bias_g,
):
    gcols, s1, s2, h1 = gate_g.shape[0], n_first_g.shape[0], b_first_g.shape[0], n_rest_g.shape[2]
    wide = n_first_g.shape[1]

    def full(work, row, count, col, width):
        return work[row : row + count, col : col + width].astype(jnp.float32)

    blocks = shares.shape[1] // 16
    for m in range(mp):
        for b in range(blocks):
            table_g[:, (m * blocks + b) * HI : (m * blocks + b + 1) * HI] = shares[
                m, b * 16 : (b + 1) * 16, :
            ].astype(jnp.float32)
    gate_g[:, 0, :] = full(c_full, 0, gcols, 0, wide)
    gate_g[:, 1, :] = full(b_full, s2, gcols, 0, wide)
    n_first_g[...] = full(c_full, gcols, s1, 0, wide)
    b_first_g[...] = full(b_full, 0, s2, 0, wide)
    main = a_full.shape[1]
    rest = 2 * h1 - main
    parts = main // rest
    tall_a = s2 + s1
    short = -(-tall_a // parts)
    tail = jnp.concatenate(
        [
            full(a_full, tall_a, min(short, tall_a - p * short), p * rest, rest)
            for p in range(parts)
        ],
        axis=0,
    )
    b_rest_g[:, :main] = full(a_full, 0, s2, 0, main)
    b_rest_g[:, main:] = tail[:s2]
    both = jnp.concatenate([full(a_full, s2, s1, 0, main), tail[s2:]], axis=1)
    n_rest_g[:, 0, :] = both[:, :h1]
    n_rest_g[:, 1, :] = both[:, h1:]
    heads = pair_g.shape[2]
    pairs = b_full[b_full.shape[0] - 16 :, :h1]
    row = lax.broadcasted_iota(jnp.int32, (h1, heads), 0)
    col = lax.broadcasted_iota(jnp.int32, (h1, heads), 1)
    for i in range(hx):
        choose = jnp.where(row == col * hx + i, 1.0, 0.0).astype(jnp.bfloat16)
        pair_g[i] = nn(pairs, choose)
    fields, width = num_g.shape
    gate_bias_g[...] = small[0:2, :gcols]
    spread = jnp.broadcast_to(small[2:3, : fields * width], (fields, fields * width))
    row = lax.broadcasted_iota(jnp.int32, spread.shape, 0)
    col = lax.broadcasted_iota(jnp.int32, spread.shape, 1)
    spread = jnp.where(col // width == row, spread, 0.0)
    total = spread[:, :width]
    for i in range(1, fields):
        total = total + spread[:, i * width : (i + 1) * width]
    num_g[...] = total
    logits[...] = logits_in[...]
    n_gain_g[...] = n_gain_in[...]
    n_shift_g[...] = n_shift_in[...]
    b_gain_g[...] = b_gain_in[...]
    b_shift_g[...] = b_shift_in[...]
    left_g[...] = left_in[...]
    right_g[...] = right_in[...].reshape(right_g.shape)
    bias_g[...] = bias_in[...]


def f32(*shape):
    return jax.ShapeDtypeStruct(shape, jnp.float32)


def b16(*shape):
    return jax.ShapeDtypeStruct(shape, jnp.bfloat16)


def held(*shape):
    return pltpu.VMEM(shape, jnp.float32)


def held16(*shape):
    return pltpu.VMEM(shape, jnp.bfloat16)


def dma(*shape):
    return pltpu.SemaphoreType.DMA(shape)


def shards(
    dense_values,
    field_ids,
    lengths,
    labels,
    num_embed,
    embed_table,
    gate_weight,
    gate_bias,
    narrow_first,
    narrow_rest,
    narrow_gain,
    narrow_shift,
    broad_first,
    broad_rest,
    broad_gain,
    broad_shift,
    joining_left,
    joining_right,
    joining_pair,
    joining_bias,
):
    dp, mp = lax.axis_size("dp"), lax.axis_size("mp")
    chips = mp // 2
    rows = dense_values.shape[0]
    cats, slots = field_ids.shape[:2]
    width, own_rows = embed_table.shape
    num = dense_values.shape[1] * width
    wide = gate_weight.shape[2]
    gcols = gate_weight.shape[1]
    s1, s2 = narrow_first.shape[0], broad_first.shape[0]
    h1, h2 = s1 * mp, s2 * mp
    hx = joining_pair.shape[1]
    bits = (cats * rows - 1).bit_length()
    dense_t = dense_values.T
    tall = own_rows // mp // HI * 16
    vregs = -(-(cats * slots * rows) // (2 * CHUNK)) * (2 * CHUNK) // 1024
    first_args = (
        embed_table, jnp.transpose(gate_weight, (1, 0, 2)), narrow_first, gate_bias,
        narrow_gain, narrow_shift, broad_gain, broad_shift, broad_first,
        field_ids, lengths, dense_t, num_embed, jnp.transpose(narrow_rest, (1, 0, 2)),
    )
    t2, keys, numeric, weights, vec, n_own = pl.pallas_call(
        functools.partial(first_kernel, dp, mp, own_rows, bits),
        out_shape=(
            b16(dp * tall, HI),
            jax.ShapeDtypeStruct((2, vregs * 8, 128), jnp.int32),
            b16(rows, num),
            b16(2 * wide + h1 + h2, wide),
            f32(16, 896),
            b16(2, s1, h1),
        ),
        in_specs=[ANY] * 14,
        out_specs=(VM,) * 6,
        scratch_shapes=[pltpu.VMEM(x.shape, x.dtype) for x in first_args]
        + [
            pltpu.VMEM((vregs * 8, 128), jnp.int32),
            held16(mp, 2, gcols, wide),
            held16(mp, 2, s1 // 2, wide),
            held16(mp, 2, s2 // 2, wide),
            held(mp, 16, 256),
            dma(dp - 1),
            dma(dp - 1),
            dma(2, mp),
            dma(2, mp),
            dma(2, 4 * chips),
            dma(2, 4 * chips),
            dma(14),
        ],
        compiler_params=params(0, 54),
        name="first",
    )(*first_args)
    partial = pl.pallas_call(
        functools.partial(lookup_kernel, cats, rows, bits),
        out_shape=f32(cats * 16, rows),
        in_specs=[VM] * 2,
        out_specs=VM,
        scratch_shapes=[held((cats + WINDOW) * 16, rows)],
        compiler_params=params(None, 16),
        name="lookup",
    )(keys, t2)

    def up(x, n):
        return -(-x // n) * n

    main = wide // 128 * 128 + 128
    short = -(-(s1 + s2) // (main // (h2 - main)))
    a_rows = up(s1 + s2 + short, 16 * dp)
    b_rows = up(s2 + gcols, 16) + 16
    b_rows = up(b_rows, 16 * dp)
    c_rows = up(gcols + s1, 16 * dp)
    levels = dp.bit_length() - 1
    dense_args = (
        broad_rest, joining_left.reshape(1, h1), joining_right,
        jnp.transpose(joining_pair, (1, 2, 0)), joining_bias.reshape(1, 1), labels.reshape(1, rows), dense_t,
    )
    (
        logits, grads_t, feat, fields, grad_gate, gyn1, a_part, b_part, small,
        n_gain_g, n_shift_g, b_gain_g, b_shift_g, left_g, right_g, bias_g,
    ) = pl.pallas_call(
        functools.partial(dense_kernel, dp, mp, hx, float(rows * dp)),
        out_shape=(
            f32(1, rows),
            b16(cats * 16, rows),
            b16(rows, wide),
            b16(2, rows, wide),
            b16(2, rows, wide),
            b16(rows, h1),
            b16(a_rows // 4, main),
            b16(b_rows // 2, main),
            f32(8, 256),
            f32(3, s1),
            f32(3, s1),
            f32(2, s2),
            f32(2, s2),
            f32(1, h1),
            f32(1, h2),
            f32(1, 1),
        ),
        in_specs=[VM] * 5 + [ANY] * 7,
        out_specs=(VM,) * 16,
        scratch_shapes=[
            held(cats * 8, rows),
            held16(chips, cats * 8, rows),
            held16(cats * 16, rows),
            held(2, rows, wide),
            held(rows, wide),
            held16(mp, 2, s1, h1),
            held16(mp, 2, s2 // 2, h2),
            held16(2, h1, h1),
            held16(h2, h2),
            held(3, rows, h1),
            held(3, rows, h1),
            held(2, rows, h2),
            held(2, rows, h2),
            held16(3, rows, h1),
            held16(2, rows, h2),
            held16(2, rows, h1),
            held16(rows, h2),
            held16(h1, h2),
            held16(h1, h2),
            held(h2, h1),
            held(rows, h1),
            held(11, dp, 2, 896),
            held16(s1 + s2, h2 - main),
            dma(2, chips + 1),
            dma(2, chips + 1),
            dma(2, 4 * chips),
            dma(2, 4 * chips),
            dma(11, dp - 1),
            dma(11, dp - 1),
            held16(rows, h2),
            held16(a_rows, main),
            held16(b_rows, main),
            held16(a_rows * 3 // 4, main),
            held16(b_rows // 2, main),
            dma(3),
            dma(3),
            held16(rows, up(max(gcols, s1, s2), 128)),
        ]
        + [pltpu.VMEM(x.shape, x.dtype) for x in dense_args]
        + [dma(7)],
        compiler_params=params(1, 39 + dp // 16),
        name="dense",
    )(partial, numeric, weights, n_own, vec, *dense_args)
    row_sums = pl.pallas_call(
        functools.partial(scatter_kernel, cats, rows, bits),
        out_shape=b16(dp * tall, HI),
        in_specs=[VM] * 2,
        out_specs=VM,
        scratch_shapes=[held(dp * tall, HI), held16((cats + WINDOW) * 16, rows)],
        compiler_params=params(None, 16),
        name="scatter",
    )(keys, grads_t)
    shares, a_full, b_full, c_full, small = pl.pallas_call(
        functools.partial(reduce_kernel, dp, mp),
        out_shape=(
            b16(mp, tall, HI),
            b16(a_rows, main),
            b16(b_rows, main),
            b16(c_rows, main),
            f32(8, 256),
        ),
        in_specs=[VM] * 8,
        out_specs=(VM,) * 5,
        scratch_shapes=[
            held16(dp // 2 * tall, HI),
            held16(dp // 2 * tall, HI),
            held16(dp // 2 - 1, tall, HI),
            held(dp, 8, 256),
            held16(a_rows // 4, main),
            held16(max(levels - 2, 1), a_rows // 8, main),
            held16(b_rows // 2, main),
            held16(max(levels - 1, 1), b_rows // 4, main),
            held16(c_rows, main),
            held16(c_rows // 2, main),
            held16(dp // 2 - 1, c_rows // dp, main),
            held16(rows, up(max(gcols, s1, s2), 128)),
            dma(dp // 2),
            dma(dp // 2),
            dma(mp),
            dma(mp),
            dma(dp - 1),
            dma(dp - 1),
            dma(2 * levels),
            dma(2 * levels),
            dma(2 * levels),
            dma(2 * levels),
            dma(dp),
            dma(dp),
        ],
        compiler_params=params(2, 24),
        name="reduce",
    )(row_sums, feat, fields, grad_gate, gyn1, a_part, b_part, small)
    outs = pl.pallas_call(
        functools.partial(final_kernel, mp, hx),
        out_shape=(
            f32(1, rows),
            f32(*num_embed.shape),
            f32(width, own_rows),
            f32(gcols, 2, wide),
            f32(2, gcols),
            f32(s1, wide),
            f32(s1, 2, h1),
            f32(3, s1),
            f32(3, s1),
            f32(s2, wide),
            f32(s2, h2),
            f32(2, s2),
            f32(2, s2),
            f32(1, h1),
            f32(h2),
            f32(hx, width, joining_pair.shape[0]),
            f32(1, 1),
        ),
        in_specs=[VM] * 13,
        out_specs=(VM,) * 17,
        compiler_params=params(None, 16),
        name="final",
    )(
        shares, a_full, b_full, c_full, small, logits, n_gain_g, n_shift_g, b_gain_g, b_shift_g,
        left_g, right_g, bias_g,
    )
    outs = list(outs)
    outs[0] = outs[0].reshape(rows)
    outs[3] = jnp.transpose(outs[3], (1, 0, 2))
    outs[6] = jnp.transpose(outs[6], (1, 0, 2))
    outs[13] = outs[13].reshape(h1)
    outs[15] = jnp.transpose(outs[15], (2, 0, 1))
    outs[16] = outs[16].reshape(1)
    return tuple(outs)


def solution(mesh):
    placed = (
        P("dp", None),
        P(None, None, "dp"),
        P(None, "dp"),
        P("dp"),
        P(),
        P(None, "dp"),
        P(None, "mp", None),
        P(None, "mp"),
        P("mp", None),
        P(None, "mp", None),
        P(None, "mp"),
        P(None, "mp"),
        P("mp", None),
        P("mp", None),
        P(None, "mp"),
        P(None, "mp"),
        P(),
        P(),
        P(),
        P(),
    )
    return jax.shard_map(
        shards,
        mesh=mesh,
        in_specs=placed,
        out_specs=(
            P("dp"),
            P(),
            P(None, "dp"),
            P(None, "mp", None),
            P(None, "mp"),
            P("mp", None),
            P(None, "mp", None),
            P(None, "mp"),
            P(None, "mp"),
            P("mp", None),
            P("mp", None),
            P(None, "mp"),
            P(None, "mp"),
            P(),
            P(),
            P(),
            P(),
        ),
        check_vma=False,
    )
```

```python
import functools
import jax
import jax.numpy as jnp
from jax import lax
from jax.experimental import pallas as pl
from jax.experimental.pallas import tpu as pltpu
from jax.sharding import PartitionSpec as P

MESH = pl.DeviceIdType.MESH
VM = pl.BlockSpec(memory_space=pltpu.VMEM)
ANY = pl.BlockSpec(memory_space=pltpu.HBM)
HI = 256
CHUNK = 1024


def params(cid, mib=48):
    if cid is None:
        return pltpu.CompilerParams(vmem_limit_bytes=mib << 20)
    return pltpu.CompilerParams(
        collective_id=cid, has_side_effects=True, vmem_limit_bytes=mib << 20
    )


def hail(dp, mp):
    me, mine = lax.axis_index("dp"), lax.axis_index("mp")
    barrier = pltpu.get_barrier_semaphore()
    for step in range(1, dp):
        pl.semaphore_signal(
            barrier, inc=1, device_id={"dp": lax.rem(me + step, dp)}, device_id_type=MESH
        )
    for step in range(1, mp):
        pl.semaphore_signal(
            barrier, inc=1, device_id={"mp": lax.rem(mine + step, mp)}, device_id_type=MESH
        )


def all_in(dp, mp):
    pl.semaphore_wait(pltpu.get_barrier_semaphore(), dp - 1 + mp - 1)


def remote(src, dst, send, recv, where):
    return pltpu.make_async_remote_copy(
        src_ref=src, dst_ref=dst, send_sem=send, recv_sem=recv,
        device_id=where, device_id_type=MESH,
    )


def spread_dp(dp, pick, send, recv):
    me = lax.axis_index("dp")
    out = []
    for step in range(1, dp):
        to = lax.rem(me + step, dp)
        copy = remote(pick(me), pick(me), send.at[step - 1], recv.at[step - 1], {"dp": to})
        copy.start()
        out.append(copy)
    return out


def over(x, n):
    if n & (n - 1) == 0:
        return lax.shift_right_logical(x, n.bit_length() - 1)
    return x // n


def compact_keys(key):
    count = key.shape[0]
    rows = count * 8
    dead = jnp.where(key.reshape(rows, 128) < 0, 1.0, 0.0).astype(jnp.bfloat16)
    row = lax.broadcasted_iota(jnp.int32, (128, 128), 0)
    col = lax.broadcasted_iota(jnp.int32, (128, 128), 1)
    in_row = jnp.dot(dead, jnp.where(row < col, 1.0, 0.0).astype(jnp.bfloat16), preferred_element_type=jnp.float32)
    row_sum = jnp.dot(dead, jnp.ones((128, 128), jnp.bfloat16), preferred_element_type=jnp.float32)
    row = lax.broadcasted_iota(jnp.int32, (rows, rows), 0)
    col = lax.broadcasted_iota(jnp.int32, (rows, rows), 1)
    above = jnp.where(col < row, 1.0, 0.0).astype(jnp.bfloat16)
    before = jnp.dot(above, row_sum.astype(jnp.bfloat16), preferred_element_type=jnp.float32)
    shift = (in_row + before).astype(jnp.int32).reshape(count, 8, 128)
    shift = jnp.where(key < 0, 0, shift)
    sub = lax.broadcasted_iota(jnp.int32, (8, 128), 0)
    lane = lax.broadcasted_iota(jnp.int32, (8, 128), 1)

    def rows_up(x, j):
        t = [pltpu.roll(x[v], 8 - j, 0) for v in range(count)]
        return jnp.stack([jnp.where(sub < 8 - j, t[v], t[(v + 1) % count]) for v in range(count)])

    bit = 0
    for j in (1, 2, 4, 8, 16, 32, 64):
        def lanes_up(x):
            y = jnp.stack([pltpu.roll(x[v], 128 - j, 1) for v in range(count)])
            return jnp.where(lane[None] < 128 - j, y, rows_up(y, 1))
        key, shift = settle(key, shift, lanes_up(key), lanes_up(shift), bit)
        bit += 1
    for j in (1, 2, 4):
        key, shift = settle(key, shift, rows_up(key, j), rows_up(shift, j), bit)
        bit += 1
    step = 1
    while step < count:
        moved_key = jnp.concatenate([key[step:], key[:step]], axis=0)
        moved_shift = jnp.concatenate([shift[step:], shift[:step]], axis=0)
        key, shift = settle(key, shift, moved_key, moved_shift, bit)
        bit, step = bit + 1, step * 2
    return key


def settle(key, shift, moved_key, moved_shift, bit):
    take = (moved_shift & (1 << bit)) != 0
    stay = (shift & (1 << bit)) == 0
    key = jnp.where(take, moved_key, jnp.where(stay, key, -1))
    shift = jnp.where(take, moved_shift, jnp.where(stay, shift, 0))
    return key, shift


def seat(i, dp):
    return i % 2 * (dp // 2) + i // 2


def make_keys(ids, lens, scratch, own_rows, dp, mp, bits):
    cats, slots, rows = ids.shape
    part = own_rows // mp
    mine = lax.axis_index("mp")
    scratch[...] = jnp.full_like(scratch, -1)
    slot = lax.broadcasted_iota(jnp.int32, (slots, rows), 0)
    event = lax.broadcasted_iota(jnp.int32, (slots, rows), 1)

    def body(c, carry):
        values = ids[c]
        holder = values // own_rows
        inner = values - holder * own_rows
        owner = inner // part
        place = seat(holder, dp) * part + inner - owner * part
        live = (slot < lens[pl.ds(c, 1), :]) & (owner == mine)
        key = jnp.where(live, place * (1 << bits) + c * rows + event, -1)
        for q in range(rows // 128):
            scratch[pl.ds((c * (rows // 128) + q) * slots, slots), :] = key[:, q * 128 : (q + 1) * 128]
        return carry

    lax.fori_loop(0, cats, body, 0)


WINDOW = 16


def chunk_parts(key, rows, bits):
    place = lax.shift_right_arithmetic(key, bits)
    bag = key & ((1 << bits) - 1)
    cat = over(bag, rows)
    return place, cat, bag - cat * rows


def short(row):
    return jnp.broadcast_to(row, (16, row.shape[1])).astype(jnp.int16)


def one_hot(row, size):
    apart = short(row) - lax.broadcasted_iota(jnp.int32, (16, row.shape[1]), 0).astype(jnp.int16)
    one = jnp.ones(apart.shape, jnp.bfloat16)
    zero = jnp.zeros(apart.shape, jnp.bfloat16)
    return jnp.concatenate([jnp.where(apart == i, one, zero) for i in range(0, size, 16)], axis=0)


def spread_rows(row, values, first, size):
    zero = jnp.zeros_like(values)
    apart = short(row - first)
    return jnp.concatenate([jnp.where(apart == i, values, zero) for i in range(size)], axis=0)


def chunk_key(keys, half, k):
    tall = CHUNK // 128
    key = keys[half, pl.ds(pl.multiple_of(k * tall, tall), tall), :]
    return jnp.concatenate([key[i : i + 1, :] for i in range(tall)], axis=1)


def chunk_span(keys, half, k, cats, rows, bits):
    tall = CHUNK // 128
    most = keys.shape[1] // tall - 1
    key = keys[half, pl.ds(pl.multiple_of(jnp.minimum(k, most) * tall, tall), tall), :]
    cat = over(key & ((1 << bits) - 1), rows)
    first = jnp.min(jnp.where(key >= 0, cat, cats - 1))
    last = jnp.max(jnp.where(key >= 0, cat, 0))
    return first, (last - first) // WINDOW + 1


def each_chunk(keys, half, cats, rows, bits, body):
    live = jnp.sum((keys[half] >= 0).astype(jnp.int32))
    chunks = (live + CHUNK - 1) // CHUNK

    def step(k, carry):
        later = chunk_span(keys, half, k + 1, cats, rows, bits)
        body(chunk_key(keys, half, k), *carry)
        return later

    lax.fori_loop(0, chunks, step, chunk_span(keys, half, 0, cats, rows, bits))


def lookup_kernel(cats, rows, bits, keys, t2, pooled, total):
    lows = t2.shape[0] // 32
    total[...] = jnp.zeros_like(total)

    def half_table(half, carry):
        def body(key, first, windows):
            place, cat, event = chunk_parts(key, rows, bits)
            low = jnp.broadcast_to(lax.shift_right_arithmetic(place, 8) - half * lows, (16, CHUNK))
            pick = one_hot(place & (HI - 1), HI)
            z = jnp.zeros((16, CHUNK), jnp.float32)
            for b in range(0, lows, 32):
                n = min(32, lows - b)
                at = pl.ds(pl.multiple_of((half * lows + b) * 16, 16), n * 16)
                y = jnp.dot(t2[at, :], pick, preferred_element_type=jnp.float32)
                for j in range(n):
                    z = z + jnp.where(low == b + j, y[j * 16 : (j + 1) * 16], 0.0)
            z = z.astype(jnp.bfloat16)
            cat = jnp.where(key >= 0, cat, -1)
            place_of = one_hot(event, rows)

            def window(w):
                start = first + w * WINDOW
                at = pl.ds(pl.multiple_of(start * 16, 16), WINDOW * 16)
                total[at, :] += lax.dot_general(
                    spread_rows(cat, z, start, WINDOW), place_of, (((1,), (1,)), ((), ())),
                    preferred_element_type=jnp.float32,
                )

            window(0)

            def more(w, carry):
                window(w)
                return carry

            lax.fori_loop(1, windows, more, 0)

        each_chunk(keys, half, cats, rows, bits, body)
        return carry

    lax.fori_loop(0, 2, half_table, 0)
    pooled[...] = total[: cats * 16, :].astype(pooled.dtype)


def scatter_kernel(cats, rows, bits, keys, grad, out, total, grad_pad):
    lows = total.shape[0] // 32
    total[...] = jnp.zeros_like(total)
    grad_pad[: cats * 16, :] = grad[...]
    grad_pad[cats * 16 :, :] = jnp.zeros((WINDOW * 16, rows), jnp.bfloat16)

    def half_table(half, carry):
        def body(key, first, windows):
            place, cat, event = chunk_parts(key, rows, bits)
            low = lax.shift_right_arithmetic(place, 8) - half * lows
            pick = one_hot(place & (HI - 1), HI)
            place_of = one_hot(event, rows)
            cat = jnp.broadcast_to(jnp.where(key >= 0, cat, -1), (16, CHUNK))

            def window(w, g):
                start = first + w * WINDOW
                at = pl.ds(pl.multiple_of(start * 16, 16), WINDOW * 16)
                wide = jnp.dot(grad_pad[at, :], place_of, preferred_element_type=jnp.float32)
                for c in range(WINDOW):
                    g = g + jnp.where(cat == start + c, wide[c * 16 : (c + 1) * 16], 0.0)
                return g

            g = window(0, jnp.zeros((16, CHUNK), jnp.float32))
            g = lax.fori_loop(1, windows, window, g).astype(jnp.bfloat16)
            for b in range(0, lows, 32):
                n = min(32, lows - b)
                at = pl.ds(pl.multiple_of((half * lows + b) * 16, 16), n * 16)
                total[at, :] += lax.dot_general(
                    spread_rows(low, g, b, n), pick, (((1,), (1,)), ((), ())),
                    preferred_element_type=jnp.float32,
                )

        each_chunk(keys, half, cats, rows, bits, body)
        return carry

    lax.fori_loop(0, 2, half_table, 0)
    out[...] = total[...].astype(out.dtype)


def relay_own(mp, slot, send, recv):
    mine = lax.axis_index("mp")
    core = lax.rem(mine, 2)
    other = mine + 1 - 2 * core
    chips = mp // 2
    out = []
    for k in range(1, chips):
        to = lax.rem(mine + 2 * k, mp)
        copy = remote(slot(mine), slot(mine), send.at[2 * k], recv.at[2 * k], {"mp": to})
        copy.start()
        out.append(copy)
    copy = remote(slot(mine), slot(mine), send.at[1], recv.at[1], {"mp": other})
    copy.start()
    out.append(copy)
    return out


def relay_rest(mp, slot, send, recv, started):
    mine = lax.axis_index("mp")
    core = lax.rem(mine, 2)
    other = mine + 1 - 2 * core
    chips = mp // 2
    passed = []
    for k in range(1, chips):
        source = lax.rem(mine + mp - 2 * k, mp)
        remote(slot(source), slot(source), send.at[2 * k], recv.at[2 * k], {"mp": other}).wait_recv()
        copy = remote(slot(source), slot(source), send.at[2 * k + 1], recv.at[2 * k + 1], {"mp": other})
        copy.start()
        passed.append(copy)
    remote(slot(other), slot(other), send.at[1], recv.at[1], {"mp": other}).wait_recv()
    for k in range(1, chips):
        far = lax.rem(other + mp - 2 * k, mp)
        remote(slot(far), slot(far), send.at[2 * k + 1], recv.at[2 * k + 1], {"mp": other}).wait_recv()
    for copy in started + passed:
        copy.wait_send()


def nn(a, b):
    return jnp.dot(a, b, preferred_element_type=jnp.float32)


def nt(a, b):
    return lax.dot_general(a, b, (((1,), (1,)), ((), ())), preferred_element_type=jnp.float32)


def tn(a, b):
    return lax.dot_general(a, b, (((0,), (0,)), ((), ())), preferred_element_type=jnp.float32)


def sigmoid(x):
    return 0.5 * jnp.tanh(0.5 * x) + 0.5


def low(x):
    return x.astype(jnp.bfloat16)


def column_sum(x):
    return jnp.sum(x, axis=0, keepdims=True)


def widen_dense(dense_t, width):
    fields = dense_t.shape[0]
    row = lax.broadcasted_iota(jnp.int32, (fields, fields * width), 0)
    col = lax.broadcasted_iota(jnp.int32, (fields, fields * width), 1)
    ones = jnp.where(col // width == row, 1.0, 0.0)
    return lax.dot_general(
        dense_t, ones, (((0,), (0,)), ((), ())),
        precision=lax.Precision.HIGHEST, preferred_element_type=jnp.float32,
    )


def split_relay(dp, mp, ref, send, recv, fetched=False):
    me, mine = lax.axis_index("dp"), lax.axis_index("mp")
    other = mine + 1 - 2 * lax.rem(mine, 2)
    chips = mp // 2
    near = lax.rem(me, 2)
    beside = {"dp": me + 1 - 2 * near}
    started = []

    def move(place, i, where):
        return remote(place, place, send.at[i], recv.at[i], where)

    def go(place, i, where):
        copy = move(place, i, where)
        copy.start()
        started.append(copy)

    def source(k):
        return lax.rem(mine + mp - 2 * k, mp)

    def begin():
        if not fetched:
            fetch()
        go(ref.at[mine], 0, {"mp": other})

    def fetch():
        for k in range(1, chips):
            go(ref.at[mine, near], k, {"mp": lax.rem(mine + 2 * k, mp)})

    def arrive():
        for k in range(1, chips):
            move(ref.at[source(k), near], k, beside).wait_recv()
        for copy in started:
            copy.wait_send()

    def middle():
        for k in range(1, chips):
            place = ref.at[source(k), near]
            if not fetched:
                move(place, k, beside).wait_recv()
            go(place, 2 * chips + k, beside)
            go(place, chips + k, {"mp": other})

    def later():
        for k in range(1, chips):
            place = ref.at[source(k), 1 - near]
            move(place, 2 * chips + k, beside).wait_recv()
            go(place, 3 * chips + k, {"mp": other})

    def end():
        move(ref.at[other], 0, beside).wait_recv()
        for k in range(1, chips):
            far = lax.rem(other + mp - 2 * k, mp)
            move(ref.at[far, near], chips + k, beside).wait_recv()
            move(ref.at[far, 1 - near], 3 * chips + k, beside).wait_recv()
        for copy in started:
            copy.wait_send()

    return begin, middle, later, end, fetch, arrive


def bring(sources, places, sem):
    copies = []
    for i, (source, place) in enumerate(zip(sources, places)):
        copy = pltpu.make_async_copy(source, place, sem.at[i])
        copy.start()
        copies.append(copy)
    return copies


def first_kernel(dp, mp, own_rows, bits, *refs):
    count = 15
    sources, refs = refs[:count], refs[count:]
    t2, keys, numeric, weights, vec, n_next, b_next = refs[:7]
    places, refs = refs[7 : 7 + count], refs[7 + count :]
    (
        scratch, gate_slots, g_slots, n_slots, b_slots, v_slots,
        send, recv, send2, recv2, send3, recv3, send4, recv4, sem,
    ) = refs
    brought = bring(sources, places, sem)
    (
        table, gate_w, n_first, gate_b, n_gain, n_shift, b_gain, b_shift, b_first,
        ids, lens, dense_t, num_embed, n_rest, b_rest,
    ) = places
    part = own_rows // mp
    blocks = part // HI
    tall = blocks * 16
    me, mine = lax.axis_index("dp"), lax.axis_index("mp")
    hail(dp, mp)
    for copy in brought[:9]:
        copy.wait()
    own = table[:, pl.ds(pl.multiple_of(mine * part, HI), part)].astype(jnp.bfloat16)
    for b in range(blocks):
        t2[pl.ds(pl.multiple_of(seat(me, dp) * tall + b * 16, 16), 16), :] = own[:, b * HI : (b + 1) * HI]
    gate_slots[mine] = gate_w[:, 0, :]
    second = gate_w[:, 1, :]
    cols = g_slots.shape[2]
    for k in range(2):
        g_slots[mine, k] = second[k * cols : (k + 1) * cols, :]
    small, large = n_slots.shape[2], b_slots.shape[2]
    for k in range(2):
        n_slots[mine, k] = n_first[k * small : (k + 1) * small, :]
        b_slots[mine, k] = b_first[k * large : (k + 1) * large, :]
    row = 0
    for ref in (gate_b, n_gain, n_shift, b_gain, b_shift):
        v_slots[mine, row : row + ref.shape[0], : ref.shape[1]] = ref[...]
        row += ref.shape[0]
    all_in(dp, mp)

    def slot(i):
        return t2.at[pl.ds(pl.multiple_of(seat(i, dp) * tall, 16), tall), :]

    pairs = [
        split_relay(dp, mp, ref, send3.at[i], recv3.at[i]) for i, ref in enumerate((g_slots, n_slots, b_slots))
    ]
    for steps in pairs:
        steps[0]()
    groups = []
    for i, ref in enumerate((gate_slots, v_slots)):
        started = relay_own(mp, lambda k, ref=ref: ref.at[k], send2.at[i], recv2.at[i])
        groups.append((ref, i, started))
    copies = spread_dp(dp, slot, send, recv)
    for copy in brought[9:]:
        copy.wait()
    half_b = b_next.shape[2]
    for k in range(2):
        n_next[mine, k] = n_rest[:, k, :]
        b_next[mine, k] = b_rest[k * half_b : (k + 1) * half_b, :]
    fields, width = num_embed.shape
    tiled = jnp.concatenate([num_embed[...]] * fields, axis=1)
    row = lax.broadcasted_iota(jnp.int32, tiled.shape, 0)
    col = lax.broadcasted_iota(jnp.int32, tiled.shape, 1)
    num_row = column_sum(jnp.where(col // width == row, tiled, 0.0))
    numeric[...] = low(widen_dense(dense_t[...], width) * num_row)
    make_keys(ids, lens, scratch, own_rows, dp, mp, bits)
    count = scratch.shape[0] // 8
    middle = (dp * part // 2) << bits

    def pack(half, carry):
        key = scratch[...]
        key = jnp.where((key < middle) == (half == 0), key, -1)
        keys[half] = compact_keys(key.reshape(count, 8, 128)).reshape(count * 8, 128)
        return carry

    lax.fori_loop(0, 2, pack, 0)
    for steps in pairs:
        steps[1]()
    nexts = [
        split_relay(dp, mp, ref, send4.at[i], recv4.at[i]) for i, ref in enumerate((n_next, b_next))
    ]
    for steps in nexts:
        steps[4]()
    for ref, i, started in groups:
        relay_rest(mp, lambda k, ref=ref: ref.at[k], send2.at[i], recv2.at[i], started)
    cols, wide = gate_slots.shape[1:]
    for m in range(mp):
        weights[m * cols : (m + 1) * cols, :] = gate_slots[m]
    for steps in pairs:
        steps[2]()
    row = wide
    for ref, steps in zip((g_slots, n_slots, b_slots), pairs):
        steps[3]()
        tall = ref.shape[2]
        for m in range(mp):
            for k in range(2):
                weights[row : row + tall, :] = ref[m, k]
                row += tall
    row = 0
    for ref in (gate_b, n_gain, n_shift, b_gain, b_shift):
        r, w = ref.shape
        vec[row : row + r, : mp * w] = jnp.concatenate(
            [v_slots[m, row : row + r, :w] for m in range(mp)], axis=1
        )
        row += r
    for steps in nexts:
        steps[5]()
    for copy in copies:
        copy.wait()


def own_columns(x, mine, width, mp):
    out = jnp.zeros((x.shape[0], width), x.dtype)
    for m in range(mp):
        out = jnp.where(mine == m, x[:, m * width : (m + 1) * width], out)
    return out


def up16(x):
    return -(-x // 16) * 16


def weight_grad(grad_y, inputs, own, mine, width, mp):
    for m in range(mp):

        @pl.when(mine == m)
        def _():
            own[:, :width] = grad_y[:, m * width : (m + 1) * width]

    return low(tn(own[:, :width], inputs))


def flip(me, level):
    bit = 1 << level
    return me + bit - 2 * bit * lax.rem(me // bit, 2)


def upper(me, level):
    return lax.rem(me // (1 << level), 2)


def give_half(me, level, start, size, work, land, send, recv):
    half = size // 2
    mine = upper(me, level)
    at = pl.ds(pl.multiple_of(start + (1 - mine) * half, 16), half)
    copy = remote(work.at[at, :], land, send, recv, {"dp": flip(me, level)})
    copy.start()
    return copy, start + mine * half


def add_half(copy, start, half, work, land):
    copy.wait_recv()
    at = pl.ds(pl.multiple_of(start, 16), half)
    return low(work[at, :].astype(jnp.float32) + land[...].astype(jnp.float32))


def dense_kernel(
    dp, mp, hx, batch,
    partial, numeric, weights, n_next, b_next, vec,
    left_hbm, right_hbm, pair_hbm, bias_hbm, labels_hbm, dense_hbm,
    logits, grads_t, feat, fields, grad_gate, gyn1, a_out, b_out, small,
    n_gain_g, n_shift_g, b_gain_g, b_shift_g, left_g, right_g, bias_g,
    half_a, half_c, pooled, gate, own_term, n_slots, b_slots, n23, b2,
    yn, dn, yb, db, un, ub, gyn, gyb, pair_hi, pair_lo, pair_g, to_first, sums, spill,
    fsend, frecv, wsend, wrecv, ssend, srecv,
    gyb1, a_work, b_work, a_land, b_land, hsend, hrecv, own_cols,
    left, right, pair_t, bias, labels, dense_t, sem,
):
    brought = bring(
        (left_hbm, right_hbm, pair_hbm, bias_hbm, labels_hbm, dense_hbm),
        (left, right, pair_t, bias, labels, dense_t),
        sem,
    )
    me, mine = lax.axis_index("dp"), lax.axis_index("mp")
    core = lax.rem(mine, 2)
    chip = mine // 2
    chips = mp // 2
    other = mine + 1 - 2 * core
    rows = feat.shape[0]
    block = 256
    steps = rows // block
    h1, h2 = n23.shape[1], b2.shape[0]
    s1, s2 = h1 // mp, h2 // mp
    wide = feat.shape[1]
    gates = (weights.at[pl.ds(0, wide), :], weights.at[pl.ds(wide, wide), :])
    n1 = weights.at[pl.ds(2 * wide, h1), :]
    b1 = weights.at[pl.ds(2 * wide + h1, h2), :]
    num = numeric.shape[1]
    gcols = wide // mp
    half = partial.shape[0] // 2
    hail(dp, mp)
    near = lax.rem(me, 2)
    for slots, given in ((n_slots, n_next), (b_slots, b_next)):
        slots[mine] = given[mine]
        for k in range(1, chips):
            source = lax.rem(mine + 2 * k, mp)
            slots[source, near] = given[source, near]
    all_in(dp, mp)

    def rowset(i):
        return pl.ds(pl.multiple_of(i * block, block), block)

    def part(c):
        return pl.ds(pl.multiple_of(c * half, 16), half)

    def events(h):
        return pl.ds(h * (rows // 2), rows // 2)

    copies_a, copies_y, copies_b = [], [], []
    for h in range(2):
        copy = remote(
            partial.at[part(1 - core), events(h)], half_a.at[:, events(h)], fsend.at[h, 0], frecv.at[h, 0],
            {"mp": other},
        )
        copy.start()
        copies_a.append(copy)
    for copy in brought:
        copy.wait()
    for h in range(2):
        copies_a[h].wait_recv()
        half_c[chip, :, events(h)] = low(partial[part(core), events(h)] + half_a[:, events(h)])
        for k in range(1, chips):
            place = half_c.at[chip, :, events(h)]
            copy = remote(
                place, place, fsend.at[h, k], frecv.at[h, k], {"mp": lax.rem(mine + 2 * k, mp)}
            )
            copy.start()
            copies_y.append(copy)
    n_steps = split_relay(dp, mp, n_slots, wsend.at[0], wrecv.at[0], True)
    b_steps = split_relay(dp, mp, b_slots, wsend.at[1], wrecv.at[1], True)
    for relay in (n_steps, b_steps):
        relay[0]()
        relay[1]()
    heads = pair_t.shape[2]
    by_head = jnp.transpose(pair_t[...].reshape(hx * 16, heads))
    row = lax.broadcasted_iota(jnp.int32, (h1, heads), 0)
    col = lax.broadcasted_iota(jnp.int32, (h1, heads), 1)
    repeat = jnp.where(row // hx == col, 1.0, 0.0)
    tall = jnp.dot(repeat, by_head, precision=lax.Precision.HIGHEST, preferred_element_type=jnp.float32)
    row = lax.broadcasted_iota(jnp.int32, (h1, 16), 0)
    pick = jnp.zeros((h1, 16), jnp.float32)
    for i in range(hx):
        pick = jnp.where(row % hx == i, tall[:, i * 16 : (i + 1) * 16], pick)
    for i in range(0, h1, 80):
        row = lax.broadcasted_iota(jnp.int32, (80, h2), 0) + i
        col = lax.broadcasted_iota(jnp.int32, (80, h2), 1)
        pieces = jnp.concatenate([pick[i : i + 80, :]] * heads, axis=1)
        spread = jnp.where(row // hx == col // 16, pieces, 0.0)
        high = low(spread)
        pair_hi[i : i + 80, :] = high
        pair_lo[i : i + 80, :] = low(spread - high.astype(jnp.float32))
    for h in range(2):
        for copy in copies_y[h * (chips - 1) : (h + 1) * (chips - 1)]:
            copy.wait_recv()
        total = half_c[0, :, events(h)].astype(jnp.float32)
        for k in range(1, chips):
            total = total + half_c[k, :, events(h)].astype(jnp.float32)
        pooled[part(core), events(h)] = low(total)
        place = pooled.at[part(core), events(h)]
        copy = remote(place, place, fsend.at[h, chips], frecv.at[h, chips], {"mp": other})
        copy.start()
        copies_b.append(copy)
    feat[:, :num] = numeric[...]
    started = []

    def push(slot, *values):
        width = -(-values[0].shape[1] // 128) * 128
        for r, value in enumerate(values):
            sums[slot, me, r : r + 1, : value.shape[1]] = value
        out = []
        for step in range(1, dp):
            at = sums.at[slot, me, :, pl.ds(0, width)]
            copy = remote(
                at, at, ssend.at[slot, step - 1], srecv.at[slot, step - 1], {"dp": lax.rem(me + step, dp)}
            )
            copy.start()
            out.append(copy)
        started.append(out)
        return slot, width, out

    def pull(sent):
        slot, width, out = sent
        for copy in out:
            copy.wait_recv()
        total = sums[slot, 0, :, :width]
        for d in range(1, dp):
            total = total + sums[slot, d, :, :width]
        return total

    def norm(sent, width):
        total = pull(sent)
        mean = total[0:1, :width] / batch
        var = total[1:2, :width] / batch - mean * mean
        return mean, lax.rsqrt(var + 1e-05)

    def activate(y_ref, d_ref, u_ref, layer, at, mean, rstd, gain, shift):
        normed = (y_ref[layer, at, :] - mean) * rstd
        z = gain * normed + shift
        s = sigmoid(z)
        u = z * s
        y_ref[layer, at, :] = normed
        d_ref[layer, at, :] = s + u * (1.0 - s)
        u = low(u)
        u_ref[layer, at, :] = u
        return u

    def gain_n(layer):
        return vec[2 + layer : 3 + layer, :h1], vec[5 + layer : 6 + layer, :h1]

    def gain_b(layer):
        return vec[8 + layer : 9 + layer, :h2], vec[10 + layer : 11 + layer, :h2]

    zero1 = jnp.zeros((1, h1), jnp.float32)
    zero2 = jnp.zeros((1, h2), jnp.float32)

    def loop(body, *start):
        return lax.fori_loop(0, steps, lambda i, carry: body(rowset(i), *carry), tuple(start))

    def gates_and_first(at, a, b):
        x = feat[at, :]
        wide_x = x.astype(jnp.float32)
        for k in range(2):
            value = 2.0 * sigmoid(nt(x, gates[k][...]) + vec[k : k + 1, :wide])
            gate[k, at, :] = value
            fields[k, at, :] = low(wide_x * value)
        y = nt(fields[0, at, :], n1[...])
        yn[0, at, :] = y
        return a + column_sum(y), b + column_sum(y * y)

    a, b = zero1, zero1
    for h in range(2):
        copies_b[h].wait_recv()
        at = events(h)
        feat[at, num:] = low(jnp.transpose(pooled[:, at].astype(jnp.float32)))
        a, b = gates_and_first(at, a, b)
    sent_n = push(0, a, b)

    def broad_first(at, a, b):
        y = nt(fields[1, at, :], b1[...])
        yb[0, at, :] = y
        return a + column_sum(y), b + column_sum(y * y)

    sent_b = push(1, *loop(broad_first, zero2, zero2))
    n_steps[2]()
    b_steps[2]()
    n_steps[3]()
    for m in range(mp):
        for k in range(2):
            n23[k, m * s1 : (m + 1) * s1, :] = n_slots[m, k]
    mean_n1, rstd_n1 = norm(sent_n, h1)

    def narrow_second(at, a, b):
        y = nt(activate(yn, dn, un, 0, at, mean_n1, rstd_n1, *gain_n(0)), n23[0])
        yn[1, at, :] = y
        return a + column_sum(y), b + column_sum(y * y)

    sent_n = push(2, *loop(narrow_second, zero1, zero1))
    b_steps[3]()
    for m in range(mp):
        for k in range(2):
            row = (2 * m + k) * (s2 // 2)
            b2[row : row + s2 // 2, :] = b_slots[m, k]
    mean_b1, rstd_b1 = norm(sent_b, h2)

    def broad_second(at, a, b):
        y = nt(activate(yb, db, ub, 0, at, mean_b1, rstd_b1, *gain_b(0)), b2[...])
        yb[1, at, :] = y
        return a + column_sum(y), b + column_sum(y * y)

    sent_b = push(3, *loop(broad_second, zero2, zero2))
    mean_n2, rstd_n2 = norm(sent_n, h1)

    def narrow_third(at, a, b):
        y = nt(activate(yn, dn, un, 1, at, mean_n2, rstd_n2, *gain_n(1)), n23[1])
        yn[2, at, :] = y
        return a + column_sum(y), b + column_sum(y * y)

    sent_n = push(4, *loop(narrow_third, zero1, zero1))
    label = jnp.transpose(jnp.broadcast_to(labels[...].astype(jnp.float32), (8, rows)))[:, 0:1]
    own_term[:, 0:1] = label
    pair_g[...] = jnp.zeros_like(pair_g)
    mean_b2, rstd_b2 = norm(sent_b, h2)

    def broad_out(at):
        second = activate(yb, db, ub, 1, at, mean_b2, rstd_b2, *gain_b(1))
        to_first[at, :] = left[...] + (nt(second, pair_hi[...]) + nt(second, pair_lo[...]))
        return ()

    loop(broad_out)
    mean_n3, rstd_n3 = norm(sent_n, h1)
    to_right = right[...].reshape(1, h2)

    def join_narrow(at, l_sum, g_sum, a, b):
        first = activate(yn, dn, un, 2, at, mean_n3, rstd_n3, *gain_n(2)).astype(jnp.float32)
        second = ub[1, at, :].astype(jnp.float32)
        logit = (
            jnp.sum(first * to_first[at, :], axis=1, keepdims=True)
            + jnp.sum(second * to_right, axis=1, keepdims=True)
            + bias[...]
        )
        g = sigmoid(logit) - own_term[at, 0:1]
        own_term[at, 1:2] = logit
        own_term[at, 2:3] = g
        gz = g * to_first[at, :] * dn[2, at, :]
        dn[2, at, :] = gz
        return (
            l_sum + column_sum(g * first), g_sum + column_sum(g),
            a + column_sum(gz), b + column_sum(gz * yn[2, at, :]),
        )

    l_sum, g_sum, a, b = loop(join_narrow, zero1, jnp.zeros((1, 1), jnp.float32), zero1, zero1)
    sent_n = push(5, a, b)

    def join_broad(at, r_sum, a, b):
        first = un[2, at, :]
        second = ub[1, at, :]
        g = own_term[at, 2:3]
        turned = nn(first, pair_hi[...]) + nn(first, pair_lo[...])
        pair_g[...] += tn(second, low(g * first.astype(jnp.float32)))
        gz = g * (to_right + turned) * db[1, at, :]
        db[1, at, :] = gz
        return (
            r_sum + column_sum(g * second.astype(jnp.float32)),
            a + column_sum(gz), b + column_sum(gz * yb[1, at, :]),
        )

    r_sum, a, b = loop(join_broad, zero2, zero2, zero2)
    sent_b = push(6, a, b)
    sums[10, me, 1:2, 512:513] = g_sum
    sent_join = push(10, r_sum, l_sum)
    logits[...] = jnp.transpose(own_term[:, 0:128])[1:2, :]

    def grad_y(gz, normed, rstd, gain, total):
        return low(gain * rstd * (gz - total[0:1] / batch - normed * (total[1:2] / batch)))

    t_n3 = pull(sent_n)[:, :h1]

    def back_n3(at, a, b):
        g = grad_y(dn[2, at, :], yn[2, at, :], rstd_n3, gain_n(2)[0], t_n3)
        gyn[1, at, :] = g
        gz = nn(g, n23[1]) * dn[1, at, :]
        dn[1, at, :] = gz
        return a + column_sum(gz), b + column_sum(gz * yn[1, at, :])

    sent_n = push(7, *loop(back_n3, zero1, zero1))
    main = a_work.shape[1]
    rest = h2 - main
    parts = main // rest
    tall_a = s2 + s1
    short = -(-tall_a // parts)
    a_work[...] = jnp.zeros_like(a_work)
    b_work[...] = jnp.zeros_like(b_work)
    grad_n3 = weight_grad(gyn.at[1], un[1], own_cols, mine, s1, mp)
    t_b2 = pull(sent_b)[:, :h2]

    def back_b2(at, a, b):
        g = grad_y(db[1, at, :], yb[1, at, :], rstd_b2, gain_b(1)[0], t_b2)
        gyb[at, :] = g
        gz = nn(g, b2[...]) * db[0, at, :]
        db[0, at, :] = gz
        return a + column_sum(gz), b + column_sum(gz * yb[0, at, :])

    sent_b = push(8, *loop(back_b2, zero2, zero2))
    t_n2 = pull(sent_n)[:, :h1]

    def back_n2(at, a, b):
        g = grad_y(dn[1, at, :], yn[1, at, :], rstd_n2, gain_n(1)[0], t_n2)
        gyn[0, at, :] = g
        gz = nn(g, n23[0]) * dn[0, at, :]
        dn[0, at, :] = gz
        return a + column_sum(gz), b + column_sum(gz * yn[0, at, :])

    sent_n = push(9, *loop(back_n2, zero1, zero1))
    grad_n2 = weight_grad(gyn.at[0], un[0], own_cols, mine, s1, mp)
    grad_b2 = weight_grad(gyb, ub[0], own_cols, mine, s2, mp)
    a_work[:s2, :] = grad_b2[:, :main]
    a_work[s2:tall_a, :] = jnp.concatenate([grad_n2, grad_n3], axis=1)[:, :main]
    spill[:s2, :] = grad_b2[:, main:]
    spill[s2:tall_a, :] = jnp.concatenate([grad_n2, grad_n3], axis=1)[:, main:]
    for p in range(parts):
        n = min(short, tall_a - p * short)
        a_work[tall_a : tall_a + n, p * rest : (p + 1) * rest] = spill[p * short : p * short + n, :]
    size_a, size_b = a_work.shape[0], b_work.shape[0]
    copy_ax, start_a = give_half(me, 0, 0, size_a, a_work, a_land.at[pl.ds(0, size_a // 2), :], hsend.at[0], hrecv.at[0])
    folded = jnp.zeros((16, h1), jnp.float32)
    col = lax.broadcasted_iota(jnp.int32, (16, h1), 1)
    for h in range(heads):
        folded = folded + jnp.where(col // hx == h, pair_g[h * 16 : (h + 1) * 16, :], 0.0)
    b_work[size_b - 16 :, :h1] = low(folded)
    t_b1 = pull(sent_b)[:, :h2]

    def gate_back(k, at, grad):
        x = feat[at, :].astype(jnp.float32)
        value = gate[k, at, :]
        g = low(grad * x * value * (1.0 - 0.5 * value))
        grad_gate[k, at, :] = g
        return grad * value, g

    def back_b1(at):
        g = grad_y(db[0, at, :], yb[0, at, :], rstd_b1, gain_b(0)[0], t_b1)
        gyb1[at, :] = g
        own_term[at, :] = gate_back(1, at, nn(g, b1[...]))[0]
        return ()

    loop(back_b1)
    b_work[:s2, :wide] = weight_grad(gyb1, fields[1], own_cols, mine, s2, mp)
    b_work[s2 : s2 + gcols, :wide] = weight_grad(grad_gate.at[1], feat[...], own_cols, mine, gcols, mp)
    copy_bx, start_b = give_half(me, 0, 0, size_b, b_work, b_land, hsend.at[2], hrecv.at[2])
    a_work[pl.ds(pl.multiple_of(start_a, 16), size_a // 2), :] = add_half(
        copy_ax, start_a, size_a // 2, a_work, a_land.at[pl.ds(0, size_a // 2), :]
    )
    copy_az, start_a = give_half(
        me, 1, start_a, size_a // 2, a_work, a_land.at[pl.ds(size_a // 2, size_a // 4), :], hsend.at[1], hrecv.at[1]
    )
    t_n1 = pull(sent_n)[:, :h1]

    def back_n1(at, ga, gb, ne):
        g = grad_y(dn[0, at, :], yn[0, at, :], rstd_n1, gain_n(0)[0], t_n1)
        gyn1[at, :] = g
        term, g0 = gate_back(0, at, nn(g, n1[...]))
        g1 = grad_gate[1, at, :]
        whole = nn(g0, gates[0][...]) + nn(g1, gates[1][...]) + term + own_term[at, :]
        whole = low(whole).astype(jnp.float32)
        own_term[at, :] = whole
        ne = ne + column_sum(whole[:, :num] * widen_dense(dense_t[:, at], 16))
        return ga + column_sum(g0.astype(jnp.float32)), gb + column_sum(g1.astype(jnp.float32)), ne

    zero_g = jnp.zeros((1, wide), jnp.float32)
    ga, gb, ne = loop(back_n1, zero_g, zero_g, jnp.zeros((1, num), jnp.float32))
    grads_t[...] = low(jnp.transpose(own_term[:, num:]))
    small[...] = jnp.zeros_like(small)
    small[0:1, :gcols] = own_columns(ga, mine, gcols, mp)
    small[1:2, :gcols] = own_columns(gb, mine, gcols, mp)
    small[2:3, :num] = ne
    for layer, t in enumerate((t_n1, t_n2, t_n3)):
        n_shift_g[layer : layer + 1, :] = own_columns(t[0:1], mine, s1, mp)
        n_gain_g[layer : layer + 1, :] = own_columns(t[1:2], mine, s1, mp)
    for layer, t in enumerate((t_b1, t_b2)):
        b_shift_g[layer : layer + 1, :] = own_columns(t[0:1], mine, s2, mp)
        b_gain_g[layer : layer + 1, :] = own_columns(t[1:2], mine, s2, mp)
    total = pull(sent_join)
    right_g[...] = total[0:1, :h2]
    left_g[...] = total[1:2, :h1]
    bias_g[...] = total[1:2, 512:513]
    a_out[...] = add_half(
        copy_az, start_a, size_a // 4, a_work, a_land.at[pl.ds(size_a // 2, size_a // 4), :]
    )
    b_out[...] = add_half(copy_bx, start_b, size_b // 2, b_work, b_land)
    for copy in [copy_ax, copy_az, copy_bx] + copies_a + copies_y + copies_b:
        copy.wait_send()
    for group in started:
        for copy in group:
            copy.wait_send()


def reduce_kernel(
    dp, mp,
    grads, feat, fields, grad_gate, gyn1, a_in, b_in, small,
    shares, a_full, b_full, c_full, small_out,
    t_work, t_land, t_slots, s_slots, a_work, a_land, b_work, b_land, c_work, c_land, c_slots, own_cols,
    tsend, trecv, ysend, yrecv, ssend, srecv, asend, arecv, bsend, brecv, csend, crecv,
):
    tall = grads.shape[0] // dp
    me, mine = lax.axis_index("dp"), lax.axis_index("mp")
    hail(dp, mp)
    levels = dp.bit_length() - 1
    far = dp // 2
    side, place = upper(me, 0), me // 2
    size_a, size_b, size_c = a_full.shape[0], b_full.shape[0], c_full.shape[0]
    s_slots[me] = small[...]
    pending = []
    all_in(dp, mp)

    def send_to(copy):
        copy.start()
        pending.append(copy)
        return copy

    def across(k):
        return {"dp": lax.rem(me + 2 * k, dp)}

    def rows_at(start, size):
        return pl.ds(pl.multiple_of(start, 16), size)

    half_t = grads.shape[0] // 2
    copy_t = send_to(
        remote(grads.at[rows_at((1 - side) * half_t, half_t), :], t_land, tsend.at[0], trecv.at[0], {"dp": flip(me, 0)})
    )
    start_a, start_b = 0, side * (size_b // 2)
    for level in range(2):
        start_a = start_a + upper(me, level) * (size_a >> (level + 1))
    a_work[...] = a_in[...]
    b_work[...] = b_in[...]

    def halves(name, level, work, land, size, sems, off):
        half = size // 2
        mine_up = upper(me, level)
        copy = send_to(
            remote(
                work.at[rows_at(off + (1 - mine_up) * half, half), :], land.at[pl.ds(0, half), :],
                sems[0].at[level], sems[1].at[level], {"dp": flip(me, level)},
            )
        )
        return copy, off + mine_up * half, half

    def fold(step, work, land):
        copy, off, half = step
        copy.wait_recv()
        at = rows_at(off, half)
        work[at, :] = low(work[at, :].astype(jnp.float32) + land[pl.ds(0, half), :].astype(jnp.float32))
        return off, half

    def double(level, full, start, size, sems):
        at = full.at[rows_at(start, size), :]
        copy = send_to(
            remote(at, at, sems[0].at[levels + level], sems[1].at[levels + level], {"dp": flip(me, level)})
        )
        return copy, start - upper(me, level) * size, size * 2

    sems_a, sems_b = (asend, arecv), (bsend, brecv)
    step_b = halves("b", 1, b_work, b_land.at[0], size_b // 2, sems_b, 0)
    step_a = halves("a", 2, a_work, a_land.at[0], size_a // 4, sems_a, 0) if levels > 2 else None
    gcols, s1 = feat.shape[1] // mp, gyn1.shape[1] // mp
    wide = feat.shape[1]
    c_work[...] = jnp.zeros_like(c_work)
    c_work[:gcols, :wide] = weight_grad(grad_gate.at[0], feat[...], own_cols, mine, gcols, mp)
    c_work[gcols : gcols + s1, :wide] = weight_grad(gyn1, fields[0], own_cols, mine, s1, mp)
    half_c = size_c // 2
    copy_c = send_to(
        remote(c_work.at[rows_at((1 - side) * half_c, half_c), :], c_land, csend.at[0], crecv.at[0], {"dp": flip(me, 0)})
    )
    small_copies = spread_dp(dp, lambda k: s_slots.at[k], ssend, srecv)

    def onward(back, level, full, sems):
        copy, start, size = back
        copy.wait_recv()
        return double(level, full, start, size, sems)

    off_b, held_b = fold(step_b, b_work, b_land.at[0])
    step_b = halves("b", 2, b_work, b_land.at[1], held_b, sems_b, off_b)
    off_a, held_a = fold(step_a, a_work, a_land.at[0])
    for level in range(3, levels):
        step_a = halves("a", level, a_work, a_land.at[level - 2], held_a, sems_a, off_a)
        off_a, held_a = fold(step_a, a_work, a_land.at[level - 2])
    start_a = start_a + off_a
    a_full[rows_at(start_a, held_a), :] = a_work[rows_at(off_a, held_a), :]
    back_a = double(levels - 1, a_full, start_a, held_a, sems_a)
    off_b, held_b = fold(step_b, b_work, b_land.at[1])
    for level in range(3, levels):
        step_b = halves("b", level, b_work, b_land.at[level - 1], held_b, sems_b, off_b)
        off_b, held_b = fold(step_b, b_work, b_land.at[level - 1])
    start_b = start_b + off_b
    b_full[rows_at(start_b, held_b), :] = b_work[rows_at(off_b, held_b), :]
    back_b = double(levels - 1, b_full, start_b, held_b, sems_b)
    for level in range(levels - 2, 0, -1):
        back_a = onward(back_a, level, a_full, sems_a)
    copy_t.wait_recv()
    at = rows_at(side * half_t, half_t)
    t_work[...] = low(grads[at, :].astype(jnp.float32) + t_land[...].astype(jnp.float32))
    t_copies = []
    for k in range(1, far):
        to = lax.rem(place + k, far)
        t_copies.append(
            send_to(
                remote(t_work.at[rows_at(to * tall, tall), :], t_slots.at[k - 1], tsend.at[k], trecv.at[k], across(k))
            )
        )
    copy_c.wait_recv()
    at = rows_at(side * half_c, half_c)
    c_work[at, :] = low(c_work[at, :].astype(jnp.float32) + c_land[...].astype(jnp.float32))
    piece = half_c // far
    c_copies = []
    for k in range(1, far):
        to = lax.rem(place + k, far)
        c_copies.append(
            send_to(
                remote(
                    c_work.at[rows_at(side * half_c + to * piece, piece), :], c_slots.at[k - 1],
                    csend.at[k], crecv.at[k], across(k),
                )
            )
        )
    for level in range(levels - 2, 0, -1):
        back_b = onward(back_b, level, b_full, sems_b)
    back_a = onward(back_a, 0, a_full, sems_a)
    own = rows_at(side * half_c + place * piece, piece)
    total = c_work[own, :].astype(jnp.float32)
    for k in range(1, far):
        c_copies[k - 1].wait_recv()
        total = total + c_slots[k - 1].astype(jnp.float32)
    c_full[own, :] = low(total)
    c_back = []
    for k in range(1, far):
        c_back.append(
            send_to(
                remote(c_full.at[own, :], c_full.at[own, :], csend.at[far + k], crecv.at[far + k], across(k))
            )
        )
    total = t_work[rows_at(place * tall, tall), :].astype(jnp.float32)
    for k in range(1, far):
        t_copies[k - 1].wait_recv()
        total = total + t_slots[k - 1].astype(jnp.float32)
    shares[mine] = low(total)
    started = relay_own(mp, lambda k: shares.at[k], ysend, yrecv)
    back_b = onward(back_b, 0, b_full, sems_b)
    for copy in c_back:
        copy.wait_recv()
    at = c_full.at[rows_at(side * half_c, half_c), :]
    last_c = send_to(remote(at, at, csend.at[far], crecv.at[far], {"dp": flip(me, 0)}))
    relay_rest(mp, lambda k: shares.at[k], ysend, yrecv, started)
    for copy in small_copies:
        copy.wait_recv()
    value = s_slots[0]
    for d in range(1, dp):
        value = value + s_slots[d]
    small_out[...] = value
    back_a[0].wait_recv()
    last_c.wait_recv()
    back_b[0].wait_recv()
    for copy in pending + small_copies:
        copy.wait_send()


def final_kernel(
    mp, hx, shares, a_full, b_full, c_full, small, logits_in, n_gain_in, n_shift_in, b_gain_in, b_shift_in,
    left_in, right_in, bias_in,
    logits, num_g, table_g, gate_g, gate_bias_g, n_first_g, n_rest_g, n_gain_g, n_shift_g,
    b_first_g, b_rest_g, b_gain_g, b_shift_g, left_g, right_g, pair_g, bias_g,
):
    gcols, s1, s2, h1 = gate_g.shape[0], n_first_g.shape[0], b_first_g.shape[0], n_rest_g.shape[2]
    wide = n_first_g.shape[1]

    def full(work, row, count, col, width):
        return work[row : row + count, col : col + width].astype(jnp.float32)

    blocks = shares.shape[1] // 16
    for m in range(mp):
        for b in range(blocks):
            table_g[:, (m * blocks + b) * HI : (m * blocks + b + 1) * HI] = shares[
                m, b * 16 : (b + 1) * 16, :
            ].astype(jnp.float32)
    gate_g[:, 0, :] = full(c_full, 0, gcols, 0, wide)
    gate_g[:, 1, :] = full(b_full, s2, gcols, 0, wide)
    n_first_g[...] = full(c_full, gcols, s1, 0, wide)
    b_first_g[...] = full(b_full, 0, s2, 0, wide)
    main = a_full.shape[1]
    rest = 2 * h1 - main
    parts = main // rest
    tall_a = s2 + s1
    short = -(-tall_a // parts)
    tail = jnp.concatenate(
        [
            full(a_full, tall_a, min(short, tall_a - p * short), p * rest, rest)
            for p in range(parts)
        ],
        axis=0,
    )
    b_rest_g[:, :main] = full(a_full, 0, s2, 0, main)
    b_rest_g[:, main:] = tail[:s2]
    both = jnp.concatenate([full(a_full, s2, s1, 0, main), tail[s2:]], axis=1)
    n_rest_g[:, 0, :] = both[:, :h1]
    n_rest_g[:, 1, :] = both[:, h1:]
    heads = pair_g.shape[2]
    pairs = b_full[b_full.shape[0] - 16 :, :h1]
    row = lax.broadcasted_iota(jnp.int32, (h1, heads), 0)
    col = lax.broadcasted_iota(jnp.int32, (h1, heads), 1)
    for i in range(hx):
        choose = jnp.where(row == col * hx + i, 1.0, 0.0).astype(jnp.bfloat16)
        pair_g[i] = nn(pairs, choose)
    fields, width = num_g.shape
    gate_bias_g[...] = small[0:2, :gcols]
    spread = jnp.broadcast_to(small[2:3, : fields * width], (fields, fields * width))
    row = lax.broadcasted_iota(jnp.int32, spread.shape, 0)
    col = lax.broadcasted_iota(jnp.int32, spread.shape, 1)
    spread = jnp.where(col // width == row, spread, 0.0)
    total = spread[:, :width]
    for i in range(1, fields):
        total = total + spread[:, i * width : (i + 1) * width]
    num_g[...] = total
    logits[...] = logits_in[...]
    n_gain_g[...] = n_gain_in[...]
    n_shift_g[...] = n_shift_in[...]
    b_gain_g[...] = b_gain_in[...]
    b_shift_g[...] = b_shift_in[...]
    left_g[...] = left_in[...]
    right_g[...] = right_in[...].reshape(right_g.shape)
    bias_g[...] = bias_in[...]


def f32(*shape):
    return jax.ShapeDtypeStruct(shape, jnp.float32)


def b16(*shape):
    return jax.ShapeDtypeStruct(shape, jnp.bfloat16)


def held(*shape):
    return pltpu.VMEM(shape, jnp.float32)


def held16(*shape):
    return pltpu.VMEM(shape, jnp.bfloat16)


def dma(*shape):
    return pltpu.SemaphoreType.DMA(shape)


def shards(
    dense_values,
    field_ids,
    lengths,
    labels,
    num_embed,
    embed_table,
    gate_weight,
    gate_bias,
    narrow_first,
    narrow_rest,
    narrow_gain,
    narrow_shift,
    broad_first,
    broad_rest,
    broad_gain,
    broad_shift,
    joining_left,
    joining_right,
    joining_pair,
    joining_bias,
):
    dp, mp = lax.axis_size("dp"), lax.axis_size("mp")
    chips = mp // 2
    rows = dense_values.shape[0]
    cats, slots = field_ids.shape[:2]
    width, own_rows = embed_table.shape
    num = dense_values.shape[1] * width
    wide = gate_weight.shape[2]
    gcols = gate_weight.shape[1]
    s1, s2 = narrow_first.shape[0], broad_first.shape[0]
    h1, h2 = s1 * mp, s2 * mp
    hx = joining_pair.shape[1]
    bits = (cats * rows - 1).bit_length()
    dense_t = dense_values.T
    tall = own_rows // mp // HI * 16
    vregs = -(-(cats * slots * rows) // (2 * CHUNK)) * (2 * CHUNK) // 1024
    first_args = (
        embed_table, jnp.transpose(gate_weight, (1, 0, 2)), narrow_first, gate_bias,
        narrow_gain, narrow_shift, broad_gain, broad_shift, broad_first,
        field_ids, lengths, dense_t, num_embed, jnp.transpose(narrow_rest, (1, 0, 2)), broad_rest,
    )
    t2, keys, numeric, weights, vec, n_next, b_next = pl.pallas_call(
        functools.partial(first_kernel, dp, mp, own_rows, bits),
        out_shape=(
            b16(dp * tall, HI),
            jax.ShapeDtypeStruct((2, vregs * 8, 128), jnp.int32),
            b16(rows, num),
            b16(2 * wide + h1 + h2, wide),
            f32(16, 896),
            b16(mp, 2, s1, h1),
            b16(mp, 2, s2 // 2, h2),
        ),
        in_specs=[ANY] * 15,
        out_specs=(VM,) * 7,
        scratch_shapes=[pltpu.VMEM(x.shape, x.dtype) for x in first_args]
        + [
            pltpu.VMEM((vregs * 8, 128), jnp.int32),
            held16(mp, gcols, wide),
            held16(mp, 2, gcols // 2, wide),
            held16(mp, 2, s1 // 2, wide),
            held16(mp, 2, s2 // 2, wide),
            held(mp, 16, 256),
            dma(dp - 1),
            dma(dp - 1),
            dma(2, mp),
            dma(2, mp),
            dma(3, 4 * chips),
            dma(3, 4 * chips),
            dma(2, 4 * chips),
            dma(2, 4 * chips),
            dma(15),
        ],
        compiler_params=params(0, 54),
        name="first",
    )(*first_args)
    partial = pl.pallas_call(
        functools.partial(lookup_kernel, cats, rows, bits),
        out_shape=f32(cats * 16, rows),
        in_specs=[VM] * 2,
        out_specs=VM,
        scratch_shapes=[held((cats + WINDOW) * 16, rows)],
        compiler_params=params(None, 16),
        cost_estimate=pl.CostEstimate(flops=8 * 10**9, bytes_accessed=2 * 10**6, transcendentals=0),
        name="lookup",
    )(keys, t2)

    def up(x, n):
        return -(-x // n) * n

    main = wide // 128 * 128 + 128
    short = -(-(s1 + s2) // (main // (h2 - main)))
    a_rows = up(s1 + s2 + short, 16 * dp)
    b_rows = up(s2 + gcols, 16) + 16
    b_rows = up(b_rows, 16 * dp)
    c_rows = up(gcols + s1, 16 * dp)
    levels = dp.bit_length() - 1
    dense_args = (
        joining_left.reshape(1, h1), joining_right,
        jnp.transpose(joining_pair, (1, 2, 0)), joining_bias.reshape(1, 1), labels.reshape(1, rows), dense_t,
    )
    (
        logits, grads_t, feat, fields, grad_gate, gyn1, a_part, b_part, small,
        n_gain_g, n_shift_g, b_gain_g, b_shift_g, left_g, right_g, bias_g,
    ) = pl.pallas_call(
        functools.partial(dense_kernel, dp, mp, hx, float(rows * dp)),
        out_shape=(
            f32(1, rows),
            b16(cats * 16, rows),
            b16(rows, wide),
            b16(2, rows, wide),
            b16(2, rows, wide),
            b16(rows, h1),
            b16(a_rows // 4, main),
            b16(b_rows // 2, main),
            f32(8, 256),
            f32(3, s1),
            f32(3, s1),
            f32(2, s2),
            f32(2, s2),
            f32(1, h1),
            f32(1, h2),
            f32(1, 1),
        ),
        in_specs=[VM] * 6 + [ANY] * 6,
        out_specs=(VM,) * 16,
        scratch_shapes=[
            held(cats * 8, rows),
            held16(chips, cats * 8, rows),
            held16(cats * 16, rows),
            held(2, rows, wide),
            held(rows, wide),
            held16(mp, 2, s1, h1),
            held16(mp, 2, s2 // 2, h2),
            held16(2, h1, h1),
            held16(h2, h2),
            held(3, rows, h1),
            held(3, rows, h1),
            held(2, rows, h2),
            held(2, rows, h2),
            held16(3, rows, h1),
            held16(2, rows, h2),
            held16(2, rows, h1),
            held16(rows, h2),
            held16(h1, h2),
            held16(h1, h2),
            held(h2, h1),
            held(rows, h1),
            held(11, dp, 2, 896),
            held16(s1 + s2, h2 - main),
            dma(2, chips + 1),
            dma(2, chips + 1),
            dma(2, 4 * chips),
            dma(2, 4 * chips),
            dma(11, dp - 1),
            dma(11, dp - 1),
            held16(rows, h2),
            held16(a_rows, main),
            held16(b_rows, main),
            held16(a_rows * 3 // 4, main),
            held16(b_rows // 2, main),
            dma(3),
            dma(3),
            held16(rows, up(max(gcols, s1, s2), 128)),
        ]
        + [pltpu.VMEM(x.shape, x.dtype) for x in dense_args]
        + [dma(6)],
        compiler_params=params(1, 39 + dp // 16),
        name="dense",
    )(partial, numeric, weights, n_next, b_next, vec, *dense_args)
    row_sums = pl.pallas_call(
        functools.partial(scatter_kernel, cats, rows, bits),
        out_shape=b16(dp * tall, HI),
        in_specs=[VM] * 2,
        out_specs=VM,
        scratch_shapes=[held(dp * tall, HI), held16((cats + WINDOW) * 16, rows)],
        compiler_params=params(None, 16),
        cost_estimate=pl.CostEstimate(flops=8 * 10**9, bytes_accessed=2 * 10**6, transcendentals=0),
        name="scatter",
    )(keys, grads_t)
    shares, a_full, b_full, c_full, small = pl.pallas_call(
        functools.partial(reduce_kernel, dp, mp),
        out_shape=(
            b16(mp, tall, HI),
            b16(a_rows, main),
            b16(b_rows, main),
            b16(c_rows, main),
            f32(8, 256),
        ),
        in_specs=[VM] * 8,
        out_specs=(VM,) * 5,
        scratch_shapes=[
            held16(dp // 2 * tall, HI),
            held16(dp // 2 * tall, HI),
            held16(dp // 2 - 1, tall, HI),
            held(dp, 8, 256),
            held16(a_rows // 4, main),
            held16(max(levels - 2, 1), a_rows // 8, main),
            held16(b_rows // 2, main),
            held16(max(levels - 1, 1), b_rows // 4, main),
            held16(c_rows, main),
            held16(c_rows // 2, main),
            held16(dp // 2 - 1, c_rows // dp, main),
            held16(rows, up(max(gcols, s1, s2), 128)),
            dma(dp // 2),
            dma(dp // 2),
            dma(mp),
            dma(mp),
            dma(dp - 1),
            dma(dp - 1),
            dma(2 * levels),
            dma(2 * levels),
            dma(2 * levels),
            dma(2 * levels),
            dma(dp),
            dma(dp),
        ],
        compiler_params=params(2, 24),
        name="reduce",
    )(row_sums, feat, fields, grad_gate, gyn1, a_part, b_part, small)
    outs = pl.pallas_call(
        functools.partial(final_kernel, mp, hx),
        out_shape=(
            f32(1, rows),
            f32(*num_embed.shape),
            f32(width, own_rows),
            f32(gcols, 2, wide),
            f32(2, gcols),
            f32(s1, wide),
            f32(s1, 2, h1),
            f32(3, s1),
            f32(3, s1),
            f32(s2, wide),
            f32(s2, h2),
            f32(2, s2),
            f32(2, s2),
            f32(1, h1),
            f32(h2),
            f32(hx, width, joining_pair.shape[0]),
            f32(1, 1),
        ),
        in_specs=[VM] * 13,
        out_specs=(VM,) * 17,
        compiler_params=params(None, 16),
        name="final",
    )(
        shares, a_full, b_full, c_full, small, logits, n_gain_g, n_shift_g, b_gain_g, b_shift_g,
        left_g, right_g, bias_g,
    )
    outs = list(outs)
    outs[0] = outs[0].reshape(rows)
    outs[3] = jnp.transpose(outs[3], (1, 0, 2))
    outs[6] = jnp.transpose(outs[6], (1, 0, 2))
    outs[13] = outs[13].reshape(h1)
    outs[15] = jnp.transpose(outs[15], (2, 0, 1))
    outs[16] = outs[16].reshape(1)
    return tuple(outs)


def solution(mesh):
    placed = (
        P("dp", None),
        P(None, None, "dp"),
        P(None, "dp"),
        P("dp"),
        P(),
        P(None, "dp"),
        P(None, "mp", None),
        P(None, "mp"),
        P("mp", None),
        P(None, "mp", None),
        P(None, "mp"),
        P(None, "mp"),
        P("mp", None),
        P("mp", None),
        P(None, "mp"),
        P(None, "mp"),
        P(),
        P(),
        P(),
        P(),
    )
    return jax.shard_map(
        shards,
        mesh=mesh,
        in_specs=placed,
        out_specs=(
            P("dp"),
            P(),
            P(None, "dp"),
            P(None, "mp", None),
            P(None, "mp"),
            P("mp", None),
            P(None, "mp", None),
            P(None, "mp"),
            P(None, "mp"),
            P("mp", None),
            P("mp", None),
            P(None, "mp"),
            P(None, "mp"),
            P(),
            P(),
            P(),
            P(),
        ),
        check_vma=False,
    )
```

```python
import functools
import jax
import jax.numpy as jnp
from jax import lax
from jax.experimental import pallas as pl
from jax.experimental.pallas import tpu as pltpu
from jax.sharding import PartitionSpec as P

MESH = pl.DeviceIdType.MESH
VM = pl.BlockSpec(memory_space=pltpu.VMEM)
ANY = pl.BlockSpec(memory_space=pltpu.HBM)
HI = 256
CHUNK = 1024


def params(cid, mib=48):
    if cid is None:
        return pltpu.CompilerParams(vmem_limit_bytes=mib << 20)
    return pltpu.CompilerParams(
        collective_id=cid, has_side_effects=True, vmem_limit_bytes=mib << 20
    )


def hail(dp, mp):
    me, mine = lax.axis_index("dp"), lax.axis_index("mp")
    barrier = pltpu.get_barrier_semaphore()
    for step in range(1, dp):
        pl.semaphore_signal(
            barrier, inc=1, device_id={"dp": lax.rem(me + step, dp)}, device_id_type=MESH
        )
    for step in range(1, mp):
        pl.semaphore_signal(
            barrier, inc=1, device_id={"mp": lax.rem(mine + step, mp)}, device_id_type=MESH
        )


def all_in(dp, mp):
    pl.semaphore_wait(pltpu.get_barrier_semaphore(), dp - 1 + mp - 1)


def remote(src, dst, send, recv, where):
    return pltpu.make_async_remote_copy(
        src_ref=src, dst_ref=dst, send_sem=send, recv_sem=recv,
        device_id=where, device_id_type=MESH,
    )


def spread_dp(dp, pick, send, recv):
    me = lax.axis_index("dp")
    out = []
    for step in range(1, dp):
        to = lax.rem(me + step, dp)
        copy = remote(pick(me), pick(me), send.at[step - 1], recv.at[step - 1], {"dp": to})
        copy.start()
        out.append(copy)
    return out


def over(x, n):
    if n & (n - 1) == 0:
        return lax.shift_right_logical(x, n.bit_length() - 1)
    return x // n


def compact_keys(key):
    count = key.shape[0]
    rows = count * 8
    dead = jnp.where(key.reshape(rows, 128) < 0, 1.0, 0.0).astype(jnp.bfloat16)
    row = lax.broadcasted_iota(jnp.int32, (128, 128), 0)
    col = lax.broadcasted_iota(jnp.int32, (128, 128), 1)
    in_row = jnp.dot(dead, jnp.where(row < col, 1.0, 0.0).astype(jnp.bfloat16), preferred_element_type=jnp.float32)
    row_sum = jnp.dot(dead, jnp.ones((128, 128), jnp.bfloat16), preferred_element_type=jnp.float32)
    row = lax.broadcasted_iota(jnp.int32, (rows, rows), 0)
    col = lax.broadcasted_iota(jnp.int32, (rows, rows), 1)
    above = jnp.where(col < row, 1.0, 0.0).astype(jnp.bfloat16)
    before = jnp.dot(above, row_sum.astype(jnp.bfloat16), preferred_element_type=jnp.float32)
    shift = (in_row + before).astype(jnp.int32).reshape(count, 8, 128)
    shift = jnp.where(key < 0, 0, shift)
    sub = lax.broadcasted_iota(jnp.int32, (8, 128), 0)
    lane = lax.broadcasted_iota(jnp.int32, (8, 128), 1)

    def rows_up(x, j):
        t = [pltpu.roll(x[v], 8 - j, 0) for v in range(count)]
        return jnp.stack([jnp.where(sub < 8 - j, t[v], t[(v + 1) % count]) for v in range(count)])

    bit = 0
    for j in (1, 2, 4, 8, 16, 32, 64):
        def lanes_up(x):
            y = jnp.stack([pltpu.roll(x[v], 128 - j, 1) for v in range(count)])
            return jnp.where(lane[None] < 128 - j, y, rows_up(y, 1))
        key, shift = settle(key, shift, lanes_up(key), lanes_up(shift), bit)
        bit += 1
    for j in (1, 2, 4):
        key, shift = settle(key, shift, rows_up(key, j), rows_up(shift, j), bit)
        bit += 1
    step = 1
    while step < count:
        moved_key = jnp.concatenate([key[step:], key[:step]], axis=0)
        moved_shift = jnp.concatenate([shift[step:], shift[:step]], axis=0)
        key, shift = settle(key, shift, moved_key, moved_shift, bit)
        bit, step = bit + 1, step * 2
    return key


def settle(key, shift, moved_key, moved_shift, bit):
    take = (moved_shift & (1 << bit)) != 0
    stay = (shift & (1 << bit)) == 0
    key = jnp.where(take, moved_key, jnp.where(stay, key, -1))
    shift = jnp.where(take, moved_shift, jnp.where(stay, shift, 0))
    return key, shift


def seat(i, dp):
    return i % 2 * (dp // 2) + i // 2


def make_keys(ids, lens, scratch, own_rows, dp, mp, bits):
    cats, slots, rows = ids.shape
    part = own_rows // mp
    mine = lax.axis_index("mp")
    scratch[...] = jnp.full_like(scratch, -1)
    slot = lax.broadcasted_iota(jnp.int32, (slots, rows), 0)
    event = lax.broadcasted_iota(jnp.int32, (slots, rows), 1)

    def body(c, carry):
        values = ids[c]
        holder = values // own_rows
        inner = values - holder * own_rows
        owner = inner // part
        place = seat(holder, dp) * part + inner - owner * part
        live = (slot < lens[pl.ds(c, 1), :]) & (owner == mine)
        key = jnp.where(live, place * (1 << bits) + c * rows + event, -1)
        for q in range(rows // 128):
            scratch[pl.ds((c * (rows // 128) + q) * slots, slots), :] = key[:, q * 128 : (q + 1) * 128]
        return carry

    lax.fori_loop(0, cats, body, 0)


WINDOW = 16
WINDOW_BACK = 12


def chunk_parts(key, rows, bits):
    place = lax.shift_right_arithmetic(key, bits)
    bag = key & ((1 << bits) - 1)
    cat = over(bag, rows)
    return place, cat, bag - cat * rows


def short(row):
    return jnp.broadcast_to(row, (16, row.shape[1])).astype(jnp.int16)


def one_hot(row, size):
    apart = short(row) - lax.broadcasted_iota(jnp.int32, (16, row.shape[1]), 0).astype(jnp.int16)
    one = jnp.ones(apart.shape, jnp.bfloat16)
    zero = jnp.zeros(apart.shape, jnp.bfloat16)
    return jnp.concatenate([jnp.where(apart == i, one, zero) for i in range(0, size, 16)], axis=0)


def spread_rows(row, values, first, size):
    zero = jnp.zeros_like(values)
    apart = short(row - first)
    return jnp.concatenate([jnp.where(apart == i, values, zero) for i in range(size)], axis=0)


def chunk_key(keys, half, k):
    tall = CHUNK // 128
    key = keys[half, pl.ds(pl.multiple_of(k * tall, tall), tall), :]
    return jnp.concatenate([key[i : i + 1, :] for i in range(tall)], axis=1)


def chunk_span(keys, half, k, cats, rows, bits, window):
    tall = CHUNK // 128
    most = keys.shape[1] // tall - 1
    key = keys[half, pl.ds(pl.multiple_of(jnp.minimum(k, most) * tall, tall), tall), :]
    cat = over(key & ((1 << bits) - 1), rows)
    first = jnp.min(jnp.where(key >= 0, cat, cats - 1))
    last = jnp.max(jnp.where(key >= 0, cat, 0))
    return first, (last - first) // window + 1


def each_chunk(keys, half, cats, rows, bits, window, body):
    live = jnp.sum((keys[half] >= 0).astype(jnp.int32))
    chunks = (live + CHUNK - 1) // CHUNK

    def step(k, carry):
        later = chunk_span(keys, half, k + 1, cats, rows, bits, window)
        body(chunk_key(keys, half, k), *carry)
        return later

    lax.fori_loop(0, chunks, step, chunk_span(keys, half, 0, cats, rows, bits, window))


def lookup_kernel(cats, rows, bits, keys, t2, pooled, total):
    lows = t2.shape[0] // 32
    total[...] = jnp.zeros_like(total)

    def half_table(half, carry):
        def body(key, first, windows):
            place, cat, event = chunk_parts(key, rows, bits)
            low = jnp.broadcast_to(lax.shift_right_arithmetic(place, 8) - half * lows, (16, CHUNK))
            pick = one_hot(place & (HI - 1), HI)
            z = jnp.zeros((16, CHUNK), jnp.float32)
            for b in range(0, lows, 32):
                n = min(32, lows - b)
                at = pl.ds(pl.multiple_of((half * lows + b) * 16, 16), n * 16)
                y = jnp.dot(t2[at, :], pick, preferred_element_type=jnp.float32)
                for j in range(n):
                    z = z + jnp.where(low == b + j, y[j * 16 : (j + 1) * 16], 0.0)
            z = z.astype(jnp.bfloat16)
            cat = jnp.where(key >= 0, cat, -1)
            place_of = one_hot(event, rows)

            def window(w):
                start = first + w * WINDOW
                at = pl.ds(pl.multiple_of(start * 16, 16), WINDOW * 16)
                total[at, :] += lax.dot_general(
                    spread_rows(cat, z, start, WINDOW), place_of, (((1,), (1,)), ((), ())),
                    preferred_element_type=jnp.float32,
                )

            window(0)

            def more(w, carry):
                window(w)
                return carry

            lax.fori_loop(1, windows, more, 0)

        each_chunk(keys, half, cats, rows, bits, WINDOW, body)
        return carry

    lax.fori_loop(0, 2, half_table, 0)
    pooled[...] = total[: cats * 16, :].astype(pooled.dtype)


def scatter_kernel(cats, rows, bits, keys, grad, out, total, grad_pad):
    lows = total.shape[0] // 32
    total[...] = jnp.zeros_like(total)
    grad_pad[: cats * 16, :] = grad[...]
    grad_pad[cats * 16 :, :] = jnp.zeros((WINDOW_BACK * 16, rows), jnp.bfloat16)

    def half_table(half, carry):
        def body(key, first, windows):
            place, cat, event = chunk_parts(key, rows, bits)
            low = lax.shift_right_arithmetic(place, 8) - half * lows
            pick = one_hot(place & (HI - 1), HI)
            place_of = one_hot(event, rows)
            cat = jnp.broadcast_to(jnp.where(key >= 0, cat, -1), (16, CHUNK))

            def window(w, g):
                start = first + w * WINDOW_BACK
                at = pl.ds(pl.multiple_of(start * 16, 16), WINDOW_BACK * 16)
                wide = jnp.dot(grad_pad[at, :], place_of, preferred_element_type=jnp.float32)
                for c in range(WINDOW_BACK):
                    g = g + jnp.where(cat == start + c, wide[c * 16 : (c + 1) * 16], 0.0)
                return g

            g = window(0, jnp.zeros((16, CHUNK), jnp.float32))
            g = lax.fori_loop(1, windows, window, g).astype(jnp.bfloat16)
            for b in range(0, lows, 32):
                n = min(32, lows - b)
                at = pl.ds(pl.multiple_of((half * lows + b) * 16, 16), n * 16)
                total[at, :] += lax.dot_general(
                    spread_rows(low, g, b, n), pick, (((1,), (1,)), ((), ())),
                    preferred_element_type=jnp.float32,
                )

        each_chunk(keys, half, cats, rows, bits, WINDOW_BACK, body)
        return carry

    lax.fori_loop(0, 2, half_table, 0)
    out[...] = total[...].astype(out.dtype)


def relay_own(mp, slot, send, recv):
    mine = lax.axis_index("mp")
    core = lax.rem(mine, 2)
    other = mine + 1 - 2 * core
    chips = mp // 2
    out = []
    for k in range(1, chips):
        to = lax.rem(mine + 2 * k, mp)
        copy = remote(slot(mine), slot(mine), send.at[2 * k], recv.at[2 * k], {"mp": to})
        copy.start()
        out.append(copy)
    copy = remote(slot(mine), slot(mine), send.at[1], recv.at[1], {"mp": other})
    copy.start()
    out.append(copy)
    return out


def relay_rest(mp, slot, send, recv, started):
    mine = lax.axis_index("mp")
    core = lax.rem(mine, 2)
    other = mine + 1 - 2 * core
    chips = mp // 2
    passed = []
    for k in range(1, chips):
        source = lax.rem(mine + mp - 2 * k, mp)
        remote(slot(source), slot(source), send.at[2 * k], recv.at[2 * k], {"mp": other}).wait_recv()
        copy = remote(slot(source), slot(source), send.at[2 * k + 1], recv.at[2 * k + 1], {"mp": other})
        copy.start()
        passed.append(copy)
    remote(slot(other), slot(other), send.at[1], recv.at[1], {"mp": other}).wait_recv()
    for k in range(1, chips):
        far = lax.rem(other + mp - 2 * k, mp)
        remote(slot(far), slot(far), send.at[2 * k + 1], recv.at[2 * k + 1], {"mp": other}).wait_recv()
    for copy in started + passed:
        copy.wait_send()


def nn(a, b):
    return jnp.dot(a, b, preferred_element_type=jnp.float32)


def nt(a, b):
    return lax.dot_general(a, b, (((1,), (1,)), ((), ())), preferred_element_type=jnp.float32)


def tn(a, b):
    return lax.dot_general(a, b, (((0,), (0,)), ((), ())), preferred_element_type=jnp.float32)


def sigmoid(x):
    return 0.5 * jnp.tanh(0.5 * x) + 0.5


def low(x):
    return x.astype(jnp.bfloat16)


def column_sum(x):
    return jnp.sum(x, axis=0, keepdims=True)


def widen_dense(dense_t, width):
    fields = dense_t.shape[0]
    row = lax.broadcasted_iota(jnp.int32, (fields, fields * width), 0)
    col = lax.broadcasted_iota(jnp.int32, (fields, fields * width), 1)
    ones = jnp.where(col // width == row, 1.0, 0.0)
    return lax.dot_general(
        dense_t, ones, (((0,), (0,)), ((), ())),
        precision=lax.Precision.HIGHEST, preferred_element_type=jnp.float32,
    )


def split_relay(dp, mp, ref, send, recv, fetched=False):
    me, mine = lax.axis_index("dp"), lax.axis_index("mp")
    other = mine + 1 - 2 * lax.rem(mine, 2)
    chips = mp // 2
    near = lax.rem(me, 2)
    beside = {"dp": me + 1 - 2 * near}
    started = []

    def move(place, i, where):
        return remote(place, place, send.at[i], recv.at[i], where)

    def go(place, i, where):
        copy = move(place, i, where)
        copy.start()
        started.append(copy)

    def source(k):
        return lax.rem(mine + mp - 2 * k, mp)

    def begin():
        if not fetched:
            fetch()
        go(ref.at[mine], 0, {"mp": other})

    def fetch():
        for k in range(1, chips):
            go(ref.at[mine, near], k, {"mp": lax.rem(mine + 2 * k, mp)})

    def arrive():
        for k in range(1, chips):
            move(ref.at[source(k), near], k, beside).wait_recv()
        for copy in started:
            copy.wait_send()

    def middle():
        for k in range(1, chips):
            place = ref.at[source(k), near]
            if not fetched:
                move(place, k, beside).wait_recv()
            go(place, 2 * chips + k, beside)
            go(place, chips + k, {"mp": other})

    def later():
        for k in range(1, chips):
            place = ref.at[source(k), 1 - near]
            move(place, 2 * chips + k, beside).wait_recv()
            go(place, 3 * chips + k, {"mp": other})

    def end():
        move(ref.at[other], 0, beside).wait_recv()
        for k in range(1, chips):
            far = lax.rem(other + mp - 2 * k, mp)
            move(ref.at[far, near], chips + k, beside).wait_recv()
            move(ref.at[far, 1 - near], 3 * chips + k, beside).wait_recv()
        for copy in started:
            copy.wait_send()

    return begin, middle, later, end, fetch, arrive


def bring(sources, places, sem):
    copies = []
    for i, (source, place) in enumerate(zip(sources, places)):
        copy = pltpu.make_async_copy(source, place, sem.at[i])
        copy.start()
        copies.append(copy)
    return copies


def first_kernel(dp, mp, own_rows, bits, *refs):
    count = 15
    sources, refs = refs[:count], refs[count:]
    t2, keys, numeric, weights, vec, n_next, b_next = refs[:7]
    places, refs = refs[7 : 7 + count], refs[7 + count :]
    (
        scratch, gate_slots, g_slots, n_slots, b_slots, v_slots,
        send, recv, send2, recv2, send3, recv3, send4, recv4, sem,
    ) = refs
    brought = bring(sources, places, sem)
    (
        table, gate_w, n_first, gate_b, n_gain, n_shift, b_gain, b_shift, b_first,
        ids, lens, dense_t, num_embed, n_rest, b_rest,
    ) = places
    part = own_rows // mp
    blocks = part // HI
    tall = blocks * 16
    me, mine = lax.axis_index("dp"), lax.axis_index("mp")
    hail(dp, mp)
    for copy in brought[:9]:
        copy.wait()
    own = table[:, pl.ds(pl.multiple_of(mine * part, HI), part)].astype(jnp.bfloat16)
    for b in range(blocks):
        t2[pl.ds(pl.multiple_of(seat(me, dp) * tall + b * 16, 16), 16), :] = own[:, b * HI : (b + 1) * HI]
    gate_slots[mine] = gate_w[:, 0, :]
    second = gate_w[:, 1, :]
    cols = g_slots.shape[2]
    for k in range(2):
        g_slots[mine, k] = second[k * cols : (k + 1) * cols, :]
    small, large = n_slots.shape[2], b_slots.shape[2]
    for k in range(2):
        n_slots[mine, k] = n_first[k * small : (k + 1) * small, :]
        b_slots[mine, k] = b_first[k * large : (k + 1) * large, :]
    row = 0
    for ref in (gate_b, n_gain, n_shift, b_gain, b_shift):
        v_slots[mine, row : row + ref.shape[0], : ref.shape[1]] = ref[...]
        row += ref.shape[0]
    all_in(dp, mp)

    def slot(i):
        return t2.at[pl.ds(pl.multiple_of(seat(i, dp) * tall, 16), tall), :]

    pairs = [
        split_relay(dp, mp, ref, send3.at[i], recv3.at[i]) for i, ref in enumerate((g_slots, n_slots, b_slots))
    ]
    for steps in pairs:
        steps[0]()
    groups = []
    for i, ref in enumerate((gate_slots, v_slots)):
        started = relay_own(mp, lambda k, ref=ref: ref.at[k], send2.at[i], recv2.at[i])
        groups.append((ref, i, started))
    copies = spread_dp(dp, slot, send, recv)
    for copy in brought[9:]:
        copy.wait()
    half_b = b_next.shape[2]
    for k in range(2):
        n_next[mine, k] = n_rest[:, k, :]
        b_next[mine, k] = b_rest[k * half_b : (k + 1) * half_b, :]
    fields, width = num_embed.shape
    tiled = jnp.concatenate([num_embed[...]] * fields, axis=1)
    row = lax.broadcasted_iota(jnp.int32, tiled.shape, 0)
    col = lax.broadcasted_iota(jnp.int32, tiled.shape, 1)
    num_row = column_sum(jnp.where(col // width == row, tiled, 0.0))
    numeric[...] = low(widen_dense(dense_t[...], width) * num_row)
    make_keys(ids, lens, scratch, own_rows, dp, mp, bits)
    count = scratch.shape[0] // 8
    middle = (dp * part // 2) << bits

    def pack(half, carry):
        key = scratch[...]
        key = jnp.where((key < middle) == (half == 0), key, -1)
        keys[half] = compact_keys(key.reshape(count, 8, 128)).reshape(count * 8, 128)
        return carry

    lax.fori_loop(0, 2, pack, 0)
    for steps in pairs:
        steps[1]()
    nexts = [
        split_relay(dp, mp, ref, send4.at[i], recv4.at[i]) for i, ref in enumerate((n_next, b_next))
    ]
    for steps in nexts:
        steps[4]()
    for ref, i, started in groups:
        relay_rest(mp, lambda k, ref=ref: ref.at[k], send2.at[i], recv2.at[i], started)
    cols, wide = gate_slots.shape[1:]
    for m in range(mp):
        weights[m * cols : (m + 1) * cols, :] = gate_slots[m]
    for steps in pairs:
        steps[2]()
    row = wide
    for ref, steps in zip((g_slots, n_slots, b_slots), pairs):
        steps[3]()
        tall = ref.shape[2]
        for m in range(mp):
            for k in range(2):
                weights[row : row + tall, :] = ref[m, k]
                row += tall
    row = 0
    for ref in (gate_b, n_gain, n_shift, b_gain, b_shift):
        r, w = ref.shape
        vec[row : row + r, : mp * w] = jnp.concatenate(
            [v_slots[m, row : row + r, :w] for m in range(mp)], axis=1
        )
        row += r
    for steps in nexts:
        steps[5]()
    for copy in copies:
        copy.wait()


def own_columns(x, mine, width, mp):
    out = jnp.zeros((x.shape[0], width), x.dtype)
    for m in range(mp):
        out = jnp.where(mine == m, x[:, m * width : (m + 1) * width], out)
    return out


def up16(x):
    return -(-x // 16) * 16


def weight_grad(grad_y, inputs, own, mine, width, mp):
    for m in range(mp):

        @pl.when(mine == m)
        def _():
            own[:, :width] = grad_y[:, m * width : (m + 1) * width]

    return low(tn(own[:, :width], inputs))


def flip(me, level):
    bit = 1 << level
    return me + bit - 2 * bit * lax.rem(me // bit, 2)


def upper(me, level):
    return lax.rem(me // (1 << level), 2)


def give_half(me, level, start, size, work, land, send, recv):
    half = size // 2
    mine = upper(me, level)
    at = pl.ds(pl.multiple_of(start + (1 - mine) * half, 16), half)
    copy = remote(work.at[at, :], land, send, recv, {"dp": flip(me, level)})
    copy.start()
    return copy, start + mine * half


def add_half(copy, start, half, work, land):
    copy.wait_recv()
    at = pl.ds(pl.multiple_of(start, 16), half)
    return low(work[at, :].astype(jnp.float32) + land[...].astype(jnp.float32))


def dense_kernel(
    dp, mp, hx, batch,
    partial, numeric, weights, n_next, b_next, vec,
    left_hbm, right_hbm, pair_hbm, bias_hbm, labels_hbm, dense_hbm,
    logits, grads_t, feat, fields, grad_gate, gyn1, a_out, b_out, small,
    n_gain_g, n_shift_g, b_gain_g, b_shift_g, left_g, right_g, bias_g,
    half_a, half_c, pooled, gate, own_term, n_slots, b_slots, n23, b2,
    yn, dn, yb, db, un, ub, gyn, gyb, pair_hi, pair_lo, pair_g, to_first, sums, spill,
    fsend, frecv, wsend, wrecv, ssend, srecv,
    gyb1, a_work, b_work, a_land, b_land, hsend, hrecv, own_cols,
    left, right, pair_t, bias, labels, dense_t, sem,
):
    brought = bring(
        (left_hbm, right_hbm, pair_hbm, bias_hbm, labels_hbm, dense_hbm),
        (left, right, pair_t, bias, labels, dense_t),
        sem,
    )
    me, mine = lax.axis_index("dp"), lax.axis_index("mp")
    core = lax.rem(mine, 2)
    chip = mine // 2
    chips = mp // 2
    other = mine + 1 - 2 * core
    rows = feat.shape[0]
    block = 256
    steps = rows // block
    h1, h2 = n23.shape[1], b2.shape[0]
    s1, s2 = h1 // mp, h2 // mp
    wide = feat.shape[1]
    gates = (weights.at[pl.ds(0, wide), :], weights.at[pl.ds(wide, wide), :])
    n1 = weights.at[pl.ds(2 * wide, h1), :]
    b1 = weights.at[pl.ds(2 * wide + h1, h2), :]
    num = numeric.shape[1]
    gcols = wide // mp
    half = partial.shape[0] // 2
    hail(dp, mp)
    near = lax.rem(me, 2)
    for slots, given in ((n_slots, n_next), (b_slots, b_next)):
        slots[mine] = given[mine]
        for k in range(1, chips):
            source = lax.rem(mine + 2 * k, mp)
            slots[source, near] = given[source, near]
    all_in(dp, mp)

    def rowset(i):
        return pl.ds(pl.multiple_of(i * block, block), block)

    def part(c):
        return pl.ds(pl.multiple_of(c * half, 16), half)

    def events(h):
        return pl.ds(h * (rows // 2), rows // 2)

    copies_a, copies_y, copies_b = [], [], []
    for h in range(2):
        copy = remote(
            partial.at[part(1 - core), events(h)], half_a.at[:, events(h)], fsend.at[h, 0], frecv.at[h, 0],
            {"mp": other},
        )
        copy.start()
        copies_a.append(copy)
    for copy in brought:
        copy.wait()
    for h in range(2):
        copies_a[h].wait_recv()
        half_c[chip, :, events(h)] = low(partial[part(core), events(h)] + half_a[:, events(h)])
        for k in range(1, chips):
            place = half_c.at[chip, :, events(h)]
            copy = remote(
                place, place, fsend.at[h, k], frecv.at[h, k], {"mp": lax.rem(mine + 2 * k, mp)}
            )
            copy.start()
            copies_y.append(copy)
    n_steps = split_relay(dp, mp, n_slots, wsend.at[0], wrecv.at[0], True)
    b_steps = split_relay(dp, mp, b_slots, wsend.at[1], wrecv.at[1], True)
    for relay in (n_steps, b_steps):
        relay[0]()
        relay[1]()
    heads = pair_t.shape[2]
    by_head = jnp.transpose(pair_t[...].reshape(hx * 16, heads))
    row = lax.broadcasted_iota(jnp.int32, (h1, heads), 0)
    col = lax.broadcasted_iota(jnp.int32, (h1, heads), 1)
    repeat = jnp.where(row // hx == col, 1.0, 0.0)
    tall = jnp.dot(repeat, by_head, precision=lax.Precision.HIGHEST, preferred_element_type=jnp.float32)
    row = lax.broadcasted_iota(jnp.int32, (h1, 16), 0)
    pick = jnp.zeros((h1, 16), jnp.float32)
    for i in range(hx):
        pick = jnp.where(row % hx == i, tall[:, i * 16 : (i + 1) * 16], pick)
    for i in range(0, h1, 80):
        row = lax.broadcasted_iota(jnp.int32, (80, h2), 0) + i
        col = lax.broadcasted_iota(jnp.int32, (80, h2), 1)
        pieces = jnp.concatenate([pick[i : i + 80, :]] * heads, axis=1)
        spread = jnp.where(row // hx == col // 16, pieces, 0.0)
        high = low(spread)
        pair_hi[i : i + 80, :] = high
        pair_lo[i : i + 80, :] = low(spread - high.astype(jnp.float32))
    for h in range(2):
        for copy in copies_y[h * (chips - 1) : (h + 1) * (chips - 1)]:
            copy.wait_recv()
        total = half_c[0, :, events(h)].astype(jnp.float32)
        for k in range(1, chips):
            total = total + half_c[k, :, events(h)].astype(jnp.float32)
        pooled[part(core), events(h)] = low(total)
        place = pooled.at[part(core), events(h)]
        copy = remote(place, place, fsend.at[h, chips], frecv.at[h, chips], {"mp": other})
        copy.start()
        copies_b.append(copy)
    feat[:, :num] = numeric[...]
    started = []

    def flipped(bits):
        to = me
        for level in range(dp.bit_length() - 1):
            if bits >> level & 1:
                to = flip(to, level)
        return to

    def push(slot, *values):
        width = -(-values[0].shape[1] // 128) * 128
        for r, value in enumerate(values):
            sums[slot, me, r : r + 1, : value.shape[1]] = value
        out = []
        for step in range(dp - 1, 0, -1):
            at = sums.at[slot, me, :, pl.ds(0, width)]
            copy = remote(
                at, at, ssend.at[slot, step - 1], srecv.at[slot, step - 1], {"dp": flipped(step)}
            )
            copy.start()
            out.append(copy)
        started.append(out)
        return slot, width, out

    def pull(sent):
        slot, width, out = sent
        for copy in out:
            copy.wait_recv()
        total = sums[slot, 0, :, :width]
        for d in range(1, dp):
            total = total + sums[slot, d, :, :width]
        return total

    def norm(sent, width):
        total = pull(sent)
        mean = total[0:1, :width] / batch
        var = total[1:2, :width] / batch - mean * mean
        return mean, lax.rsqrt(var + 1e-05)

    def activate(y_ref, d_ref, u_ref, layer, at, mean, rstd, gain, shift):
        normed = (y_ref[layer, at, :] - mean) * rstd
        z = gain * normed + shift
        s = sigmoid(z)
        u = z * s
        y_ref[layer, at, :] = normed
        d_ref[layer, at, :] = s + u * (1.0 - s)
        u = low(u)
        u_ref[layer, at, :] = u
        return u

    def gain_n(layer):
        return vec[2 + layer : 3 + layer, :h1], vec[5 + layer : 6 + layer, :h1]

    def gain_b(layer):
        return vec[8 + layer : 9 + layer, :h2], vec[10 + layer : 11 + layer, :h2]

    zero1 = jnp.zeros((1, h1), jnp.float32)
    zero2 = jnp.zeros((1, h2), jnp.float32)

    def loop(body, *start):
        return lax.fori_loop(0, steps, lambda i, carry: body(rowset(i), *carry), tuple(start))

    def gated(k, at):
        x = feat[at, :]
        value = 2.0 * sigmoid(nt(x, gates[k][...]) + vec[k : k + 1, :wide])
        gate[k, at, :] = value
        x = low(x.astype(jnp.float32) * value)
        fields[k, at, :] = x
        return x

    def gates_and_first(at, a, b):
        y = nt(gated(0, at), n1[...])
        yn[0, at, :] = y
        return a + column_sum(y), b + column_sum(y * y)

    a, b = zero1, zero1
    for h in range(2):
        copies_b[h].wait_recv()
        at = events(h)
        feat[at, num:] = low(jnp.transpose(pooled[:, at].astype(jnp.float32)))
        a, b = gates_and_first(at, a, b)
    sent_n = push(0, a, b)

    def broad_first(at, a, b):
        y = nt(gated(1, at), b1[...])
        yb[0, at, :] = y
        return a + column_sum(y), b + column_sum(y * y)

    sent_b = push(1, *loop(broad_first, zero2, zero2))
    n_steps[2]()
    b_steps[2]()
    n_steps[3]()
    for m in range(mp):
        for k in range(2):
            n23[k, m * s1 : (m + 1) * s1, :] = n_slots[m, k]
    mean_n1, rstd_n1 = norm(sent_n, h1)

    def narrow_second(at, a, b):
        y = nt(activate(yn, dn, un, 0, at, mean_n1, rstd_n1, *gain_n(0)), n23[0])
        yn[1, at, :] = y
        return a + column_sum(y), b + column_sum(y * y)

    sent_n = push(2, *loop(narrow_second, zero1, zero1))
    b_steps[3]()
    for m in range(mp):
        for k in range(2):
            row = (2 * m + k) * (s2 // 2)
            b2[row : row + s2 // 2, :] = b_slots[m, k]
    mean_b1, rstd_b1 = norm(sent_b, h2)

    def broad_second(at, a, b):
        y = nt(activate(yb, db, ub, 0, at, mean_b1, rstd_b1, *gain_b(0)), b2[...])
        yb[1, at, :] = y
        return a + column_sum(y), b + column_sum(y * y)

    sent_b = push(3, *loop(broad_second, zero2, zero2))
    mean_n2, rstd_n2 = norm(sent_n, h1)

    def narrow_third(at, a, b):
        y = nt(activate(yn, dn, un, 1, at, mean_n2, rstd_n2, *gain_n(1)), n23[1])
        yn[2, at, :] = y
        return a + column_sum(y), b + column_sum(y * y)

    sent_n = push(4, *loop(narrow_third, zero1, zero1))
    label = jnp.transpose(jnp.broadcast_to(labels[...].astype(jnp.float32), (8, rows)))[:, 0:1]
    own_term[:, 0:1] = label
    pair_g[...] = jnp.zeros_like(pair_g)
    mean_b2, rstd_b2 = norm(sent_b, h2)

    def broad_out(at):
        second = activate(yb, db, ub, 1, at, mean_b2, rstd_b2, *gain_b(1))
        to_first[at, :] = left[...] + (nt(second, pair_hi[...]) + nt(second, pair_lo[...]))
        return ()

    loop(broad_out)
    mean_n3, rstd_n3 = norm(sent_n, h1)
    to_right = right[...].reshape(1, h2)

    def join_narrow(at, l_sum, g_sum, a, b):
        first = activate(yn, dn, un, 2, at, mean_n3, rstd_n3, *gain_n(2)).astype(jnp.float32)
        second = ub[1, at, :].astype(jnp.float32)
        logit = (
            jnp.sum(first * to_first[at, :], axis=1, keepdims=True)
            + jnp.sum(second * to_right, axis=1, keepdims=True)
            + bias[...]
        )
        g = sigmoid(logit) - own_term[at, 0:1]
        own_term[at, 1:2] = logit
        own_term[at, 2:3] = g
        gz = g * to_first[at, :] * dn[2, at, :]
        dn[2, at, :] = gz
        return (
            l_sum + column_sum(g * first), g_sum + column_sum(g),
            a + column_sum(gz), b + column_sum(gz * yn[2, at, :]),
        )

    l_sum, g_sum, a, b = loop(join_narrow, zero1, jnp.zeros((1, 1), jnp.float32), zero1, zero1)
    sent_n = push(5, a, b)

    def join_broad(at, r_sum, a, b):
        first = un[2, at, :]
        second = ub[1, at, :]
        g = own_term[at, 2:3]
        turned = nn(first, pair_hi[...]) + nn(first, pair_lo[...])
        pair_g[...] += tn(second, low(g * first.astype(jnp.float32)))
        gz = g * (to_right + turned) * db[1, at, :]
        db[1, at, :] = gz
        return (
            r_sum + column_sum(g * second.astype(jnp.float32)),
            a + column_sum(gz), b + column_sum(gz * yb[1, at, :]),
        )

    r_sum, a, b = loop(join_broad, zero2, zero2, zero2)
    sent_b = push(6, a, b)
    sums[10, me, 1:2, 512:513] = g_sum
    sent_join = push(10, r_sum, l_sum)
    logits[...] = jnp.transpose(own_term[:, 0:128])[1:2, :]

    def grad_y(gz, normed, rstd, gain, total):
        return low(gain * rstd * (gz - total[0:1] / batch - normed * (total[1:2] / batch)))

    main = a_work.shape[1]
    rest = h2 - main
    parts = main // rest
    tall_a = s2 + s1
    short = -(-tall_a // parts)
    a_work[...] = jnp.zeros_like(a_work)
    b_work[...] = jnp.zeros_like(b_work)
    size_a, size_b = a_work.shape[0], b_work.shape[0]
    folded = jnp.zeros((16, h1), jnp.float32)
    col = lax.broadcasted_iota(jnp.int32, (16, h1), 1)
    for h in range(heads):
        folded = folded + jnp.where(col // hx == h, pair_g[h * 16 : (h + 1) * 16, :], 0.0)
    b_work[size_b - 16 :, :h1] = low(folded)
    t_n3 = pull(sent_n)[:, :h1]

    def back_n3(at, a, b):
        g = grad_y(dn[2, at, :], yn[2, at, :], rstd_n3, gain_n(2)[0], t_n3)
        gyn[1, at, :] = g
        gz = nn(g, n23[1]) * dn[1, at, :]
        dn[1, at, :] = gz
        return a + column_sum(gz), b + column_sum(gz * yn[1, at, :])

    sent_n = push(7, *loop(back_n3, zero1, zero1))
    grad_n3 = weight_grad(gyn.at[1], un[1], own_cols, mine, s1, mp)
    t_b2 = pull(sent_b)[:, :h2]

    def back_b2(at, a, b):
        g = grad_y(db[1, at, :], yb[1, at, :], rstd_b2, gain_b(1)[0], t_b2)
        gyb[at, :] = g
        gz = nn(g, b2[...]) * db[0, at, :]
        db[0, at, :] = gz
        return a + column_sum(gz), b + column_sum(gz * yb[0, at, :])

    sent_b = push(8, *loop(back_b2, zero2, zero2))
    grad_b2 = weight_grad(gyb, ub[0], own_cols, mine, s2, mp)
    a_work[:s2, :] = grad_b2[:, :main]
    spill[:s2, :] = grad_b2[:, main:]
    t_n2 = pull(sent_n)[:, :h1]

    def back_n2(at, a, b):
        g = grad_y(dn[1, at, :], yn[1, at, :], rstd_n2, gain_n(1)[0], t_n2)
        gyn[0, at, :] = g
        gz = nn(g, n23[0]) * dn[0, at, :]
        dn[0, at, :] = gz
        return a + column_sum(gz), b + column_sum(gz * yn[0, at, :])

    sent_n = push(9, *loop(back_n2, zero1, zero1))
    grad_n2 = weight_grad(gyn.at[0], un[0], own_cols, mine, s1, mp)
    a_work[s2:tall_a, :] = jnp.concatenate([grad_n2, grad_n3], axis=1)[:, :main]
    spill[s2:tall_a, :] = jnp.concatenate([grad_n2, grad_n3], axis=1)[:, main:]
    for p in range(parts):
        n = min(short, tall_a - p * short)
        a_work[tall_a : tall_a + n, p * rest : (p + 1) * rest] = spill[p * short : p * short + n, :]
    copy_ax, start_a = give_half(me, 0, 0, size_a, a_work, a_land.at[pl.ds(0, size_a // 2), :], hsend.at[0], hrecv.at[0])
    t_b1 = pull(sent_b)[:, :h2]

    def gate_back(k, at, grad):
        x = feat[at, :].astype(jnp.float32)
        value = gate[k, at, :]
        g = low(grad * x * value * (1.0 - 0.5 * value))
        grad_gate[k, at, :] = g
        return grad * value, g

    def back_b1(at):
        g = grad_y(db[0, at, :], yb[0, at, :], rstd_b1, gain_b(0)[0], t_b1)
        gyb1[at, :] = g
        own_term[at, :] = gate_back(1, at, nn(g, b1[...]))[0]
        return ()

    loop(back_b1)
    b_work[:s2, :wide] = weight_grad(gyb1, fields[1], own_cols, mine, s2, mp)
    b_work[s2 : s2 + gcols, :wide] = weight_grad(grad_gate.at[1], feat[...], own_cols, mine, gcols, mp)
    copy_bx, start_b = give_half(me, 0, 0, size_b, b_work, b_land, hsend.at[2], hrecv.at[2])
    a_work[pl.ds(pl.multiple_of(start_a, 16), size_a // 2), :] = add_half(
        copy_ax, start_a, size_a // 2, a_work, a_land.at[pl.ds(0, size_a // 2), :]
    )
    copy_az, start_a = give_half(
        me, 1, start_a, size_a // 2, a_work, a_land.at[pl.ds(size_a // 2, size_a // 4), :], hsend.at[1], hrecv.at[1]
    )
    t_n1 = pull(sent_n)[:, :h1]

    def back_n1(at, ga, gb, ne):
        g = grad_y(dn[0, at, :], yn[0, at, :], rstd_n1, gain_n(0)[0], t_n1)
        gyn1[at, :] = g
        term, g0 = gate_back(0, at, nn(g, n1[...]))
        g1 = grad_gate[1, at, :]
        whole = nn(g0, gates[0][...]) + nn(g1, gates[1][...]) + term + own_term[at, :]
        whole = low(whole).astype(jnp.float32)
        own_term[at, :] = whole
        ne = ne + column_sum(whole[:, :num] * widen_dense(dense_t[:, at], 16))
        return ga + column_sum(g0.astype(jnp.float32)), gb + column_sum(g1.astype(jnp.float32)), ne

    zero_g = jnp.zeros((1, wide), jnp.float32)
    ga, gb, ne = loop(back_n1, zero_g, zero_g, jnp.zeros((1, num), jnp.float32))
    grads_t[...] = low(jnp.transpose(own_term[:, num:]))
    small[...] = jnp.zeros_like(small)
    small[0:1, :gcols] = own_columns(ga, mine, gcols, mp)
    small[1:2, :gcols] = own_columns(gb, mine, gcols, mp)
    small[2:3, :num] = ne
    for layer, t in enumerate((t_n1, t_n2, t_n3)):
        n_shift_g[layer : layer + 1, :] = own_columns(t[0:1], mine, s1, mp)
        n_gain_g[layer : layer + 1, :] = own_columns(t[1:2], mine, s1, mp)
    for layer, t in enumerate((t_b1, t_b2)):
        b_shift_g[layer : layer + 1, :] = own_columns(t[0:1], mine, s2, mp)
        b_gain_g[layer : layer + 1, :] = own_columns(t[1:2], mine, s2, mp)
    total = pull(sent_join)
    right_g[...] = total[0:1, :h2]
    left_g[...] = total[1:2, :h1]
    bias_g[...] = total[1:2, 512:513]
    a_out[...] = add_half(
        copy_az, start_a, size_a // 4, a_work, a_land.at[pl.ds(size_a // 2, size_a // 4), :]
    )
    b_out[...] = add_half(copy_bx, start_b, size_b // 2, b_work, b_land)
    for copy in [copy_ax, copy_az, copy_bx] + copies_a + copies_y + copies_b:
        copy.wait_send()
    for group in started:
        for copy in group:
            copy.wait_send()


def reduce_kernel(
    dp, mp,
    grads, feat, fields, grad_gate, gyn1, a_in, b_in, small,
    shares, a_full, b_full, c_full, small_out,
    t_work, t_land, t_slots, s_slots, a_work, a_land, b_work, b_land, c_work, c_land, c_slots, own_cols,
    tsend, trecv, ysend, yrecv, ssend, srecv, asend, arecv, bsend, brecv, csend, crecv,
):
    tall = grads.shape[0] // dp
    me, mine = lax.axis_index("dp"), lax.axis_index("mp")
    hail(dp, mp)
    levels = dp.bit_length() - 1
    far = dp // 2
    side, place = upper(me, 0), me // 2
    size_a, size_b, size_c = a_full.shape[0], b_full.shape[0], c_full.shape[0]
    s_slots[me] = small[...]
    pending = []
    all_in(dp, mp)

    def send_to(copy):
        copy.start()
        pending.append(copy)
        return copy

    def across(k):
        return {"dp": lax.rem(me + 2 * k, dp)}

    def rows_at(start, size):
        return pl.ds(pl.multiple_of(start, 16), size)

    half_t = grads.shape[0] // 2
    copy_t = send_to(
        remote(grads.at[rows_at((1 - side) * half_t, half_t), :], t_land, tsend.at[0], trecv.at[0], {"dp": flip(me, 0)})
    )
    start_a, start_b = 0, side * (size_b // 2)
    for level in range(2):
        start_a = start_a + upper(me, level) * (size_a >> (level + 1))
    a_work[...] = a_in[...]
    b_work[...] = b_in[...]

    def halves(name, level, work, land, size, sems, off):
        half = size // 2
        mine_up = upper(me, level)
        copy = send_to(
            remote(
                work.at[rows_at(off + (1 - mine_up) * half, half), :], land.at[pl.ds(0, half), :],
                sems[0].at[level], sems[1].at[level], {"dp": flip(me, level)},
            )
        )
        return copy, off + mine_up * half, half

    def fold(step, work, land):
        copy, off, half = step
        copy.wait_recv()
        at = rows_at(off, half)
        work[at, :] = low(work[at, :].astype(jnp.float32) + land[pl.ds(0, half), :].astype(jnp.float32))
        return off, half

    def double(level, full, start, size, sems):
        at = full.at[rows_at(start, size), :]
        copy = send_to(
            remote(at, at, sems[0].at[levels + level], sems[1].at[levels + level], {"dp": flip(me, level)})
        )
        return copy, start - upper(me, level) * size, size * 2

    sems_a, sems_b = (asend, arecv), (bsend, brecv)
    step_b = halves("b", 1, b_work, b_land.at[0], size_b // 2, sems_b, 0)
    step_a = halves("a", 2, a_work, a_land.at[0], size_a // 4, sems_a, 0) if levels > 2 else None
    gcols, s1 = feat.shape[1] // mp, gyn1.shape[1] // mp
    wide = feat.shape[1]
    c_work[...] = jnp.zeros_like(c_work)
    c_work[:gcols, :wide] = weight_grad(grad_gate.at[0], feat[...], own_cols, mine, gcols, mp)
    c_work[gcols : gcols + s1, :wide] = weight_grad(gyn1, fields[0], own_cols, mine, s1, mp)
    half_c = size_c // 2
    copy_c = send_to(
        remote(c_work.at[rows_at((1 - side) * half_c, half_c), :], c_land, csend.at[0], crecv.at[0], {"dp": flip(me, 0)})
    )
    small_copies = spread_dp(dp, lambda k: s_slots.at[k], ssend, srecv)

    def onward(back, level, full, sems):
        copy, start, size = back
        copy.wait_recv()
        return double(level, full, start, size, sems)

    off_b, held_b = fold(step_b, b_work, b_land.at[0])
    step_b = halves("b", 2, b_work, b_land.at[1], held_b, sems_b, off_b)
    off_a, held_a = fold(step_a, a_work, a_land.at[0])
    for level in range(3, levels):
        step_a = halves("a", level, a_work, a_land.at[level - 2], held_a, sems_a, off_a)
        off_a, held_a = fold(step_a, a_work, a_land.at[level - 2])
    start_a = start_a + off_a
    a_full[rows_at(start_a, held_a), :] = a_work[rows_at(off_a, held_a), :]
    back_a = double(levels - 1, a_full, start_a, held_a, sems_a)
    off_b, held_b = fold(step_b, b_work, b_land.at[1])
    for level in range(3, levels):
        step_b = halves("b", level, b_work, b_land.at[level - 1], held_b, sems_b, off_b)
        off_b, held_b = fold(step_b, b_work, b_land.at[level - 1])
    start_b = start_b + off_b
    b_full[rows_at(start_b, held_b), :] = b_work[rows_at(off_b, held_b), :]
    back_b = double(levels - 1, b_full, start_b, held_b, sems_b)
    for level in range(levels - 2, 0, -1):
        back_a = onward(back_a, level, a_full, sems_a)
    copy_t.wait_recv()
    at = rows_at(side * half_t, half_t)
    t_work[...] = low(grads[at, :].astype(jnp.float32) + t_land[...].astype(jnp.float32))
    t_copies = []
    for k in range(1, far):
        to = lax.rem(place + k, far)
        t_copies.append(
            send_to(
                remote(t_work.at[rows_at(to * tall, tall), :], t_slots.at[k - 1], tsend.at[k], trecv.at[k], across(k))
            )
        )
    copy_c.wait_recv()
    at = rows_at(side * half_c, half_c)
    c_work[at, :] = low(c_work[at, :].astype(jnp.float32) + c_land[...].astype(jnp.float32))
    piece = half_c // far
    c_copies = []
    for k in range(1, far):
        to = lax.rem(place + k, far)
        c_copies.append(
            send_to(
                remote(
                    c_work.at[rows_at(side * half_c + to * piece, piece), :], c_slots.at[k - 1],
                    csend.at[k], crecv.at[k], across(k),
                )
            )
        )
    for level in range(levels - 2, 0, -1):
        back_b = onward(back_b, level, b_full, sems_b)
    back_a = onward(back_a, 0, a_full, sems_a)
    own = rows_at(side * half_c + place * piece, piece)
    total = c_work[own, :].astype(jnp.float32)
    for k in range(1, far):
        c_copies[k - 1].wait_recv()
        total = total + c_slots[k - 1].astype(jnp.float32)
    c_full[own, :] = low(total)
    c_back = []
    for k in range(1, far):
        c_back.append(
            send_to(
                remote(c_full.at[own, :], c_full.at[own, :], csend.at[far + k], crecv.at[far + k], across(k))
            )
        )
    total = t_work[rows_at(place * tall, tall), :].astype(jnp.float32)
    for k in range(1, far):
        t_copies[k - 1].wait_recv()
        total = total + t_slots[k - 1].astype(jnp.float32)
    shares[mine] = low(total)
    started = relay_own(mp, lambda k: shares.at[k], ysend, yrecv)
    back_b = onward(back_b, 0, b_full, sems_b)
    for copy in c_back:
        copy.wait_recv()
    at = c_full.at[rows_at(side * half_c, half_c), :]
    last_c = send_to(remote(at, at, csend.at[far], crecv.at[far], {"dp": flip(me, 0)}))
    relay_rest(mp, lambda k: shares.at[k], ysend, yrecv, started)
    for copy in small_copies:
        copy.wait_recv()
    value = s_slots[0]
    for d in range(1, dp):
        value = value + s_slots[d]
    small_out[...] = value
    back_a[0].wait_recv()
    last_c.wait_recv()
    back_b[0].wait_recv()
    for copy in pending + small_copies:
        copy.wait_send()


def final_kernel(
    mp, hx, shares, a_full, b_full, c_full, small, logits_in, n_gain_in, n_shift_in, b_gain_in, b_shift_in,
    left_in, right_in, bias_in,
    logits, num_g, table_g, gate_g, gate_bias_g, n_first_g, n_rest_g, n_gain_g, n_shift_g,
    b_first_g, b_rest_g, b_gain_g, b_shift_g, left_g, right_g, pair_g, bias_g,
):
    gcols, s1, s2, h1 = gate_g.shape[0], n_first_g.shape[0], b_first_g.shape[0], n_rest_g.shape[2]
    wide = n_first_g.shape[1]

    def full(work, row, count, col, width):
        return work[row : row + count, col : col + width].astype(jnp.float32)

    blocks = shares.shape[1] // 16
    for m in range(mp):
        for b in range(blocks):
            table_g[:, (m * blocks + b) * HI : (m * blocks + b + 1) * HI] = shares[
                m, b * 16 : (b + 1) * 16, :
            ].astype(jnp.float32)
    gate_g[:, 0, :] = full(c_full, 0, gcols, 0, wide)
    gate_g[:, 1, :] = full(b_full, s2, gcols, 0, wide)
    n_first_g[...] = full(c_full, gcols, s1, 0, wide)
    b_first_g[...] = full(b_full, 0, s2, 0, wide)
    main = a_full.shape[1]
    rest = 2 * h1 - main
    parts = main // rest
    tall_a = s2 + s1
    short = -(-tall_a // parts)
    tail = jnp.concatenate(
        [
            full(a_full, tall_a, min(short, tall_a - p * short), p * rest, rest)
            for p in range(parts)
        ],
        axis=0,
    )
    b_rest_g[:, :main] = full(a_full, 0, s2, 0, main)
    b_rest_g[:, main:] = tail[:s2]
    both = jnp.concatenate([full(a_full, s2, s1, 0, main), tail[s2:]], axis=1)
    n_rest_g[:, 0, :] = both[:, :h1]
    n_rest_g[:, 1, :] = both[:, h1:]
    heads = pair_g.shape[2]
    pairs = b_full[b_full.shape[0] - 16 :, :h1]
    row = lax.broadcasted_iota(jnp.int32, (h1, heads), 0)
    col = lax.broadcasted_iota(jnp.int32, (h1, heads), 1)
    for i in range(hx):
        choose = jnp.where(row == col * hx + i, 1.0, 0.0).astype(jnp.bfloat16)
        pair_g[i] = nn(pairs, choose)
    fields, width = num_g.shape
    gate_bias_g[...] = small[0:2, :gcols]
    spread = jnp.broadcast_to(small[2:3, : fields * width], (fields, fields * width))
    row = lax.broadcasted_iota(jnp.int32, spread.shape, 0)
    col = lax.broadcasted_iota(jnp.int32, spread.shape, 1)
    spread = jnp.where(col // width == row, spread, 0.0)
    total = spread[:, :width]
    for i in range(1, fields):
        total = total + spread[:, i * width : (i + 1) * width]
    num_g[...] = total
    logits[...] = logits_in[...]
    n_gain_g[...] = n_gain_in[...]
    n_shift_g[...] = n_shift_in[...]
    b_gain_g[...] = b_gain_in[...]
    b_shift_g[...] = b_shift_in[...]
    left_g[...] = left_in[...]
    right_g[...] = right_in[...].reshape(right_g.shape)
    bias_g[...] = bias_in[...]


def f32(*shape):
    return jax.ShapeDtypeStruct(shape, jnp.float32)


def b16(*shape):
    return jax.ShapeDtypeStruct(shape, jnp.bfloat16)


def held(*shape):
    return pltpu.VMEM(shape, jnp.float32)


def held16(*shape):
    return pltpu.VMEM(shape, jnp.bfloat16)


def dma(*shape):
    return pltpu.SemaphoreType.DMA(shape)


def shards(
    dense_values,
    field_ids,
    lengths,
    labels,
    num_embed,
    embed_table,
    gate_weight,
    gate_bias,
    narrow_first,
    narrow_rest,
    narrow_gain,
    narrow_shift,
    broad_first,
    broad_rest,
    broad_gain,
    broad_shift,
    joining_left,
    joining_right,
    joining_pair,
    joining_bias,
):
    dp, mp = lax.axis_size("dp"), lax.axis_size("mp")
    chips = mp // 2
    rows = dense_values.shape[0]
    cats, slots = field_ids.shape[:2]
    width, own_rows = embed_table.shape
    num = dense_values.shape[1] * width
    wide = gate_weight.shape[2]
    gcols = gate_weight.shape[1]
    s1, s2 = narrow_first.shape[0], broad_first.shape[0]
    h1, h2 = s1 * mp, s2 * mp
    hx = joining_pair.shape[1]
    bits = (cats * rows - 1).bit_length()
    dense_t = dense_values.T
    tall = own_rows // mp // HI * 16
    vregs = -(-(cats * slots * rows) // (2 * CHUNK)) * (2 * CHUNK) // 1024
    first_args = (
        embed_table, jnp.transpose(gate_weight, (1, 0, 2)), narrow_first, gate_bias,
        narrow_gain, narrow_shift, broad_gain, broad_shift, broad_first,
        field_ids, lengths, dense_t, num_embed, jnp.transpose(narrow_rest, (1, 0, 2)), broad_rest,
    )
    t2, keys, numeric, weights, vec, n_next, b_next = pl.pallas_call(
        functools.partial(first_kernel, dp, mp, own_rows, bits),
        out_shape=(
            b16(dp * tall, HI),
            jax.ShapeDtypeStruct((2, vregs * 8, 128), jnp.int32),
            b16(rows, num),
            b16(2 * wide + h1 + h2, wide),
            f32(16, 896),
            b16(mp, 2, s1, h1),
            b16(mp, 2, s2 // 2, h2),
        ),
        in_specs=[ANY] * 15,
        out_specs=(VM,) * 7,
        scratch_shapes=[pltpu.VMEM(x.shape, x.dtype) for x in first_args]
        + [
            pltpu.VMEM((vregs * 8, 128), jnp.int32),
            held16(mp, gcols, wide),
            held16(mp, 2, gcols // 2, wide),
            held16(mp, 2, s1 // 2, wide),
            held16(mp, 2, s2 // 2, wide),
            held(mp, 16, 256),
            dma(dp - 1),
            dma(dp - 1),
            dma(2, mp),
            dma(2, mp),
            dma(3, 4 * chips),
            dma(3, 4 * chips),
            dma(2, 4 * chips),
            dma(2, 4 * chips),
            dma(15),
        ],
        compiler_params=params(0, 54),
        name="first",
    )(*first_args)
    partial = pl.pallas_call(
        functools.partial(lookup_kernel, cats, rows, bits),
        out_shape=f32(cats * 16, rows),
        in_specs=[VM] * 2,
        out_specs=VM,
        scratch_shapes=[held((cats + WINDOW) * 16, rows)],
        compiler_params=params(None, 16),
        cost_estimate=pl.CostEstimate(flops=8 * 10**9, bytes_accessed=2 * 10**6, transcendentals=0),
        name="lookup",
    )(keys, t2)

    def up(x, n):
        return -(-x // n) * n

    main = wide // 128 * 128 + 128
    short = -(-(s1 + s2) // (main // (h2 - main)))
    a_rows = up(s1 + s2 + short, 16 * dp)
    b_rows = up(s2 + gcols, 16) + 16
    b_rows = up(b_rows, 16 * dp)
    c_rows = up(gcols + s1, 16 * dp)
    levels = dp.bit_length() - 1
    dense_args = (
        joining_left.reshape(1, h1), joining_right,
        jnp.transpose(joining_pair, (1, 2, 0)), joining_bias.reshape(1, 1), labels.reshape(1, rows), dense_t,
    )
    (
        logits, grads_t, feat, fields, grad_gate, gyn1, a_part, b_part, small,
        n_gain_g, n_shift_g, b_gain_g, b_shift_g, left_g, right_g, bias_g,
    ) = pl.pallas_call(
        functools.partial(dense_kernel, dp, mp, hx, float(rows * dp)),
        out_shape=(
            f32(1, rows),
            b16(cats * 16, rows),
            b16(rows, wide),
            b16(2, rows, wide),
            b16(2, rows, wide),
            b16(rows, h1),
            b16(a_rows // 4, main),
            b16(b_rows // 2, main),
            f32(8, 256),
            f32(3, s1),
            f32(3, s1),
            f32(2, s2),
            f32(2, s2),
            f32(1, h1),
            f32(1, h2),
            f32(1, 1),
        ),
        in_specs=[VM] * 6 + [ANY] * 6,
        out_specs=(VM,) * 16,
        scratch_shapes=[
            held(cats * 8, rows),
            held16(chips, cats * 8, rows),
            held16(cats * 16, rows),
            held(2, rows, wide),
            held(rows, wide),
            held16(mp, 2, s1, h1),
            held16(mp, 2, s2 // 2, h2),
            held16(2, h1, h1),
            held16(h2, h2),
            held(3, rows, h1),
            held(3, rows, h1),
            held(2, rows, h2),
            held(2, rows, h2),
            held16(3, rows, h1),
            held16(2, rows, h2),
            held16(2, rows, h1),
            held16(rows, h2),
            held16(h1, h2),
            held16(h1, h2),
            held(h2, h1),
            held(rows, h1),
            held(11, dp, 2, 896),
            held16(s1 + s2, h2 - main),
            dma(2, chips + 1),
            dma(2, chips + 1),
            dma(2, 4 * chips),
            dma(2, 4 * chips),
            dma(11, dp - 1),
            dma(11, dp - 1),
            held16(rows, h2),
            held16(a_rows, main),
            held16(b_rows, main),
            held16(a_rows * 3 // 4, main),
            held16(b_rows // 2, main),
            dma(3),
            dma(3),
            held16(rows, up(max(gcols, s1, s2), 128)),
        ]
        + [pltpu.VMEM(x.shape, x.dtype) for x in dense_args]
        + [dma(6)],
        compiler_params=params(1, 39 + dp // 16),
        name="dense",
    )(partial, numeric, weights, n_next, b_next, vec, *dense_args)
    row_sums = pl.pallas_call(
        functools.partial(scatter_kernel, cats, rows, bits),
        out_shape=b16(dp * tall, HI),
        in_specs=[VM] * 2,
        out_specs=VM,
        scratch_shapes=[held(dp * tall, HI), held16((cats + WINDOW_BACK) * 16, rows)],
        compiler_params=params(None, 16),
        cost_estimate=pl.CostEstimate(flops=8 * 10**9, bytes_accessed=2 * 10**6, transcendentals=0),
        name="scatter",
    )(keys, grads_t)
    shares, a_full, b_full, c_full, small = pl.pallas_call(
        functools.partial(reduce_kernel, dp, mp),
        out_shape=(
            b16(mp, tall, HI),
            b16(a_rows, main),
            b16(b_rows, main),
            b16(c_rows, main),
            f32(8, 256),
        ),
        in_specs=[VM] * 8,
        out_specs=(VM,) * 5,
        scratch_shapes=[
            held16(dp // 2 * tall, HI),
            held16(dp // 2 * tall, HI),
            held16(dp // 2 - 1, tall, HI),
            held(dp, 8, 256),
            held16(a_rows // 4, main),
            held16(max(levels - 2, 1), a_rows // 8, main),
            held16(b_rows // 2, main),
            held16(max(levels - 1, 1), b_rows // 4, main),
            held16(c_rows, main),
            held16(c_rows // 2, main),
            held16(dp // 2 - 1, c_rows // dp, main),
            held16(rows, up(max(gcols, s1, s2), 128)),
            dma(dp // 2),
            dma(dp // 2),
            dma(mp),
            dma(mp),
            dma(dp - 1),
            dma(dp - 1),
            dma(2 * levels),
            dma(2 * levels),
            dma(2 * levels),
            dma(2 * levels),
            dma(dp),
            dma(dp),
        ],
        compiler_params=params(2, 24),
        name="reduce",
    )(row_sums, feat, fields, grad_gate, gyn1, a_part, b_part, small)
    outs = pl.pallas_call(
        functools.partial(final_kernel, mp, hx),
        out_shape=(
            f32(1, rows),
            f32(*num_embed.shape),
            f32(width, own_rows),
            f32(gcols, 2, wide),
            f32(2, gcols),
            f32(s1, wide),
            f32(s1, 2, h1),
            f32(3, s1),
            f32(3, s1),
            f32(s2, wide),
            f32(s2, h2),
            f32(2, s2),
            f32(2, s2),
            f32(1, h1),
            f32(h2),
            f32(hx, width, joining_pair.shape[0]),
            f32(1, 1),
        ),
        in_specs=[VM] * 13,
        out_specs=(VM,) * 17,
        compiler_params=params(None, 16),
        name="final",
    )(
        shares, a_full, b_full, c_full, small, logits, n_gain_g, n_shift_g, b_gain_g, b_shift_g,
        left_g, right_g, bias_g,
    )
    outs = list(outs)
    outs[0] = outs[0].reshape(rows)
    outs[3] = jnp.transpose(outs[3], (1, 0, 2))
    outs[6] = jnp.transpose(outs[6], (1, 0, 2))
    outs[13] = outs[13].reshape(h1)
    outs[15] = jnp.transpose(outs[15], (2, 0, 1))
    outs[16] = outs[16].reshape(1)
    return tuple(outs)


def solution(mesh):
    placed = (
        P("dp", None),
        P(None, None, "dp"),
        P(None, "dp"),
        P("dp"),
        P(),
        P(None, "dp"),
        P(None, "mp", None),
        P(None, "mp"),
        P("mp", None),
        P(None, "mp", None),
        P(None, "mp"),
        P(None, "mp"),
        P("mp", None),
        P("mp", None),
        P(None, "mp"),
        P(None, "mp"),
        P(),
        P(),
        P(),
        P(),
    )
    return jax.shard_map(
        shards,
        mesh=mesh,
        in_specs=placed,
        out_specs=(
            P("dp"),
            P(),
            P(None, "dp"),
            P(None, "mp", None),
            P(None, "mp"),
            P("mp", None),
            P(None, "mp", None),
            P(None, "mp"),
            P(None, "mp"),
            P("mp", None),
            P("mp", None),
            P(None, "mp"),
            P(None, "mp"),
            P(),
            P(),
            P(),
            P(),
        ),
        check_vma=False,
    )
```

```python
import functools
import jax
import jax.numpy as jnp
from jax import lax
from jax.experimental import pallas as pl
from jax.experimental.pallas import tpu as pltpu
from jax.sharding import PartitionSpec as P

MESH = pl.DeviceIdType.MESH
VM = pl.BlockSpec(memory_space=pltpu.VMEM)
ANY = pl.BlockSpec(memory_space=pltpu.HBM)
HI = 256
CHUNK = 1024


def params(cid, mib=48):
    if cid is None:
        return pltpu.CompilerParams(vmem_limit_bytes=mib << 20)
    return pltpu.CompilerParams(
        collective_id=cid, has_side_effects=True, vmem_limit_bytes=mib << 20
    )


def hail(dp, mp):
    me, mine = lax.axis_index("dp"), lax.axis_index("mp")
    barrier = pltpu.get_barrier_semaphore()
    for step in range(1, dp):
        pl.semaphore_signal(
            barrier, inc=1, device_id={"dp": lax.rem(me + step, dp)}, device_id_type=MESH
        )
    for step in range(1, mp):
        pl.semaphore_signal(
            barrier, inc=1, device_id={"mp": lax.rem(mine + step, mp)}, device_id_type=MESH
        )


def all_in(dp, mp):
    pl.semaphore_wait(pltpu.get_barrier_semaphore(), dp - 1 + mp - 1)


def remote(src, dst, send, recv, where):
    return pltpu.make_async_remote_copy(
        src_ref=src, dst_ref=dst, send_sem=send, recv_sem=recv,
        device_id=where, device_id_type=MESH,
    )


def spread_dp(dp, pick, send, recv):
    me = lax.axis_index("dp")
    out = []
    for step in range(1, dp):
        to = lax.rem(me + step, dp)
        copy = remote(pick(me), pick(me), send.at[step - 1], recv.at[step - 1], {"dp": to})
        copy.start()
        out.append(copy)
    return out


def over(x, n):
    if n & (n - 1) == 0:
        return lax.shift_right_logical(x, n.bit_length() - 1)
    return x // n


def compact_keys(key):
    count = key.shape[0]
    rows = count * 8
    dead = jnp.where(key.reshape(rows, 128) < 0, 1.0, 0.0).astype(jnp.bfloat16)
    row = lax.broadcasted_iota(jnp.int32, (128, 128), 0)
    col = lax.broadcasted_iota(jnp.int32, (128, 128), 1)
    in_row = jnp.dot(dead, jnp.where(row < col, 1.0, 0.0).astype(jnp.bfloat16), preferred_element_type=jnp.float32)
    row_sum = jnp.dot(dead, jnp.ones((128, 128), jnp.bfloat16), preferred_element_type=jnp.float32)
    row = lax.broadcasted_iota(jnp.int32, (rows, rows), 0)
    col = lax.broadcasted_iota(jnp.int32, (rows, rows), 1)
    above = jnp.where(col < row, 1.0, 0.0).astype(jnp.bfloat16)
    before = jnp.dot(above, row_sum.astype(jnp.bfloat16), preferred_element_type=jnp.float32)
    shift = (in_row + before).astype(jnp.int32).reshape(count, 8, 128)
    shift = jnp.where(key < 0, 0, shift)
    sub = lax.broadcasted_iota(jnp.int32, (8, 128), 0)
    lane = lax.broadcasted_iota(jnp.int32, (8, 128), 1)

    def rows_up(x, j):
        t = [pltpu.roll(x[v], 8 - j, 0) for v in range(count)]
        return jnp.stack([jnp.where(sub < 8 - j, t[v], t[(v + 1) % count]) for v in range(count)])

    bit = 0
    for j in (1, 2, 4, 8, 16, 32, 64):
        def lanes_up(x):
            y = jnp.stack([pltpu.roll(x[v], 128 - j, 1) for v in range(count)])
            return jnp.where(lane[None] < 128 - j, y, rows_up(y, 1))
        key, shift = settle(key, shift, lanes_up(key), lanes_up(shift), bit)
        bit += 1
    for j in (1, 2, 4):
        key, shift = settle(key, shift, rows_up(key, j), rows_up(shift, j), bit)
        bit += 1
    step = 1
    while step < count:
        moved_key = jnp.concatenate([key[step:], key[:step]], axis=0)
        moved_shift = jnp.concatenate([shift[step:], shift[:step]], axis=0)
        key, shift = settle(key, shift, moved_key, moved_shift, bit)
        bit, step = bit + 1, step * 2
    return key


def settle(key, shift, moved_key, moved_shift, bit):
    take = (moved_shift & (1 << bit)) != 0
    stay = (shift & (1 << bit)) == 0
    key = jnp.where(take, moved_key, jnp.where(stay, key, -1))
    shift = jnp.where(take, moved_shift, jnp.where(stay, shift, 0))
    return key, shift


def seat(i, dp):
    return i % 2 * (dp // 2) + i // 2


def make_keys(ids, lens, scratch, own_rows, dp, mp, bits):
    cats, slots, rows = ids.shape
    part = own_rows // mp
    mine = lax.axis_index("mp")
    scratch[...] = jnp.full_like(scratch, -1)
    slot = lax.broadcasted_iota(jnp.int32, (slots, rows), 0)
    event = lax.broadcasted_iota(jnp.int32, (slots, rows), 1)

    def body(c, carry):
        values = ids[c]
        holder = values // own_rows
        inner = values - holder * own_rows
        owner = inner // part
        place = seat(holder, dp) * part + inner - owner * part
        live = (slot < lens[pl.ds(c, 1), :]) & (owner == mine)
        key = jnp.where(live, place * (1 << bits) + c * rows + event, -1)
        for q in range(rows // 128):
            scratch[pl.ds((c * (rows // 128) + q) * slots, slots), :] = key[:, q * 128 : (q + 1) * 128]
        return carry

    lax.fori_loop(0, cats, body, 0)


WINDOW = 16
WINDOW_BACK = 12


def chunk_parts(key, rows, bits):
    place = lax.shift_right_arithmetic(key, bits)
    bag = key & ((1 << bits) - 1)
    cat = over(bag, rows)
    return place, cat, bag - cat * rows


def short(row):
    return jnp.broadcast_to(row, (16, row.shape[1])).astype(jnp.int16)


def one_hot(row, size):
    apart = short(row) - lax.broadcasted_iota(jnp.int32, (16, row.shape[1]), 0).astype(jnp.int16)
    one = jnp.ones(apart.shape, jnp.bfloat16)
    zero = jnp.zeros(apart.shape, jnp.bfloat16)
    return jnp.concatenate([jnp.where(apart == i, one, zero) for i in range(0, size, 16)], axis=0)


def spread_rows(row, values, first, size):
    zero = jnp.zeros_like(values)
    apart = short(row - first)
    return jnp.concatenate([jnp.where(apart == i, values, zero) for i in range(size)], axis=0)


def chunk_key(keys, half, k):
    tall = CHUNK // 128
    key = keys[half, pl.ds(pl.multiple_of(k * tall, tall), tall), :]
    return jnp.concatenate([key[i : i + 1, :] for i in range(tall)], axis=1)


def chunk_span(keys, half, k, cats, rows, bits, window):
    tall = CHUNK // 128
    most = keys.shape[1] // tall - 1
    key = keys[half, pl.ds(pl.multiple_of(jnp.minimum(k, most) * tall, tall), tall), :]
    cat = over(key & ((1 << bits) - 1), rows)
    first = jnp.min(jnp.where(key >= 0, cat, cats - 1))
    last = jnp.max(jnp.where(key >= 0, cat, 0))
    return first, (last - first) // window + 1


def each_chunk(keys, half, cats, rows, bits, window, body):
    live = jnp.sum((keys[half] >= 0).astype(jnp.int32))
    chunks = (live + CHUNK - 1) // CHUNK

    def step(k, carry):
        later = chunk_span(keys, half, k + 1, cats, rows, bits, window)
        body(chunk_key(keys, half, k), *carry)
        return later

    lax.fori_loop(0, chunks, step, chunk_span(keys, half, 0, cats, rows, bits, window))


def lookup_kernel(cats, rows, bits, keys, t2, pooled, total):
    lows = t2.shape[0] // 32
    total[...] = jnp.zeros_like(total)

    def half_table(half, carry):
        def body(key, first, windows):
            place, cat, event = chunk_parts(key, rows, bits)
            low = jnp.broadcast_to(lax.shift_right_arithmetic(place, 8) - half * lows, (16, CHUNK))
            pick = one_hot(place & (HI - 1), HI)
            z = jnp.zeros((16, CHUNK), jnp.float32)
            for b in range(0, lows, 32):
                n = min(32, lows - b)
                at = pl.ds(pl.multiple_of((half * lows + b) * 16, 16), n * 16)
                y = jnp.dot(t2[at, :], pick, preferred_element_type=jnp.float32)
                for j in range(n):
                    z = z + jnp.where(low == b + j, y[j * 16 : (j + 1) * 16], 0.0)
            z = z.astype(jnp.bfloat16)
            cat = jnp.where(key >= 0, cat, -1)
            place_of = one_hot(event, rows)

            def window(w):
                start = first + w * WINDOW
                at = pl.ds(pl.multiple_of(start * 16, 16), WINDOW * 16)
                total[at, :] += lax.dot_general(
                    spread_rows(cat, z, start, WINDOW), place_of, (((1,), (1,)), ((), ())),
                    preferred_element_type=jnp.float32,
                )

            window(0)

            def more(w, carry):
                window(w)
                return carry

            lax.fori_loop(1, windows, more, 0)

        each_chunk(keys, half, cats, rows, bits, WINDOW, body)
        return carry

    lax.fori_loop(0, 2, half_table, 0)
    pooled[...] = total[: cats * 16, :].astype(pooled.dtype)


def scatter_kernel(cats, rows, bits, keys, grad, out, total, grad_pad):
    lows = total.shape[0] // 32
    total[...] = jnp.zeros_like(total)
    grad_pad[: cats * 16, :] = grad[...]
    grad_pad[cats * 16 :, :] = jnp.zeros((WINDOW_BACK * 16, rows), jnp.bfloat16)

    def half_table(half, carry):
        def body(key, first, windows):
            place, cat, event = chunk_parts(key, rows, bits)
            low = lax.shift_right_arithmetic(place, 8) - half * lows
            pick = one_hot(place & (HI - 1), HI)
            place_of = one_hot(event, rows)
            cat = jnp.broadcast_to(jnp.where(key >= 0, cat, -1), (16, CHUNK))

            def window(w, g):
                start = first + w * WINDOW_BACK
                at = pl.ds(pl.multiple_of(start * 16, 16), WINDOW_BACK * 16)
                wide = jnp.dot(grad_pad[at, :], place_of, preferred_element_type=jnp.float32)
                for c in range(WINDOW_BACK):
                    g = g + jnp.where(cat == start + c, wide[c * 16 : (c + 1) * 16], 0.0)
                return g

            g = window(0, jnp.zeros((16, CHUNK), jnp.float32))
            g = lax.fori_loop(1, windows, window, g).astype(jnp.bfloat16)
            for b in range(0, lows, 32):
                n = min(32, lows - b)
                at = pl.ds(pl.multiple_of((half * lows + b) * 16, 16), n * 16)
                total[at, :] += lax.dot_general(
                    spread_rows(low, g, b, n), pick, (((1,), (1,)), ((), ())),
                    preferred_element_type=jnp.float32,
                )

        each_chunk(keys, half, cats, rows, bits, WINDOW_BACK, body)
        return carry

    lax.fori_loop(0, 2, half_table, 0)
    out[...] = total[...].astype(out.dtype)


def relay_own(mp, slot, send, recv):
    mine = lax.axis_index("mp")
    core = lax.rem(mine, 2)
    other = mine + 1 - 2 * core
    chips = mp // 2
    out = []
    for k in range(1, chips):
        to = lax.rem(mine + 2 * k, mp)
        copy = remote(slot(mine), slot(mine), send.at[2 * k], recv.at[2 * k], {"mp": to})
        copy.start()
        out.append(copy)
    copy = remote(slot(mine), slot(mine), send.at[1], recv.at[1], {"mp": other})
    copy.start()
    out.append(copy)
    return out


def relay_rest(mp, slot, send, recv, started):
    mine = lax.axis_index("mp")
    core = lax.rem(mine, 2)
    other = mine + 1 - 2 * core
    chips = mp // 2
    passed = []
    for k in range(1, chips):
        source = lax.rem(mine + mp - 2 * k, mp)
        remote(slot(source), slot(source), send.at[2 * k], recv.at[2 * k], {"mp": other}).wait_recv()
        copy = remote(slot(source), slot(source), send.at[2 * k + 1], recv.at[2 * k + 1], {"mp": other})
        copy.start()
        passed.append(copy)
    remote(slot(other), slot(other), send.at[1], recv.at[1], {"mp": other}).wait_recv()
    for k in range(1, chips):
        far = lax.rem(other + mp - 2 * k, mp)
        remote(slot(far), slot(far), send.at[2 * k + 1], recv.at[2 * k + 1], {"mp": other}).wait_recv()
    for copy in started + passed:
        copy.wait_send()


def nn(a, b):
    return jnp.dot(a, b, preferred_element_type=jnp.float32)


def nt(a, b):
    return lax.dot_general(a, b, (((1,), (1,)), ((), ())), preferred_element_type=jnp.float32)


def tn(a, b):
    return lax.dot_general(a, b, (((0,), (0,)), ((), ())), preferred_element_type=jnp.float32)


def sigmoid(x):
    return 0.5 * jnp.tanh(0.5 * x) + 0.5


def low(x):
    return x.astype(jnp.bfloat16)


def column_sum(x):
    return jnp.sum(x, axis=0, keepdims=True)


def widen_dense(dense_t, width):
    fields = dense_t.shape[0]
    row = lax.broadcasted_iota(jnp.int32, (fields, fields * width), 0)
    col = lax.broadcasted_iota(jnp.int32, (fields, fields * width), 1)
    ones = jnp.where(col // width == row, 1.0, 0.0)
    return lax.dot_general(
        dense_t, ones, (((0,), (0,)), ((), ())),
        precision=lax.Precision.HIGHEST, preferred_element_type=jnp.float32,
    )


def split_relay(dp, mp, ref, send, recv, fetched=False):
    me, mine = lax.axis_index("dp"), lax.axis_index("mp")
    other = mine + 1 - 2 * lax.rem(mine, 2)
    chips = mp // 2
    near = lax.rem(me, 2)
    beside = {"dp": me + 1 - 2 * near}
    started = []

    def move(place, i, where):
        return remote(place, place, send.at[i], recv.at[i], where)

    def go(place, i, where):
        copy = move(place, i, where)
        copy.start()
        started.append(copy)

    def source(k):
        return lax.rem(mine + mp - 2 * k, mp)

    def begin():
        if not fetched:
            fetch()
        go(ref.at[mine], 0, {"mp": other})

    def fetch():
        for k in range(1, chips):
            go(ref.at[mine, near], k, {"mp": lax.rem(mine + 2 * k, mp)})

    def arrive():
        for k in range(1, chips):
            move(ref.at[source(k), near], k, beside).wait_recv()
        for copy in started:
            copy.wait_send()

    def middle():
        for k in range(1, chips):
            place = ref.at[source(k), near]
            if not fetched:
                move(place, k, beside).wait_recv()
            go(place, 2 * chips + k, beside)
            go(place, chips + k, {"mp": other})

    def later():
        for k in range(1, chips):
            place = ref.at[source(k), 1 - near]
            move(place, 2 * chips + k, beside).wait_recv()
            go(place, 3 * chips + k, {"mp": other})

    def end():
        move(ref.at[other], 0, beside).wait_recv()
        for k in range(1, chips):
            far = lax.rem(other + mp - 2 * k, mp)
            move(ref.at[far, near], chips + k, beside).wait_recv()
            move(ref.at[far, 1 - near], 3 * chips + k, beside).wait_recv()
        for copy in started:
            copy.wait_send()

    return begin, middle, later, end, fetch, arrive


def bring(sources, places, sem):
    copies = []
    for i, (source, place) in enumerate(zip(sources, places)):
        copy = pltpu.make_async_copy(source, place, sem.at[i])
        copy.start()
        copies.append(copy)
    return copies


def first_kernel(dp, mp, own_rows, bits, *refs):
    count = 15
    sources, refs = refs[:count], refs[count:]
    t2, keys, numeric, weights, vec, n_next, b_next = refs[:7]
    places, refs = refs[7 : 7 + count], refs[7 + count :]
    (
        scratch, gate_slots, g_slots, n_slots, b_slots, v_slots,
        send, recv, send2, recv2, send3, recv3, send4, recv4, sem,
    ) = refs
    brought = bring(sources, places, sem)
    (
        table, gate_w, n_first, gate_b, n_gain, n_shift, b_gain, b_shift, b_first,
        ids, lens, dense_t, num_embed, n_rest, b_rest,
    ) = places
    part = own_rows // mp
    blocks = part // HI
    tall = blocks * 16
    me, mine = lax.axis_index("dp"), lax.axis_index("mp")
    hail(dp, mp)
    for copy in brought[:9]:
        copy.wait()
    own = table[:, pl.ds(pl.multiple_of(mine * part, HI), part)].astype(jnp.bfloat16)
    for b in range(blocks):
        t2[pl.ds(pl.multiple_of(seat(me, dp) * tall + b * 16, 16), 16), :] = own[:, b * HI : (b + 1) * HI]
    gate_slots[mine] = gate_w[:, 0, :]
    second = gate_w[:, 1, :]
    cols = g_slots.shape[2]
    for k in range(2):
        g_slots[mine, k] = second[k * cols : (k + 1) * cols, :]
    small, large = n_slots.shape[2], b_slots.shape[2]
    for k in range(2):
        n_slots[mine, k] = n_first[k * small : (k + 1) * small, :]
        b_slots[mine, k] = b_first[k * large : (k + 1) * large, :]
    row = 0
    for ref in (gate_b, n_gain, n_shift, b_gain, b_shift):
        v_slots[mine, row : row + ref.shape[0], : ref.shape[1]] = ref[...]
        row += ref.shape[0]
    all_in(dp, mp)

    def slot(i):
        return t2.at[pl.ds(pl.multiple_of(seat(i, dp) * tall, 16), tall), :]

    pairs = [
        split_relay(dp, mp, ref, send3.at[i], recv3.at[i]) for i, ref in enumerate((g_slots, n_slots, b_slots))
    ]
    for steps in pairs:
        steps[0]()
    groups = []
    for i, ref in enumerate((gate_slots, v_slots)):
        started = relay_own(mp, lambda k, ref=ref: ref.at[k], send2.at[i], recv2.at[i])
        groups.append((ref, i, started))
    copies = spread_dp(dp, slot, send, recv)
    for copy in brought[9:]:
        copy.wait()
    half_b = b_next.shape[2]
    for k in range(2):
        n_next[mine, k] = n_rest[:, k, :]
        b_next[mine, k] = b_rest[k * half_b : (k + 1) * half_b, :]
    fields, width = num_embed.shape
    tiled = jnp.concatenate([num_embed[...]] * fields, axis=1)
    row = lax.broadcasted_iota(jnp.int32, tiled.shape, 0)
    col = lax.broadcasted_iota(jnp.int32, tiled.shape, 1)
    num_row = column_sum(jnp.where(col // width == row, tiled, 0.0))
    numeric[...] = low(widen_dense(dense_t[...], width) * num_row)
    make_keys(ids, lens, scratch, own_rows, dp, mp, bits)
    count = scratch.shape[0] // 8
    middle = (dp * part // 2) << bits

    def pack(half, carry):
        key = scratch[...]
        key = jnp.where((key < middle) == (half == 0), key, -1)
        keys[half] = compact_keys(key.reshape(count, 8, 128)).reshape(count * 8, 128)
        return carry

    lax.fori_loop(0, 2, pack, 0)
    for steps in pairs:
        steps[1]()
    nexts = [
        split_relay(dp, mp, ref, send4.at[i], recv4.at[i]) for i, ref in enumerate((n_next, b_next))
    ]
    for steps in nexts:
        steps[4]()
    for ref, i, started in groups:
        relay_rest(mp, lambda k, ref=ref: ref.at[k], send2.at[i], recv2.at[i], started)
    cols, wide = gate_slots.shape[1:]
    for m in range(mp):
        weights[m * cols : (m + 1) * cols, :] = gate_slots[m]
    for steps in pairs:
        steps[2]()
    row = wide
    for ref, steps in zip((g_slots, n_slots, b_slots), pairs):
        steps[3]()
        tall = ref.shape[2]
        for m in range(mp):
            for k in range(2):
                weights[row : row + tall, :] = ref[m, k]
                row += tall
    row = 0
    for ref in (gate_b, n_gain, n_shift, b_gain, b_shift):
        r, w = ref.shape
        vec[row : row + r, : mp * w] = jnp.concatenate(
            [v_slots[m, row : row + r, :w] for m in range(mp)], axis=1
        )
        row += r
    for steps in nexts:
        steps[5]()
    for copy in copies:
        copy.wait()


def own_columns(x, mine, width, mp):
    out = jnp.zeros((x.shape[0], width), x.dtype)
    for m in range(mp):
        out = jnp.where(mine == m, x[:, m * width : (m + 1) * width], out)
    return out


def up16(x):
    return -(-x // 16) * 16


def weight_grad(grad_y, inputs, own, mine, width, mp):
    for m in range(mp):

        @pl.when(mine == m)
        def _():
            own[:, :width] = grad_y[:, m * width : (m + 1) * width]

    return low(tn(own[:, :width], inputs))


def flip(me, level):
    bit = 1 << level
    return me + bit - 2 * bit * lax.rem(me // bit, 2)


def upper(me, level):
    return lax.rem(me // (1 << level), 2)


def give_half(me, level, start, size, work, land, send, recv):
    half = size // 2
    mine = upper(me, level)
    at = pl.ds(pl.multiple_of(start + (1 - mine) * half, 16), half)
    copy = remote(work.at[at, :], land, send, recv, {"dp": flip(me, level)})
    copy.start()
    return copy, start + mine * half


def add_half(copy, start, half, work, land):
    copy.wait_recv()
    at = pl.ds(pl.multiple_of(start, 16), half)
    return low(work[at, :].astype(jnp.float32) + land[...].astype(jnp.float32))


def dense_kernel(
    dp, mp, hx, batch,
    partial, numeric, weights, n_next, b_next, vec,
    left_hbm, right_hbm, pair_hbm, bias_hbm, labels_hbm, dense_hbm,
    logits, grads_t, feat, fields, grad_gate, gyn1, a_out, b_out, small,
    n_gain_g, n_shift_g, b_gain_g, b_shift_g, left_g, right_g, bias_g,
    half_a, half_c, pooled, gate, own_term, n_slots, b_slots, n23, b2,
    yn, dn, yb, db, un, ub, gyn, gyb, pair_hi, pair_lo, pair_g, to_first, sums, spill,
    fsend, frecv, wsend, wrecv, ssend, srecv,
    gyb1, a_work, b_work, a_land, b_land, hsend, hrecv, own_cols,
    left, right, pair_t, bias, labels, dense_t, sem,
):
    brought = bring(
        (left_hbm, right_hbm, pair_hbm, bias_hbm, labels_hbm, dense_hbm),
        (left, right, pair_t, bias, labels, dense_t),
        sem,
    )
    me, mine = lax.axis_index("dp"), lax.axis_index("mp")
    core = lax.rem(mine, 2)
    chip = mine // 2
    chips = mp // 2
    other = mine + 1 - 2 * core
    rows = feat.shape[0]
    block = 256
    steps = rows // block
    h1, h2 = n23.shape[1], b2.shape[0]
    s1, s2 = h1 // mp, h2 // mp
    wide = feat.shape[1]
    gates = (weights.at[pl.ds(0, wide), :], weights.at[pl.ds(wide, wide), :])
    n1 = weights.at[pl.ds(2 * wide, h1), :]
    b1 = weights.at[pl.ds(2 * wide + h1, h2), :]
    num = numeric.shape[1]
    gcols = wide // mp
    half = partial.shape[0] // 2
    hail(dp, mp)
    near = lax.rem(me, 2)
    for slots, given in ((n_slots, n_next), (b_slots, b_next)):
        slots[mine] = given[mine]
        for k in range(1, chips):
            source = lax.rem(mine + 2 * k, mp)
            slots[source, near] = given[source, near]
    all_in(dp, mp)

    def rowset(i):
        return pl.ds(pl.multiple_of(i * block, block), block)

    def part(c):
        return pl.ds(pl.multiple_of(c * half, 16), half)

    def events(h):
        return pl.ds(h * (rows // 2), rows // 2)

    copies_a, copies_y, copies_b = [], [], []
    for h in range(2):
        copy = remote(
            partial.at[part(1 - core), events(h)], half_a.at[:, events(h)], fsend.at[h, 0], frecv.at[h, 0],
            {"mp": other},
        )
        copy.start()
        copies_a.append(copy)
    for copy in brought:
        copy.wait()
    for h in range(2):
        copies_a[h].wait_recv()
        half_c[chip, :, events(h)] = low(partial[part(core), events(h)] + half_a[:, events(h)])
        for k in range(1, chips):
            place = half_c.at[chip, :, events(h)]
            copy = remote(
                place, place, fsend.at[h, k], frecv.at[h, k], {"mp": lax.rem(mine + 2 * k, mp)}
            )
            copy.start()
            copies_y.append(copy)
    n_steps = split_relay(dp, mp, n_slots, wsend.at[0], wrecv.at[0], True)
    b_steps = split_relay(dp, mp, b_slots, wsend.at[1], wrecv.at[1], True)
    for relay in (n_steps, b_steps):
        relay[0]()
        relay[1]()
    heads = pair_t.shape[2]
    by_head = jnp.transpose(pair_t[...].reshape(hx * 16, heads))
    row = lax.broadcasted_iota(jnp.int32, (h1, heads), 0)
    col = lax.broadcasted_iota(jnp.int32, (h1, heads), 1)
    repeat = jnp.where(row // hx == col, 1.0, 0.0)
    tall = jnp.dot(repeat, by_head, precision=lax.Precision.HIGHEST, preferred_element_type=jnp.float32)
    row = lax.broadcasted_iota(jnp.int32, (h1, 16), 0)
    pick = jnp.zeros((h1, 16), jnp.float32)
    for i in range(hx):
        pick = jnp.where(row % hx == i, tall[:, i * 16 : (i + 1) * 16], pick)
    for i in range(0, h1, 80):
        row = lax.broadcasted_iota(jnp.int32, (80, h2), 0) + i
        col = lax.broadcasted_iota(jnp.int32, (80, h2), 1)
        pieces = jnp.concatenate([pick[i : i + 80, :]] * heads, axis=1)
        spread = jnp.where(row // hx == col // 16, pieces, 0.0)
        high = low(spread)
        pair_hi[i : i + 80, :] = high
        pair_lo[i : i + 80, :] = low(spread - high.astype(jnp.float32))
    for h in range(2):
        for copy in copies_y[h * (chips - 1) : (h + 1) * (chips - 1)]:
            copy.wait_recv()
        total = half_c[0, :, events(h)].astype(jnp.float32)
        for k in range(1, chips):
            total = total + half_c[k, :, events(h)].astype(jnp.float32)
        pooled[part(core), events(h)] = low(total)
        place = pooled.at[part(core), events(h)]
        copy = remote(place, place, fsend.at[h, chips], frecv.at[h, chips], {"mp": other})
        copy.start()
        copies_b.append(copy)
    feat[:, :num] = numeric[...]
    started = []

    def flipped(bits):
        to = me
        for level in range(dp.bit_length() - 1):
            if bits >> level & 1:
                to = flip(to, level)
        return to

    def push(slot, *values):
        width = -(-values[0].shape[1] // 128) * 128
        for r, value in enumerate(values):
            sums[slot, me, r : r + 1, : value.shape[1]] = value
        out = []
        for step in range(dp - 1, 0, -1):
            at = sums.at[slot, me, :, pl.ds(0, width)]
            copy = remote(
                at, at, ssend.at[slot, step - 1], srecv.at[slot, step - 1], {"dp": flipped(step)}
            )
            copy.start()
            out.append(copy)
        started.append(out)
        return slot, width, out

    def pull(sent):
        slot, width, out = sent
        for copy in out:
            copy.wait_recv()
        total = sums[slot, 0, :, :width]
        for d in range(1, dp):
            total = total + sums[slot, d, :, :width]
        return total

    def norm(sent, width):
        total = pull(sent)
        mean = total[0:1, :width] / batch
        var = total[1:2, :width] / batch - mean * mean
        return mean, lax.rsqrt(var + 1e-05)

    def activate(y_ref, d_ref, u_ref, layer, at, mean, rstd, gain, shift):
        normed = (y_ref[layer, at, :] - mean) * rstd
        z = gain * normed + shift
        s = sigmoid(z)
        u = z * s
        y_ref[layer, at, :] = normed
        d_ref[layer, at, :] = s + u * (1.0 - s)
        u = low(u)
        u_ref[layer, at, :] = u
        return u

    def gain_n(layer):
        return vec[2 + layer : 3 + layer, :h1], vec[5 + layer : 6 + layer, :h1]

    def gain_b(layer):
        return vec[8 + layer : 9 + layer, :h2], vec[10 + layer : 11 + layer, :h2]

    zero1 = jnp.zeros((1, h1), jnp.float32)
    zero2 = jnp.zeros((1, h2), jnp.float32)

    def loop(body, *start):
        return lax.fori_loop(0, steps, lambda i, carry: body(rowset(i), *carry), tuple(start))

    def gated(k, at):
        x = feat[at, :]
        value = 2.0 * sigmoid(nt(x, gates[k][...]) + vec[k : k + 1, :wide])
        gate[k, at, :] = value
        x = low(x.astype(jnp.float32) * value)
        fields[k, at, :] = x
        return x

    def gates_and_first(at, a, b):
        y = nt(gated(0, at), n1[...])
        yn[0, at, :] = y
        return a + column_sum(y), b + column_sum(y * y)

    a, b = zero1, zero1
    for h in range(2):
        copies_b[h].wait_recv()
        at = events(h)
        feat[at, num:] = low(jnp.transpose(pooled[:, at].astype(jnp.float32)))
        a, b = gates_and_first(at, a, b)
    sent_n = push(0, a, b)

    def broad_first(at, a, b):
        y = nt(gated(1, at), b1[...])
        yb[0, at, :] = y
        return a + column_sum(y), b + column_sum(y * y)

    sent_b = push(1, *loop(broad_first, zero2, zero2))
    n_steps[2]()
    b_steps[2]()
    n_steps[3]()
    for m in range(mp):
        for k in range(2):
            n23[k, m * s1 : (m + 1) * s1, :] = n_slots[m, k]
    mean_n1, rstd_n1 = norm(sent_n, h1)

    def narrow_second(at, a, b):
        y = nt(activate(yn, dn, un, 0, at, mean_n1, rstd_n1, *gain_n(0)), n23[0])
        yn[1, at, :] = y
        return a + column_sum(y), b + column_sum(y * y)

    sent_n = push(2, *loop(narrow_second, zero1, zero1))
    b_steps[3]()
    for m in range(mp):
        for k in range(2):
            row = (2 * m + k) * (s2 // 2)
            b2[row : row + s2 // 2, :] = b_slots[m, k]
    mean_b1, rstd_b1 = norm(sent_b, h2)

    def broad_second(at, a, b):
        y = nt(activate(yb, db, ub, 0, at, mean_b1, rstd_b1, *gain_b(0)), b2[...])
        yb[1, at, :] = y
        return a + column_sum(y), b + column_sum(y * y)

    sent_b = push(3, *loop(broad_second, zero2, zero2))
    mean_n2, rstd_n2 = norm(sent_n, h1)

    def narrow_third(at, a, b):
        y = nt(activate(yn, dn, un, 1, at, mean_n2, rstd_n2, *gain_n(1)), n23[1])
        yn[2, at, :] = y
        return a + column_sum(y), b + column_sum(y * y)

    sent_n = push(4, *loop(narrow_third, zero1, zero1))
    label = jnp.transpose(jnp.broadcast_to(labels[...].astype(jnp.float32), (8, rows)))[:, 0:1]
    own_term[:, 0:1] = label
    pair_g[...] = jnp.zeros_like(pair_g)
    mean_b2, rstd_b2 = norm(sent_b, h2)

    def broad_out(at):
        second = activate(yb, db, ub, 1, at, mean_b2, rstd_b2, *gain_b(1))
        to_first[at, :] = left[...] + (nt(second, pair_hi[...]) + nt(second, pair_lo[...]))
        return ()

    loop(broad_out)
    mean_n3, rstd_n3 = norm(sent_n, h1)
    to_right = right[...].reshape(1, h2)

    def join_narrow(at, l_sum, g_sum, a, b):
        first = activate(yn, dn, un, 2, at, mean_n3, rstd_n3, *gain_n(2)).astype(jnp.float32)
        second = ub[1, at, :].astype(jnp.float32)
        logit = (
            jnp.sum(first * to_first[at, :], axis=1, keepdims=True)
            + jnp.sum(second * to_right, axis=1, keepdims=True)
            + bias[...]
        )
        g = sigmoid(logit) - own_term[at, 0:1]
        own_term[at, 1:2] = logit
        own_term[at, 2:3] = g
        gz = g * to_first[at, :] * dn[2, at, :]
        dn[2, at, :] = gz
        return (
            l_sum + column_sum(g * first), g_sum + column_sum(g),
            a + column_sum(gz), b + column_sum(gz * yn[2, at, :]),
        )

    l_sum, g_sum, a, b = loop(join_narrow, zero1, jnp.zeros((1, 1), jnp.float32), zero1, zero1)
    sent_n = push(5, a, b)

    def join_broad(at, r_sum, a, b):
        first = un[2, at, :]
        second = ub[1, at, :]
        g = own_term[at, 2:3]
        turned = nn(first, pair_hi[...]) + nn(first, pair_lo[...])
        pair_g[...] += tn(second, low(g * first.astype(jnp.float32)))
        gz = g * (to_right + turned) * db[1, at, :]
        db[1, at, :] = gz
        return (
            r_sum + column_sum(g * second.astype(jnp.float32)),
            a + column_sum(gz), b + column_sum(gz * yb[1, at, :]),
        )

    r_sum, a, b = loop(join_broad, zero2, zero2, zero2)
    sent_b = push(6, a, b)
    sums[10, me, 1:2, 512:513] = g_sum
    sent_join = push(10, r_sum, l_sum)
    logits[...] = jnp.transpose(own_term[:, 0:128])[1:2, :]

    def grad_y(gz, normed, rstd, gain, total):
        return low(gain * rstd * (gz - total[0:1] / batch - normed * (total[1:2] / batch)))

    main = a_work.shape[1]
    rest = h2 - main
    parts = main // rest
    tall_a = s2 + s1
    short = -(-tall_a // parts)
    a_work[...] = jnp.zeros_like(a_work)
    b_work[...] = jnp.zeros_like(b_work)
    size_a, size_b = a_work.shape[0], b_work.shape[0]
    folded = jnp.zeros((16, h1), jnp.float32)
    col = lax.broadcasted_iota(jnp.int32, (16, h1), 1)
    for h in range(heads):
        folded = folded + jnp.where(col // hx == h, pair_g[h * 16 : (h + 1) * 16, :], 0.0)
    b_work[size_b - 16 :, :h1] = low(folded)
    t_n3 = pull(sent_n)[:, :h1]

    def back_n3(at, a, b):
        g = grad_y(dn[2, at, :], yn[2, at, :], rstd_n3, gain_n(2)[0], t_n3)
        gyn[1, at, :] = g
        gz = nn(g, n23[1]) * dn[1, at, :]
        dn[1, at, :] = gz
        return a + column_sum(gz), b + column_sum(gz * yn[1, at, :])

    sent_n = push(7, *loop(back_n3, zero1, zero1))
    grad_n3 = weight_grad(gyn.at[1], un[1], own_cols, mine, s1, mp)
    t_b2 = pull(sent_b)[:, :h2]

    def back_b2(at, a, b):
        g = grad_y(db[1, at, :], yb[1, at, :], rstd_b2, gain_b(1)[0], t_b2)
        gyb[at, :] = g
        gz = nn(g, b2[...]) * db[0, at, :]
        db[0, at, :] = gz
        return a + column_sum(gz), b + column_sum(gz * yb[0, at, :])

    sent_b = push(8, *loop(back_b2, zero2, zero2))
    grad_b2 = weight_grad(gyb, ub[0], own_cols, mine, s2, mp)
    a_work[:s2, :] = grad_b2[:, :main]
    spill[:s2, :] = grad_b2[:, main:]
    t_n2 = pull(sent_n)[:, :h1]

    def back_n2(at, a, b):
        g = grad_y(dn[1, at, :], yn[1, at, :], rstd_n2, gain_n(1)[0], t_n2)
        gyn[0, at, :] = g
        gz = nn(g, n23[0]) * dn[0, at, :]
        dn[0, at, :] = gz
        return a + column_sum(gz), b + column_sum(gz * yn[0, at, :])

    sent_n = push(9, *loop(back_n2, zero1, zero1))
    grad_n2 = weight_grad(gyn.at[0], un[0], own_cols, mine, s1, mp)
    a_work[s2:tall_a, :] = jnp.concatenate([grad_n2, grad_n3], axis=1)[:, :main]
    spill[s2:tall_a, :] = jnp.concatenate([grad_n2, grad_n3], axis=1)[:, main:]
    for p in range(parts):
        n = min(short, tall_a - p * short)
        a_work[tall_a : tall_a + n, p * rest : (p + 1) * rest] = spill[p * short : p * short + n, :]
    copy_ax, start_a = give_half(me, 0, 0, size_a, a_work, a_land.at[pl.ds(0, size_a // 2), :], hsend.at[0], hrecv.at[0])
    t_b1 = pull(sent_b)[:, :h2]

    def gate_back(k, at, grad):
        x = feat[at, :].astype(jnp.float32)
        value = gate[k, at, :]
        g = low(grad * x * value * (1.0 - 0.5 * value))
        grad_gate[k, at, :] = g
        return grad * value, g

    def back_b1(at):
        g = grad_y(db[0, at, :], yb[0, at, :], rstd_b1, gain_b(0)[0], t_b1)
        gyb1[at, :] = g
        own_term[at, :] = gate_back(1, at, nn(g, b1[...]))[0]
        return ()

    loop(back_b1)
    b_work[:s2, :wide] = weight_grad(gyb1, fields[1], own_cols, mine, s2, mp)
    b_work[s2 : s2 + gcols, :wide] = weight_grad(grad_gate.at[1], feat[...], own_cols, mine, gcols, mp)
    copy_bx, start_b = give_half(me, 0, 0, size_b, b_work, b_land, hsend.at[2], hrecv.at[2])
    a_work[pl.ds(pl.multiple_of(start_a, 16), size_a // 2), :] = add_half(
        copy_ax, start_a, size_a // 2, a_work, a_land.at[pl.ds(0, size_a // 2), :]
    )
    copy_az, start_a = give_half(
        me, 1, start_a, size_a // 2, a_work, a_land.at[pl.ds(size_a // 2, size_a // 4), :], hsend.at[1], hrecv.at[1]
    )
    t_n1 = pull(sent_n)[:, :h1]

    def back_n1(at, ga, gb, ne):
        g = grad_y(dn[0, at, :], yn[0, at, :], rstd_n1, gain_n(0)[0], t_n1)
        gyn1[at, :] = g
        term, g0 = gate_back(0, at, nn(g, n1[...]))
        g1 = grad_gate[1, at, :]
        whole = nn(g0, gates[0][...]) + nn(g1, gates[1][...]) + term + own_term[at, :]
        whole = low(whole).astype(jnp.float32)
        own_term[at, :] = whole
        ne = ne + column_sum(whole[:, :num] * widen_dense(dense_t[:, at], 16))
        return ga + column_sum(g0.astype(jnp.float32)), gb + column_sum(g1.astype(jnp.float32)), ne

    zero_g = jnp.zeros((1, wide), jnp.float32)
    ga, gb, ne = loop(back_n1, zero_g, zero_g, jnp.zeros((1, num), jnp.float32))
    grads_t[...] = low(jnp.transpose(own_term[:, num:]))
    small[...] = jnp.zeros_like(small)
    small[0:1, :gcols] = own_columns(ga, mine, gcols, mp)
    small[1:2, :gcols] = own_columns(gb, mine, gcols, mp)
    small[2:3, :num] = ne
    for layer, t in enumerate((t_n1, t_n2, t_n3)):
        n_shift_g[layer : layer + 1, :] = own_columns(t[0:1], mine, s1, mp)
        n_gain_g[layer : layer + 1, :] = own_columns(t[1:2], mine, s1, mp)
    for layer, t in enumerate((t_b1, t_b2)):
        b_shift_g[layer : layer + 1, :] = own_columns(t[0:1], mine, s2, mp)
        b_gain_g[layer : layer + 1, :] = own_columns(t[1:2], mine, s2, mp)
    total = pull(sent_join)
    right_g[...] = total[0:1, :h2]
    left_g[...] = total[1:2, :h1]
    bias_g[...] = total[1:2, 512:513]
    a_out[...] = add_half(
        copy_az, start_a, size_a // 4, a_work, a_land.at[pl.ds(size_a // 2, size_a // 4), :]
    )
    b_out[...] = add_half(copy_bx, start_b, size_b // 2, b_work, b_land)
    for copy in [copy_ax, copy_az, copy_bx] + copies_a + copies_y + copies_b:
        copy.wait_send()
    for group in started:
        for copy in group:
            copy.wait_send()


def reduce_kernel(
    dp, mp,
    grads, feat, fields, grad_gate, gyn1, a_in, b_in, small,
    shares, a_full, b_full, c_full, small_out,
    t_work, t_land, t_slots, s_slots, a_work, a_land, b_work, b_land, c_work, c_land, c_slots, own_cols,
    tsend, trecv, ysend, yrecv, ssend, srecv, asend, arecv, bsend, brecv, csend, crecv,
):
    tall = grads.shape[0] // dp
    me, mine = lax.axis_index("dp"), lax.axis_index("mp")
    hail(dp, mp)
    levels = dp.bit_length() - 1
    far = dp // 2
    side, place = upper(me, 0), me // 2
    size_a, size_b, size_c = a_full.shape[0], b_full.shape[0], c_full.shape[0]
    s_slots[me] = small[...]
    pending = []
    all_in(dp, mp)

    def send_to(copy):
        copy.start()
        pending.append(copy)
        return copy

    def across(k):
        return {"dp": lax.rem(me + 2 * k, dp)}

    def rows_at(start, size):
        return pl.ds(pl.multiple_of(start, 16), size)

    half_t = grads.shape[0] // 2
    copy_t = send_to(
        remote(grads.at[rows_at((1 - side) * half_t, half_t), :], t_land, tsend.at[0], trecv.at[0], {"dp": flip(me, 0)})
    )
    start_a, start_b = 0, side * (size_b // 2)
    for level in range(2):
        start_a = start_a + upper(me, level) * (size_a >> (level + 1))
    a_work[...] = a_in[...]
    b_work[...] = b_in[...]

    def halves(name, level, work, land, size, sems, off):
        half = size // 2
        mine_up = upper(me, level)
        copy = send_to(
            remote(
                work.at[rows_at(off + (1 - mine_up) * half, half), :], land.at[pl.ds(0, half), :],
                sems[0].at[level], sems[1].at[level], {"dp": flip(me, level)},
            )
        )
        return copy, off + mine_up * half, half

    def fold(step, work, land):
        copy, off, half = step
        copy.wait_recv()
        at = rows_at(off, half)
        work[at, :] = low(work[at, :].astype(jnp.float32) + land[pl.ds(0, half), :].astype(jnp.float32))
        return off, half

    def double(level, full, start, size, sems):
        at = full.at[rows_at(start, size), :]
        copy = send_to(
            remote(at, at, sems[0].at[levels + level], sems[1].at[levels + level], {"dp": flip(me, level)})
        )
        return copy, start - upper(me, level) * size, size * 2

    sems_a, sems_b = (asend, arecv), (bsend, brecv)
    step_b = halves("b", 1, b_work, b_land.at[0], size_b // 2, sems_b, 0)
    step_a = halves("a", 2, a_work, a_land.at[0], size_a // 4, sems_a, 0) if levels > 2 else None
    gcols, s1 = feat.shape[1] // mp, gyn1.shape[1] // mp
    wide = feat.shape[1]
    c_work[...] = jnp.zeros_like(c_work)
    c_work[:gcols, :wide] = weight_grad(grad_gate.at[0], feat[...], own_cols, mine, gcols, mp)
    c_work[gcols : gcols + s1, :wide] = weight_grad(gyn1, fields[0], own_cols, mine, s1, mp)
    half_c = size_c // 2
    copy_c = send_to(
        remote(c_work.at[rows_at((1 - side) * half_c, half_c), :], c_land, csend.at[0], crecv.at[0], {"dp": flip(me, 0)})
    )
    small_copies = spread_dp(dp, lambda k: s_slots.at[k], ssend, srecv)

    def onward(back, level, full, sems):
        copy, start, size = back
        copy.wait_recv()
        return double(level, full, start, size, sems)

    off_b, held_b = fold(step_b, b_work, b_land.at[0])
    step_b = halves("b", 2, b_work, b_land.at[1], held_b, sems_b, off_b)
    off_a, held_a = fold(step_a, a_work, a_land.at[0])
    for level in range(3, levels):
        step_a = halves("a", level, a_work, a_land.at[level - 2], held_a, sems_a, off_a)
        off_a, held_a = fold(step_a, a_work, a_land.at[level - 2])
    start_a = start_a + off_a
    a_full[rows_at(start_a, held_a), :] = a_work[rows_at(off_a, held_a), :]
    back_a = double(levels - 1, a_full, start_a, held_a, sems_a)
    off_b, held_b = fold(step_b, b_work, b_land.at[1])
    for level in range(3, levels):
        step_b = halves("b", level, b_work, b_land.at[level - 1], held_b, sems_b, off_b)
        off_b, held_b = fold(step_b, b_work, b_land.at[level - 1])
    start_b = start_b + off_b
    b_full[rows_at(start_b, held_b), :] = b_work[rows_at(off_b, held_b), :]
    back_b = double(levels - 1, b_full, start_b, held_b, sems_b)
    for level in range(levels - 2, 0, -1):
        back_a = onward(back_a, level, a_full, sems_a)
    copy_t.wait_recv()
    at = rows_at(side * half_t, half_t)
    t_work[...] = low(grads[at, :].astype(jnp.float32) + t_land[...].astype(jnp.float32))
    t_copies = []
    for k in range(1, far):
        to = lax.rem(place + k, far)
        t_copies.append(
            send_to(
                remote(t_work.at[rows_at(to * tall, tall), :], t_slots.at[k - 1], tsend.at[k], trecv.at[k], across(k))
            )
        )
    copy_c.wait_recv()
    at = rows_at(side * half_c, half_c)
    c_work[at, :] = low(c_work[at, :].astype(jnp.float32) + c_land[...].astype(jnp.float32))
    piece = half_c // far
    c_copies = []
    for k in range(1, far):
        to = lax.rem(place + k, far)
        c_copies.append(
            send_to(
                remote(
                    c_work.at[rows_at(side * half_c + to * piece, piece), :], c_slots.at[k - 1],
                    csend.at[k], crecv.at[k], across(k),
                )
            )
        )
    for level in range(levels - 2, 0, -1):
        back_b = onward(back_b, level, b_full, sems_b)
    back_a = onward(back_a, 0, a_full, sems_a)
    own = rows_at(side * half_c + place * piece, piece)
    total = c_work[own, :].astype(jnp.float32)
    for k in range(1, far):
        c_copies[k - 1].wait_recv()
        total = total + c_slots[k - 1].astype(jnp.float32)
    c_full[own, :] = low(total)
    c_back = []
    for k in range(1, far):
        c_back.append(
            send_to(
                remote(c_full.at[own, :], c_full.at[own, :], csend.at[far + k], crecv.at[far + k], across(k))
            )
        )
    total = t_work[rows_at(place * tall, tall), :].astype(jnp.float32)
    for k in range(1, far):
        t_copies[k - 1].wait_recv()
        total = total + t_slots[k - 1].astype(jnp.float32)
    shares[mine] = low(total)
    started = relay_own(mp, lambda k: shares.at[k], ysend, yrecv)
    back_b = onward(back_b, 0, b_full, sems_b)
    for copy in c_back:
        copy.wait_recv()
    at = c_full.at[rows_at(side * half_c, half_c), :]
    last_c = send_to(remote(at, at, csend.at[far], crecv.at[far], {"dp": flip(me, 0)}))
    relay_rest(mp, lambda k: shares.at[k], ysend, yrecv, started)
    for copy in small_copies:
        copy.wait_recv()
    value = s_slots[0]
    for d in range(1, dp):
        value = value + s_slots[d]
    small_out[...] = value
    back_a[0].wait_recv()
    last_c.wait_recv()
    back_b[0].wait_recv()
    for copy in pending + small_copies:
        copy.wait_send()


def final_kernel(mp, hx, *refs):
    (
        shares, a_full, b_full, c_full, small, logits_in, n_gain_in, n_shift_in, b_gain_in, b_shift_in,
        left_in, right_in, bias_in,
    ) = refs[:13]
    results, places, sem = refs[13:30], refs[30:47], refs[47]
    (
        logits, num_g, table_g, gate_g, gate_bias_g, n_first_g, n_rest_g, n_gain_g, n_shift_g,
        b_first_g, b_rest_g, b_gain_g, b_shift_g, left_g, right_g, pair_g, bias_g,
    ) = places
    leaving = {}

    def leave(*which):
        for i in which:
            leaving[i] = pltpu.make_async_copy(places[i], results[i], sem.at[i])
            leaving[i].start()

    gcols, s1, s2, h1 = gate_g.shape[0], n_first_g.shape[0], b_first_g.shape[0], n_rest_g.shape[2]
    wide = n_first_g.shape[1]

    def full(work, row, count, col, width):
        return work[row : row + count, col : col + width].astype(jnp.float32)

    blocks = shares.shape[1] // 16
    for m in range(mp):
        for b in range(blocks):
            table_g[:, (m * blocks + b) * HI : (m * blocks + b + 1) * HI] = shares[
                m, b * 16 : (b + 1) * 16, :
            ].astype(jnp.float32)
    leave(2)
    gate_g[:, 0, :] = full(c_full, 0, gcols, 0, wide)
    gate_g[:, 1, :] = full(b_full, s2, gcols, 0, wide)
    leave(3)
    n_first_g[...] = full(c_full, gcols, s1, 0, wide)
    b_first_g[...] = full(b_full, 0, s2, 0, wide)
    leave(5, 9)
    main = a_full.shape[1]
    rest = 2 * h1 - main
    parts = main // rest
    tall_a = s2 + s1
    short = -(-tall_a // parts)
    tail = jnp.concatenate(
        [
            full(a_full, tall_a, min(short, tall_a - p * short), p * rest, rest)
            for p in range(parts)
        ],
        axis=0,
    )
    b_rest_g[:, :main] = full(a_full, 0, s2, 0, main)
    b_rest_g[:, main:] = tail[:s2]
    leave(10)
    both = jnp.concatenate([full(a_full, s2, s1, 0, main), tail[s2:]], axis=1)
    n_rest_g[:, 0, :] = both[:, :h1]
    n_rest_g[:, 1, :] = both[:, h1:]
    leave(6)
    heads = pair_g.shape[2]
    pairs = b_full[b_full.shape[0] - 16 :, :h1]
    row = lax.broadcasted_iota(jnp.int32, (h1, heads), 0)
    col = lax.broadcasted_iota(jnp.int32, (h1, heads), 1)
    for i in range(hx):
        choose = jnp.where(row == col * hx + i, 1.0, 0.0).astype(jnp.bfloat16)
        pair_g[i] = nn(pairs, choose)
    fields, width = num_g.shape
    gate_bias_g[...] = small[0:2, :gcols]
    spread = jnp.broadcast_to(small[2:3, : fields * width], (fields, fields * width))
    row = lax.broadcasted_iota(jnp.int32, spread.shape, 0)
    col = lax.broadcasted_iota(jnp.int32, spread.shape, 1)
    spread = jnp.where(col // width == row, spread, 0.0)
    total = spread[:, :width]
    for i in range(1, fields):
        total = total + spread[:, i * width : (i + 1) * width]
    num_g[...] = total
    logits[...] = logits_in[...]
    n_gain_g[...] = n_gain_in[...]
    n_shift_g[...] = n_shift_in[...]
    b_gain_g[...] = b_gain_in[...]
    b_shift_g[...] = b_shift_in[...]
    left_g[...] = left_in[...]
    right_g[...] = right_in[...].reshape(right_g.shape)
    bias_g[...] = bias_in[...]
    leave(*[i for i in range(17) if i not in leaving])
    for copy in leaving.values():
        copy.wait()


def f32(*shape):
    return jax.ShapeDtypeStruct(shape, jnp.float32)


def b16(*shape):
    return jax.ShapeDtypeStruct(shape, jnp.bfloat16)


def held(*shape):
    return pltpu.VMEM(shape, jnp.float32)


def held16(*shape):
    return pltpu.VMEM(shape, jnp.bfloat16)


def dma(*shape):
    return pltpu.SemaphoreType.DMA(shape)


def shards(
    dense_values,
    field_ids,
    lengths,
    labels,
    num_embed,
    embed_table,
    gate_weight,
    gate_bias,
    narrow_first,
    narrow_rest,
    narrow_gain,
    narrow_shift,
    broad_first,
    broad_rest,
    broad_gain,
    broad_shift,
    joining_left,
    joining_right,
    joining_pair,
    joining_bias,
):
    dp, mp = lax.axis_size("dp"), lax.axis_size("mp")
    chips = mp // 2
    rows = dense_values.shape[0]
    cats, slots = field_ids.shape[:2]
    width, own_rows = embed_table.shape
    num = dense_values.shape[1] * width
    wide = gate_weight.shape[2]
    gcols = gate_weight.shape[1]
    s1, s2 = narrow_first.shape[0], broad_first.shape[0]
    h1, h2 = s1 * mp, s2 * mp
    hx = joining_pair.shape[1]
    bits = (cats * rows - 1).bit_length()
    dense_t = dense_values.T
    tall = own_rows // mp // HI * 16
    vregs = -(-(cats * slots * rows) // (2 * CHUNK)) * (2 * CHUNK) // 1024
    first_args = (
        embed_table, jnp.transpose(gate_weight, (1, 0, 2)), narrow_first, gate_bias,
        narrow_gain, narrow_shift, broad_gain, broad_shift, broad_first,
        field_ids, lengths, dense_t, num_embed, jnp.transpose(narrow_rest, (1, 0, 2)), broad_rest,
    )
    t2, keys, numeric, weights, vec, n_next, b_next = pl.pallas_call(
        functools.partial(first_kernel, dp, mp, own_rows, bits),
        out_shape=(
            b16(dp * tall, HI),
            jax.ShapeDtypeStruct((2, vregs * 8, 128), jnp.int32),
            b16(rows, num),
            b16(2 * wide + h1 + h2, wide),
            f32(16, 896),
            b16(mp, 2, s1, h1),
            b16(mp, 2, s2 // 2, h2),
        ),
        in_specs=[ANY] * 15,
        out_specs=(VM,) * 7,
        scratch_shapes=[pltpu.VMEM(x.shape, x.dtype) for x in first_args]
        + [
            pltpu.VMEM((vregs * 8, 128), jnp.int32),
            held16(mp, gcols, wide),
            held16(mp, 2, gcols // 2, wide),
            held16(mp, 2, s1 // 2, wide),
            held16(mp, 2, s2 // 2, wide),
            held(mp, 16, 256),
            dma(dp - 1),
            dma(dp - 1),
            dma(2, mp),
            dma(2, mp),
            dma(3, 4 * chips),
            dma(3, 4 * chips),
            dma(2, 4 * chips),
            dma(2, 4 * chips),
            dma(15),
        ],
        compiler_params=params(0, 54),
        name="first",
    )(*first_args)
    partial = pl.pallas_call(
        functools.partial(lookup_kernel, cats, rows, bits),
        out_shape=f32(cats * 16, rows),
        in_specs=[VM] * 2,
        out_specs=VM,
        scratch_shapes=[held((cats + WINDOW) * 16, rows)],
        compiler_params=params(None, 16),
        cost_estimate=pl.CostEstimate(flops=8 * 10**9, bytes_accessed=2 * 10**6, transcendentals=0),
        name="lookup",
    )(keys, t2)

    def up(x, n):
        return -(-x // n) * n

    main = wide // 128 * 128 + 128
    short = -(-(s1 + s2) // (main // (h2 - main)))
    a_rows = up(s1 + s2 + short, 16 * dp)
    b_rows = up(s2 + gcols, 16) + 16
    b_rows = up(b_rows, 16 * dp)
    c_rows = up(gcols + s1, 16 * dp)
    levels = dp.bit_length() - 1
    dense_args = (
        joining_left.reshape(1, h1), joining_right,
        jnp.transpose(joining_pair, (1, 2, 0)), joining_bias.reshape(1, 1), labels.reshape(1, rows), dense_t,
    )
    (
        logits, grads_t, feat, fields, grad_gate, gyn1, a_part, b_part, small,
        n_gain_g, n_shift_g, b_gain_g, b_shift_g, left_g, right_g, bias_g,
    ) = pl.pallas_call(
        functools.partial(dense_kernel, dp, mp, hx, float(rows * dp)),
        out_shape=(
            f32(1, rows),
            b16(cats * 16, rows),
            b16(rows, wide),
            b16(2, rows, wide),
            b16(2, rows, wide),
            b16(rows, h1),
            b16(a_rows // 4, main),
            b16(b_rows // 2, main),
            f32(8, 256),
            f32(3, s1),
            f32(3, s1),
            f32(2, s2),
            f32(2, s2),
            f32(1, h1),
            f32(1, h2),
            f32(1, 1),
        ),
        in_specs=[VM] * 6 + [ANY] * 6,
        out_specs=(VM,) * 16,
        scratch_shapes=[
            held(cats * 8, rows),
            held16(chips, cats * 8, rows),
            held16(cats * 16, rows),
            held(2, rows, wide),
            held(rows, wide),
            held16(mp, 2, s1, h1),
            held16(mp, 2, s2 // 2, h2),
            held16(2, h1, h1),
            held16(h2, h2),
            held(3, rows, h1),
            held(3, rows, h1),
            held(2, rows, h2),
            held(2, rows, h2),
            held16(3, rows, h1),
            held16(2, rows, h2),
            held16(2, rows, h1),
            held16(rows, h2),
            held16(h1, h2),
            held16(h1, h2),
            held(h2, h1),
            held(rows, h1),
            held(11, dp, 2, 896),
            held16(s1 + s2, h2 - main),
            dma(2, chips + 1),
            dma(2, chips + 1),
            dma(2, 4 * chips),
            dma(2, 4 * chips),
            dma(11, dp - 1),
            dma(11, dp - 1),
            held16(rows, h2),
            held16(a_rows, main),
            held16(b_rows, main),
            held16(a_rows * 3 // 4, main),
            held16(b_rows // 2, main),
            dma(3),
            dma(3),
            held16(rows, up(max(gcols, s1, s2), 128)),
        ]
        + [pltpu.VMEM(x.shape, x.dtype) for x in dense_args]
        + [dma(6)],
        compiler_params=params(1, 39 + dp // 16),
        name="dense",
    )(partial, numeric, weights, n_next, b_next, vec, *dense_args)
    row_sums = pl.pallas_call(
        functools.partial(scatter_kernel, cats, rows, bits),
        out_shape=b16(dp * tall, HI),
        in_specs=[VM] * 2,
        out_specs=VM,
        scratch_shapes=[held(dp * tall, HI), held16((cats + WINDOW_BACK) * 16, rows)],
        compiler_params=params(None, 16),
        cost_estimate=pl.CostEstimate(flops=8 * 10**9, bytes_accessed=2 * 10**6, transcendentals=0),
        name="scatter",
    )(keys, grads_t)
    shares, a_full, b_full, c_full, small = pl.pallas_call(
        functools.partial(reduce_kernel, dp, mp),
        out_shape=(
            b16(mp, tall, HI),
            b16(a_rows, main),
            b16(b_rows, main),
            b16(c_rows, main),
            f32(8, 256),
        ),
        in_specs=[VM] * 8,
        out_specs=(VM,) * 5,
        scratch_shapes=[
            held16(dp // 2 * tall, HI),
            held16(dp // 2 * tall, HI),
            held16(dp // 2 - 1, tall, HI),
            held(dp, 8, 256),
            held16(a_rows // 4, main),
            held16(max(levels - 2, 1), a_rows // 8, main),
            held16(b_rows // 2, main),
            held16(max(levels - 1, 1), b_rows // 4, main),
            held16(c_rows, main),
            held16(c_rows // 2, main),
            held16(dp // 2 - 1, c_rows // dp, main),
            held16(rows, up(max(gcols, s1, s2), 128)),
            dma(dp // 2),
            dma(dp // 2),
            dma(mp),
            dma(mp),
            dma(dp - 1),
            dma(dp - 1),
            dma(2 * levels),
            dma(2 * levels),
            dma(2 * levels),
            dma(2 * levels),
            dma(dp),
            dma(dp),
        ],
        compiler_params=params(2, 24),
        name="reduce",
    )(row_sums, feat, fields, grad_gate, gyn1, a_part, b_part, small)
    final_shapes = (
        f32(1, rows),
        f32(*num_embed.shape),
        f32(width, own_rows),
        f32(gcols, 2, wide),
        f32(2, gcols),
        f32(s1, wide),
        f32(s1, 2, h1),
        f32(3, s1),
        f32(3, s1),
        f32(s2, wide),
        f32(s2, h2),
        f32(2, s2),
        f32(2, s2),
        f32(1, h1),
        f32(h2),
        f32(hx, width, joining_pair.shape[0]),
        f32(1, 1),
    )
    outs = pl.pallas_call(
        functools.partial(final_kernel, mp, hx),
        out_shape=final_shapes,
        in_specs=[VM] * 13,
        out_specs=(ANY,) * 17,
        scratch_shapes=[pltpu.VMEM(x.shape, x.dtype) for x in final_shapes] + [dma(17)],
        compiler_params=params(None, 16),
        name="final",
    )(
        shares, a_full, b_full, c_full, small, logits, n_gain_g, n_shift_g, b_gain_g, b_shift_g,
        left_g, right_g, bias_g,
    )
    outs = list(outs)
    outs[0] = outs[0].reshape(rows)
    outs[3] = jnp.transpose(outs[3], (1, 0, 2))
    outs[6] = jnp.transpose(outs[6], (1, 0, 2))
    outs[13] = outs[13].reshape(h1)
    outs[15] = jnp.transpose(outs[15], (2, 0, 1))
    outs[16] = outs[16].reshape(1)
    return tuple(outs)


def solution(mesh):
    placed = (
        P("dp", None),
        P(None, None, "dp"),
        P(None, "dp"),
        P("dp"),
        P(),
        P(None, "dp"),
        P(None, "mp", None),
        P(None, "mp"),
        P("mp", None),
        P(None, "mp", None),
        P(None, "mp"),
        P(None, "mp"),
        P("mp", None),
        P("mp", None),
        P(None, "mp"),
        P(None, "mp"),
        P(),
        P(),
        P(),
        P(),
    )
    return jax.shard_map(
        shards,
        mesh=mesh,
        in_specs=placed,
        out_specs=(
            P("dp"),
            P(),
            P(None, "dp"),
            P(None, "mp", None),
            P(None, "mp"),
            P("mp", None),
            P(None, "mp", None),
            P(None, "mp"),
            P(None, "mp"),
            P("mp", None),
            P("mp", None),
            P(None, "mp"),
            P(None, "mp"),
            P(),
            P(),
            P(),
            P(),
        ),
        check_vma=False,
    )
```
